128 devices in a mesh: fsdp: 8 (over z, core), ctx: 2 (over y_hi), tp: 8 (over x, y_lo).
Axes of the slice: x: 4, y: 4 (y_hi: 2, y_lo: 2; y = y_hi * 2 + y_lo), z: 4, core: 2. Of those that a mesh axis runs over, the one named last changes fastest.
Arguments:
- inputs: bfloat16 [8, 2048, 2048], P('fsdp', ('ctx', 'tp')), may hold values from -6 to 6
- cotangent: bfloat16 [8, 2048, 2048], P('fsdp', 'ctx'), may hold values from -6 to 6
- document_index: int32 [8, 2048], P('fsdp'), may hold values from 0 to 20, as said below
- positions: int32 [8, 2048], P('fsdp'), may hold values from 0 to 1310, as said below
- gains: float32 [4352], P(('fsdp', 'ctx')), may hold values from 0.5 to 1.5
- gains_first: float32 [4352], P(('fsdp', 'ctx')), may hold values from -128 to 128
- gains_second: float32 [4352], P(('fsdp', 'ctx')), may hold values from 1939.0464 to 7741.44
- project_weight: float32 [2048, 4096], P(('fsdp', 'ctx'), 'tp'), may hold values from -0.125 to 0.125
- project_first: float32 [2048, 4096], P(('fsdp', 'ctx'), 'tp'), may hold values from -80 to 80
- project_second: float32 [2048, 4096], P(('fsdp', 'ctx'), 'tp'), may hold values from 861.7984 to 3440.64
- output_weight: float32 [2048, 2048], P('tp', ('fsdp', 'ctx')), may hold values from -1 to 1
- output_first: float32 [2048, 2048], P('tp', ('fsdp', 'ctx')), may hold values from -12 to 12
- output_second: float32 [2048, 2048], P('tp', ('fsdp', 'ctx')), may hold values from 19.390465 to 77.4144
- expand_weight: float32 [2048, 12288], P(('fsdp', 'ctx'), 'tp'), may hold values from -0.125 to 0.125
- expand_first: float32 [2048, 12288], P(('fsdp', 'ctx'), 'tp'), may hold values from -32 to 32
- expand_second: float32 [2048, 12288], P(('fsdp', 'ctx'), 'tp'), may hold values from 105.570305 to 421.4784
- shrink_weight: float32 [6144, 2048], P('tp', ('fsdp', 'ctx')), may hold values from -0.078125 to 0.078125
- shrink_first: float32 [6144, 2048], P('tp', ('fsdp', 'ctx')), may hold values from -48 to 48
- shrink_second: float32 [6144, 2048], P('tp', ('fsdp', 'ctx')), may hold values from 310.24744 to 1238.6304
Outputs:
- outputs: bfloat16 [8, 2048, 2048], P('fsdp', ('ctx', 'tp'))
- input_grad: bfloat16 [8, 2048, 2048], P('fsdp', ('ctx', 'tp'))
- gains_mean: float32 [4352], P(('fsdp', 'ctx'))
- gains_square: float32 [4352], P(('fsdp', 'ctx'))
- gains_updated: float32 [4352], P(('fsdp', 'ctx'))
- project_mean: float32 [2048, 4096], P(('fsdp', 'ctx'), 'tp')
- project_square: float32 [2048, 4096], P(('fsdp', 'ctx'), 'tp')
- project_updated: float32 [2048, 4096], P(('fsdp', 'ctx'), 'tp')
- output_mean: float32 [2048, 2048], P('tp', ('fsdp', 'ctx'))
- output_square: float32 [2048, 2048], P('tp', ('fsdp', 'ctx'))
- output_updated: float32 [2048, 2048], P('tp', ('fsdp', 'ctx'))
- expand_mean: float32 [2048, 12288], P(('fsdp', 'ctx'), 'tp')
- expand_square: float32 [2048, 12288], P(('fsdp', 'ctx'), 'tp')
- expand_updated: float32 [2048, 12288], P(('fsdp', 'ctx'), 'tp')
- shrink_mean: float32 [6144, 2048], P('tp', ('fsdp', 'ctx'))
- shrink_square: float32 [6144, 2048], P('tp', ('fsdp', 'ctx'))
- shrink_updated: float32 [6144, 2048], P('tp', ('fsdp', 'ctx'))
The draws below stay inside these ranges and needn't reach their ends.
Inputs may be any that keep to these rules, and one draw needn't show every extreme that they name: `document_index`: in each sequence the numbers start at 0 and never fall; each document holds 60 to 800 tokens, and every sequence holds one document of exactly 800 tokens that covers the sequence's middle; in each draw at least one sequence holds the most documents that this allows. `positions`: within a document they rise by one from token to token, from a first position below 512; a sequence's first document starts at 0 and its document of 800 tokens at 511.
All inputs are finite; a program needn't handle non-finite values.
Results may differ from the reference program's by a relative error of at most 0.03.
Values may be sent and summed in bfloat16 or wider, within the bound.
No kernel may reach another device: no remote copies, remote signals or barrier semaphores. Data moves between devices by JAX's collectives and lax.ppermute only.
A program may use at most 192 MiB of HBM per device.

```python
import math
import jax
import jax.numpy as jnp
from jax import lax

D = 2048
QUERY_HEADS = 16
KEY_VALUE_HEADS = 8
HEAD_SIZE = 128
FF = 6144
PACKED_LENGTH = 2048
DOC_LEAST = 60
DOC_MOST = 800
OFFSET = 512
STEP = 5
SEQUENCES = 8
TOKENS = 16384
QKV = 4096
GAINS = 4352
N_TP = 8


def document_layout(key):
    pieces = PACKED_LENGTH // DOC_LEAST + 1
    key_dense, key_seqs = jax.random.split(key, 2)
    dense_seq = jax.random.randint(key_dense, (), 0, SEQUENCES)
    keys = jax.random.split(key_seqs, SEQUENCES)
    lowest_start = PACKED_LENGTH // 2 - DOC_MOST + 1
    aligned_start = (lowest_start + DOC_LEAST - 1) // DOC_LEAST * DOC_LEAST

    def single(seq_key, seq_number):
        key_start, key_left, key_right, key_offset = jax.random.split(seq_key, 4)
        dense = seq_number == dense_seq
        random_start = PACKED_LENGTH // 2 - jax.random.randint(key_start, (), 1, DOC_MOST)
        start_big = jnp.where(dense, aligned_start, random_start)
        end_big = start_big + DOC_MOST
        left_lengths = jnp.where(dense, DOC_LEAST, jax.random.randint(key_left, (pieces,), DOC_LEAST, DOC_MOST - DOC_LEAST + 1))
        right_lengths = jnp.where(dense, DOC_LEAST, jax.random.randint(key_right, (pieces,), DOC_LEAST, DOC_MOST - DOC_LEAST + 1))
        left_cuts = start_big - jnp.cumsum(left_lengths)
        right_cuts = end_big + jnp.cumsum(right_lengths)
        left_valid = left_cuts >= DOC_LEAST
        right_valid = right_cuts <= PACKED_LENGTH - DOC_LEAST
        places = jnp.arange(PACKED_LENGTH)
        flags = (places == start_big) | (places == end_big)
        flags = flags | jnp.any((places[:, None] == left_cuts[None, :]) & left_valid[None, :], axis=1)
        flags = flags | jnp.any((places[:, None] == right_cuts[None, :]) & right_valid[None, :], axis=1)
        ids = jnp.cumsum(flags.astype(jnp.int32)).astype(jnp.int32)
        starts = lax.cummax(jnp.where(flags, places, 0), axis=0)
        slots = jnp.arange(2 * pieces + 4)
        big_id = jnp.sum(jnp.where(places == start_big, ids, 0))
        offsets = jax.random.randint(key_offset, (2 * pieces + 4,), 0, OFFSET)
        offsets = jnp.where(slots == 0, 0, offsets)
        offsets = jnp.where(slots == big_id, OFFSET - 1, offsets)
        return (ids, (places - starts + offsets[ids]).astype(jnp.int32))
    return jax.vmap(single)(keys, jnp.arange(SEQUENCES))


def draw_document_index(key, part):
    ids, places = document_layout(key)
    return ids


def draw_positions(key, part):
    ids, places = document_layout(key)
    return places


def steps_of(key, dims, cuts, low, top_value):
    factor_of = 1.0
    for axis_at, shards_of in cuts:
        steps = jax.random.uniform(jax.random.fold_in(jax.random.fold_in(key, 6), axis_at), (shards_of,), jnp.float32, low / len(cuts), top_value / len(cuts))
        factor_of = factor_of * jnp.repeat(jnp.exp(steps), dims[axis_at] // shards_of).reshape((-1,) + (1,) * (len(dims) - 1 - axis_at))
    return factor_of


def scatter_about(rng, dims, width, reach, cuts=(), kind=jnp.bfloat16):
    drawn = jax.random.normal(rng, dims, jnp.float32) * width
    if len(cuts) > 0:
        drawn = steps_of(rng, dims, cuts, -0.22, 0.18) * drawn
    return jnp.clip(drawn, min=-reach, max=reach).astype(kind)


def setup_inputs(seed: int = 0) -> dict:
    splits = jax.random.split(jax.random.key(seed), 20)
    return {
        "inputs": scatter_about(splits[0], (SEQUENCES, PACKED_LENGTH, D), 1.0, 6.0, ((0, 8), (1, 16))),
        "cotangent": scatter_about(splits[1], (SEQUENCES, PACKED_LENGTH, D), 1.0, 6.0, ((0, 8), (1, 2))),
        "document_index": draw_document_index(jax.random.fold_in(splits[19], 71), 0),
        "positions": draw_positions(jax.random.fold_in(splits[19], 71), 0),
        "gains": jnp.clip(1.0 + 0.1 * jax.random.normal(splits[4], (GAINS,), jnp.float32), 0.5, 1.5),
        "gains_first": scatter_about(splits[5], (GAINS,), (0.111 * 1.5 * TOKENS ** 0.5), 128.0, ((0, 16),), jnp.float32),
        "gains_second": jnp.clip(jnp.exp(math.log(7741.44) - 1.3843914 * jax.random.uniform(splits[6], (GAINS,), jnp.float32) ** steps_of(splits[6], (GAINS,), ((0, 16),), -0.2, 0.2)), 1939.0464, 7741.44),
        "project_weight": scatter_about(splits[7], (D, QKV), D ** -0.5, 0.125, ((0, 16), (1, 8)), jnp.float32),
        "project_first": scatter_about(splits[8], (D, QKV), (0.111 * 1.0 * TOKENS ** 0.5), 80.0, ((0, 16), (1, 8)), jnp.float32),
        "project_second": jnp.clip(jnp.exp(math.log(3440.64) - 1.3843914 * jax.random.uniform(splits[9], (D, QKV), jnp.float32) ** steps_of(splits[9], (D, QKV), ((0, 16), (1, 8)), -0.2, 0.2)), 861.7984, 3440.64),
        "output_weight": scatter_about(splits[10], (QUERY_HEADS * HEAD_SIZE, D), (QUERY_HEADS * HEAD_SIZE // 64) ** -0.5, 1.0, ((0, 8), (1, 16)), jnp.float32),
        "output_first": scatter_about(splits[11], (QUERY_HEADS * HEAD_SIZE, D), (0.111 * 0.15 * TOKENS ** 0.5), 12.0, ((0, 8), (1, 16)), jnp.float32),
        "output_second": jnp.clip(jnp.exp(math.log(77.4144) - 1.3843913 * jax.random.uniform(splits[12], (QUERY_HEADS * HEAD_SIZE, D), jnp.float32) ** steps_of(splits[12], (QUERY_HEADS * HEAD_SIZE, D), ((0, 8), (1, 16)), -0.2, 0.2)), 19.390465, 77.4144),
        "expand_weight": scatter_about(splits[13], (D, 2 * FF), D ** -0.5, 0.125, ((0, 16), (1, 8)), jnp.float32),
        "expand_first": scatter_about(splits[14], (D, 2 * FF), (0.111 * 0.35 * TOKENS ** 0.5), 32.0, ((0, 16), (1, 8)), jnp.float32),
        "expand_second": jnp.clip(jnp.exp(math.log(421.4784) - 1.3843914 * jax.random.uniform(splits[15], (D, 2 * FF), jnp.float32) ** steps_of(splits[15], (D, 2 * FF), ((0, 16), (1, 8)), -0.2, 0.2)), 105.570305, 421.4784),
        "shrink_weight": scatter_about(splits[16], (FF, D), FF ** -0.5, 0.078125, ((0, 8), (1, 16)), jnp.float32),
        "shrink_first": scatter_about(splits[17], (FF, D), (0.111 * 0.6 * TOKENS ** 0.5), 48.0, ((0, 8), (1, 16)), jnp.float32),
        "shrink_second": jnp.clip(jnp.exp(math.log(1238.6304) - 1.3843913 * jax.random.uniform(splits[18], (FF, D), jnp.float32) ** steps_of(splits[18], (FF, D), ((0, 8), (1, 16)), -0.2, 0.2)), 310.24744, 1238.6304),
    }


epsilon = 1e-06
theta = 1000000.0
beta_first = 0.9
beta_second = 0.95
adam_epsilon = 1e-08
weight_decay = 0.1

@jax.custom_vjp
def low(v):
    return lax.optimization_barrier(v.astype(jnp.bfloat16)).astype(jnp.float32)

@jax.custom_vjp
def low_back(v):
    return v

def low_keep(v):
    return (low(v), None)

def low_pass(kept, grad):
    return (grad,)

def back_keep(v):
    return (v, None)

def back_low(kept, grad):
    return (low(grad),)
low.defvjp(low_keep, low_pass)
low_back.defvjp(back_keep, back_low)

def rms_norm(values, gain):
    return values * lax.rsqrt(lax.optimization_barrier(jnp.mean(values * values, axis=-1, keepdims=True)) + epsilon) * gain

def rotate(values, position):
    half = values.shape[-1] // 2
    frequency = jnp.exp(jnp.arange(half, dtype=jnp.float32) * (-2.0 * math.log(theta) / values.shape[-1]))
    angle = position.astype(jnp.float32)[..., None] * frequency
    cosine = jnp.cos(angle)[..., None, :]
    sine = jnp.sin(angle)[..., None, :]
    first = values[..., :half]
    second = values[..., half:]
    return jnp.concatenate([first * cosine - second * sine, second * cosine + first * sine], axis=-1)

def head_norm(raw_projection, gain, position):
    return rotate(rms_norm(raw_projection, gain), position)

def block_mask(query_ids, key_ids, query_start, block, length):
    query_place = query_start + jnp.arange(block)
    key_place = jnp.arange(length)
    return (query_ids[:, None] == key_ids[None, :]) & (key_place[None, :] <= query_place[:, None])

def highest(left, right):
    return jnp.dot(left, right, precision=lax.Precision.HIGHEST)

def layer(values, gains_in, project_in, output_in, expand_in, shrink_in, ids, places):
    gain_low = low(gains_in)
    gain_one = gain_low[:D]
    gain_two = gain_low[D:2 * D]
    gain_query = gain_low[2 * D:2 * D + HEAD_SIZE]
    gain_key = gain_low[2 * D + HEAD_SIZE:]
    normed = low(rms_norm(values, gain_one))
    raw_projection = low_back(highest(normed, low(project_in)))
    query_portion = QUERY_HEADS // N_TP
    key_portion = KEY_VALUE_HEADS // N_TP
    raw_projection = raw_projection.reshape(PACKED_LENGTH, N_TP, query_portion + 2 * key_portion, HEAD_SIZE)
    query_state = raw_projection[:, :, :query_portion].reshape(PACKED_LENGTH, QUERY_HEADS, HEAD_SIZE)
    key = raw_projection[:, :, query_portion:query_portion + key_portion].reshape(PACKED_LENGTH, KEY_VALUE_HEADS, HEAD_SIZE)
    value_state = raw_projection[:, :, query_portion + key_portion:].reshape(PACKED_LENGTH, KEY_VALUE_HEADS, HEAD_SIZE)
    query_state = low(head_norm(query_state, gain_query, places))
    key = low(head_norm(key, gain_key, places))
    value_state = low(value_state)
    query_group = QUERY_HEADS // KEY_VALUE_HEADS
    grouped_queries = query_state.reshape(PACKED_LENGTH, KEY_VALUE_HEADS, query_group, HEAD_SIZE)
    block = min(512, PACKED_LENGTH)
    scale = HEAD_SIZE ** (-0.5)

    @jax.checkpoint
    def one_block(index):
        start = index * block
        query_block = lax.dynamic_slice_in_dim(grouped_queries, start, block, 0)
        ids_block = lax.dynamic_slice_in_dim(ids, start, block, 0)
        mask = block_mask(ids_block, ids, start, block, PACKED_LENGTH)
        scores = jnp.einsum('qkgd,tkd->kgqt', query_block, key, precision=lax.Precision.HIGHEST)
        scores = low_back(scores * scale)
        masked = jnp.where(mask, scores, -1e+30)
        top = lax.optimization_barrier(jnp.max(masked, axis=-1, keepdims=True))
        unnormed = jnp.where(mask, jnp.exp(masked - top), 0.0)
        probs = low(unnormed / lax.optimization_barrier(jnp.sum(unnormed, axis=-1, keepdims=True)))
        return jnp.einsum('kgqt,tkd->qkgd', probs, value_state, precision=lax.Precision.HIGHEST)
    attention_output = lax.map(one_block, jnp.arange(PACKED_LENGTH // block))
    attention_output = low(low_back(attention_output.reshape(PACKED_LENGTH, QUERY_HEADS * HEAD_SIZE)))
    middle = values + low_back(highest(attention_output, low(output_in)))
    normed_two = low(rms_norm(middle, gain_two))
    expanded = low_back(highest(normed_two, low(expand_in)))
    expanded = expanded.reshape(PACKED_LENGTH, N_TP, 2, FF // N_TP)
    gate = expanded[:, :, 0].reshape(PACKED_LENGTH, FF)
    upward = expanded[:, :, 1].reshape(PACKED_LENGTH, FF)
    hidden_state = low(jax.nn.silu(gate) * upward)
    return middle + highest(hidden_state, low(shrink_in))

def adam(weight, first, second, grad, rate, decay_rate):
    mean = beta_first * first + (1.0 - beta_first) * grad
    square = beta_second * second + (1.0 - beta_second) * grad * grad
    mean_hat = mean / (1.0 - beta_first ** STEP)
    square_hat = square / (1.0 - beta_second ** STEP)
    updated = weight - rate * (mean_hat / (jnp.sqrt(square_hat) + adam_epsilon) + decay_rate * weight)
    return (mean, square, updated)

def reference(inputs, cotangent, document_index, positions, gains, gains_first, gains_second, project_weight, project_first, project_second, output_weight, output_first, output_second, expand_weight, expand_first, expand_second, shrink_weight, shrink_first, shrink_second):
    params = (gains, project_weight, output_weight, expand_weight, shrink_weight)

    def step(totals, packed):
        tokens, back, ids, places = packed

        def forward(values, gains_in, project_in, output_in, expand_in, shrink_in):
            return layer(values, gains_in, project_in, output_in, expand_in, shrink_in, ids, places)
        result, pull = jax.vjp(forward, tokens.astype(jnp.float32), gains, project_weight, output_weight, expand_weight, shrink_weight)
        grads = pull(back.astype(jnp.float32))
        totals = tuple((total + grad for total, grad in zip(totals, grads[1:])))
        return (totals, (result.astype(jnp.bfloat16), grads[0].astype(jnp.bfloat16)))
    zeros = tuple((jnp.zeros(param.shape, jnp.float32) for param in params))
    totals, (outputs, input_grad) = lax.scan(step, zeros, (inputs, cotangent, document_index, positions))
    gains_mean, gains_square, gains_updated = adam(gains, gains_first, gains_second, totals[0], 0.5, 0.0)
    project_mean, project_square, project_updated = adam(project_weight, project_first, project_second, totals[1], 0.05, weight_decay)
    output_mean, output_square, output_updated = adam(output_weight, output_first, output_second, totals[2], 0.4, weight_decay)
    expand_mean, expand_square, expand_updated = adam(expand_weight, expand_first, expand_second, totals[3], 0.05, weight_decay)
    shrink_mean, shrink_square, shrink_updated = adam(shrink_weight, shrink_first, shrink_second, totals[4], 0.03, weight_decay)
    return (outputs, input_grad, gains_mean, gains_square, gains_updated, project_mean, project_square, project_updated, output_mean, output_square, output_updated, expand_mean, expand_square, expand_updated, shrink_mean, shrink_square, shrink_updated)
```

```python
import functools
import math

import jax
import jax.numpy as jnp
from jax import lax
from jax.experimental import pallas as pl
from jax.experimental.pallas import tpu as pltpu
from jax.sharding import Mesh
from jax.sharding import PartitionSpec as P

QUERY_HEADS = 16
KEY_VALUE_HEADS = 8
HEAD = 128
STEP = 5
LONGEST = 800
BLOCK = 128
LOCAL = 1024
BACK = 896
QUERIES = 256
WINDOW = BACK + QUERIES

epsilon = 1e-06
theta = 1000000.0
beta_first = 0.9
beta_second = 0.95
adam_epsilon = 1e-08
weight_decay = 0.1

low = jnp.bfloat16
wide = jnp.float32
MIB = 1024 * 1024


def rms_norm(values, gain):
    return values * lax.rsqrt(jnp.mean(values * values, axis=-1, keepdims=True) + epsilon) * gain


def swiglu(gate, upward):
    return jax.nn.silu(gate) * upward


def adam(weight, first, second, grad, rate, decay_rate):
    mean = beta_first * first + (1.0 - beta_first) * grad
    square = beta_second * second + (1.0 - beta_second) * grad * grad
    mean_hat = mean / (1.0 - beta_first**STEP)
    square_hat = square / (1.0 - beta_second**STEP)
    updated = weight - rate * (
        mean_hat / (jnp.sqrt(square_hat) + adam_epsilon) + decay_rate * weight
    )
    return (mean, square, updated)


def dot(left, right, dims):
    return lax.dot_general(left, right, ((dims[:1], dims[1:]), ((), ())), preferred_element_type=wide)


def move(values, axis, pairs):
    return lax.ppermute(values, axis, pairs)


def shift(values, steps):
    return move(values, "x", [(i, (i + steps) % 4) for i in range(4)])


def other_core(values):
    return move(values, "core", [(0, 1), (1, 0)])


def trade(values):
    return move(values, ("core", "yl"), [(a * 2 + b, b * 2 + a) for a in range(2) for b in range(2)])


def to_group(values):
    pairs = [
        ((a * 2 + b) * 2 + d, (d * 2 + a) * 2 + b)
        for a in range(2)
        for b in range(2)
        for d in range(2)
    ]
    return move(values, ("core", "yh", "yl"), pairs)


def to_owner(values):
    pairs = [
        ((d * 2 + a) * 2 + b, (a * 2 + b) * 2 + d)
        for a in range(2)
        for b in range(2)
        for d in range(2)
    ]
    return move(values, ("core", "yh", "yl"), pairs)


def gather_rows(values):
    mine = jnp.concatenate([values, shift(values, 1), shift(values, 2), shift(values, 3)], axis=0)
    return jnp.concatenate([mine, other_core(mine)], axis=0)


def core_sum(left, right, dims):
    rows = left.shape[0] // 2
    away = other_core(dot(left[rows:], right, dims).astype(low))
    return (dot(left[:rows], right, dims) + away.astype(wide)).astype(low)


def chip_sum(both):
    pieces = both.reshape(4, BLOCK, -1)
    total = pieces[0].astype(wide)
    for k in (2, 1, 3):
        total = total + shift(pieces[k], 4 - k).astype(wide)
    return total


def scatter_rows(left, right, dims):
    return chip_sum(core_sum(left, right, dims))


def after(values, *others):
    return lax.optimization_barrier((values, *others))[0]


def shift_z(values, steps):
    return move(values, "z", [(i, (i + steps) % 4) for i in range(4)])


def flip(values, a, b):
    pairs = [
        ((c * 2 + h) * 2 + d, ((d ^ b) * 2 + (h ^ a)) * 2 + c)
        for c in range(2)
        for h in range(2)
        for d in range(2)
    ]
    return move(values, ("core", "yh", "yl"), pairs)


def sum_steps(pieces):
    total = pieces[0].astype(wide)
    for k in (2, 1, 3):
        total = total + shift_z(pieces[k], k).astype(wide)
    return total


def sum_flips(pieces):
    total = 0.0
    for a in (1, 0):
        for b in (1, 0):
            total = total + flip(pieces[a, b], a, b).astype(wide)
    return total


GROUP = ("z", "yh", "yl")


def spec(shape, index):
    return pl.BlockSpec(shape, index)


def once(shape, index):
    return pl.BlockSpec(shape, index, pipeline_mode=pl.Buffered(1))


def params(mib):
    return pltpu.CompilerParams(vmem_limit_bytes=mib * MIB)


def cost(flops, moved, special=0):
    return pl.CostEstimate(flops=flops, bytes_accessed=moved, transcendentals=special)


def choose_kernel(place, flag, own, away, out, arrived):
    def copies(source):
        return [
            pltpu.make_async_copy(
                source.at[pl.ds(pl.multiple_of(place[i] * BLOCK, BLOCK), BLOCK)],
                out.at[pl.ds(i * BLOCK, BLOCK)],
                arrived.at[i],
            )
            for i in range(8)
        ]

    @pl.when(flag[0] == 1)
    def _():
        for copy in copies(own):
            copy.start()

    @pl.when(flag[0] == 0)
    def _():
        for copy in copies(away):
            copy.start()

    for copy in copies(own):
        copy.wait()


def choose(place, flag, own, away):
    scalar = pl.BlockSpec(memory_space=pltpu.SMEM)
    there = pl.BlockSpec(memory_space=pl.ANY)
    return pl.pallas_call(
        choose_kernel,
        out_shape=jax.ShapeDtypeStruct(own.shape, own.dtype),
        in_specs=[scalar, scalar, there, there],
        out_specs=there,
        scratch_shapes=[pltpu.SemaphoreType.DMA((8,))],
        compiler_params=params(4),
        cost_estimate=cost(0, 2 * own.size * 2),
    )(place, flag, own, away)


def heads_kernel(place, raw, cosine, sine, gq, gk, query, pair):
    for i in range(8):
        here = pl.ds(i * BLOCK, BLOCK)
        there = pl.ds(pl.multiple_of(place[i] * BLOCK, BLOCK), BLOCK)
        c, s = cosine[there], sine[there]
        for h in range(4):
            part = slice(h * HEAD, (h + 1) * HEAD)
            v = raw[here, part]
            if h < 3:
                v = rms_norm(v, gq[...] if h < 2 else gk[...])
                v = v * c + pltpu.roll(v, HEAD // 2, 1) * s
            if h < 2:
                query[there, part] = v.astype(low)
            else:
                pair[there, (h - 2) * HEAD : (h - 1) * HEAD] = v.astype(low)


def heads(place, raw, cosine, sine, gq, gk):
    scalar = pl.BlockSpec(memory_space=pltpu.SMEM)
    there = pl.BlockSpec(memory_space=pltpu.VMEM)
    return pl.pallas_call(
        heads_kernel,
        out_shape=[jax.ShapeDtypeStruct((LOCAL, 2 * HEAD), low)] * 2,
        in_specs=[scalar] + [there] * 5,
        out_specs=[there] * 2,
        compiler_params=params(12),
        cost_estimate=cost(LOCAL * 512 * 10, LOCAL * 512 * 8),
    )(place, raw, cosine, sine, gq, gk)


def heads_back_kernel(place, raw, cosine, sine, gq, gk, dquery, dpair, later, draw, dgain):
    sums = [jnp.zeros((1, HEAD), wide)] * 2
    for i in range(8):
        here = pl.ds(i * BLOCK, BLOCK)
        there = pl.ds(pl.multiple_of(place[i] * BLOCK, BLOCK), BLOCK)
        c, s = cosine[there], sine[there]
        dp = dpair[pl.ds(pl.multiple_of(place[i] * BLOCK + BACK, BLOCK), BLOCK)]
        from_later = later[pl.ds(pl.multiple_of(jnp.maximum(place[i] - 1, 0) * BLOCK, BLOCK), BLOCK)]
        dp = dp + jnp.where(place[i] > 0, from_later.astype(wide), 0.0)
        for h in range(4):
            part = slice(h * HEAD, (h + 1) * HEAD)
            if h == 3:
                draw[here, part] = dp[:, HEAD:].astype(low)
                continue
            g = gq[...] if h < 2 else gk[...]
            d = dquery[there, part] if h < 2 else dp[:, :HEAD]
            d = d * c + pltpu.roll(d * s, HEAD // 2, 1)
            v = raw[here, part]
            r = lax.rsqrt(jnp.mean(v * v, axis=-1, keepdims=True) + epsilon)
            u = v * r
            sums[h // 2] += jnp.sum(d * u, axis=0, keepdims=True)
            e = d * g
            draw[here, part] = (r * (e - u * jnp.mean(u * e, axis=-1, keepdims=True))).astype(low)
    row = lax.broadcasted_iota(jnp.int32, (8, HEAD), 0)
    dgain[...] = jnp.where(row == 0, sums[0], jnp.where(row == 1, sums[1], 0.0))


def heads_back(place, raw, cosine, sine, gq, gk, dquery, dpair, later):
    scalar = pl.BlockSpec(memory_space=pltpu.SMEM)
    there = pl.BlockSpec(memory_space=pltpu.VMEM)
    return pl.pallas_call(
        heads_back_kernel,
        out_shape=[
            jax.ShapeDtypeStruct((LOCAL, 4 * HEAD), low),
            jax.ShapeDtypeStruct((8, HEAD), wide),
        ],
        in_specs=[scalar] + [there] * 8,
        out_specs=[there] * 2,
        compiler_params=params(16),
        cost_estimate=cost(LOCAL * 512 * 20, LOCAL * 512 * 12),
    )(place, raw, cosine, sine, gq, gk, dquery, dpair, later)


ROWS = 256


def grads_kernel(count, *refs):
    lefts, rights, out = refs[:count], refs[count : 2 * count], refs[-1]
    at = 0
    for left, right in zip(lefts, rights):
        n = right.shape[1]
        out[:, at : at + n] = dot(left[...], right[...], (0, 0)).astype(low)
        at += n
    for extra in refs[2 * count : -1]:
        out[:, at : at + extra.shape[1]] = extra[...]
        at += extra.shape[1]


def grads(lefts, rights, extras=()):
    depth, rows = lefts[0].shape
    total = sum(v.shape[1] for v in [*rights, *extras])
    flops = 2 * depth * rows * sum(v.shape[1] for v in rights)
    return pl.pallas_call(
        functools.partial(grads_kernel, len(lefts)),
        out_shape=jax.ShapeDtypeStruct((rows, total), low),
        grid=(rows // ROWS,),
        in_specs=[spec((depth, ROWS), lambda i: (0, i))] * len(lefts)
        + [once(v.shape, lambda i: (0, 0)) for v in rights]
        + [spec((ROWS, v.shape[1]), lambda i: (i, 0)) for v in extras],
        out_specs=spec((ROWS, total), lambda i: (i, 0)),
        compiler_params=params(28),
        cost_estimate=cost(flops, 2 * (len(lefts) * depth * rows + total * (rows + depth))),
    )(*lefts, *rights, *extras)


HALF = 384
TALL = BLOCK + 16


def first_grads_kernel(spot, normed, dmiddle, draw, attended, dgains, left, right):
    project = dot(normed[...], draw[...], (0, 0)).astype(low)
    output = dot(dmiddle[...], attended[...], (0, 0)).astype(low)
    for j in range(2):
        rows = slice(j * BLOCK, (j + 1) * BLOCK)
        a = j ^ spot[1]
        left[0, a, 0] = project[rows, :HALF]
        right[a, 0, 0, :BLOCK, : 4 * HEAD - HALF] = project[rows, HALF:]
        right[a, 0, 0, :BLOCK, 4 * HEAD - HALF :] = output[rows]
        right[a, 0, 0, BLOCK:] = dgains[j]


def first_grads(spot, normed, dmiddle, draw, attended, dgains):
    whole = lambda i, s: (0, 0)
    columns = lambda i, s: (0, i)
    steps = lambda i, s: lax.rem(i // 2 - s[0] + 4, 4)
    return pl.pallas_call(
        first_grads_kernel,
        out_shape=[
            jax.ShapeDtypeStruct((4, 2, 2, BLOCK, HALF), low),
            jax.ShapeDtypeStruct((2, 2, 4, TALL, HALF), low),
        ],
        grid_spec=pltpu.PrefetchScalarGridSpec(
            num_scalar_prefetch=1,
            grid=(8,),
            in_specs=[
                spec((LOCAL, 2 * BLOCK), columns),
                spec((LOCAL, 2 * BLOCK), columns),
                once((LOCAL, 4 * HEAD), whole),
                once((LOCAL, 2 * HEAD), whole),
                spec((2, 16, HALF), lambda i, s: (i, 0, 0)),
            ],
            out_specs=[
                spec((1, 2, 1, BLOCK, HALF), lambda i, s: (steps(i, s), 0, i % 2 ^ s[2], 0, 0)),
                spec((2, 1, 1, TALL, HALF), lambda i, s: (0, i % 2 ^ s[2], steps(i, s), 0, 0)),
            ],
        ),
        compiler_params=params(24),
        cost_estimate=cost(2 * LOCAL * 2048 * 768, 14 * MIB),
    )(spot, normed, dmiddle, draw, attended, dgains)


SCALE = HEAD ** (-0.5)


def allowed(query_ids, key_ids, start):
    keys = key_ids[:, pl.ds(start, WINDOW)]
    row = lax.broadcasted_iota(jnp.int32, (QUERIES, WINDOW), 0)
    column = lax.broadcasted_iota(jnp.int32, (QUERIES, WINDOW), 1)
    return (query_ids[...] == keys) & (column <= row + BACK)


def attend_kernel(place, core, query, pair, query_ids, key_ids, out, logsum):
    i = pl.program_id(0)
    start = pl.multiple_of(i * QUERIES, QUERIES)
    mask = allowed(query_ids, key_ids, start)
    logs = []
    for h in range(2):
        part = slice(h * HEAD, (h + 1) * HEAD)
        scores = dot(query[:, part], pair[pl.ds(start, WINDOW), :HEAD], (1, 1)) * SCALE
        scores = jnp.where(mask, scores, -1e30)
        top = jnp.max(scores, axis=-1, keepdims=True)
        unnormed = jnp.exp(scores - top)
        total = jnp.sum(unnormed, axis=-1, keepdims=True)
        probs = (unnormed * (1.0 / total)).astype(low)
        result = dot(probs, pair[pl.ds(start, WINDOW), HEAD:], (1, 0)).astype(low)
        for j in range(2):
            out[j ^ core[0], 0, :, part] = result[j * BLOCK : (j + 1) * BLOCK]
        logs.append(top + jnp.log(total))
    lane = lax.broadcasted_iota(jnp.int32, (QUERIES, HEAD), 1)
    logsum[...] = jnp.where(lane < HEAD // 2, logs[0], logs[1])


def attend(place, core, query, pair, query_ids, key_ids):
    rows = lambda i, p, c: (i, 0)
    whole = lambda i, p, c: (0, 0)
    keys = BACK + LOCAL
    return pl.pallas_call(
        attend_kernel,
        out_shape=[
            jax.ShapeDtypeStruct((2, 4, BLOCK, 2 * HEAD), low),
            jax.ShapeDtypeStruct((LOCAL, HEAD), wide),
        ],
        grid_spec=pltpu.PrefetchScalarGridSpec(
            num_scalar_prefetch=2,
            grid=(LOCAL // QUERIES,),
            in_specs=[
                spec((QUERIES, 2 * HEAD), rows),
                once((keys, 2 * HEAD), whole),
                spec((QUERIES, 1), rows),
                spec((1, keys), whole),
            ],
            out_specs=[
                spec((2, 1, BLOCK, 2 * HEAD), lambda i, p, c: (0, p[i], 0, 0)),
                spec((QUERIES, HEAD), rows),
            ],
        ),
        compiler_params=params(24),
        cost_estimate=cost(
            4 * 2 * LOCAL * WINDOW * HEAD, 4 * LOCAL * 512, 2 * LOCAL * WINDOW
        ),
    )(place, core, query, pair, query_ids, key_ids)


def attend_back_kernel(
    place, core, query, pair, query_ids, key_ids, grad, logsum, dquery, dpair
):
    i = pl.program_id(0)

    @pl.when(i == 0)
    def _():
        dpair[...] = jnp.zeros_like(dpair)

    start = pl.multiple_of(i * QUERIES, QUERIES)
    window = pl.ds(start, WINDOW)
    mask = allowed(query_ids, key_ids, start)
    dkey, dvalue = None, None
    for h in range(2):
        part = slice(h * HEAD, (h + 1) * HEAD)
        q = query[:, part]
        g = jnp.concatenate([grad[j ^ core[0], 0, :, part] for j in range(2)], axis=0)
        scores = dot(q, pair[window, :HEAD], (1, 1)) * SCALE
        probs = jnp.where(mask, jnp.exp(scores - logsum[:, h * 64 : h * 64 + 1]), 0.0)
        dprobs = dot(g, pair[window, HEAD:], (1, 1))
        inner = jnp.sum(probs * dprobs, axis=-1, keepdims=True)
        dscores = (probs * (dprobs - inner)).astype(low)
        dquery[:, part] = dot(dscores, pair[window, :HEAD], (1, 0)) * SCALE
        dv = dot(probs.astype(low), g, (0, 0))
        dk = dot(dscores, q, (0, 0))
        dkey = dk if dkey is None else dkey + dk
        dvalue = dv if dvalue is None else dvalue + dv
    dpair[window, :HEAD] += dkey * SCALE
    dpair[window, HEAD:] += dvalue


def attend_back(place, core, query, pair, query_ids, key_ids, grad, logsum):
    rows = lambda i, p, c: (i, 0)
    whole = lambda i, p, c: (0, 0)
    keys = BACK + LOCAL
    return pl.pallas_call(
        attend_back_kernel,
        out_shape=[
            jax.ShapeDtypeStruct((LOCAL, 2 * HEAD), wide),
            jax.ShapeDtypeStruct((keys, 2 * HEAD), wide),
        ],
        grid_spec=pltpu.PrefetchScalarGridSpec(
            num_scalar_prefetch=2,
            grid=(LOCAL // QUERIES,),
            in_specs=[
                spec((QUERIES, 2 * HEAD), rows),
                once((keys, 2 * HEAD), whole),
                spec((QUERIES, 1), rows),
                spec((1, keys), whole),
                spec((2, 1, BLOCK, 2 * HEAD), lambda i, p, c: (0, p[i], 0, 0)),
                spec((QUERIES, HEAD), rows),
            ],
            out_specs=[spec((QUERIES, 2 * HEAD), rows), once((keys, 2 * HEAD), whole)],
        ),
        compiler_params=params(28),
        cost_estimate=cost(
            10 * 2 * LOCAL * WINDOW * HEAD, 8 * LOCAL * 512, 2 * LOCAL * WINDOW
        ),
    )(place, core, query, pair, query_ids, key_ids, grad, logsum)


def per_device(
    inputs,
    cotangent,
    document_index,
    positions,
    gains,
    gains_first,
    gains_second,
    project_weight,
    project_first,
    project_second,
    output_weight,
    output_first,
    output_second,
    expand_weight,
    expand_first,
    expand_second,
    shrink_weight,
    shrink_first,
    shrink_second,
):
    core, x = lax.axis_index("core"), lax.axis_index("x")
    half, yl = lax.axis_index("yh"), lax.axis_index("yl")
    width = inputs.shape[-1]
    qkv = project_weight.shape[1]
    ff = shrink_weight.shape[0]
    at_home = core == yl
    steps = jnp.arange(8, dtype=jnp.int32)
    place = lax.rem(x - steps % 4 + 4, 4) * 2 + (core ^ (steps // 4))
    turn = lax.rem(x - jnp.arange(4, dtype=jnp.int32) + 4, 4)
    core_of = core.reshape(1).astype(jnp.int32)
    flag = at_home.astype(jnp.int32).reshape(1)

    gain_block = jnp.pad(gains.astype(low), (0, BLOCK * BLOCK - gains.shape[0])).reshape(BLOCK, BLOCK)
    first_shard = jnp.concatenate(
        [project_weight.astype(low), output_weight.astype(low).T, gain_block], axis=1
    )
    second_shard = jnp.concatenate([expand_weight.astype(low), shrink_weight.astype(low).T], axis=1)
    marks = jnp.stack([document_index[0], positions[0] // 32, positions[0] % 32])
    marks = jnp.pad(marks.astype(low), ((0, 13), (0, 0)))
    message = trade(jnp.concatenate([inputs[0], marks], axis=0))
    rows = message[:BLOCK]
    marks = message[BLOCK:].astype(jnp.int32)
    ids, places = marks[0], marks[1] * 32 + marks[2]
    first_all = lax.all_gather(to_group(first_shard), GROUP, axis=0, tiled=True)
    second_shard = after(second_shard, message)
    second_all = lax.all_gather(to_group(second_shard), GROUP, axis=0, tiled=True)
    project_all = first_all[:, :qkv]
    output_all = first_all[:, qkv : qkv + 2 * HEAD]
    expand_all = second_all[:, : 2 * ff]
    shrink_all = second_all[:, 2 * ff :]
    gain_all = first_all[:, qkv + 2 * HEAD :].reshape(16, BLOCK * BLOCK)[:, : gains.shape[0]]
    gain_all = gain_all.reshape(-1).astype(wide)
    gain_one = gain_all[:width]
    gain_two = gain_all[width : 2 * width]
    gain_query = gain_all[2 * width : 2 * width + HEAD].reshape(1, HEAD)
    gain_key = gain_all[2 * width + HEAD :].reshape(1, HEAD)

    ids_here = lax.dynamic_slice_in_dim(ids, half * LOCAL, LOCAL)
    places_here = lax.dynamic_slice_in_dim(places, half * LOCAL, LOCAL)
    ids_keys = jnp.where(
        half == 0,
        jnp.concatenate([jnp.full((BACK,), -1, jnp.int32), ids[:LOCAL]]),
        ids[LOCAL - BACK :],
    )
    query_ids, key_ids = ids_here.reshape(-1, 1), ids_keys.reshape(1, -1)
    frequency = jnp.exp(jnp.arange(HEAD // 2, dtype=wide) * (-2.0 * math.log(theta) / HEAD))
    angle = places_here.astype(wide)[:, None] * frequency
    cosine, sine = jnp.cos(angle), jnp.sin(angle)
    cosine = jnp.concatenate([cosine, cosine], axis=1)
    sine = jnp.concatenate([-sine, sine], axis=1)
    back = choose(place, flag, cotangent[0], other_core(cotangent[0]))

    rows_all = gather_rows(rows)
    values = rows.astype(wide)
    values_all = rows_all.astype(wide)
    scale_all = lax.rsqrt(jnp.mean(values_all * values_all, axis=-1, keepdims=True) + epsilon)
    normed = (values_all * scale_all * gain_one).astype(low)
    raw = dot(normed, project_all, (1, 0))
    query, pair = heads(place, raw, cosine, sine, gain_query, gain_key)
    earlier = move(pair[LOCAL - BACK :], "yh", [(0, 1)])
    pair_all = jnp.concatenate([earlier, pair], axis=0)
    attended, logsum = attend(turn, core_of, query, pair_all, query_ids, key_ids)
    attended = attended.reshape(LOCAL, 2 * HEAD)
    middle = values + scatter_rows(attended, output_all, (1, 1))

    normed_two = gather_rows(rms_norm(middle, gain_two).astype(low))
    expanded = dot(normed_two, expand_all, (1, 0))
    activated, pull_act = jax.vjp(swiglu, expanded[:, :ff], expanded[:, ff:])
    hidden = activated.astype(low)
    dhidden = dot(back, shrink_all, (1, 0))
    dgate, dup = pull_act(dhidden)
    dexpanded = jnp.concatenate([dgate, dup], axis=1).astype(low)
    drows_two = scatter_rows(dexpanded, expand_all, (1, 1))
    second_grads = grads([normed_two, back], [dexpanded, hidden])
    second_red = lax.psum_scatter(second_grads, GROUP, scatter_dimension=0, tiled=True)
    drows_two = after(drows_two, second_grads)
    shrunk = core_sum(after(hidden, second_grads), shrink_all, (1, 1))

    _, pull_two = jax.vjp(rms_norm, middle, gain_two)
    dmiddle, dgain_two = pull_two(drows_two)
    dmiddle = back[:BLOCK].astype(wide) + dmiddle
    dmiddle_all = after(gather_rows(dmiddle.astype(low)), shrunk)
    dattended = dot(dmiddle_all, output_all, (1, 0)).astype(low).reshape(2, 4, BLOCK, 2 * HEAD)
    outputs = (middle + chip_sum(after(shrunk, dmiddle_all))).astype(low)
    dquery, dpair = attend_back(
        turn, core_of, query, pair_all, query_ids, key_ids, dattended, logsum
    )
    later = move(dpair[:BACK].astype(low), "yh", [(1, 0)])
    later = after(later, outputs)
    outputs = trade(outputs)
    draw, dgain_heads = heads_back(
        place, raw, cosine, sine, gain_query, gain_key, dquery, dpair, later
    )
    drows_one = scatter_rows(draw, project_all, (1, 1))
    dnormed = dot(draw, project_all, (1, 1))
    dgain_one = jnp.sum(dnormed * values_all * scale_all, axis=0)
    _, pull_one = jax.vjp(rms_norm, values, gain_one)
    dvalues, _ = pull_one(drows_one)
    input_grad = trade((dmiddle + dvalues).astype(low))

    dgains = jnp.concatenate([dgain_one, dgain_two, dgain_heads[0], dgain_heads[1]]).astype(low)
    dgains = jnp.pad(dgains.reshape(16, 1, -1), ((0, 0), (0, 15), (0, HALF - gains.shape[0])))
    spot = jnp.stack([lax.axis_index("z"), half, yl]).astype(jnp.int32)
    left, right = first_grads(spot, normed, dmiddle_all, draw, attended, dgains)
    left, right = sum_steps(left).astype(low), sum_flips(right).astype(low)
    left, right = after((left, right), second_red)
    left, right = sum_flips(left), sum_steps(right)
    second_red = to_owner(second_red).astype(wide)
    project_grad = jnp.concatenate([left, right[:BLOCK, : qkv - HALF]], axis=1)
    output_grad = right[:BLOCK, qkv - HALF :].T
    dgains = right[BLOCK : BLOCK + 8]
    dgains = dgains + move(dgains, "yl", [(0, 1), (1, 0)])
    dgains = dgains + shift(dgains, 1) + shift(dgains, 2) + shift(dgains, 3)
    dgains = dgains[0, : gains.shape[0]]
    return (
        outputs[None],
        input_grad[None],
        *adam(gains, gains_first, gains_second, dgains, 0.5, 0.0),
        *adam(project_weight, project_first, project_second, project_grad, 0.05, weight_decay),
        *adam(
            output_weight,
            output_first,
            output_second,
            output_grad,
            0.4,
            weight_decay,
        ),
        *adam(
            expand_weight, expand_first, expand_second, second_red[:, : 2 * ff], 0.05, weight_decay
        ),
        *adam(
            shrink_weight, shrink_first, shrink_second, second_red[:, 2 * ff :].T, 0.03, weight_decay
        ),
    )


def solution(mesh):
    fine = Mesh(mesh.devices.reshape(4, 2, 2, 4, 2), ("z", "core", "yh", "x", "yl"))
    tokens = P(("z", "core"), ("yh", "x", "yl"), None)
    marks = P(("z", "core"), None)
    gain = P(("z", "core", "yh"))
    tall = P(("z", "core", "yh"), ("x", "yl"))
    flat = P(("x", "yl"), ("z", "core", "yh"))
    in_specs = (
        tokens,
        P(("z", "core"), "yh", None),
        marks,
        marks,
        *[gain] * 3,
        *[tall] * 3,
        *[flat] * 3,
        *[tall] * 3,
        *[flat] * 3,
    )
    out_specs = (
        tokens,
        tokens,
        *[gain] * 3,
        *[tall] * 3,
        *[flat] * 3,
        *[tall] * 3,
        *[flat] * 3,
    )
    return jax.shard_map(
        per_device, mesh=fine, in_specs=in_specs, out_specs=out_specs, check_vma=False
    )
```

```python
import functools
import math

import jax
import jax.numpy as jnp
from jax import lax
from jax.experimental import pallas as pl
from jax.experimental.pallas import tpu as pltpu
from jax.sharding import Mesh
from jax.sharding import PartitionSpec as P

QUERY_HEADS = 16
KEY_VALUE_HEADS = 8
HEAD = 128
STEP = 5
LONGEST = 800
BLOCK = 128
LOCAL = 1024
BACK = 896
QUERIES = 256
WINDOW = BACK + QUERIES

epsilon = 1e-06
theta = 1000000.0
beta_first = 0.9
beta_second = 0.95
adam_epsilon = 1e-08
weight_decay = 0.1

low = jnp.bfloat16
wide = jnp.float32
MIB = 1024 * 1024


def rms_norm(values, gain):
    return values * lax.rsqrt(jnp.mean(values * values, axis=-1, keepdims=True) + epsilon) * gain


def swiglu(gate, upward):
    return jax.nn.silu(gate) * upward


def adam(weight, first, second, grad, rate, decay_rate):
    mean = beta_first * first + (1.0 - beta_first) * grad
    square = beta_second * second + (1.0 - beta_second) * grad * grad
    mean_hat = mean / (1.0 - beta_first**STEP)
    square_hat = square / (1.0 - beta_second**STEP)
    updated = weight - rate * (
        mean_hat / (jnp.sqrt(square_hat) + adam_epsilon) + decay_rate * weight
    )
    return (mean, square, updated)


def dot(left, right, dims):
    return lax.dot_general(left, right, ((dims[:1], dims[1:]), ((), ())), preferred_element_type=wide)


def move(values, axis, pairs):
    return lax.ppermute(values, axis, pairs)


def along_x(blocks):
    return lax.all_to_all(blocks, "x", 0, 0, tiled=True)


def shift(values, steps):
    return move(values, "x", [(i, (i + steps) % 4) for i in range(4)])


def other_core(values):
    return move(values, "core", [(0, 1), (1, 0)])


def trade(values):
    return move(values, ("core", "yl"), [(a * 2 + b, b * 2 + a) for a in range(2) for b in range(2)])


def to_group(values):
    pairs = [
        ((a * 2 + b) * 2 + d, (d * 2 + a) * 2 + b)
        for a in range(2)
        for b in range(2)
        for d in range(2)
    ]
    return move(values, ("core", "yh", "yl"), pairs)


def to_owner(values):
    pairs = [
        ((d * 2 + a) * 2 + b, (a * 2 + b) * 2 + d)
        for a in range(2)
        for b in range(2)
        for d in range(2)
    ]
    return move(values, ("core", "yh", "yl"), pairs)


def gather_rows(values):
    mine = along_x(jnp.broadcast_to(values, (4, *values.shape))).reshape(4 * BLOCK, -1)
    return mine, other_core(mine)


def core_sum(mine, away):
    return (mine.astype(wide) + other_core(away).astype(wide)).astype(low)


def chip_sum(both):
    return jnp.sum(along_x(both.reshape(4, BLOCK, -1)).astype(wide), axis=0)


def after(values, *others):
    return lax.optimization_barrier((values, *others))[0]


def shift_z(values, steps):
    return move(values, "z", [(i, (i + steps) % 4) for i in range(4)])


def flip(values, a, b):
    pairs = [
        ((c * 2 + h) * 2 + d, ((d ^ b) * 2 + (h ^ a)) * 2 + c)
        for c in range(2)
        for h in range(2)
        for d in range(2)
    ]
    return move(values, ("core", "yh", "yl"), pairs)


def sum_steps(pieces):
    total = pieces[0].astype(wide)
    for k in (2, 1, 3):
        total = total + shift_z(pieces[k], k).astype(wide)
    return total


def sum_flips(pieces):
    total = 0.0
    for a in (1, 0):
        for b in (1, 0):
            total = total + flip(pieces[a, b], a, b).astype(wide)
    return total


GROUP = ("z", "yh", "yl")


def spec(shape, index):
    return pl.BlockSpec(shape, index)


def once(shape, index):
    return pl.BlockSpec(shape, index, pipeline_mode=pl.Buffered(1))


def params(mib):
    return pltpu.CompilerParams(vmem_limit_bytes=mib * MIB)


def cost(flops, moved, special=0):
    return pl.CostEstimate(flops=flops, bytes_accessed=moved, transcendentals=special)


def choose_kernel(place, flag, own, away, out, arrived):
    def copies(source):
        return [
            pltpu.make_async_copy(
                source.at[pl.ds(pl.multiple_of(place[i] * BLOCK, BLOCK), BLOCK)],
                out.at[pl.ds(i * BLOCK, BLOCK)],
                arrived.at[i],
            )
            for i in range(8)
        ]

    @pl.when(flag[0] == 1)
    def _():
        for copy in copies(own):
            copy.start()

    @pl.when(flag[0] == 0)
    def _():
        for copy in copies(away):
            copy.start()

    for copy in copies(own):
        copy.wait()


def choose(place, flag, own, away):
    scalar = pl.BlockSpec(memory_space=pltpu.SMEM)
    there = pl.BlockSpec(memory_space=pl.ANY)
    return pl.pallas_call(
        choose_kernel,
        out_shape=jax.ShapeDtypeStruct(own.shape, own.dtype),
        in_specs=[scalar, scalar, there, there],
        out_specs=there,
        scratch_shapes=[pltpu.SemaphoreType.DMA((8,))],
        compiler_params=params(4),
        cost_estimate=cost(0, 2 * own.size * 2),
    )(place, flag, own, away)


def heads_kernel(place, mine, away, cosine, sine, gq, gk, query, pair):
    for i in range(8):
        raw = (mine, away)[i // 4]
        here = pl.ds(i % 4 * BLOCK, BLOCK)
        there = pl.ds(pl.multiple_of(place[i] * BLOCK, BLOCK), BLOCK)
        c, s = cosine[there], sine[there]
        for h in range(4):
            part = slice(h * HEAD, (h + 1) * HEAD)
            v = raw[here, part]
            if h < 3:
                v = rms_norm(v, gq[...] if h < 2 else gk[...])
                v = v * c + pltpu.roll(v, HEAD // 2, 1) * s
            if h < 2:
                query[there, part] = v.astype(low)
            else:
                pair[there, (h - 2) * HEAD : (h - 1) * HEAD] = v.astype(low)


SCALARS = pl.BlockSpec(memory_space=pltpu.SMEM)
WHOLE = pl.BlockSpec(memory_space=pltpu.VMEM)


def heads(place, raw, cosine, sine, gq, gk):
    return pl.pallas_call(
        heads_kernel,
        out_shape=[jax.ShapeDtypeStruct((LOCAL, 2 * HEAD), low)] * 2,
        in_specs=[SCALARS] + [WHOLE] * 6,
        out_specs=[WHOLE] * 2,
        compiler_params=params(12),
        cost_estimate=cost(LOCAL * 512 * 10, LOCAL * 512 * 8),
    )(place, *raw, cosine, sine, gq, gk)


def heads_back_kernel(
    place, mine, away, cosine, sine, gq, gk, dquery, dpair, later, dmine, daway, dgain
):
    sums = [jnp.zeros((1, HEAD), wide)] * 2
    for i in range(8):
        raw, draw = (mine, away)[i // 4], (dmine, daway)[i // 4]
        here = pl.ds(i % 4 * BLOCK, BLOCK)
        there = pl.ds(pl.multiple_of(place[i] * BLOCK, BLOCK), BLOCK)
        c, s = cosine[there], sine[there]
        dp = dpair[pl.ds(pl.multiple_of(place[i] * BLOCK + BACK, BLOCK), BLOCK)]
        from_later = later[pl.ds(pl.multiple_of(jnp.maximum(place[i] - 1, 0) * BLOCK, BLOCK), BLOCK)]
        dp = dp + jnp.where(place[i] > 0, from_later.astype(wide), 0.0)
        for h in range(4):
            part = slice(h * HEAD, (h + 1) * HEAD)
            if h == 3:
                draw[here, part] = dp[:, HEAD:].astype(low)
                continue
            g = gq[...] if h < 2 else gk[...]
            d = dquery[there, part] if h < 2 else dp[:, :HEAD]
            d = d * c + pltpu.roll(d * s, HEAD // 2, 1)
            v = raw[here, part]
            r = lax.rsqrt(jnp.mean(v * v, axis=-1, keepdims=True) + epsilon)
            u = v * r
            sums[h // 2] += jnp.sum(d * u, axis=0, keepdims=True)
            e = d * g
            draw[here, part] = (r * (e - u * jnp.mean(u * e, axis=-1, keepdims=True))).astype(low)
    row = lax.broadcasted_iota(jnp.int32, (8, HEAD), 0)
    dgain[...] = jnp.where(row == 0, sums[0], jnp.where(row == 1, sums[1], 0.0))


def heads_back(place, raw, cosine, sine, gq, gk, dquery, dpair, later):
    return pl.pallas_call(
        heads_back_kernel,
        out_shape=[
            jax.ShapeDtypeStruct((LOCAL // 2, 4 * HEAD), low),
            jax.ShapeDtypeStruct((LOCAL // 2, 4 * HEAD), low),
            jax.ShapeDtypeStruct((8, HEAD), wide),
        ],
        in_specs=[SCALARS] + [WHOLE] * 9,
        out_specs=[WHOLE] * 3,
        compiler_params=params(16),
        cost_estimate=cost(LOCAL * 512 * 20, LOCAL * 512 * 12),
    )(place, *raw, cosine, sine, gq, gk, dquery, dpair, later)


ROWS = 256


def both_dots(lefts, rights, dims):
    return dot(lefts[0][...], rights[0][...], dims) + dot(lefts[1][...], rights[1][...], dims)


def grads_kernel(*refs):
    lefts, rights, out = refs[:4], refs[4:8], refs[8]
    n = rights[0].shape[1]
    out[:, :n] = both_dots(lefts[:2], rights[:2], (0, 0)).astype(low)
    out[:, n:] = both_dots(lefts[2:], rights[2:], (0, 0)).astype(low)


def grads(lefts, rights):
    depth, rows = lefts[0].shape
    total = rights[0].shape[1] + rights[2].shape[1]
    return pl.pallas_call(
        grads_kernel,
        out_shape=jax.ShapeDtypeStruct((rows, total), low),
        grid=(rows // ROWS,),
        in_specs=[spec((depth, ROWS), lambda i: (0, i))] * 4
        + [once(v.shape, lambda i: (0, 0)) for v in rights],
        out_specs=spec((ROWS, total), lambda i: (i, 0)),
        compiler_params=params(28),
        cost_estimate=cost(4 * depth * rows * total, 8 * depth * rows + 2 * total * (rows + depth)),
    )(*lefts, *rights)


def back_kernel(mine, away, right, out_mine, out_away):
    out_away[...] = dot(away[...], right[...], (1, 1)).astype(low)
    out_mine[...] = dot(mine[...], right[...], (1, 1)).astype(low)


def back_products(lefts, right):
    rows, depth = lefts[0].shape
    width = right.shape[0]
    return pl.pallas_call(
        back_kernel,
        out_shape=[jax.ShapeDtypeStruct((rows, width), low)] * 2,
        grid=(width // ROWS,),
        in_specs=[once((rows, depth), lambda i: (0, 0))] * 2
        + [spec((ROWS, depth), lambda i: (i, 0))],
        out_specs=[spec((rows, ROWS), lambda i: (0, i))] * 2,
        compiler_params=params(20),
        cost_estimate=cost(4 * rows * depth * width, 2 * width * (depth + 2 * rows)),
    )(*lefts, right)


def back_gain_kernel(mine, away, right, mine_in, away_in, mine_scale, away_scale, out_mine, out_away, gain):
    total = 0.0
    for left, values, scale, out in (
        (away, away_in, away_scale, out_away),
        (mine, mine_in, mine_scale, out_mine),
    ):
        product = dot(left[...], right[...], (1, 1))
        out[...] = product.astype(low)
        total += jnp.sum(product * (values[...].astype(wide) * scale[...]), axis=0, keepdims=True)
    gain[...] = total


def back_products_gain(lefts, right, values, scales):
    rows, depth = lefts[0].shape
    width = right.shape[0]
    columns = lambda i: (0, i)
    fixed = lambda i: (0, 0)
    return pl.pallas_call(
        back_gain_kernel,
        out_shape=[jax.ShapeDtypeStruct((rows, width), low)] * 2
        + [jax.ShapeDtypeStruct((1, width), wide)],
        grid=(width // ROWS,),
        in_specs=[once((rows, depth), fixed)] * 2
        + [spec((ROWS, depth), lambda i: (i, 0))]
        + [spec((rows, ROWS), columns)] * 2
        + [once((rows, 1), fixed)] * 2,
        out_specs=[spec((rows, ROWS), columns)] * 2 + [spec((1, ROWS), columns)],
        compiler_params=params(20),
        cost_estimate=cost(4 * rows * depth * width, 2 * width * (depth + 4 * rows)),
    )(*lefts, right, *values, *scales)


def adam_kernel(flipped, rates, *refs):
    grad = refs[0]
    at = 0
    for k, (turn, rate) in enumerate(zip(flipped, rates)):
        weight, first, second = refs[1 + 3 * k : 4 + 3 * k]
        outs = refs[1 + 3 * (len(rates) + k) : 4 + 3 * (len(rates) + k)]
        n = weight.shape[0] if turn else weight.shape[1]
        g = grad[:, at : at + n].astype(wide)
        at += n
        if turn:
            g = g.T
        for out, value in zip(outs, adam(weight[...], first[...], second[...], g, rate, weight_decay)):
            out[...] = value


def adam_weights(grad, weights, flipped, rates):
    states = [v for group in weights for v in group]
    out = pl.pallas_call(
        functools.partial(adam_kernel, flipped, rates),
        out_shape=[jax.ShapeDtypeStruct(v.shape, v.dtype) for v in states],
        in_specs=[WHOLE] * (1 + len(states)),
        out_specs=[WHOLE] * len(states),
        compiler_params=params(24),
        cost_estimate=cost(20 * grad.size, 26 * grad.size),
    )(grad, *states)
    return [tuple(out[3 * k : 3 * k + 3]) for k in range(len(weights))]


HALF = 384
TALL = BLOCK + 16


def first_grads_kernel(spot, *refs):
    normed, dmiddle, draw, attended, (dgains, left, right) = refs[:2], refs[2:4], refs[4:6], refs[6:8], refs[8:]
    project = both_dots(normed, draw, (0, 0)).astype(low)
    output = both_dots(dmiddle, attended, (0, 0)).astype(low)
    for j in range(2):
        rows = slice(j * BLOCK, (j + 1) * BLOCK)
        a = j ^ spot[1]
        left[0, a, 0] = project[rows, :HALF]
        right[a, 0, 0, :BLOCK, : 4 * HEAD - HALF] = project[rows, HALF:]
        right[a, 0, 0, :BLOCK, 4 * HEAD - HALF :] = output[rows]
        right[a, 0, 0, BLOCK:] = dgains[j]


def first_grads(spot, normed, dmiddle, draw, attended, dgains):
    whole = lambda i, s: (0, 0)
    columns = lambda i, s: (0, i)
    steps = lambda i, s: lax.rem(i // 2 - s[0] + 4, 4)
    return pl.pallas_call(
        first_grads_kernel,
        out_shape=[
            jax.ShapeDtypeStruct((4, 2, 2, BLOCK, HALF), low),
            jax.ShapeDtypeStruct((2, 2, 4, TALL, HALF), low),
        ],
        grid_spec=pltpu.PrefetchScalarGridSpec(
            num_scalar_prefetch=1,
            grid=(8,),
            in_specs=[
                *[spec((LOCAL // 2, 2 * BLOCK), columns)] * 4,
                *[once((LOCAL // 2, 4 * HEAD), whole)] * 2,
                *[once((LOCAL // 2, 2 * HEAD), whole)] * 2,
                spec((2, 16, HALF), lambda i, s: (i, 0, 0)),
            ],
            out_specs=[
                spec((1, 2, 1, BLOCK, HALF), lambda i, s: (steps(i, s), 0, i % 2 ^ s[2], 0, 0)),
                spec((2, 1, 1, TALL, HALF), lambda i, s: (0, i % 2 ^ s[2], steps(i, s), 0, 0)),
            ],
        ),
        compiler_params=params(24),
        cost_estimate=cost(2 * LOCAL * 2048 * 768, 14 * MIB),
    )(spot, *normed, *dmiddle, *draw, *attended, dgains)


SCALE = HEAD ** (-0.5)


def allowed(query_ids, key_ids, start):
    keys = key_ids[:, pl.ds(start, WINDOW)]
    row = lax.broadcasted_iota(jnp.int32, (QUERIES, WINDOW), 0)
    column = lax.broadcasted_iota(jnp.int32, (QUERIES, WINDOW), 1)
    return (query_ids[...] == keys) & (column <= row + BACK)


def attend_kernel(core, query, pair, query_ids, key_ids, out, logsum):
    i = pl.program_id(0)
    start = pl.multiple_of(i * QUERIES, QUERIES)
    mask = allowed(query_ids, key_ids, start)
    logs = []
    for h in range(2):
        part = slice(h * HEAD, (h + 1) * HEAD)
        scores = dot(query[:, part], pair[pl.ds(start, WINDOW), :HEAD], (1, 1)) * SCALE
        scores = jnp.where(mask, scores, -1e30)
        top = jnp.max(scores, axis=-1, keepdims=True)
        unnormed = jnp.exp(scores - top)
        total = jnp.sum(unnormed, axis=-1, keepdims=True)
        probs = (unnormed * (1.0 / total)).astype(low)
        result = dot(probs, pair[pl.ds(start, WINDOW), HEAD:], (1, 0)).astype(low)
        for j in range(2):
            out[j ^ core[0], 0, :, part] = result[j * BLOCK : (j + 1) * BLOCK]
        logs.append(top + jnp.log(total))
    lane = lax.broadcasted_iota(jnp.int32, (QUERIES, HEAD), 1)
    logsum[...] = jnp.where(lane < HEAD // 2, logs[0], logs[1])


def attend(core, query, pair, query_ids, key_ids):
    rows = lambda i, c: (i, 0)
    whole = lambda i, c: (0, 0)
    keys = BACK + LOCAL
    return pl.pallas_call(
        attend_kernel,
        out_shape=[
            jax.ShapeDtypeStruct((2, 4, BLOCK, 2 * HEAD), low),
            jax.ShapeDtypeStruct((LOCAL, HEAD), wide),
        ],
        grid_spec=pltpu.PrefetchScalarGridSpec(
            num_scalar_prefetch=1,
            grid=(LOCAL // QUERIES,),
            in_specs=[
                spec((QUERIES, 2 * HEAD), rows),
                once((keys, 2 * HEAD), whole),
                spec((QUERIES, 1), rows),
                spec((1, keys), whole),
            ],
            out_specs=[
                spec((2, 1, BLOCK, 2 * HEAD), lambda i, c: (0, i, 0, 0)),
                spec((QUERIES, HEAD), rows),
            ],
        ),
        compiler_params=params(24),
        cost_estimate=cost(
            4 * 2 * LOCAL * WINDOW * HEAD, 4 * LOCAL * 512, 2 * LOCAL * WINDOW
        ),
    )(core, query, pair, query_ids, key_ids)


def attend_back_kernel(
    core, query, pair, query_ids, key_ids, grad, logsum, dquery, dpair
):
    i = pl.program_id(0)

    @pl.when(i == 0)
    def _():
        dpair[...] = jnp.zeros_like(dpair)

    start = pl.multiple_of(i * QUERIES, QUERIES)
    window = pl.ds(start, WINDOW)
    mask = allowed(query_ids, key_ids, start)
    dkey, dvalue = None, None
    for h in range(2):
        part = slice(h * HEAD, (h + 1) * HEAD)
        q = query[:, part]
        g = jnp.concatenate([grad[j ^ core[0], 0, :, part] for j in range(2)], axis=0)
        scores = dot(q, pair[window, :HEAD], (1, 1)) * SCALE
        probs = jnp.where(mask, jnp.exp(scores - logsum[:, h * 64 : h * 64 + 1]), 0.0)
        dprobs = dot(g, pair[window, HEAD:], (1, 1))
        inner = jnp.sum(probs * dprobs, axis=-1, keepdims=True)
        dscores = (probs * (dprobs - inner)).astype(low)
        dquery[:, part] = dot(dscores, pair[window, :HEAD], (1, 0)) * SCALE
        dv = dot(probs.astype(low), g, (0, 0))
        dk = dot(dscores, q, (0, 0))
        dkey = dk if dkey is None else dkey + dk
        dvalue = dv if dvalue is None else dvalue + dv
    dpair[window, :HEAD] += dkey * SCALE
    dpair[window, HEAD:] += dvalue


def attend_back(core, query, pair, query_ids, key_ids, grad, logsum):
    rows = lambda i, c: (i, 0)
    whole = lambda i, c: (0, 0)
    keys = BACK + LOCAL
    return pl.pallas_call(
        attend_back_kernel,
        out_shape=[
            jax.ShapeDtypeStruct((LOCAL, 2 * HEAD), wide),
            jax.ShapeDtypeStruct((keys, 2 * HEAD), wide),
        ],
        grid_spec=pltpu.PrefetchScalarGridSpec(
            num_scalar_prefetch=1,
            grid=(LOCAL // QUERIES,),
            in_specs=[
                spec((QUERIES, 2 * HEAD), rows),
                once((keys, 2 * HEAD), whole),
                spec((QUERIES, 1), rows),
                spec((1, keys), whole),
                spec((2, 1, BLOCK, 2 * HEAD), lambda i, c: (0, i, 0, 0)),
                spec((QUERIES, HEAD), rows),
            ],
            out_specs=[spec((QUERIES, 2 * HEAD), rows), once((keys, 2 * HEAD), whole)],
        ),
        compiler_params=params(28),
        cost_estimate=cost(
            260 * 2 * LOCAL * WINDOW * HEAD, 8 * LOCAL * 512, 2 * LOCAL * WINDOW
        ),
    )(core, query, pair, query_ids, key_ids, grad, logsum)


def per_device(
    inputs,
    cotangent,
    document_index,
    positions,
    gains,
    gains_first,
    gains_second,
    project_weight,
    project_first,
    project_second,
    output_weight,
    output_first,
    output_second,
    expand_weight,
    expand_first,
    expand_second,
    shrink_weight,
    shrink_first,
    shrink_second,
):
    core, x = lax.axis_index("core"), lax.axis_index("x")
    half, yl = lax.axis_index("yh"), lax.axis_index("yl")
    width = inputs.shape[-1]
    qkv = project_weight.shape[1]
    ff = shrink_weight.shape[0]
    at_home = core == yl
    steps = jnp.arange(8, dtype=jnp.int32)
    place = steps % 4 * 2 + (core ^ (steps // 4))
    core_of = core.reshape(1).astype(jnp.int32)
    flag = at_home.astype(jnp.int32).reshape(1)

    marks = jnp.stack([document_index[0], positions[0] // 32, positions[0] % 32])
    marks = jnp.pad(marks.astype(low), ((0, 13), (0, 0)))
    message = trade(jnp.concatenate([inputs[0], marks], axis=0))
    rows = message[:BLOCK]
    marks = message[BLOCK:].astype(jnp.int32)
    ids, places = marks[0], marks[1] * 32 + marks[2]

    gain_block = jnp.pad(gains.astype(low), (0, BLOCK * BLOCK - gains.shape[0])).reshape(BLOCK, BLOCK)
    first_shard = jnp.concatenate(
        [project_weight.astype(low), output_weight.astype(low).T, gain_block], axis=1
    )
    second_shard = jnp.concatenate([expand_weight.astype(low), shrink_weight.astype(low).T], axis=1)
    first_all = lax.all_gather(to_group(first_shard), GROUP, axis=0, tiled=True)
    rows_all = gather_rows(rows)
    second_shard = after(second_shard, rows_all[1])
    second_all = lax.all_gather(to_group(second_shard), GROUP, axis=0, tiled=True)
    project_all = first_all[:, :qkv]
    output_all = first_all[:, qkv : qkv + 2 * HEAD]
    expand_all = second_all[:, : 2 * ff]
    shrink_all = second_all[:, 2 * ff :]
    gain_all = first_all[:, qkv + 2 * HEAD :].reshape(16, BLOCK * BLOCK)[:, : gains.shape[0]]
    gain_all = gain_all.reshape(-1).astype(wide)
    gain_one = gain_all[:width]
    gain_two = gain_all[width : 2 * width]
    gain_query = gain_all[2 * width : 2 * width + HEAD].reshape(1, HEAD)
    gain_key = gain_all[2 * width + HEAD :].reshape(1, HEAD)

    ids_here = lax.dynamic_slice_in_dim(ids, half * LOCAL, LOCAL)
    places_here = lax.dynamic_slice_in_dim(places, half * LOCAL, LOCAL)
    ids_keys = jnp.where(
        half == 0,
        jnp.concatenate([jnp.full((BACK,), -1, jnp.int32), ids[:LOCAL]]),
        ids[LOCAL - BACK :],
    )
    query_ids, key_ids = ids_here.reshape(-1, 1), ids_keys.reshape(1, -1)
    frequency = jnp.exp(jnp.arange(HEAD // 2, dtype=wide) * (-2.0 * math.log(theta) / HEAD))
    angle = places_here.astype(wide)[:, None] * frequency
    cosine, sine = jnp.cos(angle), jnp.sin(angle)
    cosine = jnp.concatenate([cosine, cosine], axis=1)
    sine = jnp.concatenate([-sine, sine], axis=1)

    values = rows.astype(wide)
    scale_all = [
        lax.rsqrt(jnp.mean(jnp.square(v.astype(wide)), axis=-1, keepdims=True) + epsilon)
        for v in rows_all
    ]
    normed = [(v.astype(wide) * r * gain_one).astype(low) for v, r in zip(rows_all, scale_all)]
    raw = [dot(v, project_all, (1, 0)) for v in normed]
    query, pair = heads(place, raw, cosine, sine, gain_query, gain_key)
    earlier = move(pair[LOCAL - BACK :], "yh", [(0, 1)])
    pair_all = jnp.concatenate([earlier, pair], axis=0)
    attended, logsum = attend(core_of, query, pair_all, query_ids, key_ids)
    attended = [attended[j].reshape(LOCAL // 2, 2 * HEAD) for j in range(2)]
    mine, away = [dot(v, output_all, (1, 1)).astype(low) for v in attended]
    middle = values + chip_sum(core_sum(mine, away))

    normed_two = gather_rows(rms_norm(middle, gain_two).astype(low))
    back_all = choose(place, flag, cotangent[0], other_core(cotangent[0]))
    back = [back_all[: LOCAL // 2], back_all[LOCAL // 2 :]]
    hidden, dexpanded = [], []
    for v, dy in zip(normed_two, back):
        expanded = dot(v, expand_all, (1, 0))
        activated, pull_act = jax.vjp(swiglu, expanded[:, :ff], expanded[:, ff:])
        hidden.append(activated.astype(low))
        dgate, dup = pull_act(dot(dy, shrink_all, (1, 0)))
        dexpanded.append(jnp.concatenate([dgate, dup], axis=1).astype(low))
    both_two = core_sum(*back_products(dexpanded, second_all))
    drows_two = chip_sum(both_two)
    second_grads = grads(
        [*after(tuple(normed_two), both_two), *back], [*dexpanded, *hidden]
    )
    second_red = lax.psum_scatter(second_grads, GROUP, scatter_dimension=0, tiled=True)
    drows_two = after(drows_two, second_grads)
    shrunk = core_sum(
        *[dot(v, shrink_all, (1, 1)).astype(low) for v in after(tuple(hidden), second_grads)]
    )

    _, pull_two = jax.vjp(rms_norm, middle, gain_two)
    dmiddle, dgain_two = pull_two(drows_two)
    dmiddle = lax.dynamic_slice_in_dim(back[0], x * BLOCK, BLOCK).astype(wide) + dmiddle
    dmiddle_all = gather_rows(dmiddle.astype(low))
    dmiddle_all = after(tuple(dmiddle_all), shrunk)
    dattended = jnp.stack([dot(v, output_all, (1, 0)).astype(low) for v in dmiddle_all])
    outputs = (middle + chip_sum(after(shrunk, dmiddle_all))).astype(low)
    dquery, dpair = attend_back(
        core_of,
        query,
        pair_all,
        query_ids,
        key_ids,
        dattended.reshape(2, 4, BLOCK, 2 * HEAD),
        logsum,
    )
    later = move(dpair[:BACK].astype(low), "yh", [(1, 0)])
    later = after(later, outputs)
    *draw, dgain_heads = heads_back(
        place, raw, cosine, sine, gain_query, gain_key, dquery, dpair, later
    )
    mine, away, dgain_one = back_products_gain(draw, first_all, rows_all, scale_all)
    both_one = core_sum(mine, away)
    drows_one = chip_sum(both_one)

    dgains = jnp.concatenate([dgain_one[0], dgain_two, dgain_heads[0], dgain_heads[1]]).astype(low)
    dgains = jnp.pad(dgains.reshape(16, 1, -1), ((0, 0), (0, 15), (0, HALF - gains.shape[0])))
    spot = jnp.stack([lax.axis_index("z"), half, yl]).astype(jnp.int32)
    left, right = first_grads(spot, normed, dmiddle_all, draw, attended, dgains)
    left, right = sum_steps(left).astype(low), sum_flips(right).astype(low)
    second_red = to_owner(second_red)
    expand_new, shrink_new = adam_weights(
        second_red,
        [(expand_weight, expand_first, expand_second), (shrink_weight, shrink_first, shrink_second)],
        (False, True),
        (0.05, 0.03),
    )
    left, right = after((left, right), expand_new[0], trade_out := trade(outputs))

    _, pull_one = jax.vjp(rms_norm, values, gain_one)
    dvalues, _ = pull_one(drows_one)
    input_grad = trade((dmiddle + dvalues).astype(low))

    left, right = sum_flips(left), sum_steps(right)
    first_red = jnp.concatenate([left, right[:BLOCK]], axis=1)
    project_new, output_new = adam_weights(
        first_red,
        [(project_weight, project_first, project_second), (output_weight, output_first, output_second)],
        (False, True),
        (0.05, 0.4),
    )
    dgains = right[BLOCK : BLOCK + 8]
    dgains = dgains + move(dgains, "yl", [(0, 1), (1, 0)])
    dgains = dgains + shift(dgains, 1) + shift(dgains, 2) + shift(dgains, 3)
    dgains = dgains[0, : gains.shape[0]]
    return (
        trade_out[None],
        input_grad[None],
        *adam(gains, gains_first, gains_second, dgains, 0.5, 0.0),
        *project_new,
        *output_new,
        *expand_new,
        *shrink_new,
    )


def solution(mesh):
    fine = Mesh(mesh.devices.reshape(4, 2, 2, 4, 2), ("z", "core", "yh", "x", "yl"))
    tokens = P(("z", "core"), ("yh", "x", "yl"), None)
    marks = P(("z", "core"), None)
    gain = P(("z", "core", "yh"))
    tall = P(("z", "core", "yh"), ("x", "yl"))
    flat = P(("x", "yl"), ("z", "core", "yh"))
    in_specs = (
        tokens,
        P(("z", "core"), "yh", None),
        marks,
        marks,
        *[gain] * 3,
        *[tall] * 3,
        *[flat] * 3,
        *[tall] * 3,
        *[flat] * 3,
    )
    out_specs = (
        tokens,
        tokens,
        *[gain] * 3,
        *[tall] * 3,
        *[flat] * 3,
        *[tall] * 3,
        *[flat] * 3,
    )
    return jax.shard_map(
        per_device, mesh=fine, in_specs=in_specs, out_specs=out_specs, check_vma=False
    )
```

```python
import functools
import math

import jax
import jax.numpy as jnp
from jax import lax
from jax.experimental import pallas as pl
from jax.experimental.pallas import tpu as pltpu
from jax.sharding import Mesh
from jax.sharding import PartitionSpec as P

QUERY_HEADS = 16
KEY_VALUE_HEADS = 8
HEAD = 128
STEP = 5
LONGEST = 800
BLOCK = 128
LOCAL = 1024
BACK = 896
QUERIES = 256
WINDOW = BACK + QUERIES

epsilon = 1e-06
theta = 1000000.0
beta_first = 0.9
beta_second = 0.95
adam_epsilon = 1e-08
weight_decay = 0.1

low = jnp.bfloat16
wide = jnp.float32
MIB = 1024 * 1024
ATTEND_HINT = 300
ATTEND_BACK_HINT = 260


def rms_norm(values, gain):
    return values * lax.rsqrt(jnp.mean(values * values, axis=-1, keepdims=True) + epsilon) * gain


def swiglu(gate, upward):
    return jax.nn.silu(gate) * upward


def adam(weight, first, second, grad, rate, decay_rate):
    mean = beta_first * first + (1.0 - beta_first) * grad
    square = beta_second * second + (1.0 - beta_second) * grad * grad
    mean_hat = mean / (1.0 - beta_first**STEP)
    square_hat = square / (1.0 - beta_second**STEP)
    updated = weight - rate * (
        mean_hat / (jnp.sqrt(square_hat) + adam_epsilon) + decay_rate * weight
    )
    return (mean, square, updated)


def dot(left, right, dims):
    return lax.dot_general(left, right, ((dims[:1], dims[1:]), ((), ())), preferred_element_type=wide)


def move(values, axis, pairs):
    return lax.ppermute(values, axis, pairs)


def shift(values, steps):
    return move(values, "x", [(i, (i + steps) % 4) for i in range(4)])


def other_core(values):
    return move(values, "core", [(0, 1), (1, 0)])


def trade(values):
    return move(values, ("core", "yl"), [(a * 2 + b, b * 2 + a) for a in range(2) for b in range(2)])


def to_group(values):
    pairs = [
        ((a * 2 + b) * 2 + d, (d * 2 + a) * 2 + b)
        for a in range(2)
        for b in range(2)
        for d in range(2)
    ]
    return move(values, ("core", "yh", "yl"), pairs)


def to_owner(values):
    pairs = [
        ((d * 2 + a) * 2 + b, (a * 2 + b) * 2 + d)
        for a in range(2)
        for b in range(2)
        for d in range(2)
    ]
    return move(values, ("core", "yh", "yl"), pairs)


def gather_rows(values):
    mine = jnp.concatenate([values, shift(values, 1), shift(values, 2), shift(values, 3)], axis=0)
    return mine, other_core(mine)


def core_sum(mine, away):
    return (mine.astype(wide) + other_core(away).astype(wide)).astype(low)


def chip_sum(both):
    pieces = both.reshape(4, BLOCK, -1)
    total = pieces[0].astype(wide)
    for k in (2, 1, 3):
        total = total + shift(pieces[k], 4 - k).astype(wide)
    return total


def after(values, *others):
    return lax.optimization_barrier((values, *others))[0]


def sum_z(blocks):
    return jnp.sum(lax.all_to_all(blocks, "z", 0, 0, tiled=True).astype(wide), axis=0)


def flip(values, a, b):
    pairs = [
        ((c * 2 + h) * 2 + d, ((d ^ b) * 2 + (h ^ a)) * 2 + c)
        for c in range(2)
        for h in range(2)
        for d in range(2)
    ]
    return move(values, ("core", "yh", "yl"), pairs)


def sum_flips(pieces):
    first = [flip(pieces[1, b], 1, b) for b in (1, 0)]
    rest = after(pieces[0], *first)
    total = first[0].astype(wide) + first[1].astype(wide)
    for b in (1, 0):
        total = total + flip(rest[b], 0, b).astype(wide)
    return total


GROUP = ("z", "yh", "yl")


def spec(shape, index):
    return pl.BlockSpec(shape, index)


def once(shape, index):
    return pl.BlockSpec(shape, index, pipeline_mode=pl.Buffered(1))


def params(mib):
    return pltpu.CompilerParams(vmem_limit_bytes=mib * MIB)


def cost(flops, moved, special=0):
    return pl.CostEstimate(flops=flops, bytes_accessed=moved, transcendentals=special)


def choose_kernel(place, flag, own, away, out, arrived):
    def copies(source):
        return [
            pltpu.make_async_copy(
                source.at[pl.ds(pl.multiple_of(place[i] * BLOCK, BLOCK), BLOCK)],
                out.at[pl.ds(i * BLOCK, BLOCK)],
                arrived.at[i],
            )
            for i in range(8)
        ]

    @pl.when(flag[0] == 1)
    def _():
        for copy in copies(own):
            copy.start()

    @pl.when(flag[0] == 0)
    def _():
        for copy in copies(away):
            copy.start()

    for copy in copies(own):
        copy.wait()


def choose(place, flag, own, away):
    scalar = pl.BlockSpec(memory_space=pltpu.SMEM)
    there = pl.BlockSpec(memory_space=pl.ANY)
    return pl.pallas_call(
        choose_kernel,
        out_shape=jax.ShapeDtypeStruct(own.shape, own.dtype),
        in_specs=[scalar, scalar, there, there],
        out_specs=there,
        scratch_shapes=[pltpu.SemaphoreType.DMA((8,))],
        compiler_params=params(4),
        cost_estimate=cost(0, 2 * own.size * 2),
    )(place, flag, own, away)


def heads_kernel(place, mine, away, cosine, sine, gq, gk, query, pair):
    for i in range(8):
        raw = (mine, away)[i // 4]
        here = pl.ds(i % 4 * BLOCK, BLOCK)
        there = pl.ds(pl.multiple_of(place[i] * BLOCK, BLOCK), BLOCK)
        c, s = cosine[there], sine[there]
        for h in range(4):
            part = slice(h * HEAD, (h + 1) * HEAD)
            v = raw[here, part]
            if h < 3:
                v = rms_norm(v, gq[...] if h < 2 else gk[...])
                v = v * c + pltpu.roll(v, HEAD // 2, 1) * s
            if h < 2:
                query[there, part] = v.astype(low)
            else:
                pair[there, (h - 2) * HEAD : (h - 1) * HEAD] = v.astype(low)


SCALARS = pl.BlockSpec(memory_space=pltpu.SMEM)
WHOLE = pl.BlockSpec(memory_space=pltpu.VMEM)


def heads(place, raw, cosine, sine, gq, gk):
    return pl.pallas_call(
        heads_kernel,
        out_shape=[jax.ShapeDtypeStruct((LOCAL, 2 * HEAD), low)] * 2,
        in_specs=[SCALARS] + [WHOLE] * 6,
        out_specs=[WHOLE] * 2,
        compiler_params=params(12),
        cost_estimate=cost(LOCAL * 512 * 10, LOCAL * 512 * 8),
    )(place, *raw, cosine, sine, gq, gk)


def heads_back_kernel(
    place, mine, away, cosine, sine, gq, gk, dquery, dpair, later, dmine, daway, dgain
):
    sums = [jnp.zeros((1, HEAD), wide)] * 2
    for i in range(8):
        raw, draw = (mine, away)[i // 4], (dmine, daway)[i // 4]
        here = pl.ds(i % 4 * BLOCK, BLOCK)
        there = pl.ds(pl.multiple_of(place[i] * BLOCK, BLOCK), BLOCK)
        c, s = cosine[there], sine[there]
        dp = dpair[pl.ds(pl.multiple_of(place[i] * BLOCK + BACK, BLOCK), BLOCK)]
        from_later = later[pl.ds(pl.multiple_of(jnp.maximum(place[i] - 1, 0) * BLOCK, BLOCK), BLOCK)]
        dp = dp + jnp.where(place[i] > 0, from_later.astype(wide), 0.0)
        for h in range(4):
            part = slice(h * HEAD, (h + 1) * HEAD)
            if h == 3:
                draw[here, part] = dp[:, HEAD:].astype(low)
                continue
            g = gq[...] if h < 2 else gk[...]
            d = dquery[there, part] if h < 2 else dp[:, :HEAD]
            d = d * c + pltpu.roll(d * s, HEAD // 2, 1)
            v = raw[here, part]
            r = lax.rsqrt(jnp.mean(v * v, axis=-1, keepdims=True) + epsilon)
            u = v * r
            sums[h // 2] += jnp.sum(d * u, axis=0, keepdims=True)
            e = d * g
            draw[here, part] = (r * (e - u * jnp.mean(u * e, axis=-1, keepdims=True))).astype(low)
    row = lax.broadcasted_iota(jnp.int32, (8, HEAD), 0)
    dgain[...] = jnp.where(row == 0, sums[0], jnp.where(row == 1, sums[1], 0.0))


def heads_back(place, raw, cosine, sine, gq, gk, dquery, dpair, later):
    return pl.pallas_call(
        heads_back_kernel,
        out_shape=[
            jax.ShapeDtypeStruct((LOCAL // 2, 4 * HEAD), low),
            jax.ShapeDtypeStruct((LOCAL // 2, 4 * HEAD), low),
            jax.ShapeDtypeStruct((8, HEAD), wide),
        ],
        in_specs=[SCALARS] + [WHOLE] * 9,
        out_specs=[WHOLE] * 3,
        compiler_params=params(16),
        cost_estimate=cost(LOCAL * 512 * 20, LOCAL * 512 * 12),
    )(place, *raw, cosine, sine, gq, gk, dquery, dpair, later)


ROWS = 256


def both_dots(lefts, rights, dims):
    return dot(lefts[0][...], rights[0][...], dims) + dot(lefts[1][...], rights[1][...], dims)


def grads_kernel(*refs):
    lefts, rights, out = refs[:4], refs[4:8], refs[8]
    n = rights[0].shape[1]
    out[:, :n] = both_dots(lefts[:2], rights[:2], (0, 0)).astype(low)
    out[:, n:] = both_dots(lefts[2:], rights[2:], (0, 0)).astype(low)


def grads(lefts, rights):
    depth, rows = lefts[0].shape
    total = rights[0].shape[1] + rights[2].shape[1]
    return pl.pallas_call(
        grads_kernel,
        out_shape=jax.ShapeDtypeStruct((rows, total), low),
        grid=(rows // ROWS,),
        in_specs=[spec((depth, ROWS), lambda i: (0, i))] * 4
        + [once(v.shape, lambda i: (0, 0)) for v in rights],
        out_specs=spec((ROWS, total), lambda i: (i, 0)),
        compiler_params=params(28),
        cost_estimate=cost(4 * depth * rows * total, 8 * depth * rows + 2 * total * (rows + depth)),
    )(*lefts, *rights)


def back_kernel(mine, away, right, out_mine, out_away):
    turned = right[...].T
    out_away[...] = dot(away[...], turned, (1, 0)).astype(low)
    out_mine[...] = dot(mine[...], turned, (1, 0)).astype(low)


def back_products(lefts, right, at=0, hint=1):
    rows, depth = lefts[0].shape
    width = right.shape[0]
    return pl.pallas_call(
        back_kernel,
        out_shape=[jax.ShapeDtypeStruct((rows, width), low)] * 2,
        grid=(width // ROWS,),
        in_specs=[once((rows, depth), lambda i: (0, 0))] * 2
        + [spec((ROWS, depth), lambda i: (i, at))],
        out_specs=[spec((rows, ROWS), lambda i: (0, i))] * 2,
        compiler_params=params(20),
        cost_estimate=cost(4 * rows * depth * width * hint, 2 * width * (depth + 2 * rows) * hint),
    )(*lefts, right)


def back_gain_kernel(mine, away, right, mine_in, away_in, mine_scale, away_scale, out_mine, out_away, gain):
    total = 0.0
    turned = right[...].T
    for left, values, scale, out in (
        (away, away_in, away_scale, out_away),
        (mine, mine_in, mine_scale, out_mine),
    ):
        product = dot(left[...], turned, (1, 0))
        out[...] = product.astype(low)
        total += jnp.sum(product * (values[...].astype(wide) * scale[...]), axis=0, keepdims=True)
    gain[...] = total


def back_products_gain(lefts, right, values, scales):
    rows, depth = lefts[0].shape
    width = right.shape[0]
    columns = lambda i: (0, i)
    fixed = lambda i: (0, 0)
    return pl.pallas_call(
        back_gain_kernel,
        out_shape=[jax.ShapeDtypeStruct((rows, width), low)] * 2
        + [jax.ShapeDtypeStruct((1, width), wide)],
        grid=(width // ROWS,),
        in_specs=[once((rows, depth), fixed)] * 2
        + [spec((ROWS, depth), lambda i: (i, 0))]
        + [spec((rows, ROWS), columns)] * 2
        + [once((rows, 1), fixed)] * 2,
        out_specs=[spec((rows, ROWS), columns)] * 2 + [spec((1, ROWS), columns)],
        compiler_params=params(20),
        cost_estimate=cost(4 * rows * depth * width, 2 * width * (depth + 4 * rows)),
    )(*lefts, right, *values, *scales)


def adam_kernel(flipped, rates, *refs):
    grad = refs[0]
    at = 0
    for k, (turn, rate) in enumerate(zip(flipped, rates)):
        weight, first, second = refs[1 + 3 * k : 4 + 3 * k]
        outs = refs[1 + 3 * (len(rates) + k) : 4 + 3 * (len(rates) + k)]
        n = weight.shape[0] if turn else weight.shape[1]
        g = grad[:, at : at + n].astype(wide)
        at += n
        if turn:
            g = g.T
        for out, value in zip(outs, adam(weight[...], first[...], second[...], g, rate, weight_decay)):
            out[...] = value


def adam_weights(grad, weights, flipped, rates):
    states = [v for group in weights for v in group]
    out = pl.pallas_call(
        functools.partial(adam_kernel, flipped, rates),
        out_shape=[jax.ShapeDtypeStruct(v.shape, v.dtype) for v in states],
        in_specs=[WHOLE] * (1 + len(states)),
        out_specs=[WHOLE] * len(states),
        compiler_params=params(24),
        cost_estimate=cost(20 * grad.size, 26 * grad.size),
    )(grad, *states)
    return [tuple(out[3 * k : 3 * k + 3]) for k in range(len(weights))]


HALF = 384
TALL = BLOCK + 16


def first_grads_kernel(spot, *refs):
    normed, dmiddle, draw, attended, (dgains, left, right) = refs[:2], refs[2:4], refs[4:6], refs[6:8], refs[8:]
    project = both_dots(normed, draw, (0, 0)).astype(low)
    output = both_dots(dmiddle, attended, (0, 0)).astype(low)
    for j in range(2):
        rows = slice(j * BLOCK, (j + 1) * BLOCK)
        a = j ^ spot[0]
        left[0, a, 0] = project[rows, :HALF]
        right[a, 0, 0, :BLOCK, : 4 * HEAD - HALF] = project[rows, HALF:]
        right[a, 0, 0, :BLOCK, 4 * HEAD - HALF :] = output[rows]
        right[a, 0, 0, BLOCK:] = dgains[j]


def first_grads(spot, normed, dmiddle, draw, attended, dgains):
    whole = lambda i, s: (0, 0)
    columns = lambda i, s: (0, i)
    return pl.pallas_call(
        first_grads_kernel,
        out_shape=[
            jax.ShapeDtypeStruct((4, 2, 2, BLOCK, HALF), low),
            jax.ShapeDtypeStruct((2, 2, 4, TALL, HALF), low),
        ],
        grid_spec=pltpu.PrefetchScalarGridSpec(
            num_scalar_prefetch=1,
            grid=(8,),
            in_specs=[
                *[spec((LOCAL // 2, 2 * BLOCK), columns)] * 4,
                *[once((LOCAL // 2, 4 * HEAD), whole)] * 2,
                *[once((LOCAL // 2, 2 * HEAD), whole)] * 2,
                spec((2, 16, HALF), lambda i, s: (i, 0, 0)),
            ],
            out_specs=[
                spec((1, 2, 1, BLOCK, HALF), lambda i, s: (i // 2, 0, i % 2 ^ s[1], 0, 0)),
                spec((2, 1, 1, TALL, HALF), lambda i, s: (0, i % 2 ^ s[1], i // 2, 0, 0)),
            ],
        ),
        compiler_params=params(24),
        cost_estimate=cost(2 * LOCAL * 2048 * 768, 14 * MIB),
    )(spot, *normed, *dmiddle, *draw, *attended, dgains)


SCALE = HEAD ** (-0.5)


def allowed(query_ids, key_ids, start):
    keys = key_ids[:, pl.ds(start, WINDOW)]
    row = lax.broadcasted_iota(jnp.int32, (QUERIES, WINDOW), 0)
    column = lax.broadcasted_iota(jnp.int32, (QUERIES, WINDOW), 1)
    return (query_ids[...] == keys) & (column <= row + BACK)


def attend_kernel(turn, core, query, pair, query_ids, key_ids, out, logsum):
    i = pl.program_id(0)
    start = pl.multiple_of(i * QUERIES, QUERIES)
    mask = allowed(query_ids, key_ids, start)
    logs = []
    for h in range(2):
        part = slice(h * HEAD, (h + 1) * HEAD)
        scores = dot(query[:, part], pair[pl.ds(start, WINDOW), :HEAD], (1, 1)) * SCALE
        scores = jnp.where(mask, scores, -1e30)
        top = jnp.max(scores, axis=-1, keepdims=True)
        unnormed = jnp.exp(scores - top)
        total = jnp.sum(unnormed, axis=-1, keepdims=True)
        probs = (unnormed * (1.0 / total)).astype(low)
        result = dot(probs, pair[pl.ds(start, WINDOW), HEAD:], (1, 0)).astype(low)
        for j in range(2):
            out[j ^ core[0], 0, :, part] = result[j * BLOCK : (j + 1) * BLOCK]
        logs.append(top + jnp.log(total))
    lane = lax.broadcasted_iota(jnp.int32, (QUERIES, HEAD), 1)
    logsum[...] = jnp.where(lane < HEAD // 2, logs[0], logs[1])


def attend(turn, core, query, pair, query_ids, key_ids):
    rows = lambda i, t, c: (i, 0)
    whole = lambda i, t, c: (0, 0)
    keys = BACK + LOCAL
    return pl.pallas_call(
        attend_kernel,
        out_shape=[
            jax.ShapeDtypeStruct((2, 4, BLOCK, 2 * HEAD), low),
            jax.ShapeDtypeStruct((LOCAL, HEAD), wide),
        ],
        grid_spec=pltpu.PrefetchScalarGridSpec(
            num_scalar_prefetch=2,
            grid=(LOCAL // QUERIES,),
            in_specs=[
                spec((QUERIES, 2 * HEAD), rows),
                once((keys, 2 * HEAD), whole),
                spec((QUERIES, 1), rows),
                spec((1, keys), whole),
            ],
            out_specs=[
                spec((2, 1, BLOCK, 2 * HEAD), lambda i, t, c: (0, t[i], 0, 0)),
                spec((QUERIES, HEAD), rows),
            ],
        ),
        compiler_params=params(24),
        cost_estimate=cost(
            ATTEND_HINT * 2 * LOCAL * WINDOW * HEAD, 4 * LOCAL * 512, 2 * LOCAL * WINDOW
        ),
    )(turn, core, query, pair, query_ids, key_ids)


def attend_back_kernel(
    turn, core, query, pair, query_ids, key_ids, grad, logsum, dquery, dpair
):
    i = pl.program_id(0)

    @pl.when(i == 0)
    def _():
        dpair[...] = jnp.zeros_like(dpair)

    start = pl.multiple_of(i * QUERIES, QUERIES)
    window = pl.ds(start, WINDOW)
    mask = allowed(query_ids, key_ids, start)
    dkey, dvalue = None, None
    for h in range(2):
        part = slice(h * HEAD, (h + 1) * HEAD)
        q = query[:, part]
        g = jnp.concatenate([grad[j ^ core[0], 0, :, part] for j in range(2)], axis=0)
        scores = dot(q, pair[window, :HEAD], (1, 1)) * SCALE
        probs = jnp.where(mask, jnp.exp(scores - logsum[:, h * 64 : h * 64 + 1]), 0.0)
        dprobs = dot(g, pair[window, HEAD:], (1, 1))
        inner = jnp.sum(probs * dprobs, axis=-1, keepdims=True)
        dscores = (probs * (dprobs - inner)).astype(low)
        dquery[:, part] = dot(dscores, pair[window, :HEAD], (1, 0)) * SCALE
        dv = dot(probs.astype(low), g, (0, 0))
        dk = dot(dscores, q, (0, 0))
        dkey = dk if dkey is None else dkey + dk
        dvalue = dv if dvalue is None else dvalue + dv
    dpair[window, :HEAD] += dkey * SCALE
    dpair[window, HEAD:] += dvalue


def attend_back(turn, core, query, pair, query_ids, key_ids, grad, logsum):
    rows = lambda i, t, c: (i, 0)
    whole = lambda i, t, c: (0, 0)
    keys = BACK + LOCAL
    return pl.pallas_call(
        attend_back_kernel,
        out_shape=[
            jax.ShapeDtypeStruct((LOCAL, 2 * HEAD), wide),
            jax.ShapeDtypeStruct((keys, 2 * HEAD), wide),
        ],
        grid_spec=pltpu.PrefetchScalarGridSpec(
            num_scalar_prefetch=2,
            grid=(LOCAL // QUERIES,),
            in_specs=[
                spec((QUERIES, 2 * HEAD), rows),
                once((keys, 2 * HEAD), whole),
                spec((QUERIES, 1), rows),
                spec((1, keys), whole),
                spec((2, 1, BLOCK, 2 * HEAD), lambda i, t, c: (0, t[i], 0, 0)),
                spec((QUERIES, HEAD), rows),
            ],
            out_specs=[spec((QUERIES, 2 * HEAD), rows), once((keys, 2 * HEAD), whole)],
        ),
        compiler_params=params(28),
        cost_estimate=cost(
            ATTEND_BACK_HINT * 2 * LOCAL * WINDOW * HEAD, 8 * LOCAL * 512, 2 * LOCAL * WINDOW
        ),
    )(turn, core, query, pair, query_ids, key_ids, grad, logsum)


def per_device(
    inputs,
    cotangent,
    document_index,
    positions,
    gains,
    gains_first,
    gains_second,
    project_weight,
    project_first,
    project_second,
    output_weight,
    output_first,
    output_second,
    expand_weight,
    expand_first,
    expand_second,
    shrink_weight,
    shrink_first,
    shrink_second,
):
    core, x = lax.axis_index("core"), lax.axis_index("x")
    half, yl = lax.axis_index("yh"), lax.axis_index("yl")
    width = inputs.shape[-1]
    qkv = project_weight.shape[1]
    ff = shrink_weight.shape[0]
    at_home = core == yl
    steps = jnp.arange(8, dtype=jnp.int32)
    place = lax.rem(x - steps % 4 + 4, 4) * 2 + (core ^ (steps // 4))
    turn = lax.rem(x - jnp.arange(4, dtype=jnp.int32) + 4, 4)
    core_of = core.reshape(1).astype(jnp.int32)
    flag = at_home.astype(jnp.int32).reshape(1)

    marks = jnp.stack([document_index[0], positions[0] // 32, positions[0] % 32])
    marks = jnp.pad(marks.astype(low), ((0, 13), (0, 0)))
    message = trade(jnp.concatenate([inputs[0], marks], axis=0))
    rows = message[:BLOCK]
    marks = message[BLOCK:].astype(jnp.int32)
    ids, places = marks[0], marks[1] * 32 + marks[2]

    gain_block = jnp.pad(gains.astype(low), (0, BLOCK * BLOCK - gains.shape[0])).reshape(BLOCK, BLOCK)
    first_shard = jnp.concatenate(
        [project_weight.astype(low), output_weight.astype(low).T, gain_block], axis=1
    )
    second_shard = jnp.concatenate([expand_weight.astype(low), shrink_weight.astype(low).T], axis=1)
    first_all = lax.all_gather(to_group(first_shard), GROUP, axis=0, tiled=True)
    rows_all = gather_rows(rows)
    second_shard = after(second_shard, first_all)
    second_all = lax.all_gather(to_group(second_shard), GROUP, axis=0, tiled=True)
    project_all = first_all[:, :qkv]
    output_all = first_all[:, qkv : qkv + 2 * HEAD]
    expand_all = second_all[:, : 2 * ff]
    shrink_all = second_all[:, 2 * ff :]
    gain_all = first_all[:, qkv + 2 * HEAD :].reshape(16, BLOCK * BLOCK)[:, : gains.shape[0]]
    gain_all = gain_all.reshape(-1).astype(wide)
    gain_one = gain_all[:width]
    gain_two = gain_all[width : 2 * width]
    gain_query = gain_all[2 * width : 2 * width + HEAD].reshape(1, HEAD)
    gain_key = gain_all[2 * width + HEAD :].reshape(1, HEAD)

    ids_here = lax.dynamic_slice_in_dim(ids, half * LOCAL, LOCAL)
    places_here = lax.dynamic_slice_in_dim(places, half * LOCAL, LOCAL)
    ids_keys = jnp.where(
        half == 0,
        jnp.concatenate([jnp.full((BACK,), -1, jnp.int32), ids[:LOCAL]]),
        ids[LOCAL - BACK :],
    )
    query_ids, key_ids = ids_here.reshape(-1, 1), ids_keys.reshape(1, -1)
    frequency = jnp.exp(jnp.arange(HEAD // 2, dtype=wide) * (-2.0 * math.log(theta) / HEAD))
    angle = places_here.astype(wide)[:, None] * frequency
    cosine, sine = jnp.cos(angle), jnp.sin(angle)
    cosine = jnp.concatenate([cosine, cosine], axis=1)
    sine = jnp.concatenate([-sine, sine], axis=1)

    values = rows.astype(wide)
    scale_all = [
        lax.rsqrt(jnp.mean(jnp.square(v.astype(wide)), axis=-1, keepdims=True) + epsilon)
        for v in rows_all
    ]
    normed = [(v.astype(wide) * r * gain_one).astype(low) for v, r in zip(rows_all, scale_all)]
    raw = [dot(v, project_all, (1, 0)) for v in normed]
    query, pair = heads(place, raw, cosine, sine, gain_query, gain_key)
    earlier = move(pair[LOCAL - BACK :], "yh", [(0, 1)])
    back_all = choose(place, flag, cotangent[0], other_core(cotangent[0]))
    back = [back_all[: LOCAL // 2], back_all[LOCAL // 2 :]]
    pair_all = jnp.concatenate([after(earlier, back_all), pair], axis=0)
    attended, logsum = attend(turn, core_of, query, pair_all, query_ids, key_ids)
    attended = [attended[j].reshape(LOCAL // 2, 2 * HEAD) for j in range(2)]
    mine, away = [dot(v, output_all, (1, 1)).astype(low) for v in attended]
    middle = values + chip_sum(core_sum(mine, away))

    normed_two = gather_rows(rms_norm(middle, gain_two).astype(low))
    hidden, dexpanded = [], []
    for v, dy in zip(normed_two, back):
        expanded = dot(v, expand_all, (1, 0))
        activated, pull_act = jax.vjp(swiglu, expanded[:, :ff], expanded[:, ff:])
        hidden.append(activated.astype(low))
        dgate, dup = pull_act(dot(dy, shrink_all, (1, 0)))
        dexpanded.append(jnp.concatenate([dgate, dup], axis=1).astype(low))
    both_two = core_sum(*back_products(dexpanded, second_all))
    drows_two = chip_sum(both_two)
    second_grads = grads(
        [*after(tuple(normed_two), both_two), *back], [*dexpanded, *hidden]
    )
    second_red = lax.psum_scatter(second_grads, GROUP, scatter_dimension=0, tiled=True)
    drows_two = after(drows_two, second_grads)
    shrunk = core_sum(*back_products(after(tuple(hidden), second_grads), second_all, at=2, hint=0))

    _, pull_two = jax.vjp(rms_norm, middle, gain_two)
    dmiddle, dgain_two = pull_two(drows_two)
    dmiddle = back[0][:BLOCK].astype(wide) + dmiddle
    dmiddle_all = gather_rows(dmiddle.astype(low))
    dmiddle_all = after(tuple(dmiddle_all), shrunk)
    dattended = jnp.stack([dot(v, output_all, (1, 0)).astype(low) for v in dmiddle_all])
    outputs = (middle + chip_sum(after(shrunk, dmiddle_all))).astype(low)
    dquery, dpair = attend_back(
        turn,
        core_of,
        query,
        pair_all,
        query_ids,
        key_ids,
        dattended.reshape(2, 4, BLOCK, 2 * HEAD),
        logsum,
    )
    later = move(dpair[:BACK].astype(low), "yh", [(1, 0)])
    outputs = trade(after(outputs, dpair))
    later = after(later, outputs)
    *draw, dgain_heads = heads_back(
        place, raw, cosine, sine, gain_query, gain_key, dquery, dpair, later
    )
    mine, away, dgain_one = back_products_gain(draw, first_all, rows_all, scale_all)
    both_one = core_sum(mine, away)
    drows_one = chip_sum(both_one)

    dgains = jnp.concatenate([dgain_one[0], dgain_two, dgain_heads[0], dgain_heads[1]]).astype(low)
    dgains = jnp.pad(dgains.reshape(16, 1, -1), ((0, 0), (0, 15), (0, HALF - gains.shape[0])))
    spot = jnp.stack([half, yl]).astype(jnp.int32)
    left, right = first_grads(spot, normed, dmiddle_all, draw, attended, dgains)
    left, right = sum_z(left).astype(low), sum_flips(right).astype(low)
    second_red = to_owner(second_red)
    expand_new, shrink_new = adam_weights(
        second_red,
        [(expand_weight, expand_first, expand_second), (shrink_weight, shrink_first, shrink_second)],
        (False, True),
        (0.05, 0.03),
    )
    left, right = after((left, right), expand_new[0])

    _, pull_one = jax.vjp(rms_norm, values, gain_one)
    dvalues, _ = pull_one(drows_one)
    input_grad = trade((dmiddle + dvalues).astype(low))

    right, left = sum_z(right), sum_flips(left)
    first_red = jnp.concatenate([left, right[:BLOCK]], axis=1)
    project_new, output_new = adam_weights(
        first_red,
        [(project_weight, project_first, project_second), (output_weight, output_first, output_second)],
        (False, True),
        (0.05, 0.4),
    )
    dgains = right[BLOCK : BLOCK + 8]
    dgains = dgains + move(dgains, "yl", [(0, 1), (1, 0)])
    dgains = dgains + shift(dgains, 1) + shift(dgains, 2) + shift(dgains, 3)
    dgains = dgains[0, : gains.shape[0]]
    return (
        outputs[None],
        input_grad[None],
        *adam(gains, gains_first, gains_second, dgains, 0.5, 0.0),
        *project_new,
        *output_new,
        *expand_new,
        *shrink_new,
    )


def solution(mesh):
    fine = Mesh(mesh.devices.reshape(4, 2, 2, 4, 2), ("z", "core", "yh", "x", "yl"))
    tokens = P(("z", "core"), ("yh", "x", "yl"), None)
    marks = P(("z", "core"), None)
    gain = P(("z", "core", "yh"))
    tall = P(("z", "core", "yh"), ("x", "yl"))
    flat = P(("x", "yl"), ("z", "core", "yh"))
    in_specs = (
        tokens,
        P(("z", "core"), "yh", None),
        marks,
        marks,
        *[gain] * 3,
        *[tall] * 3,
        *[flat] * 3,
        *[tall] * 3,
        *[flat] * 3,
    )
    out_specs = (
        tokens,
        tokens,
        *[gain] * 3,
        *[tall] * 3,
        *[flat] * 3,
        *[tall] * 3,
        *[flat] * 3,
    )
    return jax.shard_map(
        per_device, mesh=fine, in_specs=in_specs, out_specs=out_specs, check_vma=False
    )
```

```python
import functools
import math

import jax
import jax.numpy as jnp
from jax import lax
from jax.experimental import pallas as pl
from jax.experimental.pallas import tpu as pltpu
from jax.sharding import Mesh
from jax.sharding import PartitionSpec as P

QUERY_HEADS = 16
KEY_VALUE_HEADS = 8
HEAD = 128
STEP = 5
LONGEST = 800
BLOCK = 128
LOCAL = 1024
BACK = 896
QUERIES = 256
WINDOW = BACK + QUERIES

epsilon = 1e-06
theta = 1000000.0
beta_first = 0.9
beta_second = 0.95
adam_epsilon = 1e-08
weight_decay = 0.1

low = jnp.bfloat16
wide = jnp.float32
MIB = 1024 * 1024
H_PROJECT = 1
H_ATTEND = 150
H_GRADS = 1
H_ATTEND_BACK = 36
H_HEADS_BACK = 1
H_BACK_GAIN = 1
H_FIRST = 1
H_ADAM = 1

epsilon = 1e-06
theta = 1000000.0
beta_first = 0.9
beta_second = 0.95
adam_epsilon = 1e-08
weight_decay = 0.1

low = jnp.bfloat16
wide = jnp.float32
MIB = 1024 * 1024
ATTEND_HINT = 300
ATTEND_BACK_HINT = 260


def rms_norm(values, gain):
    return values * lax.rsqrt(jnp.mean(values * values, axis=-1, keepdims=True) + epsilon) * gain


def swiglu(gate, upward):
    return jax.nn.silu(gate) * upward


def adam(weight, first, second, grad, rate, decay_rate):
    mean = beta_first * first + (1.0 - beta_first) * grad
    square = beta_second * second + (1.0 - beta_second) * grad * grad
    mean_hat = mean / (1.0 - beta_first**STEP)
    square_hat = square / (1.0 - beta_second**STEP)
    updated = weight - rate * (
        mean_hat / (jnp.sqrt(square_hat) + adam_epsilon) + decay_rate * weight
    )
    return (mean, square, updated)


def dot(left, right, dims):
    return lax.dot_general(left, right, ((dims[:1], dims[1:]), ((), ())), preferred_element_type=wide)


def move(values, axis, pairs):
    return lax.ppermute(values, axis, pairs)


def shift(values, steps):
    return move(values, "x", [(i, (i + steps) % 4) for i in range(4)])


def other_core(values):
    return move(values, "core", [(0, 1), (1, 0)])


def trade(values):
    return move(values, ("core", "yl"), [(a * 2 + b, b * 2 + a) for a in range(2) for b in range(2)])


def to_group(values):
    pairs = [
        ((a * 2 + b) * 2 + d, (d * 2 + a) * 2 + b)
        for a in range(2)
        for b in range(2)
        for d in range(2)
    ]
    return move(values, ("core", "yh", "yl"), pairs)


def to_owner(values):
    pairs = [
        ((d * 2 + a) * 2 + b, (a * 2 + b) * 2 + d)
        for a in range(2)
        for b in range(2)
        for d in range(2)
    ]
    return move(values, ("core", "yh", "yl"), pairs)


def gather_rows(values):
    mine = jnp.concatenate([values, shift(values, 1), shift(values, 2), shift(values, 3)], axis=0)
    return mine, other_core(mine)


def core_sum(mine, away):
    return (mine.astype(wide) + other_core(away).astype(wide)).astype(low)


def chip_sum(both):
    pieces = both.reshape(4, BLOCK, -1)
    total = pieces[0].astype(wide)
    for k in (2, 1, 3):
        total = total + shift(pieces[k], 4 - k).astype(wide)
    return total


def after(values, *others):
    return lax.optimization_barrier((values, *others))[0]


def sum_z(blocks):
    return jnp.sum(lax.all_to_all(blocks, "z", 0, 0, tiled=True).astype(wide), axis=0)


def flip(values, a, b):
    pairs = [
        ((c * 2 + h) * 2 + d, ((d ^ b) * 2 + (h ^ a)) * 2 + c)
        for c in range(2)
        for h in range(2)
        for d in range(2)
    ]
    return move(values, ("core", "yh", "yl"), pairs)


def sum_flips(pieces, *others):
    first = [flip(pieces[1, b], 1, b) for b in (1, 0)]
    rest = after(pieces[0], *first, *others)
    total = first[0].astype(wide) + first[1].astype(wide)
    for b in (1, 0):
        total = total + flip(rest[b], 0, b).astype(wide)
    return total


GROUP = ("z", "yh", "yl")


def spec(shape, index):
    return pl.BlockSpec(shape, index)


def once(shape, index):
    return pl.BlockSpec(shape, index, pipeline_mode=pl.Buffered(1))


def params(mib):
    return pltpu.CompilerParams(vmem_limit_bytes=mib * MIB)


def cost(flops, moved, special=0, hint=1):
    return pl.CostEstimate(
        flops=flops * hint, bytes_accessed=moved * hint, transcendentals=special * hint
    )


def choose_kernel(place, flag, own, away, out, arrived):
    def copies(source):
        return [
            pltpu.make_async_copy(
                source.at[pl.ds(pl.multiple_of(place[i] * BLOCK, BLOCK), BLOCK)],
                out.at[pl.ds(i * BLOCK, BLOCK)],
                arrived.at[i],
            )
            for i in range(8)
        ]

    @pl.when(flag[0] == 1)
    def _():
        for copy in copies(own):
            copy.start()

    @pl.when(flag[0] == 0)
    def _():
        for copy in copies(away):
            copy.start()

    for copy in copies(own):
        copy.wait()


def choose(place, flag, own, away):
    scalar = pl.BlockSpec(memory_space=pltpu.SMEM)
    there = pl.BlockSpec(memory_space=pl.ANY)
    return pl.pallas_call(
        choose_kernel,
        out_shape=jax.ShapeDtypeStruct(own.shape, own.dtype),
        in_specs=[scalar, scalar, there, there],
        out_specs=there,
        scratch_shapes=[pltpu.SemaphoreType.DMA((8,))],
        compiler_params=params(4),
        cost_estimate=cost(0, 2 * own.size * 2),
    )(place, flag, own, away)


def project_kernel(
    place, mine, away, weight, gain, gq, gk, cosine, sine, normed, raw, scale, query, pair
):
    i = pl.program_id(0)

    def work(rows):
        v = rows[...].astype(wide)
        r = lax.rsqrt(jnp.mean(v * v, axis=-1, keepdims=True) + epsilon)
        n = (v * r * gain[...]).astype(low)
        normed[...] = n
        scale[...] = jnp.broadcast_to(r, scale.shape)
        raw[...] = dot(n, weight[...], (1, 0))

    pl.when(i < 2)(lambda: work(mine))
    pl.when(i >= 2)(lambda: work(away))
    for k in range(2):
        here = slice(k * BLOCK, (k + 1) * BLOCK)
        there = pl.ds(pl.multiple_of(place[2 * i + k] * BLOCK, BLOCK), BLOCK)
        c, s = cosine[there], sine[there]
        for h in range(4):
            part = slice(h * HEAD, (h + 1) * HEAD)
            v = raw[here, part]
            if h < 3:
                v = rms_norm(v, gq[...] if h < 2 else gk[...])
                v = v * c + pltpu.roll(v, HEAD // 2, 1) * s
            if h < 2:
                query[there, part] = v.astype(low)
            else:
                pair[there, (h - 2) * HEAD : (h - 1) * HEAD] = v.astype(low)


SCALARS = pl.BlockSpec(memory_space=pltpu.SMEM)
WHOLE = pl.BlockSpec(memory_space=pltpu.VMEM)


def project(place, rows, weight, gain, gq, gk, cosine, sine):
    width = rows[0].shape[1]
    fixed = lambda i, p: (0, 0)
    moving = lambda i, p: (i, 0)
    tall = 2 * BLOCK
    return pl.pallas_call(
        project_kernel,
        out_shape=[
            jax.ShapeDtypeStruct((LOCAL, width), low),
            jax.ShapeDtypeStruct((LOCAL, 4 * HEAD), wide),
            jax.ShapeDtypeStruct((LOCAL, HEAD), wide),
            jax.ShapeDtypeStruct((LOCAL, 2 * HEAD), low),
            jax.ShapeDtypeStruct((LOCAL, 2 * HEAD), low),
        ],
        grid_spec=pltpu.PrefetchScalarGridSpec(
            num_scalar_prefetch=1,
            grid=(LOCAL // tall,),
            in_specs=[
                spec((tall, width), lambda i, p: (jnp.minimum(i, 1), 0)),
                spec((tall, width), lambda i, p: (jnp.maximum(i - 2, 0), 0)),
                once((width, 4 * HEAD), fixed),
                once((1, width), fixed),
                once((1, HEAD), fixed),
                once((1, HEAD), fixed),
                once((LOCAL, HEAD), fixed),
                once((LOCAL, HEAD), fixed),
            ],
            out_specs=[
                spec((tall, width), moving),
                spec((tall, 4 * HEAD), moving),
                spec((tall, HEAD), moving),
                once((LOCAL, 2 * HEAD), fixed),
                once((LOCAL, 2 * HEAD), fixed),
            ],
        ),
        compiler_params=params(24),
        cost_estimate=cost(2 * LOCAL * width * 512, 16 * MIB, hint=H_PROJECT),
    )(place, *rows, weight, gain, gq, gk, cosine, sine)


def heads_back_kernel(
    place, raw, cosine, sine, gq, gk, dquery, dpair, later, draw, dgain
):
    sums = [jnp.zeros((1, HEAD), wide)] * 2
    for i in range(8):
        here = pl.ds(i * BLOCK, BLOCK)
        there = pl.ds(pl.multiple_of(place[i] * BLOCK, BLOCK), BLOCK)
        c, s = cosine[there], sine[there]
        dp = dpair[pl.ds(pl.multiple_of(place[i] * BLOCK + BACK, BLOCK), BLOCK)]
        from_later = later[pl.ds(pl.multiple_of(jnp.maximum(place[i] - 1, 0) * BLOCK, BLOCK), BLOCK)]
        dp = dp + jnp.where(place[i] > 0, from_later.astype(wide), 0.0)
        for h in range(4):
            part = slice(h * HEAD, (h + 1) * HEAD)
            if h == 3:
                draw[here, part] = dp[:, HEAD:].astype(low)
                continue
            g = gq[...] if h < 2 else gk[...]
            d = dquery[there, part] if h < 2 else dp[:, :HEAD]
            d = d * c + pltpu.roll(d * s, HEAD // 2, 1)
            v = raw[here, part]
            r = lax.rsqrt(jnp.mean(v * v, axis=-1, keepdims=True) + epsilon)
            u = v * r
            sums[h // 2] += jnp.sum(d * u, axis=0, keepdims=True)
            e = d * g
            draw[here, part] = (r * (e - u * jnp.mean(u * e, axis=-1, keepdims=True))).astype(low)
    row = lax.broadcasted_iota(jnp.int32, (8, HEAD), 0)
    dgain[...] = jnp.where(row == 0, sums[0], jnp.where(row == 1, sums[1], 0.0))


def heads_back(place, raw, cosine, sine, gq, gk, dquery, dpair, later):
    return pl.pallas_call(
        heads_back_kernel,
        out_shape=[
            jax.ShapeDtypeStruct((LOCAL, 4 * HEAD), low),
            jax.ShapeDtypeStruct((8, HEAD), wide),
        ],
        in_specs=[SCALARS] + [WHOLE] * 8,
        out_specs=[WHOLE] * 2,
        compiler_params=params(16),
        cost_estimate=cost(LOCAL * 512 * 20, LOCAL * 512 * 12, hint=H_HEADS_BACK),
    )(place, raw, cosine, sine, gq, gk, dquery, dpair, later)


ROWS = 256


def both_dots(lefts, rights, dims):
    return dot(lefts[0][...], rights[0][...], dims) + dot(lefts[1][...], rights[1][...], dims)


def grads_kernel(*refs):
    lefts, rights, out = refs[:4], refs[4:8], refs[8]
    n = rights[0].shape[1]
    out[:, :n] = both_dots(lefts[:2], rights[:2], (0, 0)).astype(low)
    out[:, n:] = both_dots(lefts[2:], rights[2:], (0, 0)).astype(low)


def grads(lefts, rights):
    depth, rows = lefts[0].shape
    total = rights[0].shape[1] + rights[2].shape[1]
    return pl.pallas_call(
        grads_kernel,
        out_shape=jax.ShapeDtypeStruct((rows, total), low),
        grid=(rows // ROWS,),
        in_specs=[spec((depth, ROWS), lambda i: (0, i))] * 4
        + [once(v.shape, lambda i: (0, 0)) for v in rights],
        out_specs=spec((ROWS, total), lambda i: (i, 0)),
        compiler_params=params(28),
        cost_estimate=cost(
            4 * depth * rows * total, 8 * depth * rows + 2 * total * (rows + depth), hint=H_GRADS
        ),
    )(*lefts, *rights)


def back_kernel(mine, away, right, out_mine, out_away):
    turned = right[...].T
    out_away[...] = dot(away[...], turned, (1, 0)).astype(low)
    out_mine[...] = dot(mine[...], turned, (1, 0)).astype(low)


def back_products(lefts, right, at=0, hint=1):
    rows, depth = lefts[0].shape
    width = right.shape[0]
    return pl.pallas_call(
        back_kernel,
        out_shape=[jax.ShapeDtypeStruct((rows, width), low)] * 2,
        grid=(width // ROWS,),
        in_specs=[once((rows, depth), lambda i: (0, 0))] * 2
        + [spec((ROWS, depth), lambda i: (i, at))],
        out_specs=[spec((rows, ROWS), lambda i: (0, i))] * 2,
        compiler_params=params(20),
        cost_estimate=cost(4 * rows * depth * width * hint, 2 * width * (depth + 2 * rows) * hint),
    )(*lefts, right)


def back_gain_kernel(left, right, mine_in, away_in, scale, out_mine, out_away, gain):
    total = 0.0
    half = LOCAL // 2
    turned = right[...].T
    for at, values, out in ((half, away_in, out_away), (0, mine_in, out_mine)):
        rows = pl.ds(at, half)
        product = dot(left[rows], turned, (1, 0))
        out[...] = product.astype(low)
        scaled = values[...].astype(wide) * scale[rows, :1]
        total += jnp.sum(product * scaled, axis=0, keepdims=True)
    gain[...] = total


def back_products_gain(left, right, values, scale):
    depth = left.shape[1]
    rows = LOCAL // 2
    width = right.shape[0]
    columns = lambda i: (0, i)
    fixed = lambda i: (0, 0)
    return pl.pallas_call(
        back_gain_kernel,
        out_shape=[jax.ShapeDtypeStruct((rows, width), low)] * 2
        + [jax.ShapeDtypeStruct((1, width), wide)],
        grid=(width // ROWS,),
        in_specs=[
            once((LOCAL, depth), fixed),
            spec((ROWS, depth), lambda i: (i, 0)),
            spec((rows, ROWS), columns),
            spec((rows, ROWS), columns),
            once((LOCAL, HEAD), fixed),
        ],
        out_specs=[spec((rows, ROWS), columns)] * 2 + [spec((1, ROWS), columns)],
        compiler_params=params(20),
        cost_estimate=cost(
            4 * rows * depth * width, 2 * width * (depth + 4 * rows), hint=H_BACK_GAIN
        ),
    )(left, right, *values, scale)


def adam_kernel(flipped, rates, extras, *refs):
    grad = refs[0]
    at = 0
    for k, (turn, rate) in enumerate(zip(flipped, rates)):
        weight, first, second = refs[1 + 3 * k : 4 + 3 * k]
        outs = refs[1 + extras + 3 * (len(rates) + k) : 4 + extras + 3 * (len(rates) + k)]
        n = weight.shape[0] if turn else weight.shape[1]
        g = grad[:, at : at + n].astype(wide)
        at += n
        if turn:
            g = g.T
        for out, value in zip(outs, adam(weight[...], first[...], second[...], g, rate, weight_decay)):
            out[...] = value
    for k in range(extras):
        refs[k - extras][...] = refs[1 + 3 * len(rates) + k][...]


def adam_weights(grad, weights, flipped, rates, extras=()):
    states = [v for group in weights for v in group] + list(extras)
    out = pl.pallas_call(
        functools.partial(adam_kernel, flipped, rates, len(extras)),
        out_shape=[jax.ShapeDtypeStruct(v.shape, v.dtype) for v in states],
        in_specs=[WHOLE] * (1 + len(states)),
        out_specs=[WHOLE] * len(states),
        compiler_params=params(24),
        cost_estimate=cost(20 * grad.size, 26 * grad.size, hint=H_ADAM),
    )(grad, *states)
    return [tuple(out[3 * k : 3 * k + 3]) for k in range(len(weights))] + list(out[3 * len(weights) :])


HALF = 384
TALL = BLOCK + 16


def first_grads_kernel(spot, *refs):
    normed, mine, away, draw, attended, dgains, left, right = refs
    half = LOCAL // 2
    project = dot(normed[...], draw[...], (0, 0)).astype(low)
    output = dot(mine[...], attended[:half], (0, 0)) + dot(away[...], attended[half:], (0, 0))
    output = output.astype(low)
    for j in range(2):
        rows = slice(j * BLOCK, (j + 1) * BLOCK)
        a = j ^ spot[0]
        left[0, a, 0] = project[rows, :HALF]
        right[a, 0, 0, :BLOCK, : 4 * HEAD - HALF] = project[rows, HALF:]
        right[a, 0, 0, :BLOCK, 4 * HEAD - HALF :] = output[rows]
        right[a, 0, 0, BLOCK:] = dgains[j]


def first_grads(spot, normed, dmiddle, draw, attended, dgains):
    whole = lambda i, s: (0, 0)
    columns = lambda i, s: (0, i)
    return pl.pallas_call(
        first_grads_kernel,
        out_shape=[
            jax.ShapeDtypeStruct((4, 2, 2, BLOCK, HALF), low),
            jax.ShapeDtypeStruct((2, 2, 4, TALL, HALF), low),
        ],
        grid_spec=pltpu.PrefetchScalarGridSpec(
            num_scalar_prefetch=1,
            grid=(8,),
            in_specs=[
                spec((LOCAL, 2 * BLOCK), columns),
                spec((LOCAL // 2, 2 * BLOCK), columns),
                spec((LOCAL // 2, 2 * BLOCK), columns),
                once((LOCAL, 4 * HEAD), whole),
                once((LOCAL, 2 * HEAD), whole),
                spec((2, 16, HALF), lambda i, s: (i, 0, 0)),
            ],
            out_specs=[
                spec((1, 2, 1, BLOCK, HALF), lambda i, s: (i // 2, 0, i % 2 ^ s[1], 0, 0)),
                spec((2, 1, 1, TALL, HALF), lambda i, s: (0, i % 2 ^ s[1], i // 2, 0, 0)),
            ],
        ),
        compiler_params=params(24),
        cost_estimate=cost(2 * LOCAL * 2048 * 768, 14 * MIB, hint=H_FIRST),
    )(spot, normed, *dmiddle, draw, attended, dgains)


SCALE = HEAD ** (-0.5)


def allowed(query_ids, key_ids, start):
    keys = key_ids[:, pl.ds(start, WINDOW)]
    row = lax.broadcasted_iota(jnp.int32, (QUERIES, WINDOW), 0)
    column = lax.broadcasted_iota(jnp.int32, (QUERIES, WINDOW), 1)
    return (query_ids[...] == keys) & (column <= row + BACK)


def attend_kernel(turn, core, query, pair, query_ids, key_ids, out, logsum):
    i = pl.program_id(0)
    start = pl.multiple_of(i * QUERIES, QUERIES)
    mask = allowed(query_ids, key_ids, start)
    logs = []
    for h in range(2):
        part = slice(h * HEAD, (h + 1) * HEAD)
        scores = dot(query[:, part], pair[pl.ds(start, WINDOW), :HEAD], (1, 1)) * SCALE
        scores = jnp.where(mask, scores, -1e30)
        top = jnp.max(scores, axis=-1, keepdims=True)
        unnormed = jnp.exp(scores - top)
        total = jnp.sum(unnormed, axis=-1, keepdims=True)
        probs = (unnormed * (1.0 / total)).astype(low)
        result = dot(probs, pair[pl.ds(start, WINDOW), HEAD:], (1, 0)).astype(low)
        for j in range(2):
            out[j ^ core[0], 0, :, part] = result[j * BLOCK : (j + 1) * BLOCK]
        logs.append(top + jnp.log(total))
    lane = lax.broadcasted_iota(jnp.int32, (QUERIES, HEAD), 1)
    logsum[...] = jnp.where(lane < HEAD // 2, logs[0], logs[1])


def attend(turn, core, query, pair, query_ids, key_ids):
    rows = lambda i, t, c: (i, 0)
    whole = lambda i, t, c: (0, 0)
    keys = BACK + LOCAL
    return pl.pallas_call(
        attend_kernel,
        out_shape=[
            jax.ShapeDtypeStruct((2, 4, BLOCK, 2 * HEAD), low),
            jax.ShapeDtypeStruct((LOCAL, HEAD), wide),
        ],
        grid_spec=pltpu.PrefetchScalarGridSpec(
            num_scalar_prefetch=2,
            grid=(LOCAL // QUERIES,),
            in_specs=[
                spec((QUERIES, 2 * HEAD), rows),
                once((keys, 2 * HEAD), whole),
                spec((QUERIES, 1), rows),
                spec((1, keys), whole),
            ],
            out_specs=[
                spec((2, 1, BLOCK, 2 * HEAD), lambda i, t, c: (0, t[i], 0, 0)),
                spec((QUERIES, HEAD), rows),
            ],
        ),
        compiler_params=params(24),
        cost_estimate=cost(
            8 * LOCAL * WINDOW * HEAD, 4 * LOCAL * 512, 2 * LOCAL * WINDOW, hint=H_ATTEND
        ),
    )(turn, core, query, pair, query_ids, key_ids)


def attend_back_kernel(
    turn, core, query, pair, query_ids, key_ids, grad, logsum, dquery, dpair
):
    i = pl.program_id(0)

    @pl.when(i == 0)
    def _():
        dpair[...] = jnp.zeros_like(dpair)

    start = pl.multiple_of(i * QUERIES, QUERIES)
    window = pl.ds(start, WINDOW)
    mask = allowed(query_ids, key_ids, start)
    dkey, dvalue = None, None
    for h in range(2):
        part = slice(h * HEAD, (h + 1) * HEAD)
        q = query[:, part]
        g = jnp.concatenate([grad[j ^ core[0], 0, :, part] for j in range(2)], axis=0)
        scores = dot(q, pair[window, :HEAD], (1, 1)) * SCALE
        probs = jnp.where(mask, jnp.exp(scores - logsum[:, h * 64 : h * 64 + 1]), 0.0)
        dprobs = dot(g, pair[window, HEAD:], (1, 1))
        inner = jnp.sum(probs * dprobs, axis=-1, keepdims=True)
        dscores = (probs * (dprobs - inner)).astype(low)
        dquery[:, part] = dot(dscores, pair[window, :HEAD], (1, 0)) * SCALE
        dv = dot(probs.astype(low), g, (0, 0))
        dk = dot(dscores, q, (0, 0))
        dkey = dk if dkey is None else dkey + dk
        dvalue = dv if dvalue is None else dvalue + dv
    dpair[window, :HEAD] += dkey * SCALE
    dpair[window, HEAD:] += dvalue


def attend_back(turn, core, query, pair, query_ids, key_ids, grad, logsum):
    rows = lambda i, t, c: (i, 0)
    whole = lambda i, t, c: (0, 0)
    keys = BACK + LOCAL
    return pl.pallas_call(
        attend_back_kernel,
        out_shape=[
            jax.ShapeDtypeStruct((LOCAL, 2 * HEAD), wide),
            jax.ShapeDtypeStruct((keys, 2 * HEAD), wide),
        ],
        grid_spec=pltpu.PrefetchScalarGridSpec(
            num_scalar_prefetch=2,
            grid=(LOCAL // QUERIES,),
            in_specs=[
                spec((QUERIES, 2 * HEAD), rows),
                once((keys, 2 * HEAD), whole),
                spec((QUERIES, 1), rows),
                spec((1, keys), whole),
                spec((2, 1, BLOCK, 2 * HEAD), lambda i, t, c: (0, t[i], 0, 0)),
                spec((QUERIES, HEAD), rows),
            ],
            out_specs=[spec((QUERIES, 2 * HEAD), rows), once((keys, 2 * HEAD), whole)],
        ),
        compiler_params=params(28),
        cost_estimate=cost(
            20 * LOCAL * WINDOW * HEAD, 8 * LOCAL * 512, 2 * LOCAL * WINDOW, hint=H_ATTEND_BACK
        ),
    )(turn, core, query, pair, query_ids, key_ids, grad, logsum)


def per_device(
    inputs,
    cotangent,
    document_index,
    positions,
    gains,
    gains_first,
    gains_second,
    project_weight,
    project_first,
    project_second,
    output_weight,
    output_first,
    output_second,
    expand_weight,
    expand_first,
    expand_second,
    shrink_weight,
    shrink_first,
    shrink_second,
):
    core, x = lax.axis_index("core"), lax.axis_index("x")
    half, yl = lax.axis_index("yh"), lax.axis_index("yl")
    width = inputs.shape[-1]
    qkv = project_weight.shape[1]
    ff = shrink_weight.shape[0]
    at_home = core == yl
    steps = jnp.arange(8, dtype=jnp.int32)
    place = lax.rem(x - steps % 4 + 4, 4) * 2 + (core ^ (steps // 4))
    turn = lax.rem(x - jnp.arange(4, dtype=jnp.int32) + 4, 4)
    core_of = core.reshape(1).astype(jnp.int32)
    flag = at_home.astype(jnp.int32).reshape(1)

    marks = jnp.stack([document_index[0], positions[0] // 32, positions[0] % 32])
    marks = jnp.pad(marks.astype(low), ((0, 13), (0, 0)))
    message = trade(jnp.concatenate([inputs[0], marks], axis=0))
    rows = message[:BLOCK]
    marks = message[BLOCK:].astype(jnp.int32)
    ids, places = marks[0], marks[1] * 32 + marks[2]

    gain_block = jnp.pad(gains.astype(low), (0, BLOCK * BLOCK - gains.shape[0])).reshape(BLOCK, BLOCK)
    first_shard = jnp.concatenate(
        [project_weight.astype(low), output_weight.astype(low).T, gain_block], axis=1
    )
    second_shard = jnp.concatenate([expand_weight.astype(low), shrink_weight.astype(low).T], axis=1)
    first_all = lax.all_gather(to_group(first_shard), GROUP, axis=0, tiled=True)
    rows_all = gather_rows(rows)
    second_shard = after(second_shard, first_all)
    second_all = lax.all_gather(to_group(second_shard), GROUP, axis=0, tiled=True)
    project_all = first_all[:, :qkv]
    output_all = first_all[:, qkv : qkv + 2 * HEAD]
    expand_all = second_all[:, : 2 * ff]
    shrink_all = second_all[:, 2 * ff :]
    gain_all = first_all.reshape(16, BLOCK, -1)[:, :3, qkv + 2 * HEAD :].reshape(16, 3 * BLOCK)
    gain_all = gain_all[:, : gains.shape[0]].reshape(-1).astype(wide)
    gain_one = gain_all[:width]
    gain_two = gain_all[width : 2 * width]
    gain_query = gain_all[2 * width : 2 * width + HEAD].reshape(1, HEAD)
    gain_key = gain_all[2 * width + HEAD :].reshape(1, HEAD)

    ids_here = lax.dynamic_slice_in_dim(ids, half * LOCAL, LOCAL)
    places_here = lax.dynamic_slice_in_dim(places, half * LOCAL, LOCAL)
    ids_keys = jnp.where(
        half == 0,
        jnp.concatenate([jnp.full((BACK,), -1, jnp.int32), ids[:LOCAL]]),
        ids[LOCAL - BACK :],
    )
    query_ids, key_ids = ids_here.reshape(-1, 1), ids_keys.reshape(1, -1)
    frequency = jnp.exp(jnp.arange(HEAD // 2, dtype=wide) * (-2.0 * math.log(theta) / HEAD))
    angle = places_here.astype(wide)[:, None] * frequency
    cosine, sine = jnp.cos(angle), jnp.sin(angle)
    cosine = jnp.concatenate([cosine, cosine], axis=1)
    sine = jnp.concatenate([-sine, sine], axis=1)

    values = rows.astype(wide)
    normed, raw, scale, query, pair = project(
        place, rows_all, first_all, gain_one.reshape(1, -1), gain_query, gain_key, cosine, sine
    )
    earlier = move(pair[LOCAL - BACK :], "yh", [(0, 1)])
    back_all = choose(place, flag, cotangent[0], other_core(cotangent[0]))
    back = [back_all[: LOCAL // 2], back_all[LOCAL // 2 :]]
    pair_all = jnp.concatenate([after(earlier, back_all), pair], axis=0)
    attended, logsum = attend(turn, core_of, query, pair_all, query_ids, key_ids)
    attended = attended.reshape(LOCAL, 2 * HEAD)
    mine = dot(attended[: LOCAL // 2], output_all, (1, 1)).astype(low)
    away = dot(attended[LOCAL // 2 :], output_all, (1, 1)).astype(low)
    middle = values + chip_sum(core_sum(mine, away))

    normed_two = gather_rows(rms_norm(middle, gain_two).astype(low))
    hidden, dexpanded = [], []
    for v, dy in zip(normed_two, back):
        expanded = dot(v, expand_all, (1, 0))
        activated, pull_act = jax.vjp(swiglu, expanded[:, :ff], expanded[:, ff:])
        hidden.append(activated.astype(low))
        dgate, dup = pull_act(dot(dy, shrink_all, (1, 0)))
        dexpanded.append(jnp.concatenate([dgate, dup], axis=1).astype(low))
    both_two = core_sum(*back_products(dexpanded, second_all))
    drows_two = chip_sum(both_two)
    second_grads = grads(
        [*after(tuple(normed_two), both_two), *back], [*dexpanded, *hidden]
    )
    second_red = lax.psum_scatter(second_grads, GROUP, scatter_dimension=0, tiled=True)
    drows_two = after(drows_two, second_grads)
    shrunk = core_sum(*back_products(after(tuple(hidden), second_grads), second_all, at=2, hint=0))

    _, pull_two = jax.vjp(rms_norm, middle, gain_two)
    dmiddle, dgain_two = pull_two(drows_two)
    dmiddle = back[0][:BLOCK].astype(wide) + dmiddle
    dmiddle_all = gather_rows(dmiddle.astype(low))
    dmiddle_all = after(tuple(dmiddle_all), shrunk)
    dattended = jnp.stack([dot(v, output_all, (1, 0)).astype(low) for v in dmiddle_all])
    mlp = chip_sum(after(shrunk, dmiddle_all))
    dquery, dpair = attend_back(
        turn,
        core_of,
        query,
        pair_all,
        query_ids,
        key_ids,
        dattended.reshape(2, 4, BLOCK, 2 * HEAD),
        logsum,
    )
    later = move(dpair[:BACK].astype(low), "yh", [(1, 0)])
    later = after(later, mlp)
    draw, dgain_heads = heads_back(
        place, raw, cosine, sine, gain_query, gain_key, dquery, dpair, later
    )
    outputs = trade((middle + after(mlp, draw)).astype(low))
    mine, away, dgain_one = back_products_gain(draw, first_all, rows_all, scale)
    both_one = core_sum(mine, away)
    drows_one = chip_sum(both_one)

    dgains = jnp.concatenate([dgain_one[0], dgain_two, dgain_heads[0], dgain_heads[1]]).astype(low)
    dgains = jnp.pad(dgains.reshape(16, 1, -1), ((0, 0), (0, 15), (0, HALF - gains.shape[0])))
    spot = jnp.stack([half, yl]).astype(jnp.int32)
    left, right = first_grads(spot, normed, dmiddle_all, draw, attended, dgains)
    second_red = to_owner(second_red)
    expand_new, shrink_new = adam_weights(
        second_red,
        [(expand_weight, expand_first, expand_second), (shrink_weight, shrink_first, shrink_second)],
        (False, True),
        (0.05, 0.03),
    )
    left, right = sum_z(left).astype(low), sum_flips(right, expand_new[0]).astype(low)
    left, right = after((left, right), drows_one, outputs)

    _, pull_one = jax.vjp(rms_norm, values, gain_one)
    dvalues, _ = pull_one(drows_one)
    input_grad = trade((dmiddle + dvalues).astype(low))

    right, left = sum_z(right), sum_flips(left)
    first_red = jnp.concatenate([left, right[:BLOCK]], axis=1)
    project_new, output_new, outputs, input_grad = adam_weights(
        first_red,
        [(project_weight, project_first, project_second), (output_weight, output_first, output_second)],
        (False, True),
        (0.05, 0.4),
        (outputs, input_grad),
    )
    dgains = right[BLOCK : BLOCK + 8]
    dgains = dgains + move(dgains, "yl", [(0, 1), (1, 0)])
    dgains = dgains + shift(dgains, 1) + shift(dgains, 2) + shift(dgains, 3)
    dgains = dgains[0, : gains.shape[0]]
    return (
        outputs[None],
        input_grad[None],
        *adam(gains, gains_first, gains_second, dgains, 0.5, 0.0),
        *project_new,
        *output_new,
        *expand_new,
        *shrink_new,
    )


def solution(mesh):
    fine = Mesh(mesh.devices.reshape(4, 2, 2, 4, 2), ("z", "core", "yh", "x", "yl"))
    tokens = P(("z", "core"), ("yh", "x", "yl"), None)
    marks = P(("z", "core"), None)
    gain = P(("z", "core", "yh"))
    tall = P(("z", "core", "yh"), ("x", "yl"))
    flat = P(("x", "yl"), ("z", "core", "yh"))
    in_specs = (
        tokens,
        P(("z", "core"), "yh", None),
        marks,
        marks,
        *[gain] * 3,
        *[tall] * 3,
        *[flat] * 3,
        *[tall] * 3,
        *[flat] * 3,
    )
    out_specs = (
        tokens,
        tokens,
        *[gain] * 3,
        *[tall] * 3,
        *[flat] * 3,
        *[tall] * 3,
        *[flat] * 3,
    )
    return jax.shard_map(
        per_device, mesh=fine, in_specs=in_specs, out_specs=out_specs, check_vma=False
    )
```

```python
import functools
import math

import jax
import jax.numpy as jnp
from jax import lax
from jax.experimental import pallas as pl
from jax.experimental.pallas import tpu as pltpu
from jax.sharding import Mesh
from jax.sharding import PartitionSpec as P

QUERY_HEADS = 16
KEY_VALUE_HEADS = 8
HEAD = 128
STEP = 5
LONGEST = 800
BLOCK = 128
LOCAL = 1024
BACK = 896
QUERIES = 256
WINDOW = BACK + QUERIES

epsilon = 1e-06
theta = 1000000.0
beta_first = 0.9
beta_second = 0.95
adam_epsilon = 1e-08
weight_decay = 0.1

low = jnp.bfloat16
wide = jnp.float32
MIB = 1024 * 1024
FIRST_MIB = 24
H_PROJECT = 1
H_ATTEND = 150
H_GRADS = 1
H_ATTEND_BACK = 36
H_HEADS_BACK = 1
H_BACK = 1
H_FIRST = 1
H_ADAM = 1

epsilon = 1e-06
theta = 1000000.0
beta_first = 0.9
beta_second = 0.95
adam_epsilon = 1e-08
weight_decay = 0.1

low = jnp.bfloat16
wide = jnp.float32
MIB = 1024 * 1024
ATTEND_HINT = 300
ATTEND_BACK_HINT = 260


def rms_norm(values, gain):
    return values * lax.rsqrt(jnp.mean(values * values, axis=-1, keepdims=True) + epsilon) * gain


def swiglu(gate, upward):
    return jax.nn.silu(gate) * upward


def adam(weight, first, second, grad, rate, decay_rate):
    mean = beta_first * first + (1.0 - beta_first) * grad
    square = beta_second * second + (1.0 - beta_second) * grad * grad
    mean_hat = mean / (1.0 - beta_first**STEP)
    square_hat = square / (1.0 - beta_second**STEP)
    updated = weight - rate * (
        mean_hat / (jnp.sqrt(square_hat) + adam_epsilon) + decay_rate * weight
    )
    return (mean, square, updated)


def dot(left, right, dims):
    return lax.dot_general(left, right, ((dims[:1], dims[1:]), ((), ())), preferred_element_type=wide)


def move(values, axis, pairs):
    return lax.ppermute(values, axis, pairs)


def shift(values, steps):
    return move(values, "x", [(i, (i + steps) % 4) for i in range(4)])


def other_core(values):
    return move(values, "core", [(0, 1), (1, 0)])


def trade(values):
    return move(values, ("core", "yl"), [(a * 2 + b, b * 2 + a) for a in range(2) for b in range(2)])


def to_group(values):
    pairs = [
        ((a * 2 + b) * 2 + d, (d * 2 + a) * 2 + b)
        for a in range(2)
        for b in range(2)
        for d in range(2)
    ]
    return move(values, ("core", "yh", "yl"), pairs)


def to_owner(values):
    pairs = [
        ((d * 2 + a) * 2 + b, (a * 2 + b) * 2 + d)
        for a in range(2)
        for b in range(2)
        for d in range(2)
    ]
    return move(values, ("core", "yh", "yl"), pairs)


def gather_rows(values):
    mine = jnp.concatenate([values, shift(values, 1), shift(values, 2), shift(values, 3)], axis=0)
    return mine, other_core(mine)


def core_sum(mine, away):
    return (mine.astype(wide) + other_core(away).astype(wide)).astype(low)


def chip_sum(both):
    pieces = both.reshape(4, BLOCK, -1)
    total = pieces[0].astype(wide)
    for k in (2, 1, 3):
        total = total + shift(pieces[k], 4 - k).astype(wide)
    return total


def after(values, *others):
    return lax.optimization_barrier((values, *others))[0]


def sum_z(blocks):
    return jnp.sum(lax.all_to_all(blocks, "z", 0, 0, tiled=True).astype(wide), axis=0)


def flip(values, a, b):
    pairs = [
        ((c * 2 + h) * 2 + d, ((d ^ b) * 2 + (h ^ a)) * 2 + c)
        for c in range(2)
        for h in range(2)
        for d in range(2)
    ]
    return move(values, ("core", "yh", "yl"), pairs)


def sum_flips(pieces, *others):
    first = [flip(pieces[1, b], 1, b) for b in (1, 0)]
    rest = after(pieces[0], *first, *others)
    total = first[0].astype(wide) + first[1].astype(wide)
    for b in (1, 0):
        total = total + flip(rest[b], 0, b).astype(wide)
    return total


GROUP = ("z", "yh", "yl")


def spec(shape, index):
    return pl.BlockSpec(shape, index)


def once(shape, index):
    return pl.BlockSpec(shape, index, pipeline_mode=pl.Buffered(1))


def params(mib):
    return pltpu.CompilerParams(vmem_limit_bytes=mib * MIB)


def cost(flops, moved, special=0, hint=1):
    return pl.CostEstimate(
        flops=flops * hint, bytes_accessed=moved * hint, transcendentals=special * hint
    )


def choose_kernel(place, flag, own, away, out, arrived):
    def copies(source):
        return [
            pltpu.make_async_copy(
                source.at[pl.ds(pl.multiple_of(place[i] * BLOCK, BLOCK), BLOCK)],
                out.at[pl.ds(i * BLOCK, BLOCK)],
                arrived.at[i],
            )
            for i in range(8)
        ]

    @pl.when(flag[0] == 1)
    def _():
        for copy in copies(own):
            copy.start()

    @pl.when(flag[0] == 0)
    def _():
        for copy in copies(away):
            copy.start()

    for copy in copies(own):
        copy.wait()


def choose(place, flag, own, away):
    scalar = pl.BlockSpec(memory_space=pltpu.SMEM)
    there = pl.BlockSpec(memory_space=pl.ANY)
    return pl.pallas_call(
        choose_kernel,
        out_shape=jax.ShapeDtypeStruct(own.shape, own.dtype),
        in_specs=[scalar, scalar, there, there],
        out_specs=there,
        scratch_shapes=[pltpu.SemaphoreType.DMA((8,))],
        compiler_params=params(4),
        cost_estimate=cost(0, 2 * own.size * 2),
    )(place, flag, own, away)


def project_kernel(
    place, mine, away, weight, gain, gq, gk, cosine, sine, normed, raw, scale, query, pair
):
    i = pl.program_id(0)

    def work(rows):
        v = rows[...].astype(wide)
        r = lax.rsqrt(jnp.mean(v * v, axis=-1, keepdims=True) + epsilon)
        n = (v * r * gain[...]).astype(low)
        normed[...] = n
        scale[...] = jnp.broadcast_to(r, scale.shape)
        raw[...] = dot(n, weight[...], (1, 0))

    pl.when(i < 2)(lambda: work(mine))
    pl.when(i >= 2)(lambda: work(away))
    for k in range(2):
        here = slice(k * BLOCK, (k + 1) * BLOCK)
        there = pl.ds(pl.multiple_of(place[2 * i + k] * BLOCK, BLOCK), BLOCK)
        c, s = cosine[there], sine[there]
        for h in range(4):
            part = slice(h * HEAD, (h + 1) * HEAD)
            v = raw[here, part]
            if h < 3:
                v = rms_norm(v, gq[...] if h < 2 else gk[...])
                v = v * c + pltpu.roll(v, HEAD // 2, 1) * s
            if h < 2:
                query[there, part] = v.astype(low)
            else:
                pair[there, (h - 2) * HEAD : (h - 1) * HEAD] = v.astype(low)


SCALARS = pl.BlockSpec(memory_space=pltpu.SMEM)
WHOLE = pl.BlockSpec(memory_space=pltpu.VMEM)


def project(place, rows, weight, gain, gq, gk, cosine, sine):
    width = rows[0].shape[1]
    fixed = lambda i, p: (0, 0)
    moving = lambda i, p: (i, 0)
    tall = 2 * BLOCK
    return pl.pallas_call(
        project_kernel,
        out_shape=[
            jax.ShapeDtypeStruct((LOCAL, width), low),
            jax.ShapeDtypeStruct((LOCAL, 4 * HEAD), wide),
            jax.ShapeDtypeStruct((LOCAL, HEAD), wide),
            jax.ShapeDtypeStruct((LOCAL, 2 * HEAD), low),
            jax.ShapeDtypeStruct((LOCAL, 2 * HEAD), low),
        ],
        grid_spec=pltpu.PrefetchScalarGridSpec(
            num_scalar_prefetch=1,
            grid=(LOCAL // tall,),
            in_specs=[
                spec((tall, width), lambda i, p: (jnp.minimum(i, 1), 0)),
                spec((tall, width), lambda i, p: (jnp.maximum(i - 2, 0), 0)),
                once((width, 4 * HEAD), fixed),
                once((1, width), fixed),
                once((1, HEAD), fixed),
                once((1, HEAD), fixed),
                once((LOCAL, HEAD), fixed),
                once((LOCAL, HEAD), fixed),
            ],
            out_specs=[
                spec((tall, width), moving),
                spec((tall, 4 * HEAD), moving),
                spec((tall, HEAD), moving),
                once((LOCAL, 2 * HEAD), fixed),
                once((LOCAL, 2 * HEAD), fixed),
            ],
        ),
        compiler_params=params(24),
        cost_estimate=cost(2 * LOCAL * width * 512, 16 * MIB, hint=H_PROJECT),
    )(place, *rows, weight, gain, gq, gk, cosine, sine)


def heads_back_kernel(
    place, raw, cosine, sine, gq, gk, dquery, dpair, later, draw, dgain
):
    sums = [jnp.zeros((1, HEAD), wide)] * 2
    for i in range(8):
        here = pl.ds(i * BLOCK, BLOCK)
        there = pl.ds(pl.multiple_of(place[i] * BLOCK, BLOCK), BLOCK)
        c, s = cosine[there], sine[there]
        dp = dpair[pl.ds(pl.multiple_of(place[i] * BLOCK + BACK, BLOCK), BLOCK)]
        from_later = later[pl.ds(pl.multiple_of(jnp.maximum(place[i] - 1, 0) * BLOCK, BLOCK), BLOCK)]
        dp = dp + jnp.where(place[i] > 0, from_later.astype(wide), 0.0)
        for h in range(4):
            part = slice(h * HEAD, (h + 1) * HEAD)
            if h == 3:
                draw[here, part] = dp[:, HEAD:].astype(low)
                continue
            g = gq[...] if h < 2 else gk[...]
            d = dquery[there, part] if h < 2 else dp[:, :HEAD]
            d = d * c + pltpu.roll(d * s, HEAD // 2, 1)
            v = raw[here, part]
            r = lax.rsqrt(jnp.mean(v * v, axis=-1, keepdims=True) + epsilon)
            u = v * r
            sums[h // 2] += jnp.sum(d * u, axis=0, keepdims=True)
            e = d * g
            draw[here, part] = (r * (e - u * jnp.mean(u * e, axis=-1, keepdims=True))).astype(low)
    row = lax.broadcasted_iota(jnp.int32, (8, HEAD), 0)
    dgain[...] = jnp.where(row == 0, sums[0], jnp.where(row == 1, sums[1], 0.0))


def heads_back(place, raw, cosine, sine, gq, gk, dquery, dpair, later):
    return pl.pallas_call(
        heads_back_kernel,
        out_shape=[
            jax.ShapeDtypeStruct((LOCAL, 4 * HEAD), low),
            jax.ShapeDtypeStruct((8, HEAD), wide),
        ],
        in_specs=[SCALARS] + [WHOLE] * 8,
        out_specs=[WHOLE] * 2,
        compiler_params=params(16),
        cost_estimate=cost(LOCAL * 512 * 20, LOCAL * 512 * 12, hint=H_HEADS_BACK),
    )(place, raw, cosine, sine, gq, gk, dquery, dpair, later)


ROWS = 256


def both_dots(lefts, rights, dims):
    return dot(lefts[0][...], rights[0][...], dims) + dot(lefts[1][...], rights[1][...], dims)


def grads_kernel(*refs):
    lefts, rights, out = refs[:4], refs[4:8], refs[8]
    n = rights[0].shape[1]
    out[:, :n] = both_dots(lefts[:2], rights[:2], (0, 0)).astype(low)
    out[:, n:] = both_dots(lefts[2:], rights[2:], (0, 0)).astype(low)


def grads(lefts, rights):
    depth, rows = lefts[0].shape
    total = rights[0].shape[1] + rights[2].shape[1]
    return pl.pallas_call(
        grads_kernel,
        out_shape=jax.ShapeDtypeStruct((rows, total), low),
        grid=(rows // ROWS,),
        in_specs=[spec((depth, ROWS), lambda i: (0, i))] * 4
        + [once(v.shape, lambda i: (0, 0)) for v in rights],
        out_specs=spec((ROWS, total), lambda i: (i, 0)),
        compiler_params=params(28),
        cost_estimate=cost(
            4 * depth * rows * total, 8 * depth * rows + 2 * total * (rows + depth), hint=H_GRADS
        ),
    )(*lefts, *rights)


def back_kernel(*refs):
    *lefts, right, out_mine, out_away = refs
    turned = right[...].T
    half = LOCAL // 2
    away = lefts[1][...] if len(lefts) > 1 else lefts[0][half:]
    out_away[...] = dot(away, turned, (1, 0)).astype(low)
    out_mine[...] = dot(lefts[0][:half], turned, (1, 0)).astype(low)


def back_products(lefts, right, at=0, hint=1):
    rows, depth = LOCAL // 2, lefts[0].shape[1]
    width = right.shape[0]
    return pl.pallas_call(
        back_kernel,
        out_shape=[jax.ShapeDtypeStruct((rows, width), low)] * 2,
        grid=(width // ROWS,),
        in_specs=[once(v.shape, lambda i: (0, 0)) for v in lefts]
        + [spec((ROWS, depth), lambda i: (i, at))],
        out_specs=[spec((rows, ROWS), lambda i: (0, i))] * 2,
        compiler_params=params(20),
        cost_estimate=cost(
            4 * rows * depth * width, 2 * width * (depth + 2 * rows), hint=hint
        ),
    )(*lefts, right)


def adam_kernel(flipped, rates, extras, *refs):
    grad = refs[0]
    at = 0
    for k, (turn, rate) in enumerate(zip(flipped, rates)):
        weight, first, second = refs[1 + 3 * k : 4 + 3 * k]
        outs = refs[1 + extras + 3 * (len(rates) + k) : 4 + extras + 3 * (len(rates) + k)]
        n = weight.shape[0] if turn else weight.shape[1]
        g = grad[:, at : at + n].astype(wide)
        at += n
        if turn:
            g = g.T
        for out, value in zip(outs, adam(weight[...], first[...], second[...], g, rate, weight_decay)):
            out[...] = value
    for k in range(extras):
        refs[k - extras][...] = refs[1 + 3 * len(rates) + k][...]


def adam_weights(grad, weights, flipped, rates, extras=()):
    states = [v for group in weights for v in group] + list(extras)
    out = pl.pallas_call(
        functools.partial(adam_kernel, flipped, rates, len(extras)),
        out_shape=[jax.ShapeDtypeStruct(v.shape, v.dtype) for v in states],
        in_specs=[WHOLE] * (1 + len(states)),
        out_specs=[WHOLE] * len(states),
        compiler_params=params(24),
        cost_estimate=cost(20 * grad.size, 26 * grad.size, hint=H_ADAM),
    )(grad, *states)
    return [tuple(out[3 * k : 3 * k + 3]) for k in range(len(weights))] + list(out[3 * len(weights) :])


HALF = 384
TALL = BLOCK + 16


def first_grads_kernel(spot, *refs):
    normed, mine, away, draw, attended, weight, gain, left, right, dgain = refs
    half = LOCAL // 2
    project = dot(normed[...], draw[...], (0, 0))
    product = (project * weight[...].astype(wide)).astype(low)
    ones = jnp.ones((8, product.shape[1]), low)
    dgain[...] = dot(ones, product, (1, 1)) / gain[...]
    project = project.astype(low)
    output = dot(mine[...], attended[:half], (0, 0)) + dot(away[...], attended[half:], (0, 0))
    output = output.astype(low)
    for j in range(2):
        rows = slice(j * BLOCK, (j + 1) * BLOCK)
        a = j ^ spot[0]
        left[0, a, 0] = project[rows, :HALF]
        right[a, 0, 0, :BLOCK, : 4 * HEAD - HALF] = project[rows, HALF:]
        right[a, 0, 0, :BLOCK, 4 * HEAD - HALF :] = output[rows]


def first_grads(spot, normed, dmiddle, draw, attended, weight, gain):
    whole = lambda i, s: (0, 0)
    columns = lambda i, s: (0, i)
    return pl.pallas_call(
        first_grads_kernel,
        out_shape=[
            jax.ShapeDtypeStruct((4, 2, 2, BLOCK, HALF), low),
            jax.ShapeDtypeStruct((2, 2, 4, TALL, HALF), low),
            jax.ShapeDtypeStruct((8, 16 * BLOCK), wide),
        ],
        grid_spec=pltpu.PrefetchScalarGridSpec(
            num_scalar_prefetch=1,
            grid=(8,),
            in_specs=[
                spec((LOCAL, 2 * BLOCK), columns),
                spec((LOCAL // 2, 2 * BLOCK), columns),
                spec((LOCAL // 2, 2 * BLOCK), columns),
                once((LOCAL, 4 * HEAD), whole),
                once((LOCAL, 2 * HEAD), whole),
                spec((2 * BLOCK, 4 * HEAD), lambda i, s: (i, 0)),
                spec((1, 2 * BLOCK), columns),
            ],
            out_specs=[
                spec((1, 2, 1, BLOCK, HALF), lambda i, s: (i // 2, 0, i % 2 ^ s[1], 0, 0)),
                spec((2, 1, 1, TALL, HALF), lambda i, s: (0, i % 2 ^ s[1], i // 2, 0, 0)),
                spec((8, 2 * BLOCK), columns),
            ],
        ),
        compiler_params=params(FIRST_MIB),
        cost_estimate=cost(2 * LOCAL * 2048 * 768, 14 * MIB, hint=H_FIRST),
    )(spot, normed, *dmiddle, draw, attended, weight, gain)


SCALE = HEAD ** (-0.5)


def allowed(query_ids, key_ids, start):
    keys = key_ids[:, pl.ds(start, WINDOW)]
    row = lax.broadcasted_iota(jnp.int32, (QUERIES, WINDOW), 0)
    column = lax.broadcasted_iota(jnp.int32, (QUERIES, WINDOW), 1)
    return (query_ids[...] == keys) & (column <= row + BACK)


def attend_kernel(turn, core, query, pair, query_ids, key_ids, out, logsum):
    i = pl.program_id(0)
    start = pl.multiple_of(i * QUERIES, QUERIES)
    mask = allowed(query_ids, key_ids, start)
    logs = []
    for h in range(2):
        part = slice(h * HEAD, (h + 1) * HEAD)
        scores = dot(query[:, part], pair[pl.ds(start, WINDOW), :HEAD], (1, 1)) * SCALE
        scores = jnp.where(mask, scores, -1e30)
        top = jnp.max(scores, axis=-1, keepdims=True)
        unnormed = jnp.exp(scores - top)
        total = jnp.sum(unnormed, axis=-1, keepdims=True)
        probs = (unnormed * (1.0 / total)).astype(low)
        result = dot(probs, pair[pl.ds(start, WINDOW), HEAD:], (1, 0)).astype(low)
        for j in range(2):
            out[j ^ core[0], 0, :, part] = result[j * BLOCK : (j + 1) * BLOCK]
        logs.append(top + jnp.log(total))
    lane = lax.broadcasted_iota(jnp.int32, (QUERIES, HEAD), 1)
    logsum[...] = jnp.where(lane < HEAD // 2, logs[0], logs[1])


def attend(turn, core, query, pair, query_ids, key_ids):
    rows = lambda i, t, c: (i, 0)
    whole = lambda i, t, c: (0, 0)
    keys = BACK + LOCAL
    return pl.pallas_call(
        attend_kernel,
        out_shape=[
            jax.ShapeDtypeStruct((2, 4, BLOCK, 2 * HEAD), low),
            jax.ShapeDtypeStruct((LOCAL, HEAD), wide),
        ],
        grid_spec=pltpu.PrefetchScalarGridSpec(
            num_scalar_prefetch=2,
            grid=(LOCAL // QUERIES,),
            in_specs=[
                spec((QUERIES, 2 * HEAD), rows),
                once((keys, 2 * HEAD), whole),
                spec((QUERIES, 1), rows),
                spec((1, keys), whole),
            ],
            out_specs=[
                spec((2, 1, BLOCK, 2 * HEAD), lambda i, t, c: (0, t[i], 0, 0)),
                spec((QUERIES, HEAD), rows),
            ],
        ),
        compiler_params=params(24),
        cost_estimate=cost(
            8 * LOCAL * WINDOW * HEAD, 4 * LOCAL * 512, 2 * LOCAL * WINDOW, hint=H_ATTEND
        ),
    )(turn, core, query, pair, query_ids, key_ids)


def attend_back_kernel(
    turn, core, query, pair, query_ids, key_ids, grad, logsum, dquery, dpair
):
    i = pl.program_id(0)

    @pl.when(i == 0)
    def _():
        dpair[...] = jnp.zeros_like(dpair)

    start = pl.multiple_of(i * QUERIES, QUERIES)
    window = pl.ds(start, WINDOW)
    mask = allowed(query_ids, key_ids, start)
    dkey, dvalue = None, None
    for h in range(2):
        part = slice(h * HEAD, (h + 1) * HEAD)
        q = query[:, part]
        g = jnp.concatenate([grad[j ^ core[0], 0, :, part] for j in range(2)], axis=0)
        scores = dot(q, pair[window, :HEAD], (1, 1)) * SCALE
        probs = jnp.where(mask, jnp.exp(scores - logsum[:, h * 64 : h * 64 + 1]), 0.0)
        dprobs = dot(g, pair[window, HEAD:], (1, 1))
        inner = jnp.sum(probs * dprobs, axis=-1, keepdims=True)
        dscores = (probs * (dprobs - inner)).astype(low)
        dquery[:, part] = dot(dscores, pair[window, :HEAD], (1, 0)) * SCALE
        dv = dot(probs.astype(low), g, (0, 0))
        dk = dot(dscores, q, (0, 0))
        dkey = dk if dkey is None else dkey + dk
        dvalue = dv if dvalue is None else dvalue + dv
    dpair[window, :HEAD] += dkey * SCALE
    dpair[window, HEAD:] += dvalue


def attend_back(turn, core, query, pair, query_ids, key_ids, grad, logsum):
    rows = lambda i, t, c: (i, 0)
    whole = lambda i, t, c: (0, 0)
    keys = BACK + LOCAL
    return pl.pallas_call(
        attend_back_kernel,
        out_shape=[
            jax.ShapeDtypeStruct((LOCAL, 2 * HEAD), wide),
            jax.ShapeDtypeStruct((keys, 2 * HEAD), wide),
        ],
        grid_spec=pltpu.PrefetchScalarGridSpec(
            num_scalar_prefetch=2,
            grid=(LOCAL // QUERIES,),
            in_specs=[
                spec((QUERIES, 2 * HEAD), rows),
                once((keys, 2 * HEAD), whole),
                spec((QUERIES, 1), rows),
                spec((1, keys), whole),
                spec((2, 1, BLOCK, 2 * HEAD), lambda i, t, c: (0, t[i], 0, 0)),
                spec((QUERIES, HEAD), rows),
            ],
            out_specs=[spec((QUERIES, 2 * HEAD), rows), once((keys, 2 * HEAD), whole)],
        ),
        compiler_params=params(28),
        cost_estimate=cost(
            20 * LOCAL * WINDOW * HEAD, 8 * LOCAL * 512, 2 * LOCAL * WINDOW, hint=H_ATTEND_BACK
        ),
    )(turn, core, query, pair, query_ids, key_ids, grad, logsum)


def per_device(
    inputs,
    cotangent,
    document_index,
    positions,
    gains,
    gains_first,
    gains_second,
    project_weight,
    project_first,
    project_second,
    output_weight,
    output_first,
    output_second,
    expand_weight,
    expand_first,
    expand_second,
    shrink_weight,
    shrink_first,
    shrink_second,
):
    core, x = lax.axis_index("core"), lax.axis_index("x")
    half, yl = lax.axis_index("yh"), lax.axis_index("yl")
    width = inputs.shape[-1]
    qkv = project_weight.shape[1]
    ff = shrink_weight.shape[0]
    at_home = core == yl
    steps = jnp.arange(8, dtype=jnp.int32)
    place = lax.rem(x - steps % 4 + 4, 4) * 2 + (core ^ (steps // 4))
    turn = lax.rem(x - jnp.arange(4, dtype=jnp.int32) + 4, 4)
    core_of = core.reshape(1).astype(jnp.int32)
    flag = at_home.astype(jnp.int32).reshape(1)

    marks = jnp.stack([document_index[0], positions[0] // 32, positions[0] % 32])
    marks = jnp.pad(marks.astype(low), ((0, 13), (0, 0)))
    message = trade(jnp.concatenate([inputs[0], marks], axis=0))
    rows = message[:BLOCK]
    marks = message[BLOCK:].astype(jnp.int32)
    ids, places = marks[0], marks[1] * 32 + marks[2]

    gain_block = jnp.pad(gains.astype(low), (0, BLOCK * BLOCK - gains.shape[0])).reshape(BLOCK, BLOCK)
    first_shard = jnp.concatenate(
        [project_weight.astype(low), output_weight.astype(low).T, gain_block], axis=1
    )
    second_shard = jnp.concatenate([expand_weight.astype(low), shrink_weight.astype(low).T], axis=1)
    first_all = lax.all_gather(to_group(first_shard), GROUP, axis=0, tiled=True)
    rows_all = gather_rows(rows)
    second_shard = to_group(after(second_shard, message))
    second_all = lax.all_gather(after(second_shard, first_all), GROUP, axis=0, tiled=True)
    project_all = first_all[:, :qkv]
    output_all = first_all[:, qkv : qkv + 2 * HEAD]
    expand_all = second_all[:, : 2 * ff]
    shrink_all = second_all[:, 2 * ff :]
    gain_all = first_all.reshape(16, BLOCK, -1)[:, :3, qkv + 2 * HEAD :].reshape(16, 3 * BLOCK)
    gain_all = gain_all[:, : gains.shape[0]].reshape(-1).astype(wide)
    gain_one = gain_all[:width]
    gain_two = gain_all[width : 2 * width]
    gain_query = gain_all[2 * width : 2 * width + HEAD].reshape(1, HEAD)
    gain_key = gain_all[2 * width + HEAD :].reshape(1, HEAD)

    ids_here = lax.dynamic_slice_in_dim(ids, half * LOCAL, LOCAL)
    places_here = lax.dynamic_slice_in_dim(places, half * LOCAL, LOCAL)
    ids_keys = jnp.where(
        half == 0,
        jnp.concatenate([jnp.full((BACK,), -1, jnp.int32), ids[:LOCAL]]),
        ids[LOCAL - BACK :],
    )
    query_ids, key_ids = ids_here.reshape(-1, 1), ids_keys.reshape(1, -1)
    frequency = jnp.exp(jnp.arange(HEAD // 2, dtype=wide) * (-2.0 * math.log(theta) / HEAD))
    angle = places_here.astype(wide)[:, None] * frequency
    cosine, sine = jnp.cos(angle), jnp.sin(angle)
    cosine = jnp.concatenate([cosine, cosine], axis=1)
    sine = jnp.concatenate([-sine, sine], axis=1)

    values = rows.astype(wide)
    normed, raw, scale, query, pair = project(
        place, rows_all, first_all, gain_one.reshape(1, -1), gain_query, gain_key, cosine, sine
    )
    earlier = move(pair[LOCAL - BACK :], "yh", [(0, 1)])
    back_all = choose(place, flag, cotangent[0], other_core(cotangent[0]))
    back = [back_all[: LOCAL // 2], back_all[LOCAL // 2 :]]
    pair_all = jnp.concatenate([after(earlier, back_all), pair], axis=0)
    attended, logsum = attend(turn, core_of, query, pair_all, query_ids, key_ids)
    attended = attended.reshape(LOCAL, 2 * HEAD)
    mine = dot(attended[: LOCAL // 2], output_all, (1, 1)).astype(low)
    away = dot(attended[LOCAL // 2 :], output_all, (1, 1)).astype(low)
    middle = values + chip_sum(core_sum(mine, away))

    normed_two = gather_rows(rms_norm(middle, gain_two).astype(low))
    hidden, dexpanded = [], []
    for v, dy in zip(normed_two, back):
        expanded = dot(v, expand_all, (1, 0))
        activated, pull_act = jax.vjp(swiglu, expanded[:, :ff], expanded[:, ff:])
        hidden.append(activated.astype(low))
        dgate, dup = pull_act(dot(dy, shrink_all, (1, 0)))
        dexpanded.append(jnp.concatenate([dgate, dup], axis=1).astype(low))
    both_two = core_sum(*back_products(dexpanded, second_all))
    drows_two = chip_sum(both_two)
    second_grads = grads(
        [*after(tuple(normed_two), both_two), *back], [*dexpanded, *hidden]
    )
    second_red = lax.psum_scatter(second_grads, GROUP, scatter_dimension=0, tiled=True)
    drows_two = after(drows_two, second_grads)
    shrunk = core_sum(*back_products(after(tuple(hidden), second_grads), second_all, at=2, hint=0))

    _, pull_two = jax.vjp(rms_norm, middle, gain_two)
    dmiddle, dgain_two = pull_two(drows_two)
    dmiddle = back[0][:BLOCK].astype(wide) + dmiddle
    dmiddle_all = gather_rows(dmiddle.astype(low))
    dmiddle_all = after(tuple(dmiddle_all), shrunk)
    dattended = jnp.stack([dot(v, output_all, (1, 0)).astype(low) for v in dmiddle_all])
    mlp = chip_sum(after(shrunk, dmiddle_all))
    dquery, dpair = attend_back(
        turn,
        core_of,
        query,
        pair_all,
        query_ids,
        key_ids,
        dattended.reshape(2, 4, BLOCK, 2 * HEAD),
        logsum,
    )
    later = move(dpair[:BACK].astype(low), "yh", [(1, 0)])
    later = after(later, mlp)
    draw, dgain_heads = heads_back(
        place, raw, cosine, sine, gain_query, gain_key, dquery, dpair, later
    )
    outputs = trade((middle + after(mlp, draw)).astype(low))

    spot = jnp.stack([half, yl]).astype(jnp.int32)
    left, right, dgain_one = first_grads(
        spot, normed, dmiddle_all, draw, attended, first_all, gain_one.reshape(1, -1)
    )
    dgains = jnp.concatenate([dgain_one[0], dgain_two, dgain_heads[0], dgain_heads[1]]).astype(low)
    dgains = dgains.reshape(4, 2, 2, 1, -1)
    dgains = jnp.where(half == 0, dgains, dgains[:, :, ::-1])
    dgains = jnp.where(yl == 0, dgains, dgains[:, ::-1]).transpose(2, 1, 0, 3, 4)
    dgains = jnp.pad(dgains, ((0, 0), (0, 0), (0, 0), (0, 15), (0, HALF - gains.shape[0])))
    right = lax.dynamic_update_slice(right, dgains, (0, 0, 0, BLOCK, 0))
    drows_one = chip_sum(core_sum(*back_products([after(draw, left)], first_all, hint=H_BACK)))
    second_red = to_owner(second_red)
    expand_new, shrink_new = adam_weights(
        second_red,
        [(expand_weight, expand_first, expand_second), (shrink_weight, shrink_first, shrink_second)],
        (False, True),
        (0.05, 0.03),
    )
    left, right = sum_z(left).astype(low), sum_flips(right).astype(low)
    left, right = after((left, right), outputs, second_red)

    _, pull_one = jax.vjp(rms_norm, values, gain_one)
    dvalues, _ = pull_one(drows_one)
    input_grad = trade((dmiddle + dvalues).astype(low))

    right, left = sum_z(right), sum_flips(left)
    first_red = jnp.concatenate([left, right[:BLOCK]], axis=1)
    project_new, output_new, outputs, input_grad = adam_weights(
        first_red,
        [(project_weight, project_first, project_second), (output_weight, output_first, output_second)],
        (False, True),
        (0.05, 0.4),
        (outputs, input_grad),
    )
    dgains = right[BLOCK : BLOCK + 8]
    dgains = dgains + move(dgains, "yl", [(0, 1), (1, 0)])
    dgains = dgains + shift(dgains, 1) + shift(dgains, 2) + shift(dgains, 3)
    dgains = dgains[0, : gains.shape[0]]
    return (
        outputs[None],
        input_grad[None],
        *adam(gains, gains_first, gains_second, dgains, 0.5, 0.0),
        *project_new,
        *output_new,
        *expand_new,
        *shrink_new,
    )


def solution(mesh):
    fine = Mesh(mesh.devices.reshape(4, 2, 2, 4, 2), ("z", "core", "yh", "x", "yl"))
    tokens = P(("z", "core"), ("yh", "x", "yl"), None)
    marks = P(("z", "core"), None)
    gain = P(("z", "core", "yh"))
    tall = P(("z", "core", "yh"), ("x", "yl"))
    flat = P(("x", "yl"), ("z", "core", "yh"))
    in_specs = (
        tokens,
        P(("z", "core"), "yh", None),
        marks,
        marks,
        *[gain] * 3,
        *[tall] * 3,
        *[flat] * 3,
        *[tall] * 3,
        *[flat] * 3,
    )
    out_specs = (
        tokens,
        tokens,
        *[gain] * 3,
        *[tall] * 3,
        *[flat] * 3,
        *[tall] * 3,
        *[flat] * 3,
    )
    return jax.shard_map(
        per_device, mesh=fine, in_specs=in_specs, out_specs=out_specs, check_vma=False
    )
```

```python
import functools
import math

import jax
import jax.numpy as jnp
from jax import lax
from jax.experimental import pallas as pl
from jax.experimental.pallas import tpu as pltpu
from jax.sharding import Mesh
from jax.sharding import PartitionSpec as P

QUERY_HEADS = 16
KEY_VALUE_HEADS = 8
HEAD = 128
STEP = 5
LONGEST = 800
BLOCK = 128
LOCAL = 1024
BACK = 896
QUERIES = 256
WINDOW = BACK + QUERIES

epsilon = 1e-06
theta = 1000000.0
beta_first = 0.9
beta_second = 0.95
adam_epsilon = 1e-08
weight_decay = 0.1

low = jnp.bfloat16
wide = jnp.float32
MIB = 1024 * 1024
H_PROJECT = 1
H_ATTEND = 150
H_GRADS = 1
H_ATTEND_BACK = 36
H_HEADS_BACK = 1
H_BACK = 1
H_FIRST = 1
H_ADAM = 1

epsilon = 1e-06
theta = 1000000.0
beta_first = 0.9
beta_second = 0.95
adam_epsilon = 1e-08
weight_decay = 0.1

low = jnp.bfloat16
wide = jnp.float32
MIB = 1024 * 1024
ATTEND_HINT = 300
ATTEND_BACK_HINT = 260


def rms_norm(values, gain):
    return values * lax.rsqrt(jnp.mean(values * values, axis=-1, keepdims=True) + epsilon) * gain


def swiglu(gate, upward):
    return jax.nn.silu(gate) * upward


def adam(weight, first, second, grad, rate, decay_rate):
    mean = beta_first * first + (1.0 - beta_first) * grad
    square = beta_second * second + (1.0 - beta_second) * grad * grad
    mean_hat = mean / (1.0 - beta_first**STEP)
    square_hat = square / (1.0 - beta_second**STEP)
    updated = weight - rate * (
        mean_hat / (jnp.sqrt(square_hat) + adam_epsilon) + decay_rate * weight
    )
    return (mean, square, updated)


def dot(left, right, dims):
    return lax.dot_general(left, right, ((dims[:1], dims[1:]), ((), ())), preferred_element_type=wide)


def move(values, axis, pairs):
    return lax.ppermute(values, axis, pairs)


def shift(values, steps):
    return move(values, "x", [(i, (i + steps) % 4) for i in range(4)])


def other_core(values):
    return move(values, "core", [(0, 1), (1, 0)])


def trade(values):
    return move(values, ("core", "yl"), [(a * 2 + b, b * 2 + a) for a in range(2) for b in range(2)])


def to_group(values):
    pairs = [
        ((a * 2 + b) * 2 + d, (d * 2 + a) * 2 + b)
        for a in range(2)
        for b in range(2)
        for d in range(2)
    ]
    return move(values, ("core", "yh", "yl"), pairs)


def to_owner(values):
    pairs = [
        ((d * 2 + a) * 2 + b, (a * 2 + b) * 2 + d)
        for a in range(2)
        for b in range(2)
        for d in range(2)
    ]
    return move(values, ("core", "yh", "yl"), pairs)


def gather_rows(values):
    mine = jnp.concatenate([values, shift(values, 1), shift(values, 2), shift(values, 3)], axis=0)
    return mine, other_core(mine)


def core_sum(mine, away):
    return (mine.astype(wide) + other_core(away).astype(wide)).astype(low)


def chip_sum(both):
    pieces = both.reshape(4, BLOCK, -1)
    total = pieces[0].astype(wide)
    for k in (2, 1, 3):
        total = total + shift(pieces[k], 4 - k).astype(wide)
    return total


def chip_sum_at_once(both, x):
    pieces = both.reshape(4, BLOCK, -1)
    blocks = [lax.dynamic_index_in_dim(pieces, lax.rem(x - i + 4, 4), 0) for i in range(4)]
    blocks = lax.all_to_all(jnp.concatenate(blocks, axis=0), "x", 0, 0, tiled=True)
    return jnp.sum(blocks.astype(wide), axis=0)


def after(values, *others):
    return lax.optimization_barrier((values, *others))[0]


def sum_z(pieces):
    total = pieces[0].astype(wide)
    for k in (2, 1, 3):
        there = move(pieces[k], "z", [(i, (i + k) % 4) for i in range(4)])
        total = total + there.astype(wide)
    return total


def flip(values, a, b):
    pairs = [
        ((c * 2 + h) * 2 + d, ((d ^ b) * 2 + (h ^ a)) * 2 + c)
        for c in range(2)
        for h in range(2)
        for d in range(2)
    ]
    return move(values, ("core", "yh", "yl"), pairs)


def sum_flips(pieces):
    total = 0.0
    for a in (1, 0):
        for b in (1, 0):
            total = total + flip(pieces[a, b], a, b).astype(wide)
    return total


GROUP = ("z", "yh", "yl")


def spec(shape, index):
    return pl.BlockSpec(shape, index)


def once(shape, index):
    return pl.BlockSpec(shape, index, pipeline_mode=pl.Buffered(1))


def params(mib):
    return pltpu.CompilerParams(vmem_limit_bytes=mib * MIB)


def cost(flops, moved, special=0, hint=1):
    return pl.CostEstimate(
        flops=flops * hint, bytes_accessed=moved * hint, transcendentals=special * hint
    )


def choose_kernel(place, flag, own, away, out, arrived):
    def copies(source):
        return [
            pltpu.make_async_copy(
                source.at[pl.ds(pl.multiple_of(place[i] * BLOCK, BLOCK), BLOCK)],
                out.at[pl.ds(i * BLOCK, BLOCK)],
                arrived.at[i],
            )
            for i in range(8)
        ]

    @pl.when(flag[0] == 1)
    def _():
        for copy in copies(own):
            copy.start()

    @pl.when(flag[0] == 0)
    def _():
        for copy in copies(away):
            copy.start()

    for copy in copies(own):
        copy.wait()


def choose(place, flag, own, away):
    scalar = pl.BlockSpec(memory_space=pltpu.SMEM)
    there = pl.BlockSpec(memory_space=pl.ANY)
    return pl.pallas_call(
        choose_kernel,
        out_shape=jax.ShapeDtypeStruct(own.shape, own.dtype),
        in_specs=[scalar, scalar, there, there],
        out_specs=there,
        scratch_shapes=[pltpu.SemaphoreType.DMA((8,))],
        compiler_params=params(4),
        cost_estimate=cost(0, 2 * own.size * 2),
    )(place, flag, own, away)


def project_kernel(
    place, mine, away, weight, gain, gq, gk, cosine, sine, normed, raw, scale, query, pair
):
    i = pl.program_id(0)

    def work(rows):
        v = rows[...].astype(wide)
        r = lax.rsqrt(jnp.mean(v * v, axis=-1, keepdims=True) + epsilon)
        n = (v * r * gain[...]).astype(low)
        normed[...] = n
        scale[...] = jnp.broadcast_to(r, scale.shape)
        raw[...] = dot(n, weight[...], (1, 0))

    pl.when(i < 2)(lambda: work(mine))
    pl.when(i >= 2)(lambda: work(away))
    for k in range(2):
        here = slice(k * BLOCK, (k + 1) * BLOCK)
        there = pl.ds(pl.multiple_of(place[2 * i + k] * BLOCK, BLOCK), BLOCK)
        c, s = cosine[there], sine[there]
        for h in range(4):
            part = slice(h * HEAD, (h + 1) * HEAD)
            v = raw[here, part]
            if h < 3:
                v = rms_norm(v, gq[...] if h < 2 else gk[...])
                v = v * c + pltpu.roll(v, HEAD // 2, 1) * s
            if h < 2:
                query[there, part] = v.astype(low)
            else:
                pair[there, (h - 2) * HEAD : (h - 1) * HEAD] = v.astype(low)


SCALARS = pl.BlockSpec(memory_space=pltpu.SMEM)
WHOLE = pl.BlockSpec(memory_space=pltpu.VMEM)


def project(place, rows, weight, gain, gq, gk, cosine, sine):
    width = rows[0].shape[1]
    fixed = lambda i, p: (0, 0)
    moving = lambda i, p: (i, 0)
    tall = 2 * BLOCK
    return pl.pallas_call(
        project_kernel,
        out_shape=[
            jax.ShapeDtypeStruct((LOCAL, width), low),
            jax.ShapeDtypeStruct((LOCAL, 4 * HEAD), wide),
            jax.ShapeDtypeStruct((LOCAL, HEAD), wide),
            jax.ShapeDtypeStruct((LOCAL, 2 * HEAD), low),
            jax.ShapeDtypeStruct((LOCAL, 2 * HEAD), low),
        ],
        grid_spec=pltpu.PrefetchScalarGridSpec(
            num_scalar_prefetch=1,
            grid=(LOCAL // tall,),
            in_specs=[
                spec((tall, width), lambda i, p: (jnp.minimum(i, 1), 0)),
                spec((tall, width), lambda i, p: (jnp.maximum(i - 2, 0), 0)),
                once((width, 4 * HEAD), fixed),
                once((1, width), fixed),
                once((1, HEAD), fixed),
                once((1, HEAD), fixed),
                once((LOCAL, HEAD), fixed),
                once((LOCAL, HEAD), fixed),
            ],
            out_specs=[
                spec((tall, width), moving),
                spec((tall, 4 * HEAD), moving),
                spec((tall, HEAD), moving),
                once((LOCAL, 2 * HEAD), fixed),
                once((LOCAL, 2 * HEAD), fixed),
            ],
        ),
        compiler_params=params(24),
        cost_estimate=cost(2 * LOCAL * width * 512, 16 * MIB, hint=H_PROJECT),
    )(place, *rows, weight, gain, gq, gk, cosine, sine)


def turn_back(d, v, c, s, g):
    d = d * c + pltpu.roll(d * s, HEAD // 2, 1)
    r = lax.rsqrt(jnp.mean(v * v, axis=-1, keepdims=True) + epsilon)
    u = v * r
    e = d * g
    before = r * (e - u * jnp.mean(u * e, axis=-1, keepdims=True))
    return before.astype(low), jnp.sum(d * u, axis=0, keepdims=True)


def query_back_kernel(place, raw, cosine, sine, gq, dquery, draw, dgain):
    total = 0.0
    for i in range(8):
        here = pl.ds(i * BLOCK, BLOCK)
        there = pl.ds(pl.multiple_of(place[i] * BLOCK, BLOCK), BLOCK)
        for h in range(2):
            part = slice(h * HEAD, (h + 1) * HEAD)
            draw[here, part], add = turn_back(
                dquery[there, part], raw[here, part], cosine[there], sine[there], gq[...]
            )
            total += add
    dgain[...] = jnp.broadcast_to(total, dgain.shape)


def pair_back_kernel(place, raw, cosine, sine, gk, dpair, later, draw, dgain):
    total = 0.0
    for i in range(8):
        here = pl.ds(i * BLOCK, BLOCK)
        there = pl.ds(pl.multiple_of(place[i] * BLOCK, BLOCK), BLOCK)
        dp = dpair[pl.ds(pl.multiple_of(place[i] * BLOCK + BACK, BLOCK), BLOCK)]
        from_later = later[pl.ds(pl.multiple_of(jnp.maximum(place[i] - 1, 0) * BLOCK, BLOCK), BLOCK)]
        dp = dp + jnp.where(place[i] > 0, from_later.astype(wide), 0.0)
        draw[here, :HEAD], add = turn_back(
            dp[:, :HEAD], raw[here, 2 * HEAD : 3 * HEAD], cosine[there], sine[there], gk[...]
        )
        draw[here, HEAD:] = dp[:, HEAD:].astype(low)
        total += add
    dgain[...] = jnp.broadcast_to(total, dgain.shape)


def heads_back(kernel, place, *inputs):
    return pl.pallas_call(
        kernel,
        out_shape=[
            jax.ShapeDtypeStruct((LOCAL, 2 * HEAD), low),
            jax.ShapeDtypeStruct((8, HEAD), wide),
        ],
        in_specs=[SCALARS] + [WHOLE] * len(inputs),
        out_specs=[WHOLE] * 2,
        compiler_params=params(16),
        cost_estimate=cost(LOCAL * 512 * 10, LOCAL * 512 * 6, hint=H_HEADS_BACK),
    )(place, *inputs)


ROWS = 256


def both_dots(lefts, rights, dims):
    return dot(lefts[0][...], rights[0][...], dims) + dot(lefts[1][...], rights[1][...], dims)


def grads_kernel(*refs):
    lefts, rights, out = refs[:4], refs[4:8], refs[8]
    n = rights[0].shape[1]
    out[:, :n] = both_dots(lefts[:2], rights[:2], (0, 0)).astype(low)
    out[:, n:] = both_dots(lefts[2:], rights[2:], (0, 0)).astype(low)


def grads(lefts, rights):
    depth, rows = lefts[0].shape
    total = rights[0].shape[1] + rights[2].shape[1]
    return pl.pallas_call(
        grads_kernel,
        out_shape=jax.ShapeDtypeStruct((rows, total), low),
        grid=(rows // ROWS,),
        in_specs=[spec((depth, ROWS), lambda i: (0, i))] * 4
        + [once(v.shape, lambda i: (0, 0)) for v in rights],
        out_specs=spec((ROWS, total), lambda i: (i, 0)),
        compiler_params=params(28),
        cost_estimate=cost(
            4 * depth * rows * total, 8 * depth * rows + 2 * total * (rows + depth), hint=H_GRADS
        ),
    )(*lefts, *rights)


def back_kernel(parts, *refs):
    *lefts, right, out_mine, out_away = refs
    turned = right[...].T
    half = LOCAL // 2
    if parts:
        depth = lefts[0].shape[1]
        pick = lambda rows: sum(
            dot(left[rows], turned[k * depth : (k + 1) * depth], (1, 0))
            for k, left in enumerate(lefts)
        )
        mine, away = pick(pl.ds(0, half)), pick(pl.ds(half, half))
    else:
        mine, away = [dot(left[...], turned, (1, 0)) for left in lefts]
    out_away[...] = away.astype(low)
    out_mine[...] = mine.astype(low)


def back_products(lefts, right, at=0, parts=False, hint=1):
    rows = LOCAL // 2
    depth = sum(v.shape[1] for v in lefts) if parts else lefts[0].shape[1]
    width = right.shape[0]
    return pl.pallas_call(
        functools.partial(back_kernel, parts),
        out_shape=[jax.ShapeDtypeStruct((rows, width), low)] * 2,
        grid=(width // ROWS,),
        in_specs=[once(v.shape, lambda i: (0, 0)) for v in lefts]
        + [spec((ROWS, depth), lambda i: (i, at))],
        out_specs=[spec((rows, ROWS), lambda i: (0, i))] * 2,
        compiler_params=params(20),
        cost_estimate=cost(
            4 * rows * depth * width, 2 * width * (depth + 2 * rows), hint=hint
        ),
    )(*lefts, right)


def adam_kernel(columns, flipped, rates, extras, *refs):
    grad = refs[0]
    for k, (turn, rate) in enumerate(zip(flipped, rates)):
        weight, first, second = refs[1 + 3 * k : 4 + 3 * k]
        outs = refs[1 + extras + 3 * (len(rates) + k) : 4 + extras + 3 * (len(rates) + k)]
        g = [grad[:BLOCK, at : at + n] for at, n in columns[k]]
        g = (jnp.concatenate(g, axis=1) if len(g) > 1 else g[0]).astype(wide)
        if turn:
            g = g.T
        for out, value in zip(outs, adam(weight[...], first[...], second[...], g, rate, weight_decay)):
            out[...] = value
    for k in range(extras):
        refs[k - extras][...] = refs[1 + 3 * len(rates) + k][...]


def adam_weights(grad, columns, weights, flipped, rates, extras=()):
    states = [v for group in weights for v in group] + list(extras)
    out = pl.pallas_call(
        functools.partial(adam_kernel, columns, flipped, rates, len(extras)),
        out_shape=[jax.ShapeDtypeStruct(v.shape, v.dtype) for v in states],
        in_specs=[WHOLE] * (1 + len(states)),
        out_specs=[WHOLE] * len(states),
        compiler_params=params(24),
        cost_estimate=cost(20 * grad.size, 26 * grad.size, hint=H_ADAM),
    )(grad, *states)
    return [tuple(out[3 * k : 3 * k + 3]) for k in range(len(weights))] + list(out[3 * len(weights) :])


PART = 2 * HEAD
TALL = BLOCK + 16


def project_grad(normed, draw, weight, gain, dgain):
    project = dot(normed[...], draw[...], (0, 0))
    product = (project * weight[...].astype(wide)).astype(low)
    dgain[...] = dot(jnp.ones((8, PART), low), product, (1, 1)) / gain[...]
    return project.astype(low)


def query_grads_kernel(spot, normed, draw, weight, gain, mine, away, attended, out, dgain):
    project = project_grad(normed, draw, weight, gain, dgain)
    half = LOCAL // 2
    output = dot(mine[...], attended[:half], (0, 0)) + dot(away[...], attended[half:], (0, 0))
    output = output.astype(low)
    for j in range(2):
        rows = slice(j * BLOCK, (j + 1) * BLOCK)
        out[0, j ^ spot[0], 0, :, :PART] = project[rows]
        out[0, j ^ spot[0], 0, :, PART:] = output[rows]


def pair_grads_kernel(spot, normed, draw, weight, gain, out, dgain):
    project = project_grad(normed, draw, weight, gain, dgain)
    for j in range(2):
        out[0, j ^ spot[0], 0, :BLOCK] = project[j * BLOCK : (j + 1) * BLOCK]


def first_grads(spot, normed, draw, weight, gain, part, out, block, others=()):
    whole = lambda i, s: (0, 0)
    columns = lambda i, s: (0, i)
    rows = 2 * BLOCK
    return pl.pallas_call(
        query_grads_kernel if others else pair_grads_kernel,
        out_shape=[
            jax.ShapeDtypeStruct(out, low),
            jax.ShapeDtypeStruct((8, 16 * BLOCK), wide),
        ],
        grid_spec=pltpu.PrefetchScalarGridSpec(
            num_scalar_prefetch=1,
            grid=(8,),
            in_specs=[
                spec((LOCAL, rows), columns),
                once((LOCAL, PART), whole),
                spec((rows, PART), lambda i, s: (i, part)),
                spec((1, rows), columns),
            ]
            + [spec((LOCAL // 2, rows), columns)] * len(others[:2])
            + [once((LOCAL, PART), whole)] * len(others[2:]),
            out_specs=[spec(*block), spec((8, rows), columns)],
        ),
        compiler_params=params(24),
        cost_estimate=cost(2 * LOCAL * 2048 * 256, 8 * MIB, hint=H_FIRST),
    )(spot, normed, draw, weight, gain, *others)


def leaving(rows, columns):
    place = lambda i, s: (lax.rem(i // 2 - s[2] + 4, 4), 0, i % 2 ^ s[1], 0, 0)
    return (4, 2, 2, rows, columns), ((1, 2, 1, rows, columns), place)


def query_grads(spot, normed, draw, weight, gain, dmiddle, attended):
    others = (*dmiddle, attended)
    return first_grads(spot, normed, draw, weight, gain, 0, *leaving(BLOCK, 2 * PART), others)


def pair_grads(spot, normed, draw, weight, gain):
    return first_grads(spot, normed, draw, weight, gain, 1, *leaving(TALL, PART))


SCALE = HEAD ** (-0.5)


def allowed(query_ids, key_ids, start):
    keys = key_ids[:, pl.ds(start, WINDOW)]
    row = lax.broadcasted_iota(jnp.int32, (QUERIES, WINDOW), 0)
    column = lax.broadcasted_iota(jnp.int32, (QUERIES, WINDOW), 1)
    return (query_ids[...] == keys) & (column <= row + BACK)


def attend_kernel(turn, core, query, pair, query_ids, key_ids, out, logsum):
    i = pl.program_id(0)
    start = pl.multiple_of(i * QUERIES, QUERIES)
    mask = allowed(query_ids, key_ids, start)
    logs = []
    for h in range(2):
        part = slice(h * HEAD, (h + 1) * HEAD)
        scores = dot(query[:, part], pair[pl.ds(start, WINDOW), :HEAD], (1, 1)) * SCALE
        scores = jnp.where(mask, scores, -1e30)
        top = jnp.max(scores, axis=-1, keepdims=True)
        unnormed = jnp.exp(scores - top)
        total = jnp.sum(unnormed, axis=-1, keepdims=True)
        probs = (unnormed * (1.0 / total)).astype(low)
        result = dot(probs, pair[pl.ds(start, WINDOW), HEAD:], (1, 0)).astype(low)
        for j in range(2):
            out[j ^ core[0], 0, :, part] = result[j * BLOCK : (j + 1) * BLOCK]
        logs.append(top + jnp.log(total))
    lane = lax.broadcasted_iota(jnp.int32, (QUERIES, HEAD), 1)
    logsum[...] = jnp.where(lane < HEAD // 2, logs[0], logs[1])


def attend(turn, core, query, pair, query_ids, key_ids):
    rows = lambda i, t, c: (i, 0)
    whole = lambda i, t, c: (0, 0)
    keys = BACK + LOCAL
    return pl.pallas_call(
        attend_kernel,
        out_shape=[
            jax.ShapeDtypeStruct((2, 4, BLOCK, 2 * HEAD), low),
            jax.ShapeDtypeStruct((LOCAL, HEAD), wide),
        ],
        grid_spec=pltpu.PrefetchScalarGridSpec(
            num_scalar_prefetch=2,
            grid=(LOCAL // QUERIES,),
            in_specs=[
                spec((QUERIES, 2 * HEAD), rows),
                once((keys, 2 * HEAD), whole),
                spec((QUERIES, 1), rows),
                spec((1, keys), whole),
            ],
            out_specs=[
                spec((2, 1, BLOCK, 2 * HEAD), lambda i, t, c: (0, t[i], 0, 0)),
                spec((QUERIES, HEAD), rows),
            ],
        ),
        compiler_params=params(24),
        cost_estimate=cost(
            8 * LOCAL * WINDOW * HEAD, 4 * LOCAL * 512, 2 * LOCAL * WINDOW, hint=H_ATTEND
        ),
    )(turn, core, query, pair, query_ids, key_ids)


def attend_back_kernel(
    turn, core, query, pair, query_ids, key_ids, grad, logsum, dquery, dpair
):
    i = pl.program_id(0)

    @pl.when(i == 0)
    def _():
        dpair[...] = jnp.zeros_like(dpair)

    start = pl.multiple_of(i * QUERIES, QUERIES)
    window = pl.ds(start, WINDOW)
    mask = allowed(query_ids, key_ids, start)
    dkey, dvalue = None, None
    for h in range(2):
        part = slice(h * HEAD, (h + 1) * HEAD)
        q = query[:, part]
        g = jnp.concatenate([grad[j ^ core[0], 0, :, part] for j in range(2)], axis=0)
        scores = dot(q, pair[window, :HEAD], (1, 1)) * SCALE
        probs = jnp.where(mask, jnp.exp(scores - logsum[:, h * 64 : h * 64 + 1]), 0.0)
        dprobs = dot(g, pair[window, HEAD:], (1, 1))
        inner = jnp.sum(probs * dprobs, axis=-1, keepdims=True)
        dscores = (probs * (dprobs - inner)).astype(low)
        dquery[:, part] = dot(dscores, pair[window, :HEAD], (1, 0)) * SCALE
        dv = dot(probs.astype(low), g, (0, 0))
        dk = dot(dscores, q, (0, 0))
        dkey = dk if dkey is None else dkey + dk
        dvalue = dv if dvalue is None else dvalue + dv
    dpair[window, :HEAD] += dkey * SCALE
    dpair[window, HEAD:] += dvalue


def attend_back(turn, core, query, pair, query_ids, key_ids, grad, logsum):
    rows = lambda i, t, c: (i, 0)
    whole = lambda i, t, c: (0, 0)
    keys = BACK + LOCAL
    return pl.pallas_call(
        attend_back_kernel,
        out_shape=[
            jax.ShapeDtypeStruct((LOCAL, 2 * HEAD), wide),
            jax.ShapeDtypeStruct((keys, 2 * HEAD), wide),
        ],
        grid_spec=pltpu.PrefetchScalarGridSpec(
            num_scalar_prefetch=2,
            grid=(LOCAL // QUERIES,),
            in_specs=[
                spec((QUERIES, 2 * HEAD), rows),
                once((keys, 2 * HEAD), whole),
                spec((QUERIES, 1), rows),
                spec((1, keys), whole),
                spec((2, 1, BLOCK, 2 * HEAD), lambda i, t, c: (0, t[i], 0, 0)),
                spec((QUERIES, HEAD), rows),
            ],
            out_specs=[spec((QUERIES, 2 * HEAD), rows), once((keys, 2 * HEAD), whole)],
        ),
        compiler_params=params(28),
        cost_estimate=cost(
            20 * LOCAL * WINDOW * HEAD, 8 * LOCAL * 512, 2 * LOCAL * WINDOW, hint=H_ATTEND_BACK
        ),
    )(turn, core, query, pair, query_ids, key_ids, grad, logsum)


def per_device(
    inputs,
    cotangent,
    document_index,
    positions,
    gains,
    gains_first,
    gains_second,
    project_weight,
    project_first,
    project_second,
    output_weight,
    output_first,
    output_second,
    expand_weight,
    expand_first,
    expand_second,
    shrink_weight,
    shrink_first,
    shrink_second,
):
    core, x = lax.axis_index("core"), lax.axis_index("x")
    half, yl = lax.axis_index("yh"), lax.axis_index("yl")
    width = inputs.shape[-1]
    qkv = project_weight.shape[1]
    ff = shrink_weight.shape[0]
    at_home = core == yl
    steps = jnp.arange(8, dtype=jnp.int32)
    place = lax.rem(x - steps % 4 + 4, 4) * 2 + (core ^ (steps // 4))
    turn = lax.rem(x - jnp.arange(4, dtype=jnp.int32) + 4, 4)
    core_of = core.reshape(1).astype(jnp.int32)
    flag = at_home.astype(jnp.int32).reshape(1)

    marks = jnp.stack([document_index[0], positions[0] // 32, positions[0] % 32])
    marks = jnp.pad(marks.astype(low), ((0, 13), (0, 0)))
    message = trade(jnp.concatenate([inputs[0], marks], axis=0))
    rows = message[:BLOCK]
    marks = message[BLOCK:].astype(jnp.int32)
    ids, places = marks[0], marks[1] * 32 + marks[2]

    gain_block = jnp.pad(gains.astype(low), (0, BLOCK * BLOCK - gains.shape[0])).reshape(BLOCK, BLOCK)
    first_shard = jnp.concatenate(
        [project_weight.astype(low), output_weight.astype(low).T, gain_block], axis=1
    )
    second_shard = jnp.concatenate([expand_weight.astype(low), shrink_weight.astype(low).T], axis=1)
    first_all = lax.all_gather(to_group(first_shard), GROUP, axis=0, tiled=True)
    rows_all = gather_rows(rows)
    second_shard = to_group(after(second_shard, message))
    second_all = lax.all_gather(after(second_shard, first_all), GROUP, axis=0, tiled=True)
    project_all = first_all[:, :qkv]
    output_all = first_all[:, qkv : qkv + 2 * HEAD]
    expand_all = second_all[:, : 2 * ff]
    shrink_all = second_all[:, 2 * ff :]
    gain_all = first_all.reshape(16, BLOCK, -1)[:, :3, qkv + 2 * HEAD :].reshape(16, 3 * BLOCK)
    gain_all = gain_all[:, : gains.shape[0]].reshape(-1).astype(wide)
    gain_one = gain_all[:width]
    gain_two = gain_all[width : 2 * width]
    gain_query = gain_all[2 * width : 2 * width + HEAD].reshape(1, HEAD)
    gain_key = gain_all[2 * width + HEAD :].reshape(1, HEAD)

    ids_here = lax.dynamic_slice_in_dim(ids, half * LOCAL, LOCAL)
    places_here = lax.dynamic_slice_in_dim(places, half * LOCAL, LOCAL)
    ids_keys = jnp.where(
        half == 0,
        jnp.concatenate([jnp.full((BACK,), -1, jnp.int32), ids[:LOCAL]]),
        ids[LOCAL - BACK :],
    )
    query_ids, key_ids = ids_here.reshape(-1, 1), ids_keys.reshape(1, -1)
    frequency = jnp.exp(jnp.arange(HEAD // 2, dtype=wide) * (-2.0 * math.log(theta) / HEAD))
    angle = places_here.astype(wide)[:, None] * frequency
    cosine, sine = jnp.cos(angle), jnp.sin(angle)
    cosine = jnp.concatenate([cosine, cosine], axis=1)
    sine = jnp.concatenate([-sine, sine], axis=1)

    values = rows.astype(wide)
    normed, raw, scale, query, pair = project(
        place, rows_all, first_all, gain_one.reshape(1, -1), gain_query, gain_key, cosine, sine
    )
    earlier = move(pair[LOCAL - BACK :], "yh", [(0, 1)])
    back_all = choose(place, flag, cotangent[0], other_core(cotangent[0]))
    back = [back_all[: LOCAL // 2], back_all[LOCAL // 2 :]]
    pair_all = jnp.concatenate([after(earlier, back_all), pair], axis=0)
    attended, logsum = attend(turn, core_of, query, pair_all, query_ids, key_ids)
    attended = attended.reshape(LOCAL, 2 * HEAD)
    mine = dot(attended[: LOCAL // 2], output_all, (1, 1)).astype(low)
    away = dot(attended[LOCAL // 2 :], output_all, (1, 1)).astype(low)
    middle = values + chip_sum(core_sum(mine, away))

    normed_two = gather_rows(rms_norm(middle, gain_two).astype(low))
    hidden, dexpanded = [], []
    for v, dy in zip(normed_two, back):
        expanded = dot(v, expand_all, (1, 0))
        activated, pull_act = jax.vjp(swiglu, expanded[:, :ff], expanded[:, ff:])
        hidden.append(activated.astype(low))
        dgate, dup = pull_act(dot(dy, shrink_all, (1, 0)))
        dexpanded.append(jnp.concatenate([dgate, dup], axis=1).astype(low))
    both_two = core_sum(*back_products(dexpanded, second_all))
    drows_two = chip_sum(both_two)
    second_grads = grads(
        [*after(tuple(normed_two), both_two), *back], [*dexpanded, *hidden]
    )
    second_red = lax.psum_scatter(second_grads, GROUP, scatter_dimension=0, tiled=True)
    drows_two = after(drows_two, second_grads)
    shrunk = core_sum(*back_products(after(tuple(hidden), second_grads), second_all, at=2, hint=0))

    _, pull_two = jax.vjp(rms_norm, middle, gain_two)
    dmiddle, dgain_two = pull_two(drows_two)
    dmiddle = back[0][:BLOCK].astype(wide) + dmiddle
    dmiddle_all = gather_rows(dmiddle.astype(low))
    dmiddle_all = after(tuple(dmiddle_all), shrunk)
    dattended = jnp.stack([dot(v, output_all, (1, 0)).astype(low) for v in dmiddle_all])
    mlp = chip_sum_at_once(after(shrunk, dmiddle_all), x)
    dquery, dpair = attend_back(
        turn,
        core_of,
        query,
        pair_all,
        query_ids,
        key_ids,
        dattended.reshape(2, 4, BLOCK, 2 * HEAD),
        logsum,
    )
    later = move(dpair[:BACK].astype(low), "yh", [(1, 0)])
    draw_query, dgain_query = heads_back(
        query_back_kernel, place, raw, cosine, sine, gain_query, dquery
    )
    spot = jnp.stack([half, yl, lax.axis_index("z")]).astype(jnp.int32)
    gain_row = gain_one.reshape(1, -1)
    left, dgain_one = query_grads(
        spot, normed, draw_query, first_all, gain_row, dmiddle_all, attended
    )
    left = sum_z(left)
    later = after(later, mlp, left)
    draw_pair, dgain_key = heads_back(
        pair_back_kernel, place, raw, cosine, sine, gain_key, dpair, later
    )
    outputs = trade((middle + after(mlp, draw_pair)).astype(low))

    pair_right, dgain_rest = pair_grads(spot, normed, draw_pair, first_all, gain_row)
    dgains = jnp.concatenate([(dgain_one + dgain_rest)[0], dgain_two, dgain_query[0], dgain_key[0]])
    dgains = jnp.pad(dgains.reshape(-1, BLOCK), ((0, 6), (0, 0)))
    dgains = dgains + other_core(dgains)
    dgains = dgains + shift(dgains, 1) + shift(dgains, 2) + shift(dgains, 3)
    dgains = dgains[:-6].astype(low).reshape(4, 2, 2, 1, -1)
    dgains = jnp.where(half == 0, dgains, dgains[:, :, ::-1])
    dgains = jnp.where(yl == 0, dgains, dgains[:, ::-1]).transpose(0, 2, 1, 3, 4)
    dgains = jnp.roll(dgains, -lax.axis_index("z"), axis=0)
    over = dgains[..., PART:]
    dgains = jnp.concatenate([dgains[..., :PART], jnp.pad(over, ((0, 0),) * 4 + ((0, PART - over.shape[-1]),))], axis=3)
    dgains = jnp.pad(dgains, ((0, 0), (0, 0), (0, 0), (0, 14), (0, 0)))
    right = lax.dynamic_update_slice(pair_right, dgains, (0, 0, 0, BLOCK, 0))
    both_one = core_sum(
        *back_products(after((draw_query, draw_pair), dgain_rest), first_all, parts=True, hint=H_BACK)
    )
    right = sum_z(right)
    drows_one = chip_sum(after(both_one, outputs))
    second_red = to_owner(second_red)
    expand_new, shrink_new = adam_weights(
        second_red,
        (((0, 2 * ff),), ((2 * ff, ff),)),
        [(expand_weight, expand_first, expand_second), (shrink_weight, shrink_first, shrink_second)],
        (False, True),
        (0.05, 0.03),
    )
    both = jnp.concatenate([jnp.pad(left, ((0, 0), (0, 0), (0, 16), (0, 0))), right], axis=3)
    first_red = sum_flips(after(both.astype(low), second_red))

    _, pull_one = jax.vjp(rms_norm, values, gain_one)
    dvalues, _ = pull_one(drows_one)
    input_grad = trade((dmiddle + dvalues).astype(low))

    dgains = first_red[BLOCK : BLOCK + 8, 2 * PART :]
    project_new, output_new, outputs, input_grad = adam_weights(
        first_red,
        (((0, PART), (2 * PART, PART)), ((PART, PART),)),
        [(project_weight, project_first, project_second), (output_weight, output_first, output_second)],
        (False, True),
        (0.05, 0.4),
        (outputs, input_grad),
    )
    dgains = dgains[:2].reshape(-1)[: gains.shape[0]]
    return (
        outputs[None],
        input_grad[None],
        *adam(gains, gains_first, gains_second, dgains, 0.5, 0.0),
        *project_new,
        *output_new,
        *expand_new,
        *shrink_new,
    )


def solution(mesh):
    fine = Mesh(mesh.devices.reshape(4, 2, 2, 4, 2), ("z", "core", "yh", "x", "yl"))
    tokens = P(("z", "core"), ("yh", "x", "yl"), None)
    marks = P(("z", "core"), None)
    gain = P(("z", "core", "yh"))
    tall = P(("z", "core", "yh"), ("x", "yl"))
    flat = P(("x", "yl"), ("z", "core", "yh"))
    in_specs = (
        tokens,
        P(("z", "core"), "yh", None),
        marks,
        marks,
        *[gain] * 3,
        *[tall] * 3,
        *[flat] * 3,
        *[tall] * 3,
        *[flat] * 3,
    )
    out_specs = (
        tokens,
        tokens,
        *[gain] * 3,
        *[tall] * 3,
        *[flat] * 3,
        *[tall] * 3,
        *[flat] * 3,
    )
    return jax.shard_map(
        per_device, mesh=fine, in_specs=in_specs, out_specs=out_specs, check_vma=False
    )
```

```python
import functools
import math

import jax
import jax.numpy as jnp
from jax import lax
from jax.experimental import pallas as pl
from jax.experimental.pallas import tpu as pltpu
from jax.sharding import Mesh
from jax.sharding import PartitionSpec as P

QUERY_HEADS = 16
KEY_VALUE_HEADS = 8
HEAD = 128
STEP = 5
LONGEST = 800
BLOCK = 128
LOCAL = 1024
BACK = 896
QUERIES = 256
WINDOW = BACK + QUERIES

epsilon = 1e-06
theta = 1000000.0
beta_first = 0.9
beta_second = 0.95
adam_epsilon = 1e-08
weight_decay = 0.1

low = jnp.bfloat16
wide = jnp.float32
MIB = 1024 * 1024
H_PROJECT = 1
H_ATTEND = 150
H_GRADS = 1
H_ATTEND_BACK = 36
H_HEADS_BACK = 1
H_BACK = 1
H_FIRST = 1
H_ADAM = 1

epsilon = 1e-06
theta = 1000000.0
beta_first = 0.9
beta_second = 0.95
adam_epsilon = 1e-08
weight_decay = 0.1

low = jnp.bfloat16
wide = jnp.float32
MIB = 1024 * 1024
ATTEND_HINT = 300
ATTEND_BACK_HINT = 260


def rms_norm(values, gain):
    return values * lax.rsqrt(jnp.mean(values * values, axis=-1, keepdims=True) + epsilon) * gain


def swiglu(gate, upward):
    return jax.nn.silu(gate) * upward


def adam(weight, first, second, grad, rate, decay_rate):
    mean = beta_first * first + (1.0 - beta_first) * grad
    square = beta_second * second + (1.0 - beta_second) * grad * grad
    mean_hat = mean / (1.0 - beta_first**STEP)
    square_hat = square / (1.0 - beta_second**STEP)
    updated = weight - rate * (
        mean_hat / (jnp.sqrt(square_hat) + adam_epsilon) + decay_rate * weight
    )
    return (mean, square, updated)


def dot(left, right, dims):
    return lax.dot_general(left, right, ((dims[:1], dims[1:]), ((), ())), preferred_element_type=wide)


def move(values, axis, pairs):
    return lax.ppermute(values, axis, pairs)


def shift(values, steps):
    return move(values, "x", [(i, (i + steps) % 4) for i in range(4)])


def other_core(values):
    return move(values, "core", [(0, 1), (1, 0)])


def trade(values):
    return move(values, ("core", "yl"), [(a * 2 + b, b * 2 + a) for a in range(2) for b in range(2)])


def to_group(values):
    pairs = [
        ((a * 2 + b) * 2 + d, (d * 2 + a) * 2 + b)
        for a in range(2)
        for b in range(2)
        for d in range(2)
    ]
    return move(values, ("core", "yh", "yl"), pairs)


def to_owner(values):
    pairs = [
        ((d * 2 + a) * 2 + b, (a * 2 + b) * 2 + d)
        for a in range(2)
        for b in range(2)
        for d in range(2)
    ]
    return move(values, ("core", "yh", "yl"), pairs)


def gather_rows(values):
    mine = jnp.concatenate([values, shift(values, 1), shift(values, 2), shift(values, 3)], axis=0)
    return mine, other_core(mine)


def core_sum(mine, away):
    return (mine.astype(wide) + other_core(away).astype(wide)).astype(low)


def chip_sum(both):
    pieces = both.reshape(4, BLOCK, -1)
    total = pieces[0].astype(wide)
    for k in (2, 1, 3):
        total = total + shift(pieces[k], 4 - k).astype(wide)
    return total


def chip_sum_at_once(both, x):
    pieces = both.reshape(4, BLOCK, -1)
    blocks = [lax.dynamic_index_in_dim(pieces, lax.rem(x - i + 4, 4), 0) for i in range(4)]
    blocks = lax.all_to_all(jnp.concatenate(blocks, axis=0), "x", 0, 0, tiled=True)
    return jnp.sum(blocks.astype(wide), axis=0)


def after(values, *others):
    return lax.optimization_barrier((values, *others))[0]


def sum_z(pieces):
    total = pieces[0].astype(wide)
    for k in (2, 1, 3):
        there = move(pieces[k], "z", [(i, (i + k) % 4) for i in range(4)])
        total = total + there.astype(wide)
    return total


def flip(values, a, b):
    pairs = [
        ((c * 2 + h) * 2 + d, ((d ^ b) * 2 + (h ^ a)) * 2 + c)
        for c in range(2)
        for h in range(2)
        for d in range(2)
    ]
    return move(values, ("core", "yh", "yl"), pairs)


def sum_flips(pieces):
    total = 0.0
    for a in (1, 0):
        for b in (1, 0):
            total = total + flip(pieces[a, b], a, b).astype(wide)
    return total


GROUP = ("z", "yh", "yl")


def spec(shape, index):
    return pl.BlockSpec(shape, index)


def once(shape, index):
    return pl.BlockSpec(shape, index, pipeline_mode=pl.Buffered(1))


def params(mib):
    return pltpu.CompilerParams(vmem_limit_bytes=mib * MIB)


def cost(flops, moved, special=0, hint=1):
    return pl.CostEstimate(
        flops=flops * hint, bytes_accessed=moved * hint, transcendentals=special * hint
    )


def choose_kernel(place, flag, own, away, out, arrived):
    def copies(source):
        return [
            pltpu.make_async_copy(
                source.at[pl.ds(pl.multiple_of(place[i] * BLOCK, BLOCK), BLOCK)],
                out.at[pl.ds(i * BLOCK, BLOCK)],
                arrived.at[i],
            )
            for i in range(8)
        ]

    @pl.when(flag[0] == 1)
    def _():
        for copy in copies(own):
            copy.start()

    @pl.when(flag[0] == 0)
    def _():
        for copy in copies(away):
            copy.start()

    for copy in copies(own):
        copy.wait()


def choose(place, flag, own, away):
    scalar = pl.BlockSpec(memory_space=pltpu.SMEM)
    there = pl.BlockSpec(memory_space=pl.ANY)
    return pl.pallas_call(
        choose_kernel,
        out_shape=jax.ShapeDtypeStruct(own.shape, own.dtype),
        in_specs=[scalar, scalar, there, there],
        out_specs=there,
        scratch_shapes=[pltpu.SemaphoreType.DMA((8,))],
        compiler_params=params(4),
        cost_estimate=cost(0, 2 * own.size * 2),
    )(place, flag, own, away)


def project_kernel(
    place, mine, away, weight, gain, gq, gk, cosine, sine, normed, raw, scale, query, pair
):
    i = pl.program_id(0)

    def work(rows):
        v = rows[...].astype(wide)
        r = lax.rsqrt(jnp.mean(v * v, axis=-1, keepdims=True) + epsilon)
        n = (v * r * gain[...]).astype(low)
        normed[...] = n
        scale[...] = jnp.broadcast_to(r, scale.shape)
        raw[...] = dot(n, weight[...], (1, 0))

    pl.when(i < 2)(lambda: work(mine))
    pl.when(i >= 2)(lambda: work(away))
    for k in range(2):
        here = slice(k * BLOCK, (k + 1) * BLOCK)
        there = pl.ds(pl.multiple_of(place[2 * i + k] * BLOCK, BLOCK), BLOCK)
        c, s = cosine[there], sine[there]
        for h in range(4):
            part = slice(h * HEAD, (h + 1) * HEAD)
            v = raw[here, part]
            if h < 3:
                v = rms_norm(v, gq[...] if h < 2 else gk[...])
                v = v * c + pltpu.roll(v, HEAD // 2, 1) * s
            if h < 2:
                query[there, part] = v.astype(low)
            else:
                pair[there, (h - 2) * HEAD : (h - 1) * HEAD] = v.astype(low)


SCALARS = pl.BlockSpec(memory_space=pltpu.SMEM)
WHOLE = pl.BlockSpec(memory_space=pltpu.VMEM)


def project(place, rows, weight, gain, gq, gk, cosine, sine):
    width = rows[0].shape[1]
    fixed = lambda i, p: (0, 0)
    moving = lambda i, p: (i, 0)
    tall = 2 * BLOCK
    return pl.pallas_call(
        project_kernel,
        out_shape=[
            jax.ShapeDtypeStruct((LOCAL, width), low),
            jax.ShapeDtypeStruct((LOCAL, 4 * HEAD), wide),
            jax.ShapeDtypeStruct((LOCAL, HEAD), wide),
            jax.ShapeDtypeStruct((LOCAL, 2 * HEAD), low),
            jax.ShapeDtypeStruct((LOCAL, 2 * HEAD), low),
        ],
        grid_spec=pltpu.PrefetchScalarGridSpec(
            num_scalar_prefetch=1,
            grid=(LOCAL // tall,),
            in_specs=[
                spec((tall, width), lambda i, p: (jnp.minimum(i, 1), 0)),
                spec((tall, width), lambda i, p: (jnp.maximum(i - 2, 0), 0)),
                once((width, 4 * HEAD), fixed),
                once((1, width), fixed),
                once((1, HEAD), fixed),
                once((1, HEAD), fixed),
                once((LOCAL, HEAD), fixed),
                once((LOCAL, HEAD), fixed),
            ],
            out_specs=[
                spec((tall, width), moving),
                spec((tall, 4 * HEAD), moving),
                spec((tall, HEAD), moving),
                once((LOCAL, 2 * HEAD), fixed),
                once((LOCAL, 2 * HEAD), fixed),
            ],
        ),
        compiler_params=params(52),
        cost_estimate=cost(2 * LOCAL * width * 512, 16 * MIB, hint=H_PROJECT),
    )(place, *rows, weight, gain, gq, gk, cosine, sine)


def turn_back(d, v, c, s, g):
    d = d * c + pltpu.roll(d * s, HEAD // 2, 1)
    r = lax.rsqrt(jnp.mean(v * v, axis=-1, keepdims=True) + epsilon)
    u = v * r
    e = d * g
    before = r * (e - u * jnp.mean(u * e, axis=-1, keepdims=True))
    return before.astype(low), jnp.sum(d * u, axis=0, keepdims=True)


def query_back_kernel(place, raw, cosine, sine, gq, dquery, draw, dgain):
    total = 0.0
    for i in range(8):
        here = pl.ds(i * BLOCK, BLOCK)
        there = pl.ds(pl.multiple_of(place[i] * BLOCK, BLOCK), BLOCK)
        for h in range(2):
            part = slice(h * HEAD, (h + 1) * HEAD)
            draw[here, part], add = turn_back(
                dquery[there, part], raw[here, part], cosine[there], sine[there], gq[...]
            )
            total += add
    dgain[...] = jnp.broadcast_to(total, dgain.shape)


def pair_back_kernel(place, raw, cosine, sine, gk, dpair, later, draw, dgain):
    total = 0.0
    for i in range(8):
        here = pl.ds(i * BLOCK, BLOCK)
        there = pl.ds(pl.multiple_of(place[i] * BLOCK, BLOCK), BLOCK)
        dp = dpair[pl.ds(pl.multiple_of(place[i] * BLOCK + BACK, BLOCK), BLOCK)]
        from_later = later[pl.ds(pl.multiple_of(jnp.maximum(place[i] - 1, 0) * BLOCK, BLOCK), BLOCK)]
        dp = dp + jnp.where(place[i] > 0, from_later.astype(wide), 0.0)
        draw[here, :HEAD], add = turn_back(
            dp[:, :HEAD], raw[here, 2 * HEAD : 3 * HEAD], cosine[there], sine[there], gk[...]
        )
        draw[here, HEAD:] = dp[:, HEAD:].astype(low)
        total += add
    dgain[...] = jnp.broadcast_to(total, dgain.shape)


def heads_back(kernel, place, *inputs):
    return pl.pallas_call(
        kernel,
        out_shape=[
            jax.ShapeDtypeStruct((LOCAL, 2 * HEAD), low),
            jax.ShapeDtypeStruct((8, HEAD), wide),
        ],
        in_specs=[SCALARS] + [WHOLE] * len(inputs),
        out_specs=[WHOLE] * 2,
        compiler_params=params(16),
        cost_estimate=cost(LOCAL * 512 * 10, LOCAL * 512 * 6, hint=H_HEADS_BACK),
    )(place, *inputs)


ROWS = 256


def both_dots(lefts, rights, dims):
    return dot(lefts[0][...], rights[0][...], dims) + dot(lefts[1][...], rights[1][...], dims)


def grads_kernel(*refs):
    lefts, rights, out = refs[:4], refs[4:8], refs[8]
    n = rights[0].shape[1]
    out[:, :n] = both_dots(lefts[:2], rights[:2], (0, 0)).astype(low)
    out[:, n:] = both_dots(lefts[2:], rights[2:], (0, 0)).astype(low)


def grads(lefts, rights):
    depth, rows = lefts[0].shape
    total = rights[0].shape[1] + rights[2].shape[1]
    return pl.pallas_call(
        grads_kernel,
        out_shape=jax.ShapeDtypeStruct((rows, total), low),
        grid=(rows // ROWS,),
        in_specs=[spec((depth, ROWS), lambda i: (0, i))] * 4
        + [once(v.shape, lambda i: (0, 0)) for v in rights],
        out_specs=spec((ROWS, total), lambda i: (i, 0)),
        compiler_params=params(28),
        cost_estimate=cost(
            4 * depth * rows * total, 8 * depth * rows + 2 * total * (rows + depth), hint=H_GRADS
        ),
    )(*lefts, *rights)


def back_kernel(parts, *refs):
    *lefts, right, out_mine, out_away = refs
    turned = right[...].T
    half = LOCAL // 2
    if parts:
        depth = lefts[0].shape[1]
        pick = lambda rows: sum(
            dot(left[rows], turned[k * depth : (k + 1) * depth], (1, 0))
            for k, left in enumerate(lefts)
        )
        mine, away = pick(pl.ds(0, half)), pick(pl.ds(half, half))
    else:
        mine, away = [dot(left[...], turned, (1, 0)) for left in lefts]
    out_away[...] = away.astype(low)
    out_mine[...] = mine.astype(low)


def back_products(lefts, right, at=0, parts=False, hint=1):
    rows = LOCAL // 2
    depth = sum(v.shape[1] for v in lefts) if parts else lefts[0].shape[1]
    width = right.shape[0]
    return pl.pallas_call(
        functools.partial(back_kernel, parts),
        out_shape=[jax.ShapeDtypeStruct((rows, width), low)] * 2,
        grid=(width // ROWS,),
        in_specs=[once(v.shape, lambda i: (0, 0)) for v in lefts]
        + [spec((ROWS, depth), lambda i: (i, at))],
        out_specs=[spec((rows, ROWS), lambda i: (0, i))] * 2,
        compiler_params=params(20),
        cost_estimate=cost(
            4 * rows * depth * width, 2 * width * (depth + 2 * rows), hint=hint
        ),
    )(*lefts, right)


def adam_kernel(columns, flipped, rates, extras, *refs):
    grad = refs[0]
    for k, (turn, rate) in enumerate(zip(flipped, rates)):
        weight, first, second = refs[1 + 3 * k : 4 + 3 * k]
        outs = refs[1 + extras + 3 * (len(rates) + k) : 4 + extras + 3 * (len(rates) + k)]
        g = [grad[:BLOCK, at : at + n] for at, n in columns[k]]
        g = (jnp.concatenate(g, axis=1) if len(g) > 1 else g[0]).astype(wide)
        if turn:
            g = g.T
        for out, value in zip(outs, adam(weight[...], first[...], second[...], g, rate, weight_decay)):
            out[...] = value
    for k in range(extras):
        refs[k - extras][...] = refs[1 + 3 * len(rates) + k][...]


def adam_weights(grad, columns, weights, flipped, rates, extras=()):
    states = [v for group in weights for v in group] + list(extras)
    out = pl.pallas_call(
        functools.partial(adam_kernel, columns, flipped, rates, len(extras)),
        out_shape=[jax.ShapeDtypeStruct(v.shape, v.dtype) for v in states],
        in_specs=[WHOLE] * (1 + len(states)),
        out_specs=[WHOLE] * len(states),
        compiler_params=params(24),
        cost_estimate=cost(20 * grad.size, 26 * grad.size, hint=H_ADAM),
    )(grad, *states)
    return [tuple(out[3 * k : 3 * k + 3]) for k in range(len(weights))] + list(out[3 * len(weights) :])


PART = 2 * HEAD
TALL = BLOCK + 16


def project_grad(normed, draw, weight, gain, dgain):
    project = dot(normed[...], draw[...], (0, 0))
    product = (project * weight[...].astype(wide)).astype(low)
    dgain[...] = dot(jnp.ones((8, PART), low), product, (1, 1)) / gain[...]
    return project.astype(low)


def query_grads_kernel(spot, normed, draw, weight, gain, mine, away, attended, out, dgain):
    project = project_grad(normed, draw, weight, gain, dgain)
    half = LOCAL // 2
    output = dot(mine[...], attended[:half], (0, 0)) + dot(away[...], attended[half:], (0, 0))
    output = output.astype(low)
    for j in range(2):
        rows = slice(j * BLOCK, (j + 1) * BLOCK)
        out[0, j ^ spot[0], 0, :, :PART] = project[rows]
        out[0, j ^ spot[0], 0, :, PART:] = output[rows]


def pair_grads_kernel(spot, normed, draw, weight, gain, out, dgain):
    project = project_grad(normed, draw, weight, gain, dgain)
    for j in range(2):
        out[0, j ^ spot[0], 0, :BLOCK] = project[j * BLOCK : (j + 1) * BLOCK]


def first_grads(spot, normed, draw, weight, gain, part, out, block, others=()):
    whole = lambda i, s: (0, 0)
    columns = lambda i, s: (0, i)
    rows = 2 * BLOCK
    return pl.pallas_call(
        query_grads_kernel if others else pair_grads_kernel,
        out_shape=[
            jax.ShapeDtypeStruct(out, low),
            jax.ShapeDtypeStruct((8, 16 * BLOCK), wide),
        ],
        grid_spec=pltpu.PrefetchScalarGridSpec(
            num_scalar_prefetch=1,
            grid=(8,),
            in_specs=[
                spec((LOCAL, rows), columns),
                once((LOCAL, PART), whole),
                spec((rows, PART), lambda i, s: (i, part)),
                spec((1, rows), columns),
            ]
            + [spec((LOCAL // 2, rows), columns)] * len(others[:2])
            + [once((LOCAL, PART), whole)] * len(others[2:]),
            out_specs=[spec(*block), spec((8, rows), columns)],
        ),
        compiler_params=params(24),
        cost_estimate=cost(2 * LOCAL * 2048 * 256, 8 * MIB, hint=H_FIRST),
    )(spot, normed, draw, weight, gain, *others)


def leaving(rows, columns):
    place = lambda i, s: (lax.rem(i // 2 - s[2] + 4, 4), 0, i % 2 ^ s[1], 0, 0)
    return (4, 2, 2, rows, columns), ((1, 2, 1, rows, columns), place)


def query_grads(spot, normed, draw, weight, gain, dmiddle, attended):
    others = (*dmiddle, attended)
    return first_grads(spot, normed, draw, weight, gain, 0, *leaving(BLOCK, 2 * PART), others)


def pair_grads(spot, normed, draw, weight, gain):
    return first_grads(spot, normed, draw, weight, gain, 1, *leaving(TALL, PART))


SCALE = HEAD ** (-0.5)


def allowed(query_ids, key_ids, start):
    keys = key_ids[:, pl.ds(start, WINDOW)]
    row = lax.broadcasted_iota(jnp.int32, (QUERIES, WINDOW), 0)
    column = lax.broadcasted_iota(jnp.int32, (QUERIES, WINDOW), 1)
    return (query_ids[...] == keys) & (column <= row + BACK)


def attend_kernel(turn, core, query, pair, query_ids, key_ids, out, logsum):
    i = pl.program_id(0)
    start = pl.multiple_of(i * QUERIES, QUERIES)
    mask = allowed(query_ids, key_ids, start)
    logs = []
    for h in range(2):
        part = slice(h * HEAD, (h + 1) * HEAD)
        scores = dot(query[:, part], pair[pl.ds(start, WINDOW), :HEAD], (1, 1)) * SCALE
        scores = jnp.where(mask, scores, -1e30)
        top = jnp.max(scores, axis=-1, keepdims=True)
        unnormed = jnp.exp(scores - top)
        total = jnp.sum(unnormed, axis=-1, keepdims=True)
        probs = (unnormed * (1.0 / total)).astype(low)
        result = dot(probs, pair[pl.ds(start, WINDOW), HEAD:], (1, 0)).astype(low)
        for j in range(2):
            out[j ^ core[0], 0, :, part] = result[j * BLOCK : (j + 1) * BLOCK]
        logs.append(top + jnp.log(total))
    lane = lax.broadcasted_iota(jnp.int32, (QUERIES, HEAD), 1)
    logsum[...] = jnp.where(lane < HEAD // 2, logs[0], logs[1])


def attend(turn, core, query, pair, query_ids, key_ids):
    rows = lambda i, t, c: (i, 0)
    whole = lambda i, t, c: (0, 0)
    keys = BACK + LOCAL
    return pl.pallas_call(
        attend_kernel,
        out_shape=[
            jax.ShapeDtypeStruct((2, 4, BLOCK, 2 * HEAD), low),
            jax.ShapeDtypeStruct((LOCAL, HEAD), wide),
        ],
        grid_spec=pltpu.PrefetchScalarGridSpec(
            num_scalar_prefetch=2,
            grid=(LOCAL // QUERIES,),
            in_specs=[
                spec((QUERIES, 2 * HEAD), rows),
                once((keys, 2 * HEAD), whole),
                spec((QUERIES, 1), rows),
                spec((1, keys), whole),
            ],
            out_specs=[
                spec((2, 1, BLOCK, 2 * HEAD), lambda i, t, c: (0, t[i], 0, 0)),
                spec((QUERIES, HEAD), rows),
            ],
        ),
        compiler_params=params(24),
        cost_estimate=cost(
            8 * LOCAL * WINDOW * HEAD, 4 * LOCAL * 512, 2 * LOCAL * WINDOW, hint=H_ATTEND
        ),
    )(turn, core, query, pair, query_ids, key_ids)


def attend_back_kernel(
    turn, core, query, pair, query_ids, key_ids, grad, logsum, dquery, dpair
):
    i = pl.program_id(0)

    @pl.when(i == 0)
    def _():
        dpair[...] = jnp.zeros_like(dpair)

    start = pl.multiple_of(i * QUERIES, QUERIES)
    window = pl.ds(start, WINDOW)
    mask = allowed(query_ids, key_ids, start)
    dkey, dvalue = None, None
    for h in range(2):
        part = slice(h * HEAD, (h + 1) * HEAD)
        q = query[:, part]
        g = jnp.concatenate([grad[j ^ core[0], 0, :, part] for j in range(2)], axis=0)
        scores = dot(q, pair[window, :HEAD], (1, 1)) * SCALE
        probs = jnp.where(mask, jnp.exp(scores - logsum[:, h * 64 : h * 64 + 1]), 0.0)
        dprobs = dot(g, pair[window, HEAD:], (1, 1))
        inner = jnp.sum(probs * dprobs, axis=-1, keepdims=True)
        dscores = (probs * (dprobs - inner)).astype(low)
        dquery[:, part] = dot(dscores, pair[window, :HEAD], (1, 0)) * SCALE
        dv = dot(probs.astype(low), g, (0, 0))
        dk = dot(dscores, q, (0, 0))
        dkey = dk if dkey is None else dkey + dk
        dvalue = dv if dvalue is None else dvalue + dv
    dpair[window, :HEAD] += dkey * SCALE
    dpair[window, HEAD:] += dvalue


def attend_back(turn, core, query, pair, query_ids, key_ids, grad, logsum):
    rows = lambda i, t, c: (i, 0)
    whole = lambda i, t, c: (0, 0)
    keys = BACK + LOCAL
    return pl.pallas_call(
        attend_back_kernel,
        out_shape=[
            jax.ShapeDtypeStruct((LOCAL, 2 * HEAD), wide),
            jax.ShapeDtypeStruct((keys, 2 * HEAD), wide),
        ],
        grid_spec=pltpu.PrefetchScalarGridSpec(
            num_scalar_prefetch=2,
            grid=(LOCAL // QUERIES,),
            in_specs=[
                spec((QUERIES, 2 * HEAD), rows),
                once((keys, 2 * HEAD), whole),
                spec((QUERIES, 1), rows),
                spec((1, keys), whole),
                spec((2, 1, BLOCK, 2 * HEAD), lambda i, t, c: (0, t[i], 0, 0)),
                spec((QUERIES, HEAD), rows),
            ],
            out_specs=[spec((QUERIES, 2 * HEAD), rows), once((keys, 2 * HEAD), whole)],
        ),
        compiler_params=params(28),
        cost_estimate=cost(
            20 * LOCAL * WINDOW * HEAD, 8 * LOCAL * 512, 2 * LOCAL * WINDOW, hint=H_ATTEND_BACK
        ),
    )(turn, core, query, pair, query_ids, key_ids, grad, logsum)


def per_device(
    inputs,
    cotangent,
    document_index,
    positions,
    gains,
    gains_first,
    gains_second,
    project_weight,
    project_first,
    project_second,
    output_weight,
    output_first,
    output_second,
    expand_weight,
    expand_first,
    expand_second,
    shrink_weight,
    shrink_first,
    shrink_second,
):
    core, x = lax.axis_index("core"), lax.axis_index("x")
    half, yl = lax.axis_index("yh"), lax.axis_index("yl")
    width = inputs.shape[-1]
    qkv = project_weight.shape[1]
    ff = shrink_weight.shape[0]
    at_home = core == yl
    steps = jnp.arange(8, dtype=jnp.int32)
    place = lax.rem(x - steps % 4 + 4, 4) * 2 + (core ^ (steps // 4))
    turn = lax.rem(x - jnp.arange(4, dtype=jnp.int32) + 4, 4)
    core_of = core.reshape(1).astype(jnp.int32)
    flag = at_home.astype(jnp.int32).reshape(1)

    marks = jnp.stack([document_index[0], positions[0] // 32, positions[0] % 32])
    marks = jnp.pad(marks.astype(low), ((0, 13), (0, 0)))
    message = trade(jnp.concatenate([inputs[0], marks], axis=0))
    rows = message[:BLOCK]
    marks = message[BLOCK:].astype(jnp.int32)
    ids, places = marks[0], marks[1] * 32 + marks[2]

    gain_block = jnp.pad(gains.astype(low), (0, BLOCK * BLOCK - gains.shape[0])).reshape(BLOCK, BLOCK)
    first_shard = jnp.concatenate(
        [project_weight.astype(low), output_weight.astype(low).T, gain_block], axis=1
    )
    second_shard = jnp.concatenate([expand_weight.astype(low), shrink_weight.astype(low).T], axis=1)
    first_all = lax.all_gather(to_group(first_shard), GROUP, axis=0, tiled=True)
    rows_all = gather_rows(rows)
    second_shard = to_group(after(second_shard, message))
    second_all = lax.all_gather(after(second_shard, first_all), GROUP, axis=0, tiled=True)
    project_all = first_all[:, :qkv]
    output_all = first_all[:, qkv : qkv + 2 * HEAD]
    expand_all = second_all[:, : 2 * ff]
    shrink_all = second_all[:, 2 * ff :]
    gain_all = first_all.reshape(16, BLOCK, -1)[:, :3, qkv + 2 * HEAD :].reshape(16, 3 * BLOCK)
    gain_all = gain_all[:, : gains.shape[0]].reshape(-1).astype(wide)
    gain_one = gain_all[:width]
    gain_two = gain_all[width : 2 * width]
    gain_query = gain_all[2 * width : 2 * width + HEAD].reshape(1, HEAD)
    gain_key = gain_all[2 * width + HEAD :].reshape(1, HEAD)

    ids_here = lax.dynamic_slice_in_dim(ids, half * LOCAL, LOCAL)
    places_here = lax.dynamic_slice_in_dim(places, half * LOCAL, LOCAL)
    ids_keys = jnp.where(
        half == 0,
        jnp.concatenate([jnp.full((BACK,), -1, jnp.int32), ids[:LOCAL]]),
        ids[LOCAL - BACK :],
    )
    query_ids, key_ids = ids_here.reshape(-1, 1), ids_keys.reshape(1, -1)
    frequency = jnp.exp(jnp.arange(HEAD // 2, dtype=wide) * (-2.0 * math.log(theta) / HEAD))
    angle = places_here.astype(wide)[:, None] * frequency
    cosine, sine = jnp.cos(angle), jnp.sin(angle)
    cosine = jnp.concatenate([cosine, cosine], axis=1)
    sine = jnp.concatenate([-sine, sine], axis=1)

    values = rows.astype(wide)
    normed, raw, scale, query, pair = project(
        place, rows_all, first_all, gain_one.reshape(1, -1), gain_query, gain_key, cosine, sine
    )
    earlier = move(pair[LOCAL - BACK :], "yh", [(0, 1)])
    back_all = choose(place, flag, cotangent[0], other_core(cotangent[0]))
    back = [back_all[: LOCAL // 2], back_all[LOCAL // 2 :]]
    pair_all = jnp.concatenate([after(earlier, back_all), pair], axis=0)
    attended, logsum = attend(turn, core_of, query, pair_all, query_ids, key_ids)
    attended = attended.reshape(LOCAL, 2 * HEAD)
    mine = dot(attended[: LOCAL // 2], output_all, (1, 1)).astype(low)
    away = dot(attended[LOCAL // 2 :], output_all, (1, 1)).astype(low)
    middle = values + chip_sum(core_sum(mine, away))

    normed_two = gather_rows(rms_norm(middle, gain_two).astype(low))
    hidden, dexpanded = [], []
    for v, dy in zip(normed_two, back):
        expanded = dot(v, expand_all, (1, 0))
        activated, pull_act = jax.vjp(swiglu, expanded[:, :ff], expanded[:, ff:])
        hidden.append(activated.astype(low))
        dgate, dup = pull_act(dot(dy, shrink_all, (1, 0)))
        dexpanded.append(jnp.concatenate([dgate, dup], axis=1).astype(low))
    both_two = core_sum(*back_products(dexpanded, second_all))
    drows_two = chip_sum(both_two)
    second_grads = grads(
        [*after(tuple(normed_two), both_two), *back], [*dexpanded, *hidden]
    )
    second_red = lax.psum_scatter(second_grads, GROUP, scatter_dimension=0, tiled=True)
    drows_two = after(drows_two, second_grads)
    shrunk = core_sum(*back_products(after(tuple(hidden), second_grads), second_all, at=2, hint=0))

    _, pull_two = jax.vjp(rms_norm, middle, gain_two)
    dmiddle, dgain_two = pull_two(drows_two)
    dmiddle = back[0][:BLOCK].astype(wide) + dmiddle
    dmiddle_all = gather_rows(dmiddle.astype(low))
    dmiddle_all = after(tuple(dmiddle_all), shrunk)
    dattended = jnp.stack([dot(v, output_all, (1, 0)).astype(low) for v in dmiddle_all])
    mlp = chip_sum_at_once(after(shrunk, dmiddle_all), x)
    dquery, dpair = attend_back(
        turn,
        core_of,
        query,
        pair_all,
        query_ids,
        key_ids,
        dattended.reshape(2, 4, BLOCK, 2 * HEAD),
        logsum,
    )
    later = move(dpair[:BACK].astype(low), "yh", [(1, 0)])
    draw_query, dgain_query = heads_back(
        query_back_kernel, place, raw, cosine, sine, gain_query, dquery
    )
    spot = jnp.stack([half, yl, lax.axis_index("z")]).astype(jnp.int32)
    gain_row = gain_one.reshape(1, -1)
    left, dgain_one = query_grads(
        spot, normed, draw_query, first_all, gain_row, dmiddle_all, attended
    )
    left_grads = left
    left = sum_z(left)
    later = after(later, mlp, left_grads)
    draw_pair, dgain_key = heads_back(
        pair_back_kernel, place, raw, cosine, sine, gain_key, dpair, later
    )
    outputs = trade((middle + after(mlp, draw_pair)).astype(low))

    pair_right, dgain_rest = pair_grads(spot, normed, draw_pair, first_all, gain_row)
    dgains = jnp.concatenate([(dgain_one + dgain_rest)[0], dgain_two, dgain_query[0], dgain_key[0]])
    dgains = jnp.pad(dgains.reshape(-1, BLOCK), ((0, 6), (0, 0)))
    dgains = dgains + other_core(dgains)
    dgains = dgains + shift(dgains, 1) + shift(dgains, 2) + shift(dgains, 3)
    dgains = dgains[:-6].astype(low).reshape(4, 2, 2, 1, -1)
    dgains = jnp.where(half == 0, dgains, dgains[:, :, ::-1])
    dgains = jnp.where(yl == 0, dgains, dgains[:, ::-1]).transpose(0, 2, 1, 3, 4)
    dgains = jnp.roll(dgains, -lax.axis_index("z"), axis=0)
    over = dgains[..., PART:]
    dgains = jnp.concatenate([dgains[..., :PART], jnp.pad(over, ((0, 0),) * 4 + ((0, PART - over.shape[-1]),))], axis=3)
    dgains = jnp.pad(dgains, ((0, 0), (0, 0), (0, 0), (0, 14), (0, 0)))
    right = lax.dynamic_update_slice(pair_right, dgains, (0, 0, 0, BLOCK, 0))
    both_one = core_sum(
        *back_products(after((draw_query, draw_pair), dgain_rest), first_all, parts=True, hint=H_BACK)
    )
    right = sum_z(right)
    drows_one = chip_sum_at_once(both_one, x)
    second_red = to_owner(second_red)
    expand_new, shrink_new = adam_weights(
        second_red,
        (((0, 2 * ff),), ((2 * ff, ff),)),
        [(expand_weight, expand_first, expand_second), (shrink_weight, shrink_first, shrink_second)],
        (False, True),
        (0.05, 0.03),
    )
    both = jnp.concatenate([jnp.pad(left, ((0, 0), (0, 0), (0, 16), (0, 0))), right], axis=3)
    first_red = sum_flips(after(both.astype(low), second_red))

    _, pull_one = jax.vjp(rms_norm, values, gain_one)
    dvalues, _ = pull_one(drows_one)
    input_grad = trade(after((dmiddle + dvalues).astype(low), outputs))

    dgains = first_red[BLOCK : BLOCK + 8, 2 * PART :]
    project_new, output_new, outputs, input_grad = adam_weights(
        first_red,
        (((0, PART), (2 * PART, PART)), ((PART, PART),)),
        [(project_weight, project_first, project_second), (output_weight, output_first, output_second)],
        (False, True),
        (0.05, 0.4),
        (outputs, input_grad),
    )
    dgains = dgains[:2].reshape(-1)[: gains.shape[0]]
    return (
        outputs[None],
        input_grad[None],
        *adam(gains, gains_first, gains_second, dgains, 0.5, 0.0),
        *project_new,
        *output_new,
        *expand_new,
        *shrink_new,
    )


def solution(mesh):
    fine = Mesh(mesh.devices.reshape(4, 2, 2, 4, 2), ("z", "core", "yh", "x", "yl"))
    tokens = P(("z", "core"), ("yh", "x", "yl"), None)
    marks = P(("z", "core"), None)
    gain = P(("z", "core", "yh"))
    tall = P(("z", "core", "yh"), ("x", "yl"))
    flat = P(("x", "yl"), ("z", "core", "yh"))
    in_specs = (
        tokens,
        P(("z", "core"), "yh", None),
        marks,
        marks,
        *[gain] * 3,
        *[tall] * 3,
        *[flat] * 3,
        *[tall] * 3,
        *[flat] * 3,
    )
    out_specs = (
        tokens,
        tokens,
        *[gain] * 3,
        *[tall] * 3,
        *[flat] * 3,
        *[tall] * 3,
        *[flat] * 3,
    )
    return jax.shard_map(
        per_device, mesh=fine, in_specs=in_specs, out_specs=out_specs, check_vma=False
    )
```

```python
import functools
import math

import jax
import jax.numpy as jnp
from jax import lax
from jax.experimental import pallas as pl
from jax.experimental.pallas import tpu as pltpu
from jax.sharding import Mesh
from jax.sharding import PartitionSpec as P

QUERY_HEADS = 16
KEY_VALUE_HEADS = 8
HEAD = 128
STEP = 5
LONGEST = 800
BLOCK = 128
LOCAL = 1024
BACK = 896
QUERIES = 256
WINDOW = BACK + QUERIES

epsilon = 1e-06
theta = 1000000.0
beta_first = 0.9
beta_second = 0.95
adam_epsilon = 1e-08
weight_decay = 0.1

low = jnp.bfloat16
wide = jnp.float32
MIB = 1024 * 1024
H_PROJECT = 1
H_ATTEND = 150
H_GRADS = 1
H_ATTEND_BACK = 30
H_HEADS_BACK = 1
H_BACK = 1
H_FIRST = 1
H_ADAM = 1

epsilon = 1e-06
theta = 1000000.0
beta_first = 0.9
beta_second = 0.95
adam_epsilon = 1e-08
weight_decay = 0.1

low = jnp.bfloat16
wide = jnp.float32
MIB = 1024 * 1024
ATTEND_HINT = 300
ATTEND_BACK_HINT = 260


def rms_norm(values, gain):
    return values * lax.rsqrt(jnp.mean(values * values, axis=-1, keepdims=True) + epsilon) * gain


def swiglu(gate, upward):
    return jax.nn.silu(gate) * upward


def adam(weight, first, second, grad, rate, decay_rate):
    mean = beta_first * first + (1.0 - beta_first) * grad
    square = beta_second * second + (1.0 - beta_second) * grad * grad
    mean_hat = mean / (1.0 - beta_first**STEP)
    square_hat = square / (1.0 - beta_second**STEP)
    updated = weight - rate * (
        mean_hat / (jnp.sqrt(square_hat) + adam_epsilon) + decay_rate * weight
    )
    return (mean, square, updated)


def dot(left, right, dims):
    return lax.dot_general(left, right, ((dims[:1], dims[1:]), ((), ())), preferred_element_type=wide)


def move(values, axis, pairs):
    return lax.ppermute(values, axis, pairs)


def shift(values, steps):
    return move(values, "x", [(i, (i + steps) % 4) for i in range(4)])


def other_core(values):
    return move(values, "core", [(0, 1), (1, 0)])


def trade(values):
    return move(values, ("core", "yl"), [(a * 2 + b, b * 2 + a) for a in range(2) for b in range(2)])


def to_group(values):
    pairs = [
        ((a * 2 + b) * 2 + d, (d * 2 + a) * 2 + b)
        for a in range(2)
        for b in range(2)
        for d in range(2)
    ]
    return move(values, ("core", "yh", "yl"), pairs)


def to_owner(values):
    pairs = [
        ((d * 2 + a) * 2 + b, (a * 2 + b) * 2 + d)
        for a in range(2)
        for b in range(2)
        for d in range(2)
    ]
    return move(values, ("core", "yh", "yl"), pairs)


def gather_rows(values, *others):
    pieces = (values, shift(values, 1), shift(values, 2), shift(values, 3))
    mine = jnp.concatenate(after(pieces, *others) if others else pieces, axis=0)
    return mine, other_core(mine)


def core_sum(mine, away):
    return (mine.astype(wide) + other_core(away).astype(wide)).astype(low)


def chip_sum(both):
    pieces = both.reshape(4, both.shape[0] // 4, -1)
    total = pieces[0].astype(wide)
    for k in (2, 1, 3):
        total = total + shift(pieces[k], 4 - k).astype(wide)
    return total


def chunks(values):
    n = values.shape[-1]
    values = values.reshape(8, 2, BLOCK // 2, n).transpose(1, 0, 2, 3)
    return [values[c].reshape(LOCAL // 2, n) for c in range(2)]


def chip_sum_at_once(both, x):
    pieces = both.reshape(4, both.shape[0] // 4, -1)
    blocks = [lax.dynamic_index_in_dim(pieces, lax.rem(x - i + 4, 4), 0) for i in range(4)]
    blocks = lax.all_to_all(jnp.concatenate(blocks, axis=0), "x", 0, 0, tiled=True)
    return jnp.sum(blocks.astype(wide), axis=0)


def after(values, *others):
    return lax.optimization_barrier((values, *others))[0]


def sum_z(pieces):
    total = pieces[0].astype(wide)
    for k in (2, 1, 3):
        there = move(pieces[k], "z", [(i, (i + k) % 4) for i in range(4)])
        total = total + there.astype(wide)
    return total


def flip(values, a, b):
    pairs = [
        ((c * 2 + h) * 2 + d, ((d ^ b) * 2 + (h ^ a)) * 2 + c)
        for c in range(2)
        for h in range(2)
        for d in range(2)
    ]
    return move(values, ("core", "yh", "yl"), pairs)


def sum_flips(pieces):
    total = 0.0
    for a in (1, 0):
        for b in (1, 0):
            total = total + flip(pieces[a, b], a, b).astype(wide)
    return total


GROUP = ("z", "yh", "yl")


def spec(shape, index):
    return pl.BlockSpec(shape, index)


def once(shape, index):
    return pl.BlockSpec(shape, index, pipeline_mode=pl.Buffered(1))


def params(mib):
    return pltpu.CompilerParams(vmem_limit_bytes=mib * MIB)


def cost(flops, moved, special=0, hint=1):
    return pl.CostEstimate(
        flops=flops * hint, bytes_accessed=moved * hint, transcendentals=special * hint
    )


def choose_kernel(place, flag, own, away, out, arrived):
    def copies(source):
        half = BLOCK // 2
        return [
            pltpu.make_async_copy(
                source.at[pl.ds(pl.multiple_of(place[i] * BLOCK + c * half, half), half)],
                out.at[pl.ds((c * 8 + i) * half, half)],
                arrived.at[c * 8 + i],
            )
            for i in range(8)
            for c in range(2)
        ]

    @pl.when(flag[0] == 1)
    def _():
        for copy in copies(own):
            copy.start()

    @pl.when(flag[0] == 0)
    def _():
        for copy in copies(away):
            copy.start()

    for copy in copies(own):
        copy.wait()


def choose(place, flag, own, away):
    scalar = pl.BlockSpec(memory_space=pltpu.SMEM)
    there = pl.BlockSpec(memory_space=pl.ANY)
    return pl.pallas_call(
        choose_kernel,
        out_shape=jax.ShapeDtypeStruct(own.shape, own.dtype),
        in_specs=[scalar, scalar, there, there],
        out_specs=there,
        scratch_shapes=[pltpu.SemaphoreType.DMA((16,))],
        compiler_params=params(4),
        cost_estimate=cost(0, 2 * own.size * 2),
    )(place, flag, own, away)


def project_kernel(
    place, mine, away, weight, gain, gq, gk, cosine, sine, normed, raw, scale, query, pair
):
    i = pl.program_id(0)

    def work(rows):
        v = rows[...].astype(wide)
        r = lax.rsqrt(jnp.mean(v * v, axis=-1, keepdims=True) + epsilon)
        n = (v * r * gain[...]).astype(low)
        normed[...] = n
        scale[...] = jnp.broadcast_to(r, scale.shape)
        raw[...] = dot(n, weight[...], (1, 0))

    pl.when(i < 2)(lambda: work(mine))
    pl.when(i >= 2)(lambda: work(away))
    for k in range(2):
        here = slice(k * BLOCK, (k + 1) * BLOCK)
        there = pl.ds(pl.multiple_of(place[2 * i + k] * BLOCK, BLOCK), BLOCK)
        c, s = cosine[there], sine[there]
        for h in range(4):
            part = slice(h * HEAD, (h + 1) * HEAD)
            v = raw[here, part]
            if h < 3:
                v = rms_norm(v, gq[...] if h < 2 else gk[...])
                v = v * c + pltpu.roll(v, HEAD // 2, 1) * s
            if h < 2:
                query[there, part] = v.astype(low)
            else:
                pair[there, (h - 2) * HEAD : (h - 1) * HEAD] = v.astype(low)


SCALARS = pl.BlockSpec(memory_space=pltpu.SMEM)
WHOLE = pl.BlockSpec(memory_space=pltpu.VMEM)


def project(place, rows, weight, gain, gq, gk, cosine, sine):
    width = rows[0].shape[1]
    fixed = lambda i, p: (0, 0)
    moving = lambda i, p: (i, 0)
    tall = 2 * BLOCK
    return pl.pallas_call(
        project_kernel,
        out_shape=[
            jax.ShapeDtypeStruct((LOCAL, width), low),
            jax.ShapeDtypeStruct((LOCAL, 4 * HEAD), wide),
            jax.ShapeDtypeStruct((LOCAL, HEAD), wide),
            jax.ShapeDtypeStruct((LOCAL, 2 * HEAD), low),
            jax.ShapeDtypeStruct((LOCAL, 2 * HEAD), low),
        ],
        grid_spec=pltpu.PrefetchScalarGridSpec(
            num_scalar_prefetch=1,
            grid=(LOCAL // tall,),
            in_specs=[
                spec((tall, width), lambda i, p: (jnp.minimum(i, 1), 0)),
                spec((tall, width), lambda i, p: (jnp.maximum(i - 2, 0), 0)),
                once((width, 4 * HEAD), fixed),
                once((1, width), fixed),
                once((1, HEAD), fixed),
                once((1, HEAD), fixed),
                once((LOCAL, HEAD), fixed),
                once((LOCAL, HEAD), fixed),
            ],
            out_specs=[
                spec((tall, width), moving),
                spec((tall, 4 * HEAD), moving),
                spec((tall, HEAD), moving),
                once((LOCAL, 2 * HEAD), fixed),
                once((LOCAL, 2 * HEAD), fixed),
            ],
        ),
        compiler_params=params(52),
        cost_estimate=cost(2 * LOCAL * width * 512, 16 * MIB, hint=H_PROJECT),
    )(place, *rows, weight, gain, gq, gk, cosine, sine)


def turn_back(d, v, c, s, g):
    d = d * c + pltpu.roll(d * s, HEAD // 2, 1)
    r = lax.rsqrt(jnp.mean(v * v, axis=-1, keepdims=True) + epsilon)
    u = v * r
    e = d * g
    before = r * (e - u * jnp.mean(u * e, axis=-1, keepdims=True))
    return before.astype(low), jnp.sum(d * u, axis=0, keepdims=True)


def query_back_kernel(place, raw, cosine, sine, gq, dquery, draw, dgain):
    total = 0.0
    for i in range(8):
        here = pl.ds(i * BLOCK, BLOCK)
        there = pl.ds(pl.multiple_of(place[i] * BLOCK, BLOCK), BLOCK)
        for h in range(2):
            part = slice(h * HEAD, (h + 1) * HEAD)
            draw[here, part], add = turn_back(
                dquery[there, part], raw[here, part], cosine[there], sine[there], gq[...]
            )
            total += add
    dgain[...] = jnp.broadcast_to(total, dgain.shape)


def pair_back_kernel(place, raw, cosine, sine, gk, dpair, later, draw, dgain):
    total = 0.0
    for i in range(8):
        here = pl.ds(i * BLOCK, BLOCK)
        there = pl.ds(pl.multiple_of(place[i] * BLOCK, BLOCK), BLOCK)
        dp = dpair[pl.ds(pl.multiple_of(place[i] * BLOCK + BACK, BLOCK), BLOCK)]
        from_later = later[pl.ds(pl.multiple_of(jnp.maximum(place[i] - 1, 0) * BLOCK, BLOCK), BLOCK)]
        dp = dp + jnp.where(place[i] > 0, from_later.astype(wide), 0.0)
        draw[here, :HEAD], add = turn_back(
            dp[:, :HEAD], raw[here, 2 * HEAD : 3 * HEAD], cosine[there], sine[there], gk[...]
        )
        draw[here, HEAD:] = dp[:, HEAD:].astype(low)
        total += add
    dgain[...] = jnp.broadcast_to(total, dgain.shape)


def heads_back(kernel, place, *inputs):
    return pl.pallas_call(
        kernel,
        out_shape=[
            jax.ShapeDtypeStruct((LOCAL, 2 * HEAD), low),
            jax.ShapeDtypeStruct((8, HEAD), wide),
        ],
        in_specs=[SCALARS] + [WHOLE] * len(inputs),
        out_specs=[WHOLE] * 2,
        compiler_params=params(16),
        cost_estimate=cost(LOCAL * 512 * 10, LOCAL * 512 * 6, hint=H_HEADS_BACK),
    )(place, *inputs)


ROWS = 256


def both_dots(lefts, rights, dims):
    return dot(lefts[0][...], rights[0][...], dims) + dot(lefts[1][...], rights[1][...], dims)


def grads_kernel(*refs):
    lefts, rights, out = refs[:4], refs[4:8], refs[8]
    n = rights[0].shape[1]
    out[:, :n] = both_dots(lefts[:2], rights[:2], (0, 0)).astype(low)
    out[:, n:] = both_dots(lefts[2:], rights[2:], (0, 0)).astype(low)


def grads(lefts, rights):
    depth, rows = lefts[0].shape
    total = rights[0].shape[1] + rights[2].shape[1]
    return pl.pallas_call(
        grads_kernel,
        out_shape=jax.ShapeDtypeStruct((rows, total), low),
        grid=(rows // ROWS,),
        in_specs=[spec((depth, ROWS), lambda i: (0, i))] * 4
        + [once(v.shape, lambda i: (0, 0)) for v in rights],
        out_specs=spec((ROWS, total), lambda i: (i, 0)),
        compiler_params=params(28),
        cost_estimate=cost(
            4 * depth * rows * total, 8 * depth * rows + 2 * total * (rows + depth), hint=H_GRADS
        ),
    )(*lefts, *rights)


def back_kernel(*refs):
    *lefts, right, out_mine, out_away = refs
    turned = right[...].T
    depth = lefts[0].shape[1]
    half = lefts[0].shape[0] // 2
    for at, out in ((half, out_away), (0, out_mine)):
        total = 0.0
        for k, left in enumerate(lefts):
            total += dot(left[pl.ds(at, half)], turned[k * depth : (k + 1) * depth], (1, 0))
        out[...] = total.astype(low)


def back_products(lefts, right, hint=1):
    rows = lefts[0].shape[0] // 2
    depth = sum(v.shape[1] for v in lefts)
    width = right.shape[0]
    return pl.pallas_call(
        back_kernel,
        out_shape=[jax.ShapeDtypeStruct((rows, width), low)] * 2,
        grid=(width // ROWS,),
        in_specs=[once(v.shape, lambda i: (0, 0)) for v in lefts]
        + [spec((ROWS, depth), lambda i: (i, 0))],
        out_specs=[spec((rows, ROWS), lambda i: (0, i))] * 2,
        compiler_params=params(20),
        cost_estimate=cost(
            4 * rows * depth * width, 2 * width * (depth + 2 * rows), hint=hint
        ),
    )(*lefts, right)


def shrink_kernel(first, second, right, out_mine, out_away):
    turned = right[...].T
    size = BLOCK // 2
    for c, left in enumerate((first, second)):
        product = dot(left[...], turned, (1, 0)).astype(low)
        for j, out in enumerate((out_mine, out_away)):
            for k in range(4):
                at = (j * 4 + k) * size
                out[pl.ds((2 * k + c) * size, size)] = product[at : at + size]


def shrink_products(lefts, right, at):
    rows, depth = lefts[0].shape
    width = right.shape[0]
    return pl.pallas_call(
        shrink_kernel,
        out_shape=[jax.ShapeDtypeStruct((rows, width), low)] * 2,
        grid=(width // ROWS,),
        in_specs=[once((rows, depth), lambda i: (0, 0))] * 2
        + [spec((ROWS, depth), lambda i: (i, at))],
        out_specs=[spec((rows, ROWS), lambda i: (0, i))] * 2,
        compiler_params=params(20),
        cost_estimate=cost(0, 0),
    )(*lefts, right)


def adam_kernel(columns, flipped, rates, extras, *refs):
    grad = refs[0]
    for k, (turn, rate) in enumerate(zip(flipped, rates)):
        weight, first, second = refs[1 + 3 * k : 4 + 3 * k]
        outs = refs[1 + extras + 3 * (len(rates) + k) : 4 + extras + 3 * (len(rates) + k)]
        g = [grad[:BLOCK, at : at + n] for at, n in columns[k]]
        g = (jnp.concatenate(g, axis=1) if len(g) > 1 else g[0]).astype(wide)
        if turn:
            g = g.T
        for out, value in zip(outs, adam(weight[...], first[...], second[...], g, rate, weight_decay)):
            out[...] = value
    for k in range(extras):
        refs[k - extras][...] = refs[1 + 3 * len(rates) + k][...]


def adam_weights(grad, columns, weights, flipped, rates, extras=()):
    states = [v for group in weights for v in group] + list(extras)
    out = pl.pallas_call(
        functools.partial(adam_kernel, columns, flipped, rates, len(extras)),
        out_shape=[jax.ShapeDtypeStruct(v.shape, v.dtype) for v in states],
        in_specs=[WHOLE] * (1 + len(states)),
        out_specs=[WHOLE] * len(states),
        compiler_params=params(24),
        cost_estimate=cost(20 * grad.size, 26 * grad.size, hint=H_ADAM),
    )(grad, *states)
    return [tuple(out[3 * k : 3 * k + 3]) for k in range(len(weights))] + list(out[3 * len(weights) :])


PART = 2 * HEAD
TALL = BLOCK + 16


def project_grad(normed, draw, weight, gain, dgain):
    project = dot(normed[...], draw[...], (0, 0))
    product = (project * weight[...].astype(wide)).astype(low)
    dgain[...] = dot(jnp.ones((8, PART), low), product, (1, 1)) / gain[...]
    return project.astype(low)


def query_grads_kernel(
    spot, normed, draw, weight, gain, first, second, att_first, att_second, out, dgain
):
    attended = (att_first, att_second)
    project = project_grad(normed, draw, weight, gain, dgain)
    output = both_dots((first, second), attended, (0, 0)).astype(low)
    for j in range(2):
        rows = slice(j * BLOCK, (j + 1) * BLOCK)
        out[0, j ^ spot[0], 0, :, :PART] = project[rows]
        out[0, j ^ spot[0], 0, :, PART:] = output[rows]


def pair_grads_kernel(spot, normed, draw, weight, gain, out, dgain):
    project = project_grad(normed, draw, weight, gain, dgain)
    for j in range(2):
        out[0, j ^ spot[0], 0, :BLOCK] = project[j * BLOCK : (j + 1) * BLOCK]


def first_grads(spot, normed, draw, weight, gain, part, out, block, others=()):
    whole = lambda i, s: (0, 0)
    columns = lambda i, s: (0, i)
    rows = 2 * BLOCK
    return pl.pallas_call(
        query_grads_kernel if others else pair_grads_kernel,
        out_shape=[
            jax.ShapeDtypeStruct(out, low),
            jax.ShapeDtypeStruct((8, 16 * BLOCK), wide),
        ],
        grid_spec=pltpu.PrefetchScalarGridSpec(
            num_scalar_prefetch=1,
            grid=(8,),
            in_specs=[
                spec((LOCAL, rows), columns),
                once((LOCAL, PART), whole),
                spec((rows, PART), lambda i, s: (i, part)),
                spec((1, rows), columns),
            ]
            + [spec((LOCAL // 2, rows), columns)] * len(others[:2])
            + [once((LOCAL // 2, PART), whole)] * len(others[2:]),
            out_specs=[spec(*block), spec((8, rows), columns)],
        ),
        compiler_params=params(24),
        cost_estimate=cost(2 * LOCAL * 2048 * 256, 8 * MIB, hint=H_FIRST),
    )(spot, normed, draw, weight, gain, *others)


def leaving(rows, columns):
    place = lambda i, s: (lax.rem(i // 2 - s[2] + 4, 4), 0, i % 2 ^ s[1], 0, 0)
    return (4, 2, 2, rows, columns), ((1, 2, 1, rows, columns), place)


def query_grads(spot, normed, draw, weight, gain, dmiddle, attended):
    others = (*dmiddle, *attended)
    return first_grads(spot, normed, draw, weight, gain, 0, *leaving(BLOCK, 2 * PART), others)


def pair_grads(spot, normed, draw, weight, gain):
    return first_grads(spot, normed, draw, weight, gain, 1, *leaving(TALL, PART))


SCALE = HEAD ** (-0.5)


def allowed(query_ids, key_ids, start):
    keys = key_ids[:, pl.ds(start, WINDOW)]
    row = lax.broadcasted_iota(jnp.int32, (QUERIES, WINDOW), 0)
    column = lax.broadcasted_iota(jnp.int32, (QUERIES, WINDOW), 1)
    return (query_ids[...] == keys) & (column <= row + BACK)


def attend_kernel(turn, core, query, pair, query_ids, key_ids, out, logsum):
    i = pl.program_id(0)
    start = pl.multiple_of(i * QUERIES, QUERIES)
    mask = allowed(query_ids, key_ids, start)
    logs = []
    for h in range(2):
        part = slice(h * HEAD, (h + 1) * HEAD)
        scores = dot(query[:, part], pair[pl.ds(start, WINDOW), :HEAD], (1, 1)) * SCALE
        scores = jnp.where(mask, scores, -1e30)
        top = jnp.max(scores, axis=-1, keepdims=True)
        unnormed = jnp.exp(scores - top)
        total = jnp.sum(unnormed, axis=-1, keepdims=True)
        probs = (unnormed * (1.0 / total)).astype(low)
        result = dot(probs, pair[pl.ds(start, WINDOW), HEAD:], (1, 0)).astype(low)
        for j in range(2):
            out[j ^ core[0], 0, :, part] = result[j * BLOCK : (j + 1) * BLOCK]
        logs.append(top + jnp.log(total))
    lane = lax.broadcasted_iota(jnp.int32, (QUERIES, HEAD), 1)
    logsum[...] = jnp.where(lane < HEAD // 2, logs[0], logs[1])


def attend(turn, core, query, pair, query_ids, key_ids):
    rows = lambda i, t, c: (i, 0)
    whole = lambda i, t, c: (0, 0)
    keys = BACK + LOCAL
    return pl.pallas_call(
        attend_kernel,
        out_shape=[
            jax.ShapeDtypeStruct((2, 4, BLOCK, 2 * HEAD), low),
            jax.ShapeDtypeStruct((LOCAL, HEAD), wide),
        ],
        grid_spec=pltpu.PrefetchScalarGridSpec(
            num_scalar_prefetch=2,
            grid=(LOCAL // QUERIES,),
            in_specs=[
                spec((QUERIES, 2 * HEAD), rows),
                once((keys, 2 * HEAD), whole),
                spec((QUERIES, 1), rows),
                spec((1, keys), whole),
            ],
            out_specs=[
                spec((2, 1, BLOCK, 2 * HEAD), lambda i, t, c: (0, t[i], 0, 0)),
                spec((QUERIES, HEAD), rows),
            ],
        ),
        compiler_params=params(24),
        cost_estimate=cost(
            8 * LOCAL * WINDOW * HEAD, 4 * LOCAL * 512, 2 * LOCAL * WINDOW, hint=H_ATTEND
        ),
    )(turn, core, query, pair, query_ids, key_ids)


def attend_back_kernel(
    turn, core, query, pair, query_ids, key_ids, grad, logsum, dquery, dpair
):
    i = pl.program_id(0)

    @pl.when(i == 0)
    def _():
        dpair[...] = jnp.zeros_like(dpair)

    start = pl.multiple_of(i * QUERIES, QUERIES)
    window = pl.ds(start, WINDOW)
    mask = allowed(query_ids, key_ids, start)
    dkey, dvalue = None, None
    for h in range(2):
        part = slice(h * HEAD, (h + 1) * HEAD)
        q = query[:, part]
        g = jnp.concatenate([grad[j ^ core[0], 0, :, part] for j in range(2)], axis=0)
        scores = dot(q, pair[window, :HEAD], (1, 1)) * SCALE
        probs = jnp.where(mask, jnp.exp(scores - logsum[:, h * 64 : h * 64 + 1]), 0.0)
        dprobs = dot(g, pair[window, HEAD:], (1, 1))
        inner = jnp.sum(probs * dprobs, axis=-1, keepdims=True)
        dscores = (probs * (dprobs - inner)).astype(low)
        dquery[:, part] = dot(dscores, pair[window, :HEAD], (1, 0)) * SCALE
        dv = dot(probs.astype(low), g, (0, 0))
        dk = dot(dscores, q, (0, 0))
        dkey = dk if dkey is None else dkey + dk
        dvalue = dv if dvalue is None else dvalue + dv
    dpair[window, :HEAD] += dkey * SCALE
    dpair[window, HEAD:] += dvalue


def attend_back(turn, core, query, pair, query_ids, key_ids, grad, logsum):
    rows = lambda i, t, c: (i, 0)
    whole = lambda i, t, c: (0, 0)
    keys = BACK + LOCAL
    return pl.pallas_call(
        attend_back_kernel,
        out_shape=[
            jax.ShapeDtypeStruct((LOCAL, 2 * HEAD), wide),
            jax.ShapeDtypeStruct((keys, 2 * HEAD), wide),
        ],
        grid_spec=pltpu.PrefetchScalarGridSpec(
            num_scalar_prefetch=2,
            grid=(LOCAL // QUERIES,),
            in_specs=[
                spec((QUERIES, 2 * HEAD), rows),
                once((keys, 2 * HEAD), whole),
                spec((QUERIES, 1), rows),
                spec((1, keys), whole),
                spec((2, 1, BLOCK, 2 * HEAD), lambda i, t, c: (0, t[i], 0, 0)),
                spec((QUERIES, HEAD), rows),
            ],
            out_specs=[spec((QUERIES, 2 * HEAD), rows), once((keys, 2 * HEAD), whole)],
        ),
        compiler_params=params(28),
        cost_estimate=cost(
            20 * LOCAL * WINDOW * HEAD, 8 * LOCAL * 512, 2 * LOCAL * WINDOW, hint=H_ATTEND_BACK
        ),
    )(turn, core, query, pair, query_ids, key_ids, grad, logsum)


def per_device(
    inputs,
    cotangent,
    document_index,
    positions,
    gains,
    gains_first,
    gains_second,
    project_weight,
    project_first,
    project_second,
    output_weight,
    output_first,
    output_second,
    expand_weight,
    expand_first,
    expand_second,
    shrink_weight,
    shrink_first,
    shrink_second,
):
    core, x = lax.axis_index("core"), lax.axis_index("x")
    half, yl = lax.axis_index("yh"), lax.axis_index("yl")
    width = inputs.shape[-1]
    qkv = project_weight.shape[1]
    ff = shrink_weight.shape[0]
    at_home = core == yl
    steps = jnp.arange(8, dtype=jnp.int32)
    place = lax.rem(x - steps % 4 + 4, 4) * 2 + (core ^ (steps // 4))
    turn = lax.rem(x - jnp.arange(4, dtype=jnp.int32) + 4, 4)
    core_of = core.reshape(1).astype(jnp.int32)
    flag = at_home.astype(jnp.int32).reshape(1)

    marks = jnp.stack([document_index[0], positions[0] // 32, positions[0] % 32])
    marks = jnp.pad(marks.astype(low), ((0, 13), (0, 0)))
    message = trade(jnp.concatenate([inputs[0], marks], axis=0))
    rows = message[:BLOCK]
    marks = message[BLOCK:].astype(jnp.int32)
    ids, places = marks[0], marks[1] * 32 + marks[2]

    gain_block = jnp.pad(gains.astype(low), (0, BLOCK * BLOCK - gains.shape[0])).reshape(BLOCK, BLOCK)
    first_shard = jnp.concatenate(
        [project_weight.astype(low), output_weight.astype(low).T, gain_block], axis=1
    )
    second_shard = jnp.concatenate([expand_weight.astype(low), shrink_weight.astype(low).T], axis=1)
    first_all = lax.all_gather(to_group(first_shard), GROUP, axis=0, tiled=True)
    rows_all = gather_rows(rows)
    second_shard = to_group(after(second_shard, message))
    second_all = lax.all_gather(after(second_shard, first_all), GROUP, axis=0, tiled=True)
    project_all = first_all[:, :qkv]
    output_all = first_all[:, qkv : qkv + 2 * HEAD]
    expand_all = second_all[:, : 2 * ff]
    shrink_all = second_all[:, 2 * ff :]
    gain_all = first_all.reshape(16, BLOCK, -1)[:, :3, qkv + 2 * HEAD :].reshape(16, 3 * BLOCK)
    gain_all = gain_all[:, : gains.shape[0]].reshape(-1).astype(wide)
    gain_one = gain_all[:width]
    gain_two = gain_all[width : 2 * width]
    gain_query = gain_all[2 * width : 2 * width + HEAD].reshape(1, HEAD)
    gain_key = gain_all[2 * width + HEAD :].reshape(1, HEAD)

    ids_here = lax.dynamic_slice_in_dim(ids, half * LOCAL, LOCAL)
    places_here = lax.dynamic_slice_in_dim(places, half * LOCAL, LOCAL)
    ids_keys = jnp.where(
        half == 0,
        jnp.concatenate([jnp.full((BACK,), -1, jnp.int32), ids[:LOCAL]]),
        ids[LOCAL - BACK :],
    )
    query_ids, key_ids = ids_here.reshape(-1, 1), ids_keys.reshape(1, -1)
    frequency = jnp.exp(jnp.arange(HEAD // 2, dtype=wide) * (-2.0 * math.log(theta) / HEAD))
    angle = places_here.astype(wide)[:, None] * frequency
    cosine, sine = jnp.cos(angle), jnp.sin(angle)
    cosine = jnp.concatenate([cosine, cosine], axis=1)
    sine = jnp.concatenate([-sine, sine], axis=1)

    values = rows.astype(wide)
    normed, raw, scale, query, pair = project(
        place, rows_all, first_all, gain_one.reshape(1, -1), gain_query, gain_key, cosine, sine
    )
    earlier = move(pair[LOCAL - BACK :], "yh", [(0, 1)])
    back_all = choose(place, flag, cotangent[0], other_core(cotangent[0]))
    pair_all = jnp.concatenate([after(earlier, back_all), pair], axis=0)
    attended, logsum = attend(turn, core_of, query, pair_all, query_ids, key_ids)
    attended = attended.reshape(LOCAL, 2 * HEAD)
    mine = dot(attended[: LOCAL // 2], output_all, (1, 1)).astype(low)
    away = dot(attended[LOCAL // 2 :], output_all, (1, 1)).astype(low)
    attended = chunks(attended)
    back_rows = [back_all[: LOCAL // 2], back_all[LOCAL // 2 :]]
    small = BLOCK // 2
    middle = values + chip_sum(core_sum(mine, away))
    middle = [middle[:small], middle[small:]]
    normed_two, hidden, dexpanded, both_two = [], [], [], []

    dmiddle, dmiddle_all, drows_two, dgain_two = [], [], [], 0.0
    for c in range(2):
        if c == 0:
            rows_two = rms_norm(middle[0], gain_two).astype(low)
            normed_two.append(jnp.concatenate(gather_rows(rows_two), axis=0))
        source = normed_two[c] if c == 0 else after(normed_two[c], *both_two)
        expanded = dot(source, expand_all, (1, 0))
        activated, pull_act = jax.vjp(swiglu, expanded[:, :ff], expanded[:, ff:])
        hidden.append(activated.astype(low))
        dgate, dup = pull_act(dot(back_rows[c], shrink_all, (1, 0)))
        dexpanded.append(jnp.concatenate([dgate, dup], axis=1).astype(low))
        if c == 0:
            rows_two = rms_norm(middle[1], gain_two).astype(low)
            gathered = gather_rows(rows_two, dexpanded[0])
            normed_two.append(jnp.concatenate(gathered, axis=0))
        both_two.append(
            core_sum(*back_products([after(dexpanded[c], gathered[0], *drows_two)], second_all))
        )
        if c == 1:
            second_grads = grads(
                [*after(tuple(normed_two), both_two[1]), *back_rows], [*dexpanded, *hidden]
            )
        drows_two.append(chip_sum(both_two[c]) if c == 0 else chip_sum_at_once(both_two[c], x))
        if c == 1:
            drows_two[1] = after(drows_two[1], second_grads, dmiddle_all[0])
        _, pull_two = jax.vjp(rms_norm, middle[c], gain_two)
        drows, dgain = pull_two(drows_two[c])
        dgain_two = dgain_two + dgain
        dmiddle.append(back_rows[c][:small].astype(wide) + drows)
        dmiddle_all.append(jnp.concatenate(gather_rows(dmiddle[c].astype(low)), axis=0))
    second_red = lax.psum_scatter(second_grads, GROUP, scatter_dimension=0, tiled=True)
    shrunk = core_sum(*shrink_products(after(tuple(hidden), drows_two[1]), second_all, 2))
    dmiddle = jnp.concatenate(dmiddle, axis=0)
    middle = jnp.concatenate(middle, axis=0)
    dmiddle_all = after(tuple(dmiddle_all), shrunk)
    dattended = jnp.stack(
        [dot(v, output_all, (1, 0)).astype(low).reshape(8, small, -1) for v in dmiddle_all], axis=1
    )
    mlp = chip_sum_at_once(after(shrunk, dmiddle_all), x)
    dquery, dpair = attend_back(
        turn,
        core_of,
        query,
        pair_all,
        query_ids,
        key_ids,
        dattended.reshape(2, 4, BLOCK, 2 * HEAD),
        logsum,
    )
    later = move(dpair[:BACK].astype(low), "yh", [(1, 0)])
    draw_query, dgain_query = heads_back(
        query_back_kernel, place, raw, cosine, sine, gain_query, dquery
    )
    spot = jnp.stack([half, yl, lax.axis_index("z")]).astype(jnp.int32)
    gain_row = gain_one.reshape(1, -1)
    left, dgain_one = query_grads(
        spot, normed, draw_query, first_all, gain_row, dmiddle_all, attended
    )
    left_grads = left
    left = sum_z(left)
    later = after(later, mlp, left_grads)
    draw_pair, dgain_key = heads_back(
        pair_back_kernel, place, raw, cosine, sine, gain_key, dpair, later
    )
    outputs = trade((middle + after(mlp, draw_pair)).astype(low))

    pair_right, dgain_rest = pair_grads(spot, normed, draw_pair, first_all, gain_row)
    dgains = jnp.concatenate([(dgain_one + dgain_rest)[0], dgain_two, dgain_query[0], dgain_key[0]])
    dgains = jnp.pad(dgains.reshape(-1, BLOCK), ((0, 6), (0, 0)))
    dgains = dgains + other_core(dgains)
    dgains = dgains + shift(dgains, 1) + shift(dgains, 2) + shift(dgains, 3)
    dgains = dgains[:-6].astype(low).reshape(4, 2, 2, 1, -1)
    dgains = jnp.where(half == 0, dgains, dgains[:, :, ::-1])
    dgains = jnp.where(yl == 0, dgains, dgains[:, ::-1]).transpose(0, 2, 1, 3, 4)
    dgains = jnp.roll(dgains, -lax.axis_index("z"), axis=0)
    over = dgains[..., PART:]
    dgains = jnp.concatenate([dgains[..., :PART], jnp.pad(over, ((0, 0),) * 4 + ((0, PART - over.shape[-1]),))], axis=3)
    dgains = jnp.pad(dgains, ((0, 0), (0, 0), (0, 0), (0, 14), (0, 0)))
    right = lax.dynamic_update_slice(pair_right, dgains, (0, 0, 0, BLOCK, 0))
    both_one = core_sum(
        *back_products(after((draw_query, draw_pair), dgain_rest), first_all, hint=H_BACK)
    )
    right = sum_z(right)
    drows_one = chip_sum_at_once(both_one, x)
    second_red = to_owner(second_red)
    expand_new, shrink_new = adam_weights(
        second_red,
        (((0, 2 * ff),), ((2 * ff, ff),)),
        [(expand_weight, expand_first, expand_second), (shrink_weight, shrink_first, shrink_second)],
        (False, True),
        (0.05, 0.03),
    )
    both = jnp.concatenate([jnp.pad(left, ((0, 0), (0, 0), (0, 16), (0, 0))), right], axis=3)
    first_red = sum_flips(after(both.astype(low), second_red))

    _, pull_one = jax.vjp(rms_norm, values, gain_one)
    dvalues, _ = pull_one(drows_one)
    input_grad = trade(after((dmiddle + dvalues).astype(low), outputs))

    dgains = first_red[BLOCK : BLOCK + 8, 2 * PART :]
    project_new, output_new, outputs, input_grad = adam_weights(
        first_red,
        (((0, PART), (2 * PART, PART)), ((PART, PART),)),
        [(project_weight, project_first, project_second), (output_weight, output_first, output_second)],
        (False, True),
        (0.05, 0.4),
        (outputs, input_grad),
    )
    dgains = dgains[:2].reshape(-1)[: gains.shape[0]]
    return (
        outputs[None],
        input_grad[None],
        *adam(gains, gains_first, gains_second, dgains, 0.5, 0.0),
        *project_new,
        *output_new,
        *expand_new,
        *shrink_new,
    )


def solution(mesh):
    fine = Mesh(mesh.devices.reshape(4, 2, 2, 4, 2), ("z", "core", "yh", "x", "yl"))
    tokens = P(("z", "core"), ("yh", "x", "yl"), None)
    marks = P(("z", "core"), None)
    gain = P(("z", "core", "yh"))
    tall = P(("z", "core", "yh"), ("x", "yl"))
    flat = P(("x", "yl"), ("z", "core", "yh"))
    in_specs = (
        tokens,
        P(("z", "core"), "yh", None),
        marks,
        marks,
        *[gain] * 3,
        *[tall] * 3,
        *[flat] * 3,
        *[tall] * 3,
        *[flat] * 3,
    )
    out_specs = (
        tokens,
        tokens,
        *[gain] * 3,
        *[tall] * 3,
        *[flat] * 3,
        *[tall] * 3,
        *[flat] * 3,
    )
    return jax.shard_map(
        per_device, mesh=fine, in_specs=in_specs, out_specs=out_specs, check_vma=False
    )
```

```python
import functools
import math

import jax
import jax.numpy as jnp
from jax import lax
from jax.experimental import pallas as pl
from jax.experimental.pallas import tpu as pltpu
from jax.sharding import Mesh
from jax.sharding import PartitionSpec as P

QUERY_HEADS = 16
KEY_VALUE_HEADS = 8
HEAD = 128
STEP = 5
LONGEST = 800
BLOCK = 128
LOCAL = 1024
BACK = 896
QUERIES = 256
WINDOW = BACK + QUERIES

epsilon = 1e-06
theta = 1000000.0
beta_first = 0.9
beta_second = 0.95
adam_epsilon = 1e-08
weight_decay = 0.1

low = jnp.bfloat16
wide = jnp.float32
MIB = 1024 * 1024
H_PROJECT = 1
H_ATTEND = 150
H_GRADS = 1
H_ATTEND_BACK = 30
H_HEADS_BACK = 1
H_BACK = 1
H_FIRST = 1
H_ADAM = 1

epsilon = 1e-06
theta = 1000000.0
beta_first = 0.9
beta_second = 0.95
adam_epsilon = 1e-08
weight_decay = 0.1

low = jnp.bfloat16
wide = jnp.float32
MIB = 1024 * 1024
ATTEND_HINT = 300
ATTEND_BACK_HINT = 260


def rms_norm(values, gain):
    return values * lax.rsqrt(jnp.mean(values * values, axis=-1, keepdims=True) + epsilon) * gain


def swiglu(gate, upward):
    return jax.nn.silu(gate) * upward


def adam(weight, first, second, grad, rate, decay_rate):
    mean = beta_first * first + (1.0 - beta_first) * grad
    square = beta_second * second + (1.0 - beta_second) * grad * grad
    mean_hat = mean / (1.0 - beta_first**STEP)
    square_hat = square / (1.0 - beta_second**STEP)
    updated = weight - rate * (
        mean_hat / (jnp.sqrt(square_hat) + adam_epsilon) + decay_rate * weight
    )
    return (mean, square, updated)


def dot(left, right, dims):
    return lax.dot_general(left, right, ((dims[:1], dims[1:]), ((), ())), preferred_element_type=wide)


def move(values, axis, pairs):
    return lax.ppermute(values, axis, pairs)


def shift(values, steps):
    return move(values, "x", [(i, (i + steps) % 4) for i in range(4)])


def other_core(values):
    return move(values, "core", [(0, 1), (1, 0)])


def trade(values):
    return move(values, ("core", "yl"), [(a * 2 + b, b * 2 + a) for a in range(2) for b in range(2)])


def to_group(values):
    pairs = [
        ((a * 2 + b) * 2 + d, (d * 2 + a) * 2 + b)
        for a in range(2)
        for b in range(2)
        for d in range(2)
    ]
    return move(values, ("core", "yh", "yl"), pairs)


def to_owner(values):
    pairs = [
        ((d * 2 + a) * 2 + b, (a * 2 + b) * 2 + d)
        for a in range(2)
        for b in range(2)
        for d in range(2)
    ]
    return move(values, ("core", "yh", "yl"), pairs)


def gather_rows(values, *others):
    pieces = (values, shift(values, 1), shift(values, 2), shift(values, 3))
    mine = jnp.concatenate(after(pieces, *others) if others else pieces, axis=0)
    return mine, other_core(mine)


def core_sum(mine, away):
    return (mine.astype(wide) + other_core(away).astype(wide)).astype(low)


def chip_sum(both):
    pieces = both.reshape(4, BLOCK, -1)
    total = pieces[0].astype(wide)
    for k in (2, 1, 3):
        total = total + shift(pieces[k], 4 - k).astype(wide)
    return total


def chip_blocks(mine, away, x):
    mine, away = mine.reshape(4, BLOCK, -1), away.reshape(4, BLOCK, -1)
    pick = lambda v, i: lax.dynamic_index_in_dim(v, lax.rem(x - i + 4, 4), 0).astype(wide)
    return jnp.concatenate([(pick(mine, i) + pick(away, i)).astype(low) for i in range(4)], axis=0)


def chip_sum_at_once(blocks):
    return jnp.sum(lax.all_to_all(blocks, "x", 0, 0, tiled=True).astype(wide), axis=0)


def after(values, *others):
    return lax.optimization_barrier((values, *others))[0]


def sum_z(pieces):
    total = pieces[0].astype(wide)
    for k in (2, 1, 3):
        there = move(pieces[k], "z", [(i, (i + k) % 4) for i in range(4)])
        total = total + there.astype(wide)
    return total


def flip(values, a, b):
    pairs = [
        ((c * 2 + h) * 2 + d, ((d ^ b) * 2 + (h ^ a)) * 2 + c)
        for c in range(2)
        for h in range(2)
        for d in range(2)
    ]
    return move(values, ("core", "yh", "yl"), pairs)


def sum_flips(pieces):
    total = 0.0
    for a in (1, 0):
        for b in (1, 0):
            total = total + flip(pieces[a, b], a, b).astype(wide)
    return total


GROUP = ("z", "yh", "yl")


def spec(shape, index):
    return pl.BlockSpec(shape, index)


def once(shape, index):
    return pl.BlockSpec(shape, index, pipeline_mode=pl.Buffered(1))


def params(mib):
    return pltpu.CompilerParams(vmem_limit_bytes=mib * MIB)


def cost(flops, moved, special=0, hint=1):
    return pl.CostEstimate(
        flops=flops * hint, bytes_accessed=moved * hint, transcendentals=special * hint
    )


def choose_kernel(place, flag, own, away, out, arrived):
    def copies(source):
        return [
            pltpu.make_async_copy(
                source.at[pl.ds(pl.multiple_of(place[i] * BLOCK, BLOCK), BLOCK)],
                out.at[pl.ds(i * BLOCK, BLOCK)],
                arrived.at[i],
            )
            for i in range(8)
        ]

    @pl.when(flag[0] == 1)
    def _():
        for copy in copies(own):
            copy.start()

    @pl.when(flag[0] == 0)
    def _():
        for copy in copies(away):
            copy.start()

    for copy in copies(own):
        copy.wait()


def choose(place, flag, own, away):
    scalar = pl.BlockSpec(memory_space=pltpu.SMEM)
    there = pl.BlockSpec(memory_space=pl.ANY)
    return pl.pallas_call(
        choose_kernel,
        out_shape=jax.ShapeDtypeStruct(own.shape, own.dtype),
        in_specs=[scalar, scalar, there, there],
        out_specs=there,
        scratch_shapes=[pltpu.SemaphoreType.DMA((8,))],
        compiler_params=params(4),
        cost_estimate=cost(0, 2 * own.size * 2),
    )(place, flag, own, away)


def project_kernel(
    place, mine, away, weight, gain, gq, gk, cosine, sine, normed, raw, scale, query, pair
):
    i = pl.program_id(0)

    def work(rows):
        v = rows[...].astype(wide)
        r = lax.rsqrt(jnp.mean(v * v, axis=-1, keepdims=True) + epsilon)
        n = (v * r * gain[...]).astype(low)
        normed[...] = n
        scale[...] = jnp.broadcast_to(r, scale.shape)
        raw[...] = dot(n, weight[...], (1, 0))

    pl.when(i < 2)(lambda: work(mine))
    pl.when(i >= 2)(lambda: work(away))
    for k in range(2):
        here = slice(k * BLOCK, (k + 1) * BLOCK)
        there = pl.ds(pl.multiple_of(place[2 * i + k] * BLOCK, BLOCK), BLOCK)
        c, s = cosine[there], sine[there]
        for h in range(4):
            part = slice(h * HEAD, (h + 1) * HEAD)
            v = raw[here, part]
            if h < 3:
                v = rms_norm(v, gq[...] if h < 2 else gk[...])
                v = v * c + pltpu.roll(v, HEAD // 2, 1) * s
            if h < 2:
                query[there, part] = v.astype(low)
            else:
                pair[there, (h - 2) * HEAD : (h - 1) * HEAD] = v.astype(low)


SCALARS = pl.BlockSpec(memory_space=pltpu.SMEM)
WHOLE = pl.BlockSpec(memory_space=pltpu.VMEM)


def project(place, rows, weight, gain, gq, gk, cosine, sine):
    width = rows[0].shape[1]
    fixed = lambda i, p: (0, 0)
    moving = lambda i, p: (i, 0)
    tall = 2 * BLOCK
    return pl.pallas_call(
        project_kernel,
        out_shape=[
            jax.ShapeDtypeStruct((LOCAL, width), low),
            jax.ShapeDtypeStruct((LOCAL, 4 * HEAD), wide),
            jax.ShapeDtypeStruct((LOCAL, HEAD), wide),
            jax.ShapeDtypeStruct((LOCAL, 2 * HEAD), low),
            jax.ShapeDtypeStruct((LOCAL, 2 * HEAD), low),
        ],
        grid_spec=pltpu.PrefetchScalarGridSpec(
            num_scalar_prefetch=1,
            grid=(LOCAL // tall,),
            in_specs=[
                spec((tall, width), lambda i, p: (jnp.minimum(i, 1), 0)),
                spec((tall, width), lambda i, p: (jnp.maximum(i - 2, 0), 0)),
                once((width, 4 * HEAD), fixed),
                once((1, width), fixed),
                once((1, HEAD), fixed),
                once((1, HEAD), fixed),
                once((LOCAL, HEAD), fixed),
                once((LOCAL, HEAD), fixed),
            ],
            out_specs=[
                spec((tall, width), moving),
                spec((tall, 4 * HEAD), moving),
                spec((tall, HEAD), moving),
                once((LOCAL, 2 * HEAD), fixed),
                once((LOCAL, 2 * HEAD), fixed),
            ],
        ),
        compiler_params=params(52),
        cost_estimate=cost(2 * LOCAL * width * 512, 16 * MIB, hint=H_PROJECT),
    )(place, *rows, weight, gain, gq, gk, cosine, sine)


def turn_back(d, v, c, s, g):
    d = d * c + pltpu.roll(d * s, HEAD // 2, 1)
    r = lax.rsqrt(jnp.mean(v * v, axis=-1, keepdims=True) + epsilon)
    u = v * r
    e = d * g
    before = r * (e - u * jnp.mean(u * e, axis=-1, keepdims=True))
    return before.astype(low), jnp.sum(d * u, axis=0, keepdims=True)


def query_back_kernel(place, raw, cosine, sine, gq, dquery, draw, dgain):
    total = 0.0
    for i in range(8):
        here = pl.ds(i * BLOCK, BLOCK)
        there = pl.ds(pl.multiple_of(place[i] * BLOCK, BLOCK), BLOCK)
        for h in range(2):
            part = slice(h * HEAD, (h + 1) * HEAD)
            draw[here, part], add = turn_back(
                dquery[there, part], raw[here, part], cosine[there], sine[there], gq[...]
            )
            total += add
    dgain[...] = jnp.broadcast_to(total, dgain.shape)


def pair_back_kernel(place, raw, cosine, sine, gk, dpair, later, draw, dgain):
    total = 0.0
    for i in range(8):
        here = pl.ds(i * BLOCK, BLOCK)
        there = pl.ds(pl.multiple_of(place[i] * BLOCK, BLOCK), BLOCK)
        dp = dpair[pl.ds(pl.multiple_of(place[i] * BLOCK + BACK, BLOCK), BLOCK)]
        from_later = later[pl.ds(pl.multiple_of(jnp.maximum(place[i] - 1, 0) * BLOCK, BLOCK), BLOCK)]
        dp = dp + jnp.where(place[i] > 0, from_later.astype(wide), 0.0)
        draw[here, :HEAD], add = turn_back(
            dp[:, :HEAD], raw[here, 2 * HEAD : 3 * HEAD], cosine[there], sine[there], gk[...]
        )
        draw[here, HEAD:] = dp[:, HEAD:].astype(low)
        total += add
    dgain[...] = jnp.broadcast_to(total, dgain.shape)


def heads_back(kernel, place, *inputs):
    return pl.pallas_call(
        kernel,
        out_shape=[
            jax.ShapeDtypeStruct((LOCAL, 2 * HEAD), low),
            jax.ShapeDtypeStruct((8, HEAD), wide),
        ],
        in_specs=[SCALARS] + [WHOLE] * len(inputs),
        out_specs=[WHOLE] * 2,
        compiler_params=params(16),
        cost_estimate=cost(LOCAL * 512 * 10, LOCAL * 512 * 6, hint=H_HEADS_BACK),
    )(place, *inputs)


ROWS = 256


def both_dots(lefts, rights, dims):
    return dot(lefts[0][...], rights[0][...], dims) + dot(lefts[1][...], rights[1][...], dims)


def grads_kernel(*refs):
    lefts, rights, out = refs[:4], refs[4:8], refs[8]
    n = rights[0].shape[1]
    out[:, :n] = both_dots(lefts[:2], rights[:2], (0, 0)).astype(low)
    out[:, n:] = both_dots(lefts[2:], rights[2:], (0, 0)).astype(low)


def grads(lefts, rights):
    depth, rows = lefts[0].shape
    total = rights[0].shape[1] + rights[2].shape[1]
    return pl.pallas_call(
        grads_kernel,
        out_shape=jax.ShapeDtypeStruct((rows, total), low),
        grid=(rows // ROWS,),
        in_specs=[spec((depth, ROWS), lambda i: (0, i))] * 4
        + [once(v.shape, lambda i: (0, 0)) for v in rights],
        out_specs=spec((ROWS, total), lambda i: (i, 0)),
        compiler_params=params(28),
        cost_estimate=cost(
            4 * depth * rows * total, 8 * depth * rows + 2 * total * (rows + depth), hint=H_GRADS
        ),
    )(*lefts, *rights)


def back_kernel(parts, *refs):
    *lefts, right, out_mine, out_away = refs
    turned = right[...].T
    half = LOCAL // 2
    if parts:
        depth = lefts[0].shape[1]
        pick = lambda rows: sum(
            dot(left[rows], turned[k * depth : (k + 1) * depth], (1, 0))
            for k, left in enumerate(lefts)
        )
        mine, away = pick(pl.ds(0, half)), pick(pl.ds(half, half))
    else:
        mine, away = [dot(left[...], turned, (1, 0)) for left in lefts]
    out_away[...] = away.astype(low)
    out_mine[...] = mine.astype(low)


def back_products(lefts, right, at=0, parts=False, hint=1):
    rows = LOCAL // 2
    depth = sum(v.shape[1] for v in lefts) if parts else lefts[0].shape[1]
    width = right.shape[0]
    return pl.pallas_call(
        functools.partial(back_kernel, parts),
        out_shape=[jax.ShapeDtypeStruct((rows, width), low)] * 2,
        grid=(width // ROWS,),
        in_specs=[once(v.shape, lambda i: (0, 0)) for v in lefts]
        + [spec((ROWS, depth), lambda i: (i, at))],
        out_specs=[spec((rows, ROWS), lambda i: (0, i))] * 2,
        compiler_params=params(20),
        cost_estimate=cost(
            4 * rows * depth * width, 2 * width * (depth + 2 * rows), hint=hint
        ),
    )(*lefts, right)


def adam_kernel(columns, flipped, rates, extras, *refs):
    grad = refs[0]
    for k, (turn, rate) in enumerate(zip(flipped, rates)):
        weight, first, second = refs[1 + 3 * k : 4 + 3 * k]
        outs = refs[1 + extras + 3 * (len(rates) + k) : 4 + extras + 3 * (len(rates) + k)]
        g = [grad[:BLOCK, at : at + n] for at, n in columns[k]]
        g = (jnp.concatenate(g, axis=1) if len(g) > 1 else g[0]).astype(wide)
        if turn:
            g = g.T
        for out, value in zip(outs, adam(weight[...], first[...], second[...], g, rate, weight_decay)):
            out[...] = value
    for k in range(extras):
        refs[k - extras][...] = refs[1 + 3 * len(rates) + k][...]


def adam_weights(grad, columns, weights, flipped, rates, extras=()):
    states = [v for group in weights for v in group] + list(extras)
    out = pl.pallas_call(
        functools.partial(adam_kernel, columns, flipped, rates, len(extras)),
        out_shape=[jax.ShapeDtypeStruct(v.shape, v.dtype) for v in states],
        in_specs=[WHOLE] * (1 + len(states)),
        out_specs=[WHOLE] * len(states),
        compiler_params=params(24),
        cost_estimate=cost(20 * grad.size, 26 * grad.size, hint=H_ADAM),
    )(grad, *states)
    return [tuple(out[3 * k : 3 * k + 3]) for k in range(len(weights))] + list(out[3 * len(weights) :])


PART = 2 * HEAD
TALL = BLOCK + 16


def project_grad(normed, draw, weight, gain, dgain):
    project = dot(normed[...], draw[...], (0, 0))
    product = (project * weight[...].astype(wide)).astype(low)
    dgain[...] = dot(jnp.ones((8, PART), low), product, (1, 1)) / gain[...]
    return project.astype(low)


def query_grads_kernel(spot, normed, draw, weight, gain, mine, away, attended, *outs):
    *outs, dgain = outs
    project = project_grad(normed, draw, weight, gain, dgain)
    half = LOCAL // 2
    output = dot(mine[...], attended[:half], (0, 0)) + dot(away[...], attended[half:], (0, 0))
    output = output.astype(low)
    i = pl.program_id(0)
    steps = lax.rem(i // 2 - spot[2] + 4, 4)
    for k, out in enumerate(outs):

        @pl.when(steps == k)
        def _():
            for j in range(2):
                rows = slice(j * BLOCK, (j + 1) * BLOCK)
                out[j ^ spot[0], i % 2 ^ spot[1], :, :PART] = project[rows]
                out[j ^ spot[0], i % 2 ^ spot[1], :, PART:] = output[rows]


def pair_grads_kernel(spot, normed, draw, weight, gain, out, dgain):
    project = project_grad(normed, draw, weight, gain, dgain)
    for j in range(2):
        out[0, j ^ spot[0], 0, :BLOCK] = project[j * BLOCK : (j + 1) * BLOCK]


def first_grads(spot, normed, draw, weight, gain, part, out, block, others=()):
    whole = lambda i, s: (0, 0)
    columns = lambda i, s: (0, i)
    rows = 2 * BLOCK
    return pl.pallas_call(
        query_grads_kernel if others else pair_grads_kernel,
        out_shape=[jax.ShapeDtypeStruct(v, low) for v in out]
        + [jax.ShapeDtypeStruct((8, 16 * BLOCK), wide)],
        grid_spec=pltpu.PrefetchScalarGridSpec(
            num_scalar_prefetch=1,
            grid=(8,),
            in_specs=[
                spec((LOCAL, rows), columns),
                once((LOCAL, PART), whole),
                spec((rows, PART), lambda i, s: (i, part)),
                spec((1, rows), columns),
            ]
            + [spec((LOCAL // 2, rows), columns)] * len(others[:2])
            + [once((LOCAL, PART), whole)] * len(others[2:]),
            out_specs=[spec(*v) for v in block] + [spec((8, rows), columns)],
        ),
        compiler_params=params(24),
        cost_estimate=cost(2 * LOCAL * 2048 * 256, 8 * MIB, hint=H_FIRST),
    )(spot, normed, draw, weight, gain, *others)


def query_grads(spot, normed, draw, weight, gain, dmiddle, attended):
    shape = (2, 2, BLOCK, 2 * PART)
    outs = [shape] * 4, [(shape, lambda i, s: (0, 0, 0, 0))] * 4
    *left, dgain = first_grads(
        spot, normed, draw, weight, gain, 0, *outs, (*dmiddle, attended)
    )
    return left, dgain


def pair_grads(spot, normed, draw, weight, gain):
    place = lambda i, s: (lax.rem(i // 2 - s[2] + 4, 4), 0, i % 2 ^ s[1], 0, 0)
    outs = [(4, 2, 2, TALL, PART)], [((1, 2, 1, TALL, PART), place)]
    return first_grads(spot, normed, draw, weight, gain, 1, *outs)


SCALE = HEAD ** (-0.5)


def allowed(query_ids, key_ids, start):
    keys = key_ids[:, pl.ds(start, WINDOW)]
    row = lax.broadcasted_iota(jnp.int32, (QUERIES, WINDOW), 0)
    column = lax.broadcasted_iota(jnp.int32, (QUERIES, WINDOW), 1)
    return (query_ids[...] == keys) & (column <= row + BACK)


def attend_kernel(turn, core, query, pair, query_ids, key_ids, out, logsum):
    i = pl.program_id(0)
    start = pl.multiple_of(i * QUERIES, QUERIES)
    mask = allowed(query_ids, key_ids, start)
    logs = []
    for h in range(2):
        part = slice(h * HEAD, (h + 1) * HEAD)
        scores = dot(query[:, part], pair[pl.ds(start, WINDOW), :HEAD], (1, 1)) * SCALE
        scores = jnp.where(mask, scores, -1e30)
        top = jnp.max(scores, axis=-1, keepdims=True)
        unnormed = jnp.exp(scores - top)
        total = jnp.sum(unnormed, axis=-1, keepdims=True)
        probs = (unnormed * (1.0 / total)).astype(low)
        result = dot(probs, pair[pl.ds(start, WINDOW), HEAD:], (1, 0)).astype(low)
        for j in range(2):
            out[j ^ core[0], 0, :, part] = result[j * BLOCK : (j + 1) * BLOCK]
        logs.append(top + jnp.log(total))
    lane = lax.broadcasted_iota(jnp.int32, (QUERIES, HEAD), 1)
    logsum[...] = jnp.where(lane < HEAD // 2, logs[0], logs[1])


def attend(turn, core, query, pair, query_ids, key_ids):
    rows = lambda i, t, c: (i, 0)
    whole = lambda i, t, c: (0, 0)
    keys = BACK + LOCAL
    return pl.pallas_call(
        attend_kernel,
        out_shape=[
            jax.ShapeDtypeStruct((2, 4, BLOCK, 2 * HEAD), low),
            jax.ShapeDtypeStruct((LOCAL, HEAD), wide),
        ],
        grid_spec=pltpu.PrefetchScalarGridSpec(
            num_scalar_prefetch=2,
            grid=(LOCAL // QUERIES,),
            in_specs=[
                spec((QUERIES, 2 * HEAD), rows),
                once((keys, 2 * HEAD), whole),
                spec((QUERIES, 1), rows),
                spec((1, keys), whole),
            ],
            out_specs=[
                spec((2, 1, BLOCK, 2 * HEAD), lambda i, t, c: (0, t[i], 0, 0)),
                spec((QUERIES, HEAD), rows),
            ],
        ),
        compiler_params=params(24),
        cost_estimate=cost(
            8 * LOCAL * WINDOW * HEAD, 4 * LOCAL * 512, 2 * LOCAL * WINDOW, hint=H_ATTEND
        ),
    )(turn, core, query, pair, query_ids, key_ids)


def attend_back_kernel(
    turn, core, query, pair, query_ids, key_ids, grad, logsum, dquery, dpair
):
    i = pl.program_id(0)

    @pl.when(i == 0)
    def _():
        dpair[...] = jnp.zeros_like(dpair)

    start = pl.multiple_of(i * QUERIES, QUERIES)
    window = pl.ds(start, WINDOW)
    mask = allowed(query_ids, key_ids, start)
    dkey, dvalue = None, None
    for h in range(2):
        part = slice(h * HEAD, (h + 1) * HEAD)
        q = query[:, part]
        g = jnp.concatenate([grad[j ^ core[0], 0, :, part] for j in range(2)], axis=0)
        scores = dot(q, pair[window, :HEAD], (1, 1)) * SCALE
        probs = jnp.where(mask, jnp.exp(scores - logsum[:, h * 64 : h * 64 + 1]), 0.0)
        dprobs = dot(g, pair[window, HEAD:], (1, 1))
        inner = jnp.sum(probs * dprobs, axis=-1, keepdims=True)
        dscores = (probs * (dprobs - inner)).astype(low)
        dquery[:, part] = dot(dscores, pair[window, :HEAD], (1, 0)) * SCALE
        dv = dot(probs.astype(low), g, (0, 0))
        dk = dot(dscores, q, (0, 0))
        dkey = dk if dkey is None else dkey + dk
        dvalue = dv if dvalue is None else dvalue + dv
    dpair[window, :HEAD] += dkey * SCALE
    dpair[window, HEAD:] += dvalue


def attend_back(turn, core, query, pair, query_ids, key_ids, grad, logsum):
    rows = lambda i, t, c: (i, 0)
    whole = lambda i, t, c: (0, 0)
    keys = BACK + LOCAL
    return pl.pallas_call(
        attend_back_kernel,
        out_shape=[
            jax.ShapeDtypeStruct((LOCAL, 2 * HEAD), wide),
            jax.ShapeDtypeStruct((keys, 2 * HEAD), wide),
        ],
        grid_spec=pltpu.PrefetchScalarGridSpec(
            num_scalar_prefetch=2,
            grid=(LOCAL // QUERIES,),
            in_specs=[
                spec((QUERIES, 2 * HEAD), rows),
                once((keys, 2 * HEAD), whole),
                spec((QUERIES, 1), rows),
                spec((1, keys), whole),
                spec((2, 1, BLOCK, 2 * HEAD), lambda i, t, c: (0, t[i], 0, 0)),
                spec((QUERIES, HEAD), rows),
            ],
            out_specs=[spec((QUERIES, 2 * HEAD), rows), once((keys, 2 * HEAD), whole)],
        ),
        compiler_params=params(52),
        cost_estimate=cost(
            20 * LOCAL * WINDOW * HEAD, 8 * LOCAL * 512, 2 * LOCAL * WINDOW, hint=H_ATTEND_BACK
        ),
    )(turn, core, query, pair, query_ids, key_ids, grad, logsum)


def per_device(
    inputs,
    cotangent,
    document_index,
    positions,
    gains,
    gains_first,
    gains_second,
    project_weight,
    project_first,
    project_second,
    output_weight,
    output_first,
    output_second,
    expand_weight,
    expand_first,
    expand_second,
    shrink_weight,
    shrink_first,
    shrink_second,
):
    core, x = lax.axis_index("core"), lax.axis_index("x")
    half, yl = lax.axis_index("yh"), lax.axis_index("yl")
    width = inputs.shape[-1]
    qkv = project_weight.shape[1]
    ff = shrink_weight.shape[0]
    at_home = core == yl
    steps = jnp.arange(8, dtype=jnp.int32)
    place = lax.rem(x - steps % 4 + 4, 4) * 2 + (core ^ (steps // 4))
    turn = lax.rem(x - jnp.arange(4, dtype=jnp.int32) + 4, 4)
    core_of = core.reshape(1).astype(jnp.int32)
    flag = at_home.astype(jnp.int32).reshape(1)

    marks = jnp.stack([document_index[0], positions[0] // 32, positions[0] % 32])
    marks = jnp.pad(marks.astype(low), ((0, 13), (0, 0)))
    message = trade(jnp.concatenate([inputs[0], marks], axis=0))
    rows = message[:BLOCK]
    marks = message[BLOCK:].astype(jnp.int32)
    ids, places = marks[0], marks[1] * 32 + marks[2]

    gain_block = jnp.pad(gains.astype(low), (0, BLOCK * BLOCK - gains.shape[0])).reshape(BLOCK, BLOCK)
    first_shard = jnp.concatenate(
        [project_weight.astype(low), output_weight.astype(low).T, gain_block], axis=1
    )
    second_shard = jnp.concatenate([expand_weight.astype(low), shrink_weight.astype(low).T], axis=1)
    first_all = lax.all_gather(to_group(first_shard), GROUP, axis=0, tiled=True)
    second_shard = to_group(after(second_shard, message))
    rows_all = gather_rows(rows, second_shard)
    second_all = lax.all_gather(after(second_shard, first_all), GROUP, axis=0, tiled=True)
    project_all = first_all[:, :qkv]
    output_all = first_all[:, qkv : qkv + 2 * HEAD]
    expand_all = second_all[:, : 2 * ff]
    shrink_all = second_all[:, 2 * ff :]
    gain_all = first_all.reshape(16, BLOCK, -1)[:, :3, qkv + 2 * HEAD :].reshape(16, 3 * BLOCK)
    gain_all = gain_all[:, : gains.shape[0]].reshape(-1).astype(wide)
    gain_one = gain_all[:width]
    gain_two = gain_all[width : 2 * width]
    gain_query = gain_all[2 * width : 2 * width + HEAD].reshape(1, HEAD)
    gain_key = gain_all[2 * width + HEAD :].reshape(1, HEAD)

    ids_here = lax.dynamic_slice_in_dim(ids, half * LOCAL, LOCAL)
    places_here = lax.dynamic_slice_in_dim(places, half * LOCAL, LOCAL)
    ids_keys = jnp.where(
        half == 0,
        jnp.concatenate([jnp.full((BACK,), -1, jnp.int32), ids[:LOCAL]]),
        ids[LOCAL - BACK :],
    )
    query_ids, key_ids = ids_here.reshape(-1, 1), ids_keys.reshape(1, -1)
    frequency = jnp.exp(jnp.arange(HEAD // 2, dtype=wide) * (-2.0 * math.log(theta) / HEAD))
    angle = places_here.astype(wide)[:, None] * frequency
    cosine, sine = jnp.cos(angle), jnp.sin(angle)
    cosine = jnp.concatenate([cosine, cosine], axis=1)
    sine = jnp.concatenate([-sine, sine], axis=1)

    values = rows.astype(wide)
    normed, raw, scale, query, pair = project(
        place, rows_all, first_all, gain_one.reshape(1, -1), gain_query, gain_key, cosine, sine
    )
    earlier = move(pair[LOCAL - BACK :], "yh", [(0, 1)])
    back_all = choose(place, flag, cotangent[0], other_core(cotangent[0]))
    back = [back_all[: LOCAL // 2], back_all[LOCAL // 2 :]]
    pair_all = jnp.concatenate([after(earlier, back_all), pair], axis=0)
    attended, logsum = attend(turn, core_of, query, pair_all, query_ids, key_ids)
    attended = attended.reshape(LOCAL, 2 * HEAD)
    mine = dot(attended[: LOCAL // 2], output_all, (1, 1)).astype(low)
    away = dot(attended[LOCAL // 2 :], output_all, (1, 1)).astype(low)
    middle = values + chip_sum(core_sum(mine, away))

    normed_two = gather_rows(rms_norm(middle, gain_two).astype(low))
    hidden, dexpanded = [], []
    for v, dy in zip(normed_two, back):
        expanded = dot(v, expand_all, (1, 0))
        activated, pull_act = jax.vjp(swiglu, expanded[:, :ff], expanded[:, ff:])
        hidden.append(activated.astype(low))
        dgate, dup = pull_act(dot(dy, shrink_all, (1, 0)))
        dexpanded.append(jnp.concatenate([dgate, dup], axis=1).astype(low))
    both_two = core_sum(*back_products(dexpanded, second_all))
    drows_two = chip_sum(both_two)
    second_grads = grads(
        [*after(tuple(normed_two), both_two), *back], [*dexpanded, *hidden]
    )
    second_red = lax.psum_scatter(second_grads, GROUP, scatter_dimension=0, tiled=True)
    drows_two = after(drows_two, second_grads)

    _, pull_two = jax.vjp(rms_norm, middle, gain_two)
    dmiddle, dgain_two = pull_two(drows_two)
    dmiddle = back[0][:BLOCK].astype(wide) + dmiddle
    shrunk = back_products(after(tuple(hidden), second_grads), second_all, at=2, hint=0)
    shrunk = shrunk[0], other_core(shrunk[1])
    dmiddle_all = gather_rows(dmiddle.astype(low))
    dmiddle_all = after(tuple(dmiddle_all), *shrunk)
    shrunk = chip_blocks(*after(shrunk, dmiddle_all), x)
    mlp = lax.all_to_all(shrunk, "x", 0, 0, tiled=True)
    dattended = jnp.stack([dot(v, output_all, (1, 0)).astype(low) for v in dmiddle_all])
    dquery, dpair = attend_back(
        turn,
        core_of,
        query,
        pair_all,
        query_ids,
        key_ids,
        dattended.reshape(2, 4, BLOCK, 2 * HEAD),
        logsum,
    )
    later = move(dpair[:BACK].astype(low), "yh", [(1, 0)])
    draw_query, dgain_query = heads_back(
        query_back_kernel, place, raw, cosine, sine, gain_query, dquery
    )
    spot = jnp.stack([half, yl, lax.axis_index("z")]).astype(jnp.int32)
    gain_row = gain_one.reshape(1, -1)
    left, dgain_one = query_grads(
        spot, normed, draw_query, first_all, gain_row, dmiddle_all, attended
    )
    left_grads = left
    left = sum_z(left)
    mlp = jnp.sum(after(mlp, *left_grads).astype(wide), axis=0)
    later = after(later, mlp)
    draw_pair, dgain_key = heads_back(
        pair_back_kernel, place, raw, cosine, sine, gain_key, dpair, later
    )
    outputs = trade((middle + after(mlp, draw_pair)).astype(low))

    pair_right, dgain_rest = pair_grads(spot, normed, draw_pair, first_all, gain_row)
    dgains = jnp.concatenate([(dgain_one + dgain_rest)[0], dgain_two, dgain_query[0], dgain_key[0]])
    dgains = jnp.pad(dgains.reshape(-1, BLOCK), ((0, 6), (0, 0)))
    dgains = dgains + other_core(dgains)
    dgains = dgains + shift(dgains, 1) + shift(dgains, 2) + shift(dgains, 3)
    dgains = dgains[:-6].astype(low).reshape(4, 2, 2, 1, -1)
    dgains = jnp.where(half == 0, dgains, dgains[:, :, ::-1])
    dgains = jnp.where(yl == 0, dgains, dgains[:, ::-1]).transpose(0, 2, 1, 3, 4)
    dgains = jnp.roll(dgains, -lax.axis_index("z"), axis=0)
    over = dgains[..., PART:]
    dgains = jnp.concatenate([dgains[..., :PART], jnp.pad(over, ((0, 0),) * 4 + ((0, PART - over.shape[-1]),))], axis=3)
    dgains = jnp.pad(dgains, ((0, 0), (0, 0), (0, 0), (0, 14), (0, 0)))
    right = lax.dynamic_update_slice(pair_right, dgains, (0, 0, 0, BLOCK, 0))
    mine, away = back_products(
        after((draw_query, draw_pair), dgain_rest), first_all, parts=True, hint=H_BACK
    )
    right = sum_z(right)
    drows_one = chip_sum_at_once(chip_blocks(mine, other_core(away), x))
    second_red = to_owner(second_red)
    expand_new, shrink_new = adam_weights(
        second_red,
        (((0, 2 * ff),), ((2 * ff, ff),)),
        [(expand_weight, expand_first, expand_second), (shrink_weight, shrink_first, shrink_second)],
        (False, True),
        (0.05, 0.03),
    )
    both = jnp.concatenate([jnp.pad(left, ((0, 0), (0, 0), (0, 16), (0, 0))), right], axis=3)
    first_red = sum_flips(after(both.astype(low), second_red))

    _, pull_one = jax.vjp(rms_norm, values, gain_one)
    dvalues, _ = pull_one(drows_one)
    input_grad = trade(after((dmiddle + dvalues).astype(low), outputs))

    dgains = first_red[BLOCK : BLOCK + 8, 2 * PART :]
    project_new, output_new, outputs, input_grad = adam_weights(
        first_red,
        (((0, PART), (2 * PART, PART)), ((PART, PART),)),
        [(project_weight, project_first, project_second), (output_weight, output_first, output_second)],
        (False, True),
        (0.05, 0.4),
        (outputs, input_grad),
    )
    dgains = dgains[:2].reshape(-1)[: gains.shape[0]]
    return (
        outputs[None],
        input_grad[None],
        *adam(gains, gains_first, gains_second, dgains, 0.5, 0.0),
        *project_new,
        *output_new,
        *expand_new,
        *shrink_new,
    )


def solution(mesh):
    fine = Mesh(mesh.devices.reshape(4, 2, 2, 4, 2), ("z", "core", "yh", "x", "yl"))
    tokens = P(("z", "core"), ("yh", "x", "yl"), None)
    marks = P(("z", "core"), None)
    gain = P(("z", "core", "yh"))
    tall = P(("z", "core", "yh"), ("x", "yl"))
    flat = P(("x", "yl"), ("z", "core", "yh"))
    in_specs = (
        tokens,
        P(("z", "core"), "yh", None),
        marks,
        marks,
        *[gain] * 3,
        *[tall] * 3,
        *[flat] * 3,
        *[tall] * 3,
        *[flat] * 3,
    )
    out_specs = (
        tokens,
        tokens,
        *[gain] * 3,
        *[tall] * 3,
        *[flat] * 3,
        *[tall] * 3,
        *[flat] * 3,
    )
    return jax.shard_map(
        per_device, mesh=fine, in_specs=in_specs, out_specs=out_specs, check_vma=False
    )
```

```python
import functools
import math

import jax
import jax.numpy as jnp
from jax import lax
from jax.experimental import pallas as pl
from jax.experimental.pallas import tpu as pltpu
from jax.sharding import Mesh
from jax.sharding import PartitionSpec as P

QUERY_HEADS = 16
KEY_VALUE_HEADS = 8
HEAD = 128
STEP = 5
LONGEST = 800
BLOCK = 128
LOCAL = 1024
BACK = 896
QUERIES = 256
WINDOW = BACK + QUERIES

epsilon = 1e-06
theta = 1000000.0
beta_first = 0.9
beta_second = 0.95
adam_epsilon = 1e-08
weight_decay = 0.1

low = jnp.bfloat16
wide = jnp.float32
MIB = 1024 * 1024
H_PROJECT = 1
H_ATTEND = 150
H_GRADS = 1
H_ATTEND_BACK = 26
H_HEADS_BACK = 1
H_BACK = 1
H_FIRST = 1
H_ADAM = 1

epsilon = 1e-06
theta = 1000000.0
beta_first = 0.9
beta_second = 0.95
adam_epsilon = 1e-08
weight_decay = 0.1

low = jnp.bfloat16
wide = jnp.float32
MIB = 1024 * 1024
ATTEND_HINT = 300
ATTEND_BACK_HINT = 260


def rms_norm(values, gain):
    return values * lax.rsqrt(jnp.mean(values * values, axis=-1, keepdims=True) + epsilon) * gain


def swiglu(gate, upward):
    return jax.nn.silu(gate) * upward


def adam(weight, first, second, grad, rate, decay_rate):
    mean = beta_first * first + (1.0 - beta_first) * grad
    square = beta_second * second + (1.0 - beta_second) * grad * grad
    mean_hat = mean / (1.0 - beta_first**STEP)
    square_hat = square / (1.0 - beta_second**STEP)
    updated = weight - rate * (
        mean_hat / (jnp.sqrt(square_hat) + adam_epsilon) + decay_rate * weight
    )
    return (mean, square, updated)


def dot(left, right, dims):
    return lax.dot_general(left, right, ((dims[:1], dims[1:]), ((), ())), preferred_element_type=wide)


def move(values, axis, pairs):
    return lax.ppermute(values, axis, pairs)


def shift(values, steps):
    return move(values, "x", [(i, (i + steps) % 4) for i in range(4)])


def other_core(values):
    return move(values, "core", [(0, 1), (1, 0)])


def trade(values):
    return move(values, ("core", "yl"), [(a * 2 + b, b * 2 + a) for a in range(2) for b in range(2)])


def to_group(values):
    pairs = [
        ((a * 2 + b) * 2 + d, (d * 2 + a) * 2 + b)
        for a in range(2)
        for b in range(2)
        for d in range(2)
    ]
    return move(values, ("core", "yh", "yl"), pairs)


def to_owner(values):
    pairs = [
        ((d * 2 + a) * 2 + b, (a * 2 + b) * 2 + d)
        for a in range(2)
        for b in range(2)
        for d in range(2)
    ]
    return move(values, ("core", "yh", "yl"), pairs)


def gather_rows(values, *others):
    pieces = (values, shift(values, 1), shift(values, 2), shift(values, 3))
    mine = jnp.concatenate(after(pieces, *others) if others else pieces, axis=0)
    return mine, other_core(mine)


def core_sum(mine, away):
    return (mine.astype(wide) + other_core(away).astype(wide)).astype(low)


def chip_sum(both):
    pieces = both.reshape(4, BLOCK, -1)
    total = pieces[0].astype(wide)
    for k in (2, 1, 3):
        total = total + shift(pieces[k], 4 - k).astype(wide)
    return total


def chip_blocks(mine, away, x):
    mine, away = mine.reshape(4, BLOCK, -1), away.reshape(4, BLOCK, -1)
    pick = lambda v, i: lax.dynamic_index_in_dim(v, lax.rem(x - i + 4, 4), 0).astype(wide)
    return jnp.concatenate([(pick(mine, i) + pick(away, i)).astype(low) for i in range(4)], axis=0)


def chip_sum_at_once(blocks):
    return jnp.sum(lax.all_to_all(blocks, "x", 0, 0, tiled=True).astype(wide), axis=0)


def after(values, *others):
    return lax.optimization_barrier((values, *others))[0]


def sum_z(pieces):
    total = pieces[0].astype(wide)
    for k in (2, 1, 3):
        there = move(pieces[k], "z", [(i, (i + k) % 4) for i in range(4)])
        total = total + there.astype(wide)
    return total


def flip(values, a, b):
    pairs = [
        ((c * 2 + h) * 2 + d, ((d ^ b) * 2 + (h ^ a)) * 2 + c)
        for c in range(2)
        for h in range(2)
        for d in range(2)
    ]
    return move(values, ("core", "yh", "yl"), pairs)


def sum_flips(pieces):
    total = 0.0
    for a in (1, 0):
        for b in (1, 0):
            total = total + flip(pieces[a, b], a, b).astype(wide)
    return total


GROUP = ("z", "yh", "yl")


def spec(shape, index):
    return pl.BlockSpec(shape, index)


def once(shape, index):
    return pl.BlockSpec(shape, index, pipeline_mode=pl.Buffered(1))


def params(mib):
    return pltpu.CompilerParams(vmem_limit_bytes=mib * MIB)


def cost(flops, moved, special=0, hint=1):
    return pl.CostEstimate(
        flops=flops * hint, bytes_accessed=moved * hint, transcendentals=special * hint
    )


def choose_kernel(place, flag, own, away, out, arrived):
    def copies(source):
        return [
            pltpu.make_async_copy(
                source.at[pl.ds(pl.multiple_of(place[i] * BLOCK, BLOCK), BLOCK)],
                out.at[pl.ds(i * BLOCK, BLOCK)],
                arrived.at[i],
            )
            for i in range(8)
        ]

    @pl.when(flag[0] == 1)
    def _():
        for copy in copies(own):
            copy.start()

    @pl.when(flag[0] == 0)
    def _():
        for copy in copies(away):
            copy.start()

    for copy in copies(own):
        copy.wait()


def choose(place, flag, own, away):
    scalar = pl.BlockSpec(memory_space=pltpu.SMEM)
    there = pl.BlockSpec(memory_space=pl.ANY)
    return pl.pallas_call(
        choose_kernel,
        out_shape=jax.ShapeDtypeStruct(own.shape, own.dtype),
        in_specs=[scalar, scalar, there, there],
        out_specs=there,
        scratch_shapes=[pltpu.SemaphoreType.DMA((8,))],
        compiler_params=params(4),
        cost_estimate=cost(0, 2 * own.size * 2),
    )(place, flag, own, away)


def project_kernel(
    place, mine, away, weight, gain, gq, gk, cosine, sine, normed, raw, scale, query, pair
):
    i = pl.program_id(0)

    def work(rows):
        v = rows[...].astype(wide)
        r = lax.rsqrt(jnp.mean(v * v, axis=-1, keepdims=True) + epsilon)
        n = (v * r * gain[...]).astype(low)
        normed[...] = n
        scale[...] = jnp.broadcast_to(r, scale.shape)
        raw[...] = dot(n, weight[...], (1, 0))

    pl.when(i < 2)(lambda: work(mine))
    pl.when(i >= 2)(lambda: work(away))
    for k in range(2):
        here = slice(k * BLOCK, (k + 1) * BLOCK)
        there = pl.ds(pl.multiple_of(place[2 * i + k] * BLOCK, BLOCK), BLOCK)
        c, s = cosine[there], sine[there]
        for h in range(4):
            part = slice(h * HEAD, (h + 1) * HEAD)
            v = raw[here, part]
            if h < 3:
                v = rms_norm(v, gq[...] if h < 2 else gk[...])
                v = v * c + pltpu.roll(v, HEAD // 2, 1) * s
            if h < 2:
                query[there, part] = v.astype(low)
            else:
                pair[there, (h - 2) * HEAD : (h - 1) * HEAD] = v.astype(low)


SCALARS = pl.BlockSpec(memory_space=pltpu.SMEM)
WHOLE = pl.BlockSpec(memory_space=pltpu.VMEM)


def project(place, rows, weight, gain, gq, gk, cosine, sine):
    width = rows[0].shape[1]
    fixed = lambda i, p: (0, 0)
    moving = lambda i, p: (i, 0)
    tall = 2 * BLOCK
    return pl.pallas_call(
        project_kernel,
        out_shape=[
            jax.ShapeDtypeStruct((LOCAL, width), low),
            jax.ShapeDtypeStruct((LOCAL, 4 * HEAD), wide),
            jax.ShapeDtypeStruct((LOCAL, HEAD), wide),
            jax.ShapeDtypeStruct((LOCAL, 2 * HEAD), low),
            jax.ShapeDtypeStruct((LOCAL, 2 * HEAD), low),
        ],
        grid_spec=pltpu.PrefetchScalarGridSpec(
            num_scalar_prefetch=1,
            grid=(LOCAL // tall,),
            in_specs=[
                spec((tall, width), lambda i, p: (jnp.minimum(i, 1), 0)),
                spec((tall, width), lambda i, p: (jnp.maximum(i - 2, 0), 0)),
                once((width, 4 * HEAD), fixed),
                once((1, width), fixed),
                once((1, HEAD), fixed),
                once((1, HEAD), fixed),
                once((LOCAL, HEAD), fixed),
                once((LOCAL, HEAD), fixed),
            ],
            out_specs=[
                spec((tall, width), moving),
                spec((tall, 4 * HEAD), moving),
                spec((tall, HEAD), moving),
                once((LOCAL, 2 * HEAD), fixed),
                once((LOCAL, 2 * HEAD), fixed),
            ],
        ),
        compiler_params=params(52),
        cost_estimate=cost(2 * LOCAL * width * 512, 16 * MIB, hint=H_PROJECT),
    )(place, *rows, weight, gain, gq, gk, cosine, sine)


def turn_back(d, v, c, s, g):
    d = d * c + pltpu.roll(d * s, HEAD // 2, 1)
    r = lax.rsqrt(jnp.mean(v * v, axis=-1, keepdims=True) + epsilon)
    u = v * r
    e = d * g
    before = r * (e - u * jnp.mean(u * e, axis=-1, keepdims=True))
    return before.astype(low), jnp.sum(d * u, axis=0, keepdims=True)


def query_back_kernel(place, raw, cosine, sine, gq, dquery, draw, dgain):
    total = 0.0
    for i in range(8):
        here = pl.ds(i * BLOCK, BLOCK)
        there = pl.ds(pl.multiple_of(place[i] * BLOCK, BLOCK), BLOCK)
        for h in range(2):
            part = slice(h * HEAD, (h + 1) * HEAD)
            draw[here, part], add = turn_back(
                dquery[there, part], raw[here, part], cosine[there], sine[there], gq[...]
            )
            total += add
    dgain[...] = jnp.broadcast_to(total, dgain.shape)


def pair_back_kernel(place, raw, cosine, sine, gk, dpair, later, draw, dgain):
    total = 0.0
    for i in range(8):
        here = pl.ds(i * BLOCK, BLOCK)
        there = pl.ds(pl.multiple_of(place[i] * BLOCK, BLOCK), BLOCK)
        dp = dpair[pl.ds(pl.multiple_of(place[i] * BLOCK + BACK, BLOCK), BLOCK)]
        from_later = later[pl.ds(pl.multiple_of(jnp.maximum(place[i] - 1, 0) * BLOCK, BLOCK), BLOCK)]
        dp = dp + jnp.where(place[i] > 0, from_later.astype(wide), 0.0)
        draw[here, :HEAD], add = turn_back(
            dp[:, :HEAD], raw[here, 2 * HEAD : 3 * HEAD], cosine[there], sine[there], gk[...]
        )
        draw[here, HEAD:] = dp[:, HEAD:].astype(low)
        total += add
    dgain[...] = jnp.broadcast_to(total, dgain.shape)


def heads_back(kernel, place, *inputs):
    return pl.pallas_call(
        kernel,
        out_shape=[
            jax.ShapeDtypeStruct((LOCAL, 2 * HEAD), low),
            jax.ShapeDtypeStruct((8, HEAD), wide),
        ],
        in_specs=[SCALARS] + [WHOLE] * len(inputs),
        out_specs=[WHOLE] * 2,
        compiler_params=params(16),
        cost_estimate=cost(LOCAL * 512 * 10, LOCAL * 512 * 6, hint=H_HEADS_BACK),
    )(place, *inputs)


ROWS = 256


def both_dots(lefts, rights, dims):
    return dot(lefts[0][...], rights[0][...], dims) + dot(lefts[1][...], rights[1][...], dims)


def grads_kernel(*refs):
    lefts, rights, out = refs[:4], refs[4:8], refs[8]
    n = rights[0].shape[1]
    out[:, :n] = both_dots(lefts[:2], rights[:2], (0, 0)).astype(low)
    out[:, n:] = both_dots(lefts[2:], rights[2:], (0, 0)).astype(low)


def grads(lefts, rights):
    depth, rows = lefts[0].shape
    total = rights[0].shape[1] + rights[2].shape[1]
    return pl.pallas_call(
        grads_kernel,
        out_shape=jax.ShapeDtypeStruct((rows, total), low),
        grid=(rows // ROWS,),
        in_specs=[spec((depth, ROWS), lambda i: (0, i))] * 4
        + [once(v.shape, lambda i: (0, 0)) for v in rights],
        out_specs=spec((ROWS, total), lambda i: (i, 0)),
        compiler_params=params(28),
        cost_estimate=cost(
            4 * depth * rows * total, 8 * depth * rows + 2 * total * (rows + depth), hint=H_GRADS
        ),
    )(*lefts, *rights)


def back_kernel(parts, *refs):
    *lefts, right, out_mine, out_away = refs
    turned = right[...].T
    half = LOCAL // 2
    if parts:
        depth = lefts[0].shape[1]
        pick = lambda rows: sum(
            dot(left[rows], turned[k * depth : (k + 1) * depth], (1, 0))
            for k, left in enumerate(lefts)
        )
        mine, away = pick(pl.ds(0, half)), pick(pl.ds(half, half))
    else:
        mine, away = [dot(left[...], turned, (1, 0)) for left in lefts]
    out_away[...] = away.astype(low)
    out_mine[...] = mine.astype(low)


def back_products(lefts, right, at=0, parts=False, hint=1):
    rows = LOCAL // 2
    depth = sum(v.shape[1] for v in lefts) if parts else lefts[0].shape[1]
    width = right.shape[0]
    return pl.pallas_call(
        functools.partial(back_kernel, parts),
        out_shape=[jax.ShapeDtypeStruct((rows, width), low)] * 2,
        grid=(width // ROWS,),
        in_specs=[once(v.shape, lambda i: (0, 0)) for v in lefts]
        + [spec((ROWS, depth), lambda i: (i, at))],
        out_specs=[spec((rows, ROWS), lambda i: (0, i))] * 2,
        compiler_params=params(20),
        cost_estimate=cost(
            4 * rows * depth * width, 2 * width * (depth + 2 * rows), hint=hint
        ),
    )(*lefts, right)


def adam_kernel(columns, flipped, rates, extras, *refs):
    grad = refs[0]
    for k, (turn, rate) in enumerate(zip(flipped, rates)):
        weight, first, second = refs[1 + 3 * k : 4 + 3 * k]
        outs = refs[1 + extras + 3 * (len(rates) + k) : 4 + extras + 3 * (len(rates) + k)]
        g = [grad[:BLOCK, at : at + n] for at, n in columns[k]]
        g = (jnp.concatenate(g, axis=1) if len(g) > 1 else g[0]).astype(wide)
        if turn:
            g = g.T
        for out, value in zip(outs, adam(weight[...], first[...], second[...], g, rate, weight_decay)):
            out[...] = value
    for k in range(extras):
        refs[k - extras][...] = refs[1 + 3 * len(rates) + k][...]


def adam_weights(grad, columns, weights, flipped, rates, extras=()):
    states = [v for group in weights for v in group] + list(extras)
    out = pl.pallas_call(
        functools.partial(adam_kernel, columns, flipped, rates, len(extras)),
        out_shape=[jax.ShapeDtypeStruct(v.shape, v.dtype) for v in states],
        in_specs=[WHOLE] * (1 + len(states)),
        out_specs=[WHOLE] * len(states),
        compiler_params=params(24),
        cost_estimate=cost(20 * grad.size, 26 * grad.size, hint=H_ADAM),
    )(grad, *states)
    return [tuple(out[3 * k : 3 * k + 3]) for k in range(len(weights))] + list(out[3 * len(weights) :])


PART = 2 * HEAD
TALL = BLOCK + 16


def project_grad(normed, draw, weight, gain, dgain):
    project = dot(normed[...], draw[...], (0, 0))
    product = (project * weight[...].astype(wide)).astype(low)
    dgain[...] = dot(jnp.ones((8, PART), low), product, (1, 1)) / gain[...]
    return project.astype(low)


def query_grads_kernel(spot, normed, draw, weight, gain, mine, away, attended, *outs):
    *outs, dgain = outs
    project = project_grad(normed, draw, weight, gain, dgain)
    half = LOCAL // 2
    output = dot(mine[...], attended[:half], (0, 0)) + dot(away[...], attended[half:], (0, 0))
    output = output.astype(low)
    i = pl.program_id(0)
    steps = lax.rem(i // 2 - spot[2] + 4, 4)
    for k, out in enumerate(outs):

        @pl.when(steps == k)
        def _():
            for j in range(2):
                rows = slice(j * BLOCK, (j + 1) * BLOCK)
                out[j ^ spot[0], i % 2 ^ spot[1], :, :PART] = project[rows]
                out[j ^ spot[0], i % 2 ^ spot[1], :, PART:] = output[rows]


def pair_grads_kernel(spot, normed, draw, weight, gain, out, dgain):
    project = project_grad(normed, draw, weight, gain, dgain)
    for j in range(2):
        out[0, j ^ spot[0], 0, :BLOCK] = project[j * BLOCK : (j + 1) * BLOCK]


def first_grads(spot, normed, draw, weight, gain, part, out, block, others=()):
    whole = lambda i, s: (0, 0)
    columns = lambda i, s: (0, i)
    rows = 2 * BLOCK
    return pl.pallas_call(
        query_grads_kernel if others else pair_grads_kernel,
        out_shape=[jax.ShapeDtypeStruct(v, low) for v in out]
        + [jax.ShapeDtypeStruct((8, 16 * BLOCK), wide)],
        grid_spec=pltpu.PrefetchScalarGridSpec(
            num_scalar_prefetch=1,
            grid=(8,),
            in_specs=[
                spec((LOCAL, rows), columns),
                once((LOCAL, PART), whole),
                spec((rows, PART), lambda i, s: (i, part)),
                spec((1, rows), columns),
            ]
            + [spec((LOCAL // 2, rows), columns)] * len(others[:2])
            + [once((LOCAL, PART), whole)] * len(others[2:]),
            out_specs=[spec(*v) for v in block] + [spec((8, rows), columns)],
        ),
        compiler_params=params(24),
        cost_estimate=cost(2 * LOCAL * 2048 * 256, 8 * MIB, hint=H_FIRST),
    )(spot, normed, draw, weight, gain, *others)


def query_grads(spot, normed, draw, weight, gain, dmiddle, attended):
    shape = (2, 2, BLOCK, 2 * PART)
    outs = [shape] * 4, [(shape, lambda i, s: (0, 0, 0, 0))] * 4
    *left, dgain = first_grads(
        spot, normed, draw, weight, gain, 0, *outs, (*dmiddle, attended)
    )
    return left, dgain


def pair_grads(spot, normed, draw, weight, gain):
    place = lambda i, s: (lax.rem(i // 2 - s[2] + 4, 4), 0, i % 2 ^ s[1], 0, 0)
    outs = [(4, 2, 2, TALL, PART)], [((1, 2, 1, TALL, PART), place)]
    return first_grads(spot, normed, draw, weight, gain, 1, *outs)


SCALE = HEAD ** (-0.5)


def allowed(query_ids, key_ids, start):
    keys = key_ids[:, pl.ds(start, WINDOW)]
    row = lax.broadcasted_iota(jnp.int32, (QUERIES, WINDOW), 0)
    column = lax.broadcasted_iota(jnp.int32, (QUERIES, WINDOW), 1)
    return (query_ids[...] == keys) & (column <= row + BACK)


def attend_kernel(turn, core, query, pair, query_ids, key_ids, out, logsum):
    i = pl.program_id(0)
    start = pl.multiple_of(i * QUERIES, QUERIES)
    mask = allowed(query_ids, key_ids, start)
    logs = []
    for h in range(2):
        part = slice(h * HEAD, (h + 1) * HEAD)
        scores = dot(query[:, part], pair[pl.ds(start, WINDOW), :HEAD], (1, 1)) * SCALE
        scores = jnp.where(mask, scores, -1e30)
        top = jnp.max(scores, axis=-1, keepdims=True)
        unnormed = jnp.exp(scores - top)
        total = jnp.sum(unnormed, axis=-1, keepdims=True)
        probs = (unnormed * (1.0 / total)).astype(low)
        result = dot(probs, pair[pl.ds(start, WINDOW), HEAD:], (1, 0)).astype(low)
        for j in range(2):
            out[j ^ core[0], 0, :, part] = result[j * BLOCK : (j + 1) * BLOCK]
        logs.append(top + jnp.log(total))
    lane = lax.broadcasted_iota(jnp.int32, (QUERIES, HEAD), 1)
    logsum[...] = jnp.where(lane < HEAD // 2, logs[0], logs[1])


def attend(turn, core, query, pair, query_ids, key_ids):
    rows = lambda i, t, c: (i, 0)
    whole = lambda i, t, c: (0, 0)
    keys = BACK + LOCAL
    return pl.pallas_call(
        attend_kernel,
        out_shape=[
            jax.ShapeDtypeStruct((2, 4, BLOCK, 2 * HEAD), low),
            jax.ShapeDtypeStruct((LOCAL, HEAD), wide),
        ],
        grid_spec=pltpu.PrefetchScalarGridSpec(
            num_scalar_prefetch=2,
            grid=(LOCAL // QUERIES,),
            in_specs=[
                spec((QUERIES, 2 * HEAD), rows),
                once((keys, 2 * HEAD), whole),
                spec((QUERIES, 1), rows),
                spec((1, keys), whole),
            ],
            out_specs=[
                spec((2, 1, BLOCK, 2 * HEAD), lambda i, t, c: (0, t[i], 0, 0)),
                spec((QUERIES, HEAD), rows),
            ],
        ),
        compiler_params=params(24),
        cost_estimate=cost(
            8 * LOCAL * WINDOW * HEAD, 4 * LOCAL * 512, 2 * LOCAL * WINDOW, hint=H_ATTEND
        ),
    )(turn, core, query, pair, query_ids, key_ids)


def attend_back_kernel(
    turn, core, query, pair, query_ids, key_ids, grad, logsum, dquery, dpair
):
    i = pl.program_id(0)

    @pl.when(i == 0)
    def _():
        dpair[...] = jnp.zeros_like(dpair)

    start = pl.multiple_of(i * QUERIES, QUERIES)
    window = pl.ds(start, WINDOW)
    mask = allowed(query_ids, key_ids, start)
    dkey, dvalue = None, None
    for h in range(2):
        part = slice(h * HEAD, (h + 1) * HEAD)
        q = query[:, part]
        g = jnp.concatenate([grad[j ^ core[0], 0, :, part] for j in range(2)], axis=0)
        scores = dot(q, pair[window, :HEAD], (1, 1)) * SCALE
        probs = jnp.where(mask, jnp.exp(scores - logsum[:, h * 64 : h * 64 + 1]), 0.0)
        dprobs = dot(g, pair[window, HEAD:], (1, 1))
        inner = jnp.sum(probs * dprobs, axis=-1, keepdims=True)
        dscores = (probs * (dprobs - inner)).astype(low)
        dquery[:, part] = dot(dscores, pair[window, :HEAD], (1, 0)) * SCALE
        dv = dot(probs.astype(low), g, (0, 0))
        dk = dot(dscores, q, (0, 0))
        dkey = dk if dkey is None else dkey + dk
        dvalue = dv if dvalue is None else dvalue + dv
    dpair[window, :HEAD] += dkey * SCALE
    dpair[window, HEAD:] += dvalue


def attend_back(turn, core, query, pair, query_ids, key_ids, grad, logsum):
    rows = lambda i, t, c: (i, 0)
    whole = lambda i, t, c: (0, 0)
    keys = BACK + LOCAL
    return pl.pallas_call(
        attend_back_kernel,
        out_shape=[
            jax.ShapeDtypeStruct((LOCAL, 2 * HEAD), wide),
            jax.ShapeDtypeStruct((keys, 2 * HEAD), wide),
        ],
        grid_spec=pltpu.PrefetchScalarGridSpec(
            num_scalar_prefetch=2,
            grid=(LOCAL // QUERIES,),
            in_specs=[
                spec((QUERIES, 2 * HEAD), rows),
                once((keys, 2 * HEAD), whole),
                spec((QUERIES, 1), rows),
                spec((1, keys), whole),
                spec((2, 1, BLOCK, 2 * HEAD), lambda i, t, c: (0, t[i], 0, 0)),
                spec((QUERIES, HEAD), rows),
            ],
            out_specs=[spec((QUERIES, 2 * HEAD), rows), once((keys, 2 * HEAD), whole)],
        ),
        compiler_params=params(28),
        cost_estimate=cost(
            20 * LOCAL * WINDOW * HEAD, 8 * LOCAL * 512, 2 * LOCAL * WINDOW, hint=H_ATTEND_BACK
        ),
    )(turn, core, query, pair, query_ids, key_ids, grad, logsum)


def per_device(
    inputs,
    cotangent,
    document_index,
    positions,
    gains,
    gains_first,
    gains_second,
    project_weight,
    project_first,
    project_second,
    output_weight,
    output_first,
    output_second,
    expand_weight,
    expand_first,
    expand_second,
    shrink_weight,
    shrink_first,
    shrink_second,
):
    core, x = lax.axis_index("core"), lax.axis_index("x")
    half, yl = lax.axis_index("yh"), lax.axis_index("yl")
    width = inputs.shape[-1]
    qkv = project_weight.shape[1]
    ff = shrink_weight.shape[0]
    at_home = core == yl
    steps = jnp.arange(8, dtype=jnp.int32)
    place = lax.rem(x - steps % 4 + 4, 4) * 2 + (core ^ (steps // 4))
    turn = lax.rem(x - jnp.arange(4, dtype=jnp.int32) + 4, 4)
    core_of = core.reshape(1).astype(jnp.int32)
    flag = at_home.astype(jnp.int32).reshape(1)

    marks = jnp.stack([document_index[0], positions[0] // 32, positions[0] % 32])
    marks = jnp.pad(marks.astype(low), ((0, 13), (0, 0)))
    message = trade(jnp.concatenate([inputs[0], marks], axis=0))
    rows = message[:BLOCK]
    marks = message[BLOCK:].astype(jnp.int32)
    ids, places = marks[0], marks[1] * 32 + marks[2]

    gain_block = jnp.pad(gains.astype(low), (0, BLOCK * BLOCK - gains.shape[0])).reshape(BLOCK, BLOCK)
    first_shard = jnp.concatenate(
        [project_weight.astype(low), output_weight.astype(low).T, gain_block], axis=1
    )
    second_shard = jnp.concatenate([expand_weight.astype(low), shrink_weight.astype(low).T], axis=1)
    first_all = lax.all_gather(to_group(first_shard), GROUP, axis=0, tiled=True)
    second_shard = to_group(after(second_shard, message))
    rows_all = gather_rows(rows, second_shard)
    second_all = lax.all_gather(after(second_shard, first_all), GROUP, axis=0, tiled=True)
    project_all = first_all[:, :qkv]
    output_all = first_all[:, qkv : qkv + 2 * HEAD]
    expand_all = second_all[:, : 2 * ff]
    shrink_all = second_all[:, 2 * ff :]
    gain_all = first_all.reshape(16, BLOCK, -1)[:, :3, qkv + 2 * HEAD :].reshape(16, 3 * BLOCK)
    gain_all = gain_all[:, : gains.shape[0]].reshape(-1).astype(wide)
    gain_one = gain_all[:width]
    gain_two = gain_all[width : 2 * width]
    gain_query = gain_all[2 * width : 2 * width + HEAD].reshape(1, HEAD)
    gain_key = gain_all[2 * width + HEAD :].reshape(1, HEAD)

    ids_here = lax.dynamic_slice_in_dim(ids, half * LOCAL, LOCAL)
    places_here = lax.dynamic_slice_in_dim(places, half * LOCAL, LOCAL)
    ids_keys = jnp.where(
        half == 0,
        jnp.concatenate([jnp.full((BACK,), -1, jnp.int32), ids[:LOCAL]]),
        ids[LOCAL - BACK :],
    )
    query_ids, key_ids = ids_here.reshape(-1, 1), ids_keys.reshape(1, -1)
    frequency = jnp.exp(jnp.arange(HEAD // 2, dtype=wide) * (-2.0 * math.log(theta) / HEAD))
    angle = places_here.astype(wide)[:, None] * frequency
    cosine, sine = jnp.cos(angle), jnp.sin(angle)
    cosine = jnp.concatenate([cosine, cosine], axis=1)
    sine = jnp.concatenate([-sine, sine], axis=1)

    values = rows.astype(wide)
    normed, raw, scale, query, pair = project(
        place, rows_all, first_all, gain_one.reshape(1, -1), gain_query, gain_key, cosine, sine
    )
    earlier = move(pair[LOCAL - BACK :], "yh", [(0, 1)])
    back_all = choose(place, flag, cotangent[0], other_core(cotangent[0]))
    back = [back_all[: LOCAL // 2], back_all[LOCAL // 2 :]]
    pair_all = jnp.concatenate([after(earlier, back_all), pair], axis=0)
    attended, logsum = attend(turn, core_of, query, pair_all, query_ids, key_ids)
    attended = attended.reshape(LOCAL, 2 * HEAD)
    mine = dot(attended[: LOCAL // 2], output_all, (1, 1)).astype(low)
    away = dot(attended[LOCAL // 2 :], output_all, (1, 1)).astype(low)
    middle = values + chip_sum(core_sum(mine, away))

    normed_two = gather_rows(rms_norm(middle, gain_two).astype(low))
    hidden, dexpanded = [], []
    for v, dy in zip(normed_two, back):
        expanded = dot(v, expand_all, (1, 0))
        activated, pull_act = jax.vjp(swiglu, expanded[:, :ff], expanded[:, ff:])
        hidden.append(activated.astype(low))
        dgate, dup = pull_act(dot(dy, shrink_all, (1, 0)))
        dexpanded.append(jnp.concatenate([dgate, dup], axis=1).astype(low))
    both_two = core_sum(*back_products(dexpanded, second_all))
    drows_two = chip_sum(both_two)
    second_grads = grads(
        [*after(tuple(normed_two), both_two), *back], [*dexpanded, *hidden]
    )
    second_red = lax.psum_scatter(second_grads, GROUP, scatter_dimension=0, tiled=True)
    drows_two = after(drows_two, second_grads)

    _, pull_two = jax.vjp(rms_norm, middle, gain_two)
    dmiddle, dgain_two = pull_two(drows_two)
    dmiddle = back[0][:BLOCK].astype(wide) + dmiddle
    shrunk = back_products(after(tuple(hidden), second_grads), second_all, at=2, hint=0)
    shrunk = shrunk[0], other_core(shrunk[1])
    dmiddle_all = gather_rows(dmiddle.astype(low))
    dmiddle_all = after(tuple(dmiddle_all), *shrunk)
    shrunk = chip_blocks(*after(shrunk, dmiddle_all), x)
    mlp = lax.all_to_all(shrunk, "x", 0, 0, tiled=True)
    dattended = jnp.stack([dot(v, output_all, (1, 0)).astype(low) for v in dmiddle_all])
    dquery, dpair = attend_back(
        turn,
        core_of,
        query,
        pair_all,
        query_ids,
        key_ids,
        dattended.reshape(2, 4, BLOCK, 2 * HEAD),
        logsum,
    )
    later = move(dpair[:BACK].astype(low), "yh", [(1, 0)])
    draw_query, dgain_query = heads_back(
        query_back_kernel, place, raw, cosine, sine, gain_query, dquery
    )
    spot = jnp.stack([half, yl, lax.axis_index("z")]).astype(jnp.int32)
    gain_row = gain_one.reshape(1, -1)
    left, dgain_one = query_grads(
        spot, normed, draw_query, first_all, gain_row, dmiddle_all, attended
    )
    left_grads = left
    left = sum_z(left)
    mlp = jnp.sum(after(mlp, *left_grads).astype(wide), axis=0)
    later = after(later, mlp)
    draw_pair, dgain_key = heads_back(
        pair_back_kernel, place, raw, cosine, sine, gain_key, dpair, later
    )
    outputs = trade((middle + after(mlp, draw_pair)).astype(low))

    pair_right, dgain_rest = pair_grads(spot, normed, draw_pair, first_all, gain_row)
    dgains = jnp.concatenate([(dgain_one + dgain_rest)[0], dgain_two, dgain_query[0], dgain_key[0]])
    dgains = jnp.pad(dgains.reshape(-1, BLOCK), ((0, 6), (0, 0)))
    dgains = dgains + other_core(dgains)
    dgains = dgains + shift(dgains, 1) + shift(dgains, 2) + shift(dgains, 3)
    dgains = dgains[:-6].astype(low).reshape(4, 2, 2, 1, -1)
    dgains = jnp.where(half == 0, dgains, dgains[:, :, ::-1])
    dgains = jnp.where(yl == 0, dgains, dgains[:, ::-1]).transpose(0, 2, 1, 3, 4)
    dgains = jnp.roll(dgains, -lax.axis_index("z"), axis=0)
    over = dgains[..., PART:]
    dgains = jnp.concatenate([dgains[..., :PART], jnp.pad(over, ((0, 0),) * 4 + ((0, PART - over.shape[-1]),))], axis=3)
    dgains = jnp.pad(dgains, ((0, 0), (0, 0), (0, 0), (0, 14), (0, 0)))
    right = lax.dynamic_update_slice(pair_right, dgains, (0, 0, 0, BLOCK, 0))
    mine, away = back_products(
        after((draw_query, draw_pair), dgain_rest), first_all, parts=True, hint=H_BACK
    )
    right = sum_z(right)
    drows_one = chip_sum_at_once(chip_blocks(mine, other_core(away), x))
    second_red = to_owner(second_red)
    expand_new, shrink_new = adam_weights(
        second_red,
        (((0, 2 * ff),), ((2 * ff, ff),)),
        [(expand_weight, expand_first, expand_second), (shrink_weight, shrink_first, shrink_second)],
        (False, True),
        (0.05, 0.03),
    )
    both = jnp.concatenate([jnp.pad(left, ((0, 0), (0, 0), (0, 16), (0, 0))), right], axis=3)
    first_red = sum_flips(both.astype(low))

    _, pull_one = jax.vjp(rms_norm, values, gain_one)
    dvalues, _ = pull_one(drows_one)
    input_grad = trade((dmiddle + dvalues).astype(low))

    dgains = first_red[BLOCK : BLOCK + 8, 2 * PART :]
    project_new, output_new, outputs, input_grad = adam_weights(
        first_red,
        (((0, PART), (2 * PART, PART)), ((PART, PART),)),
        [(project_weight, project_first, project_second), (output_weight, output_first, output_second)],
        (False, True),
        (0.05, 0.4),
        (outputs, input_grad),
    )
    dgains = dgains[:2].reshape(-1)[: gains.shape[0]]
    return (
        outputs[None],
        input_grad[None],
        *adam(gains, gains_first, gains_second, dgains, 0.5, 0.0),
        *project_new,
        *output_new,
        *expand_new,
        *shrink_new,
    )


def solution(mesh):
    fine = Mesh(mesh.devices.reshape(4, 2, 2, 4, 2), ("z", "core", "yh", "x", "yl"))
    tokens = P(("z", "core"), ("yh", "x", "yl"), None)
    marks = P(("z", "core"), None)
    gain = P(("z", "core", "yh"))
    tall = P(("z", "core", "yh"), ("x", "yl"))
    flat = P(("x", "yl"), ("z", "core", "yh"))
    in_specs = (
        tokens,
        P(("z", "core"), "yh", None),
        marks,
        marks,
        *[gain] * 3,
        *[tall] * 3,
        *[flat] * 3,
        *[tall] * 3,
        *[flat] * 3,
    )
    out_specs = (
        tokens,
        tokens,
        *[gain] * 3,
        *[tall] * 3,
        *[flat] * 3,
        *[tall] * 3,
        *[flat] * 3,
    )
    return jax.shard_map(
        per_device, mesh=fine, in_specs=in_specs, out_specs=out_specs, check_vma=False
    )
```

```python
import functools
import math

import jax
import jax.numpy as jnp
from jax import lax
from jax.experimental import pallas as pl
from jax.experimental.pallas import tpu as pltpu
from jax.sharding import Mesh
from jax.sharding import PartitionSpec as P

QUERY_HEADS = 16
KEY_VALUE_HEADS = 8
HEAD = 128
STEP = 5
LONGEST = 800
BLOCK = 128
LOCAL = 1024
BACK = 896
QUERIES = 256
WINDOW = BACK + QUERIES

epsilon = 1e-06
theta = 1000000.0
beta_first = 0.9
beta_second = 0.95
adam_epsilon = 1e-08
weight_decay = 0.1

low = jnp.bfloat16
wide = jnp.float32
MIB = 1024 * 1024
H_PROJECT = 1
H_ATTEND = 150
H_GRADS = 1
H_ATTEND_BACK = 47
H_HEADS_BACK = 1
H_BACK = 1
H_FIRST = 1
H_ADAM = 1

epsilon = 1e-06
theta = 1000000.0
beta_first = 0.9
beta_second = 0.95
adam_epsilon = 1e-08
weight_decay = 0.1

low = jnp.bfloat16
wide = jnp.float32
MIB = 1024 * 1024
ATTEND_HINT = 300
ATTEND_BACK_HINT = 260


def rms_norm(values, gain):
    return values * lax.rsqrt(jnp.mean(values * values, axis=-1, keepdims=True) + epsilon) * gain


def swiglu(gate, upward):
    return jax.nn.silu(gate) * upward


def adam(weight, first, second, grad, rate, decay_rate):
    mean = beta_first * first + (1.0 - beta_first) * grad
    square = beta_second * second + (1.0 - beta_second) * grad * grad
    mean_hat = mean / (1.0 - beta_first**STEP)
    square_hat = square / (1.0 - beta_second**STEP)
    updated = weight - rate * (
        mean_hat / (jnp.sqrt(square_hat) + adam_epsilon) + decay_rate * weight
    )
    return (mean, square, updated)


def dot(left, right, dims):
    return lax.dot_general(left, right, ((dims[:1], dims[1:]), ((), ())), preferred_element_type=wide)


def move(values, axis, pairs):
    return lax.ppermute(values, axis, pairs)


def shift(values, steps):
    return move(values, "x", [(i, (i + steps) % 4) for i in range(4)])


def other_core(values):
    return move(values, "core", [(0, 1), (1, 0)])


def trade(values):
    return move(values, ("core", "yl"), [(a * 2 + b, b * 2 + a) for a in range(2) for b in range(2)])


def to_group(values):
    pairs = [
        ((a * 2 + b) * 2 + d, (d * 2 + a) * 2 + b)
        for a in range(2)
        for b in range(2)
        for d in range(2)
    ]
    return move(values, ("core", "yh", "yl"), pairs)


def to_owner(values):
    pairs = [
        ((d * 2 + a) * 2 + b, (a * 2 + b) * 2 + d)
        for a in range(2)
        for b in range(2)
        for d in range(2)
    ]
    return move(values, ("core", "yh", "yl"), pairs)


def gather_rows(values, *others):
    pieces = (values, shift(values, 1), shift(values, 2), shift(values, 3))
    mine = jnp.concatenate(after(pieces, *others) if others else pieces, axis=0)
    return mine, other_core(mine)


def core_sum(mine, away):
    return (mine.astype(wide) + other_core(away).astype(wide)).astype(low)


def chip_sum(both):
    pieces = both.reshape(4, BLOCK, -1)
    total = pieces[0].astype(wide)
    for k in (2, 1, 3):
        total = total + shift(pieces[k], 4 - k).astype(wide)
    return total


def chip_blocks(mine, away, x):
    mine, away = mine.reshape(4, BLOCK, -1), away.reshape(4, BLOCK, -1)
    pick = lambda v, i: lax.dynamic_index_in_dim(v, lax.rem(x - i + 4, 4), 0).astype(wide)
    return jnp.concatenate([(pick(mine, i) + pick(away, i)).astype(low) for i in range(4)], axis=0)


def chip_sum_at_once(blocks):
    return jnp.sum(lax.all_to_all(blocks, "x", 0, 0, tiled=True).astype(wide), axis=0)


def after(values, *others):
    return lax.optimization_barrier((values, *others))[0]


def sum_z(pieces):
    total = pieces[0].astype(wide)
    for k in (2, 1, 3):
        there = move(pieces[k], "z", [(i, (i + k) % 4) for i in range(4)])
        total = total + there.astype(wide)
    return total


def flip(values, a, b):
    pairs = [
        ((c * 2 + h) * 2 + d, ((d ^ b) * 2 + (h ^ a)) * 2 + c)
        for c in range(2)
        for h in range(2)
        for d in range(2)
    ]
    return move(values, ("core", "yh", "yl"), pairs)


def sum_flips(pieces):
    total = 0.0
    for a in (1, 0):
        for b in (1, 0):
            total = total + flip(pieces[a, b], a, b).astype(wide)
    return total


GROUP = ("z", "yh", "yl")


def spec(shape, index):
    return pl.BlockSpec(shape, index)


def once(shape, index):
    return pl.BlockSpec(shape, index, pipeline_mode=pl.Buffered(1))


def params(mib):
    return pltpu.CompilerParams(vmem_limit_bytes=mib * MIB)


def cost(flops, moved, special=0, hint=1):
    return pl.CostEstimate(
        flops=flops * hint, bytes_accessed=moved * hint, transcendentals=special * hint
    )


def choose_kernel(place, flag, own, away, out, arrived):
    def copies(source):
        return [
            pltpu.make_async_copy(
                source.at[pl.ds(pl.multiple_of(place[i] * BLOCK, BLOCK), BLOCK)],
                out.at[pl.ds(i * BLOCK, BLOCK)],
                arrived.at[i],
            )
            for i in range(8)
        ]

    @pl.when(flag[0] == 1)
    def _():
        for copy in copies(own):
            copy.start()

    @pl.when(flag[0] == 0)
    def _():
        for copy in copies(away):
            copy.start()

    for copy in copies(own):
        copy.wait()


def choose(place, flag, own, away):
    scalar = pl.BlockSpec(memory_space=pltpu.SMEM)
    there = pl.BlockSpec(memory_space=pl.ANY)
    return pl.pallas_call(
        choose_kernel,
        out_shape=jax.ShapeDtypeStruct(own.shape, own.dtype),
        in_specs=[scalar, scalar, there, there],
        out_specs=there,
        scratch_shapes=[pltpu.SemaphoreType.DMA((8,))],
        compiler_params=params(4),
        cost_estimate=cost(0, 2 * own.size * 2),
    )(place, flag, own, away)


def project_kernel(
    place, mine, away, weight, gain, gq, gk, cosine, sine, normed, raw, scale, query, pair
):
    i = pl.program_id(0)

    def work(rows):
        v = rows[...].astype(wide)
        r = lax.rsqrt(jnp.mean(v * v, axis=-1, keepdims=True) + epsilon)
        n = (v * r * gain[...]).astype(low)
        normed[...] = n
        scale[...] = jnp.broadcast_to(r, scale.shape)
        raw[...] = dot(n, weight[...], (1, 0))

    pl.when(i < 2)(lambda: work(mine))
    pl.when(i >= 2)(lambda: work(away))
    for k in range(2):
        here = slice(k * BLOCK, (k + 1) * BLOCK)
        there = pl.ds(pl.multiple_of(place[2 * i + k] * BLOCK, BLOCK), BLOCK)
        c, s = cosine[there], sine[there]
        for h in range(4):
            part = slice(h * HEAD, (h + 1) * HEAD)
            v = raw[here, part]
            if h < 3:
                v = rms_norm(v, gq[...] if h < 2 else gk[...])
                v = v * c + pltpu.roll(v, HEAD // 2, 1) * s
            if h < 2:
                query[there, part] = v.astype(low)
            else:
                pair[there, (h - 2) * HEAD : (h - 1) * HEAD] = v.astype(low)


SCALARS = pl.BlockSpec(memory_space=pltpu.SMEM)
WHOLE = pl.BlockSpec(memory_space=pltpu.VMEM)


def project(place, rows, weight, gain, gq, gk, cosine, sine):
    width = rows[0].shape[1]
    fixed = lambda i, p: (0, 0)
    moving = lambda i, p: (i, 0)
    tall = 2 * BLOCK
    return pl.pallas_call(
        project_kernel,
        out_shape=[
            jax.ShapeDtypeStruct((LOCAL, width), low),
            jax.ShapeDtypeStruct((LOCAL, 4 * HEAD), wide),
            jax.ShapeDtypeStruct((LOCAL, HEAD), wide),
            jax.ShapeDtypeStruct((LOCAL, 2 * HEAD), low),
            jax.ShapeDtypeStruct((LOCAL, 2 * HEAD), low),
        ],
        grid_spec=pltpu.PrefetchScalarGridSpec(
            num_scalar_prefetch=1,
            grid=(LOCAL // tall,),
            in_specs=[
                spec((tall, width), lambda i, p: (jnp.minimum(i, 1), 0)),
                spec((tall, width), lambda i, p: (jnp.maximum(i - 2, 0), 0)),
                once((width, 4 * HEAD), fixed),
                once((1, width), fixed),
                once((1, HEAD), fixed),
                once((1, HEAD), fixed),
                once((LOCAL, HEAD), fixed),
                once((LOCAL, HEAD), fixed),
            ],
            out_specs=[
                spec((tall, width), moving),
                spec((tall, 4 * HEAD), moving),
                spec((tall, HEAD), moving),
                once((LOCAL, 2 * HEAD), fixed),
                once((LOCAL, 2 * HEAD), fixed),
            ],
        ),
        compiler_params=params(52),
        cost_estimate=cost(2 * LOCAL * width * 512, 16 * MIB, hint=H_PROJECT),
    )(place, *rows, weight, gain, gq, gk, cosine, sine)


def turn_back(d, v, c, s, g):
    d = d * c + pltpu.roll(d * s, HEAD // 2, 1)
    r = lax.rsqrt(jnp.mean(v * v, axis=-1, keepdims=True) + epsilon)
    u = v * r
    e = d * g
    before = r * (e - u * jnp.mean(u * e, axis=-1, keepdims=True))
    return before.astype(low), jnp.sum(d * u, axis=0, keepdims=True)


def query_back_kernel(place, raw, cosine, sine, gq, dquery, draw, dgain):
    total = 0.0
    for i in range(8):
        here = pl.ds(i * BLOCK, BLOCK)
        there = pl.ds(pl.multiple_of(place[i] * BLOCK, BLOCK), BLOCK)
        for h in range(2):
            part = slice(h * HEAD, (h + 1) * HEAD)
            draw[here, part], add = turn_back(
                dquery[there, part], raw[here, part], cosine[there], sine[there], gq[...]
            )
            total += add
    dgain[...] = jnp.broadcast_to(total, dgain.shape)


def pair_back_kernel(place, raw, cosine, sine, gk, dpair, later, draw, dgain):
    total = 0.0
    for i in range(8):
        here = pl.ds(i * BLOCK, BLOCK)
        there = pl.ds(pl.multiple_of(place[i] * BLOCK, BLOCK), BLOCK)
        dp = dpair[pl.ds(pl.multiple_of(place[i] * BLOCK + BACK, BLOCK), BLOCK)]
        from_later = later[pl.ds(pl.multiple_of(jnp.maximum(place[i] - 1, 0) * BLOCK, BLOCK), BLOCK)]
        dp = dp + jnp.where(place[i] > 0, from_later.astype(wide), 0.0)
        draw[here, :HEAD], add = turn_back(
            dp[:, :HEAD], raw[here, 2 * HEAD : 3 * HEAD], cosine[there], sine[there], gk[...]
        )
        draw[here, HEAD:] = dp[:, HEAD:].astype(low)
        total += add
    dgain[...] = jnp.broadcast_to(total, dgain.shape)


def heads_back(kernel, place, *inputs):
    return pl.pallas_call(
        kernel,
        out_shape=[
            jax.ShapeDtypeStruct((LOCAL, 2 * HEAD), low),
            jax.ShapeDtypeStruct((8, HEAD), wide),
        ],
        in_specs=[SCALARS] + [WHOLE] * len(inputs),
        out_specs=[WHOLE] * 2,
        compiler_params=params(16),
        cost_estimate=cost(LOCAL * 512 * 10, LOCAL * 512 * 6, hint=H_HEADS_BACK),
    )(place, *inputs)


ROWS = 256


def both_dots(lefts, rights, dims):
    return dot(lefts[0][...], rights[0][...], dims) + dot(lefts[1][...], rights[1][...], dims)


def grads_kernel(*refs):
    lefts, rights, out = refs[:4], refs[4:8], refs[8]
    n = rights[0].shape[1]
    out[:, :n] = both_dots(lefts[:2], rights[:2], (0, 0)).astype(low)
    out[:, n:] = both_dots(lefts[2:], rights[2:], (0, 0)).astype(low)


def grads(lefts, rights):
    depth, rows = lefts[0].shape
    total = rights[0].shape[1] + rights[2].shape[1]
    return pl.pallas_call(
        grads_kernel,
        out_shape=jax.ShapeDtypeStruct((rows, total), low),
        grid=(rows // ROWS,),
        in_specs=[spec((depth, ROWS), lambda i: (0, i))] * 4
        + [once(v.shape, lambda i: (0, 0)) for v in rights],
        out_specs=spec((ROWS, total), lambda i: (i, 0)),
        compiler_params=params(28),
        cost_estimate=cost(
            4 * depth * rows * total, 8 * depth * rows + 2 * total * (rows + depth), hint=H_GRADS
        ),
    )(*lefts, *rights)


def back_kernel(parts, *refs):
    *lefts, right, out_mine, out_away = refs
    turned = right[...].T
    half = LOCAL // 2
    if parts:
        depth = lefts[0].shape[1]
        pick = lambda rows: sum(
            dot(left[rows], turned[k * depth : (k + 1) * depth], (1, 0))
            for k, left in enumerate(lefts)
        )
        mine, away = pick(pl.ds(0, half)), pick(pl.ds(half, half))
    else:
        mine, away = [dot(left[...], turned, (1, 0)) for left in lefts]
    out_away[...] = away.astype(low)
    out_mine[...] = mine.astype(low)


def back_products(lefts, right, at=0, parts=False, hint=1):
    rows = LOCAL // 2
    depth = sum(v.shape[1] for v in lefts) if parts else lefts[0].shape[1]
    width = right.shape[0]
    return pl.pallas_call(
        functools.partial(back_kernel, parts),
        out_shape=[jax.ShapeDtypeStruct((rows, width), low)] * 2,
        grid=(width // ROWS,),
        in_specs=[once(v.shape, lambda i: (0, 0)) for v in lefts]
        + [spec((ROWS, depth), lambda i: (i, at))],
        out_specs=[spec((rows, ROWS), lambda i: (0, i))] * 2,
        compiler_params=params(20),
        cost_estimate=cost(
            4 * rows * depth * width, 2 * width * (depth + 2 * rows), hint=hint
        ),
    )(*lefts, right)


def adam_kernel(columns, flipped, rates, extras, *refs):
    grad = refs[0]
    for k, (turn, rate) in enumerate(zip(flipped, rates)):
        weight, first, second = refs[1 + 3 * k : 4 + 3 * k]
        outs = refs[1 + extras + 3 * (len(rates) + k) : 4 + extras + 3 * (len(rates) + k)]
        g = [grad[:BLOCK, at : at + n] for at, n in columns[k]]
        g = (jnp.concatenate(g, axis=1) if len(g) > 1 else g[0]).astype(wide)
        if turn:
            g = g.T
        for out, value in zip(outs, adam(weight[...], first[...], second[...], g, rate, weight_decay)):
            out[...] = value
    for k in range(extras):
        refs[k - extras][...] = refs[1 + 3 * len(rates) + k][...]


def adam_weights(grad, columns, weights, flipped, rates, extras=()):
    states = [v for group in weights for v in group] + list(extras)
    out = pl.pallas_call(
        functools.partial(adam_kernel, columns, flipped, rates, len(extras)),
        out_shape=[jax.ShapeDtypeStruct(v.shape, v.dtype) for v in states],
        in_specs=[WHOLE] * (1 + len(states)),
        out_specs=[WHOLE] * len(states),
        compiler_params=params(24),
        cost_estimate=cost(20 * grad.size, 26 * grad.size, hint=H_ADAM),
    )(grad, *states)
    return [tuple(out[3 * k : 3 * k + 3]) for k in range(len(weights))] + list(out[3 * len(weights) :])


PART = 2 * HEAD
TALL = BLOCK + 16


def project_grad(normed, draw, weight, gain, dgain):
    project = dot(normed[...], draw[...], (0, 0))
    product = (project * weight[...].astype(wide)).astype(low)
    dgain[...] = dot(jnp.ones((8, PART), low), product, (1, 1)) / gain[...]
    return project.astype(low)


def query_grads_kernel(spot, normed, draw, weight, gain, mine, away, attended, *outs):
    *outs, dgain = outs
    project = project_grad(normed, draw, weight, gain, dgain)
    half = LOCAL // 2
    output = dot(mine[...], attended[:half], (0, 0)) + dot(away[...], attended[half:], (0, 0))
    output = output.astype(low)
    i = pl.program_id(0)
    steps = lax.rem(i // 2 - spot[2] + 4, 4)
    for k, out in enumerate(outs):

        @pl.when(steps == k)
        def _():
            for j in range(2):
                rows = slice(j * BLOCK, (j + 1) * BLOCK)
                out[j ^ spot[0], i % 2 ^ spot[1], :, :PART] = project[rows]
                out[j ^ spot[0], i % 2 ^ spot[1], :, PART:] = output[rows]


def pair_grads_kernel(spot, normed, draw, weight, gain, out, dgain):
    project = project_grad(normed, draw, weight, gain, dgain)
    for j in range(2):
        out[0, j ^ spot[0], 0, :BLOCK] = project[j * BLOCK : (j + 1) * BLOCK]


def first_grads(spot, normed, draw, weight, gain, part, out, block, others=()):
    whole = lambda i, s: (0, 0)
    columns = lambda i, s: (0, i)
    rows = 2 * BLOCK
    return pl.pallas_call(
        query_grads_kernel if others else pair_grads_kernel,
        out_shape=[jax.ShapeDtypeStruct(v, low) for v in out]
        + [jax.ShapeDtypeStruct((8, 16 * BLOCK), wide)],
        grid_spec=pltpu.PrefetchScalarGridSpec(
            num_scalar_prefetch=1,
            grid=(8,),
            in_specs=[
                spec((LOCAL, rows), columns),
                once((LOCAL, PART), whole),
                spec((rows, PART), lambda i, s: (i, part)),
                spec((1, rows), columns),
            ]
            + [spec((LOCAL // 2, rows), columns)] * len(others[:2])
            + [once((LOCAL, PART), whole)] * len(others[2:]),
            out_specs=[spec(*v) for v in block] + [spec((8, rows), columns)],
        ),
        compiler_params=params(24),
        cost_estimate=cost(2 * LOCAL * 2048 * 256, 8 * MIB, hint=H_FIRST),
    )(spot, normed, draw, weight, gain, *others)


def query_grads(spot, normed, draw, weight, gain, dmiddle, attended):
    shape = (2, 2, BLOCK, 2 * PART)
    outs = [shape] * 4, [(shape, lambda i, s: (0, 0, 0, 0))] * 4
    *left, dgain = first_grads(
        spot, normed, draw, weight, gain, 0, *outs, (*dmiddle, attended)
    )
    return left, dgain


def pair_grads(spot, normed, draw, weight, gain):
    place = lambda i, s: (lax.rem(i // 2 - s[2] + 4, 4), 0, i % 2 ^ s[1], 0, 0)
    outs = [(4, 2, 2, TALL, PART)], [((1, 2, 1, TALL, PART), place)]
    return first_grads(spot, normed, draw, weight, gain, 1, *outs)


SCALE = HEAD ** (-0.5)


def allowed(query_ids, key_ids, start):
    keys = key_ids[:, pl.ds(start, WINDOW)]
    row = lax.broadcasted_iota(jnp.int32, (QUERIES, WINDOW), 0)
    column = lax.broadcasted_iota(jnp.int32, (QUERIES, WINDOW), 1)
    return (query_ids[...] == keys) & (column <= row + BACK)


def attend_kernel(turn, core, query, pair, query_ids, key_ids, out, logsum):
    i = pl.program_id(0)
    start = pl.multiple_of(i * QUERIES, QUERIES)
    mask = allowed(query_ids, key_ids, start)
    logs = []
    for h in range(2):
        part = slice(h * HEAD, (h + 1) * HEAD)
        scores = dot(query[:, part], pair[pl.ds(start, WINDOW), :HEAD], (1, 1)) * SCALE
        scores = jnp.where(mask, scores, -1e30)
        top = jnp.max(scores, axis=-1, keepdims=True)
        unnormed = jnp.exp(scores - top)
        total = jnp.sum(unnormed, axis=-1, keepdims=True)
        probs = (unnormed * (1.0 / total)).astype(low)
        result = dot(probs, pair[pl.ds(start, WINDOW), HEAD:], (1, 0)).astype(low)
        for j in range(2):
            out[j ^ core[0], 0, :, part] = result[j * BLOCK : (j + 1) * BLOCK]
        logs.append(top + jnp.log(total))
    lane = lax.broadcasted_iota(jnp.int32, (QUERIES, HEAD), 1)
    logsum[...] = jnp.where(lane < HEAD // 2, logs[0], logs[1])


def attend(turn, core, query, pair, query_ids, key_ids):
    rows = lambda i, t, c: (i, 0)
    whole = lambda i, t, c: (0, 0)
    keys = BACK + LOCAL
    return pl.pallas_call(
        attend_kernel,
        out_shape=[
            jax.ShapeDtypeStruct((2, 4, BLOCK, 2 * HEAD), low),
            jax.ShapeDtypeStruct((LOCAL, HEAD), wide),
        ],
        grid_spec=pltpu.PrefetchScalarGridSpec(
            num_scalar_prefetch=2,
            grid=(LOCAL // QUERIES,),
            in_specs=[
                spec((QUERIES, 2 * HEAD), rows),
                once((keys, 2 * HEAD), whole),
                spec((QUERIES, 1), rows),
                spec((1, keys), whole),
            ],
            out_specs=[
                spec((2, 1, BLOCK, 2 * HEAD), lambda i, t, c: (0, t[i], 0, 0)),
                spec((QUERIES, HEAD), rows),
            ],
        ),
        compiler_params=params(24),
        cost_estimate=cost(
            8 * LOCAL * WINDOW * HEAD, 4 * LOCAL * 512, 2 * LOCAL * WINDOW, hint=H_ATTEND
        ),
    )(turn, core, query, pair, query_ids, key_ids)


def attend_back_kernel(
    turn, core, query, pair, query_ids, key_ids, grad, logsum, dquery, dpair
):
    i = pl.program_id(0)

    @pl.when(i == 0)
    def _():
        dpair[...] = jnp.zeros_like(dpair)

    start = pl.multiple_of(i * QUERIES, QUERIES)
    window = pl.ds(start, WINDOW)
    mask = allowed(query_ids, key_ids, start)
    dkey, dvalue = None, None
    for h in range(2):
        part = slice(h * HEAD, (h + 1) * HEAD)
        q = query[:, part]
        g = jnp.concatenate([grad[j ^ core[0], 0, :, part] for j in range(2)], axis=0)
        scores = dot(q, pair[window, :HEAD], (1, 1)) * SCALE
        probs = jnp.where(mask, jnp.exp(scores - logsum[:, h * 64 : h * 64 + 1]), 0.0)
        dprobs = dot(g, pair[window, HEAD:], (1, 1))
        inner = jnp.sum(probs * dprobs, axis=-1, keepdims=True)
        dscores = (probs * (dprobs - inner)).astype(low)
        dquery[:, part] = dot(dscores, pair[window, :HEAD], (1, 0)) * SCALE
        dv = dot(probs.astype(low), g, (0, 0))
        dk = dot(dscores, q, (0, 0))
        dkey = dk if dkey is None else dkey + dk
        dvalue = dv if dvalue is None else dvalue + dv
    dpair[window, :HEAD] += dkey * SCALE
    dpair[window, HEAD:] += dvalue


def attend_back(turn, core, query, pair, query_ids, key_ids, grad, logsum):
    rows = lambda i, t, c: (i, 0)
    whole = lambda i, t, c: (0, 0)
    keys = BACK + LOCAL
    return pl.pallas_call(
        attend_back_kernel,
        out_shape=[
            jax.ShapeDtypeStruct((LOCAL, 2 * HEAD), wide),
            jax.ShapeDtypeStruct((keys, 2 * HEAD), wide),
        ],
        grid_spec=pltpu.PrefetchScalarGridSpec(
            num_scalar_prefetch=2,
            grid=(LOCAL // QUERIES,),
            in_specs=[
                spec((QUERIES, 2 * HEAD), rows),
                once((keys, 2 * HEAD), whole),
                spec((QUERIES, 1), rows),
                spec((1, keys), whole),
                spec((2, 1, BLOCK, 2 * HEAD), lambda i, t, c: (0, t[i], 0, 0)),
                spec((QUERIES, HEAD), rows),
            ],
            out_specs=[spec((QUERIES, 2 * HEAD), rows), once((keys, 2 * HEAD), whole)],
        ),
        compiler_params=params(28),
        cost_estimate=cost(
            20 * LOCAL * WINDOW * HEAD, 8 * LOCAL * 512, 2 * LOCAL * WINDOW, hint=H_ATTEND_BACK
        ),
    )(turn, core, query, pair, query_ids, key_ids, grad, logsum)


def per_device(
    inputs,
    cotangent,
    document_index,
    positions,
    gains,
    gains_first,
    gains_second,
    project_weight,
    project_first,
    project_second,
    output_weight,
    output_first,
    output_second,
    expand_weight,
    expand_first,
    expand_second,
    shrink_weight,
    shrink_first,
    shrink_second,
):
    core, x = lax.axis_index("core"), lax.axis_index("x")
    half, yl = lax.axis_index("yh"), lax.axis_index("yl")
    width = inputs.shape[-1]
    qkv = project_weight.shape[1]
    ff = shrink_weight.shape[0]
    at_home = core == yl
    steps = jnp.arange(8, dtype=jnp.int32)
    place = lax.rem(x - steps % 4 + 4, 4) * 2 + (core ^ (steps // 4))
    turn = lax.rem(x - jnp.arange(4, dtype=jnp.int32) + 4, 4)
    core_of = core.reshape(1).astype(jnp.int32)
    flag = at_home.astype(jnp.int32).reshape(1)

    marks = jnp.stack([document_index[0], positions[0] // 32, positions[0] % 32])
    marks = jnp.pad(marks.astype(low), ((0, 13), (0, 0)))
    message = trade(jnp.concatenate([inputs[0], marks], axis=0))
    rows = message[:BLOCK]
    marks = message[BLOCK:].astype(jnp.int32)
    ids, places = marks[0], marks[1] * 32 + marks[2]

    gain_block = jnp.pad(gains.astype(low), (0, BLOCK * BLOCK - gains.shape[0])).reshape(BLOCK, BLOCK)
    first_shard = jnp.concatenate(
        [project_weight.astype(low), output_weight.astype(low).T, gain_block], axis=1
    )
    second_shard = jnp.concatenate([expand_weight.astype(low), shrink_weight.astype(low).T], axis=1)
    first_all = lax.all_gather(to_group(first_shard), GROUP, axis=0, tiled=True)
    second_shard = to_group(after(second_shard, message))
    rows_all = gather_rows(rows, second_shard)
    second_all = lax.all_gather(after(second_shard, first_all), GROUP, axis=0, tiled=True)
    project_all = first_all[:, :qkv]
    output_all = first_all[:, qkv : qkv + 2 * HEAD]
    expand_all = second_all[:, : 2 * ff]
    shrink_all = second_all[:, 2 * ff :]
    gain_all = first_all.reshape(16, BLOCK, -1)[:, :3, qkv + 2 * HEAD :].reshape(16, 3 * BLOCK)
    gain_all = gain_all[:, : gains.shape[0]].reshape(-1).astype(wide)
    gain_one = gain_all[:width]
    gain_two = gain_all[width : 2 * width]
    gain_query = gain_all[2 * width : 2 * width + HEAD].reshape(1, HEAD)
    gain_key = gain_all[2 * width + HEAD :].reshape(1, HEAD)

    ids_here = lax.dynamic_slice_in_dim(ids, half * LOCAL, LOCAL)
    places_here = lax.dynamic_slice_in_dim(places, half * LOCAL, LOCAL)
    ids_keys = jnp.where(
        half == 0,
        jnp.concatenate([jnp.full((BACK,), -1, jnp.int32), ids[:LOCAL]]),
        ids[LOCAL - BACK :],
    )
    query_ids, key_ids = ids_here.reshape(-1, 1), ids_keys.reshape(1, -1)
    frequency = jnp.exp(jnp.arange(HEAD // 2, dtype=wide) * (-2.0 * math.log(theta) / HEAD))
    angle = places_here.astype(wide)[:, None] * frequency
    cosine, sine = jnp.cos(angle), jnp.sin(angle)
    cosine = jnp.concatenate([cosine, cosine], axis=1)
    sine = jnp.concatenate([-sine, sine], axis=1)

    values = rows.astype(wide)
    normed, raw, scale, query, pair = project(
        place, rows_all, first_all, gain_one.reshape(1, -1), gain_query, gain_key, cosine, sine
    )
    earlier = move(pair[LOCAL - BACK :], "yh", [(0, 1)])
    back_all = choose(place, flag, cotangent[0], other_core(cotangent[0]))
    back = [back_all[: LOCAL // 2], back_all[LOCAL // 2 :]]
    pair_all = jnp.concatenate([after(earlier, back_all), pair], axis=0)
    attended, logsum = attend(turn, core_of, query, pair_all, query_ids, key_ids)
    attended = attended.reshape(LOCAL, 2 * HEAD)
    mine = dot(attended[: LOCAL // 2], output_all, (1, 1)).astype(low)
    away = dot(attended[LOCAL // 2 :], output_all, (1, 1)).astype(low)
    middle = values + chip_sum(core_sum(mine, away))

    normed_two = gather_rows(rms_norm(middle, gain_two).astype(low))
    hidden, dexpanded = [], []
    for v, dy in zip(normed_two, back):
        expanded = dot(v, expand_all, (1, 0))
        activated, pull_act = jax.vjp(swiglu, expanded[:, :ff], expanded[:, ff:])
        hidden.append(activated.astype(low))
        dgate, dup = pull_act(dot(dy, shrink_all, (1, 0)))
        dexpanded.append(jnp.concatenate([dgate, dup], axis=1).astype(low))
    both_two = core_sum(*back_products(dexpanded, second_all))
    drows_two = chip_sum(both_two)
    second_grads = grads(
        [*after(tuple(normed_two), both_two), *back], [*dexpanded, *hidden]
    )
    second_red = lax.psum_scatter(second_grads, GROUP, scatter_dimension=0, tiled=True)
    drows_two = after(drows_two, second_grads)

    _, pull_two = jax.vjp(rms_norm, middle, gain_two)
    dmiddle, dgain_two = pull_two(drows_two)
    dmiddle = back[0][:BLOCK].astype(wide) + dmiddle
    shrunk = back_products(after(tuple(hidden), second_grads), second_all, at=2, hint=0)
    shrunk = shrunk[0], other_core(shrunk[1])
    dmiddle_all = gather_rows(dmiddle.astype(low))
    dmiddle_all = after(tuple(dmiddle_all), *shrunk)
    shrunk = chip_blocks(*after(shrunk, dmiddle_all), x)
    mlp = lax.all_to_all(shrunk, "x", 0, 0, tiled=True)
    dattended = jnp.stack([dot(v, output_all, (1, 0)).astype(low) for v in dmiddle_all])
    dquery, dpair = attend_back(
        turn,
        core_of,
        query,
        pair_all,
        query_ids,
        key_ids,
        dattended.reshape(2, 4, BLOCK, 2 * HEAD),
        logsum,
    )
    later = move(dpair[:BACK].astype(low), "yh", [(1, 0)])
    draw_query, dgain_query = heads_back(
        query_back_kernel, place, raw, cosine, sine, gain_query, dquery
    )
    spot = jnp.stack([half, yl, lax.axis_index("z")]).astype(jnp.int32)
    gain_row = gain_one.reshape(1, -1)
    left, dgain_one = query_grads(
        spot, normed, draw_query, first_all, gain_row, dmiddle_all, attended
    )
    left_grads = left
    left = sum_z(left)
    mlp = jnp.sum(after(mlp, *left_grads).astype(wide), axis=0)
    later = after(later, mlp)
    draw_pair, dgain_key = heads_back(
        pair_back_kernel, place, raw, cosine, sine, gain_key, dpair, later
    )
    outputs = trade((middle + after(mlp, draw_pair)).astype(low))

    pair_right, dgain_rest = pair_grads(spot, normed, draw_pair, first_all, gain_row)
    dgains = jnp.concatenate([(dgain_one + dgain_rest)[0], dgain_two, dgain_query[0], dgain_key[0]])
    dgains = jnp.pad(dgains.reshape(-1, BLOCK), ((0, 6), (0, 0)))
    dgains = dgains + other_core(dgains)
    dgains = dgains + shift(dgains, 1) + shift(dgains, 2) + shift(dgains, 3)
    dgains = dgains[:-6].astype(low).reshape(4, 2, 2, 1, -1)
    dgains = jnp.where(half == 0, dgains, dgains[:, :, ::-1])
    dgains = jnp.where(yl == 0, dgains, dgains[:, ::-1]).transpose(0, 2, 1, 3, 4)
    dgains = jnp.roll(dgains, -lax.axis_index("z"), axis=0)
    over = dgains[..., PART:]
    dgains = jnp.concatenate([dgains[..., :PART], jnp.pad(over, ((0, 0),) * 4 + ((0, PART - over.shape[-1]),))], axis=3)
    dgains = jnp.pad(dgains, ((0, 0), (0, 0), (0, 0), (0, 14), (0, 0)))
    right = lax.dynamic_update_slice(pair_right, dgains, (0, 0, 0, BLOCK, 0))
    second_red = to_owner(after(second_red, draw_pair))
    mine, away = back_products(
        after((draw_query, draw_pair), dgain_rest, second_red), first_all, parts=True, hint=H_BACK
    )
    right = sum_z(right)
    drows_one = chip_sum_at_once(chip_blocks(mine, other_core(away), x))
    expand_new, shrink_new = adam_weights(
        second_red,
        (((0, 2 * ff),), ((2 * ff, ff),)),
        [(expand_weight, expand_first, expand_second), (shrink_weight, shrink_first, shrink_second)],
        (False, True),
        (0.05, 0.03),
    )
    both = jnp.concatenate([jnp.pad(left, ((0, 0), (0, 0), (0, 16), (0, 0))), right], axis=3)
    first_red = sum_flips(both.astype(low))

    _, pull_one = jax.vjp(rms_norm, values, gain_one)
    dvalues, _ = pull_one(drows_one)
    input_grad = trade((dmiddle + dvalues).astype(low))

    dgains = first_red[BLOCK : BLOCK + 8, 2 * PART :]
    project_new, output_new, outputs, input_grad = adam_weights(
        first_red,
        (((0, PART), (2 * PART, PART)), ((PART, PART),)),
        [(project_weight, project_first, project_second), (output_weight, output_first, output_second)],
        (False, True),
        (0.05, 0.4),
        (outputs, input_grad),
    )
    dgains = dgains[:2].reshape(-1)[: gains.shape[0]]
    return (
        outputs[None],
        input_grad[None],
        *adam(gains, gains_first, gains_second, dgains, 0.5, 0.0),
        *project_new,
        *output_new,
        *expand_new,
        *shrink_new,
    )


def solution(mesh):
    fine = Mesh(mesh.devices.reshape(4, 2, 2, 4, 2), ("z", "core", "yh", "x", "yl"))
    tokens = P(("z", "core"), ("yh", "x", "yl"), None)
    marks = P(("z", "core"), None)
    gain = P(("z", "core", "yh"))
    tall = P(("z", "core", "yh"), ("x", "yl"))
    flat = P(("x", "yl"), ("z", "core", "yh"))
    in_specs = (
        tokens,
        P(("z", "core"), "yh", None),
        marks,
        marks,
        *[gain] * 3,
        *[tall] * 3,
        *[flat] * 3,
        *[tall] * 3,
        *[flat] * 3,
    )
    out_specs = (
        tokens,
        tokens,
        *[gain] * 3,
        *[tall] * 3,
        *[flat] * 3,
        *[tall] * 3,
        *[flat] * 3,
    )
    return jax.shard_map(
        per_device, mesh=fine, in_specs=in_specs, out_specs=out_specs, check_vma=False
    )
```

```python
import functools
import math

import jax
import jax.numpy as jnp
from jax import lax
from jax.experimental import pallas as pl
from jax.experimental.pallas import tpu as pltpu
from jax.sharding import Mesh
from jax.sharding import PartitionSpec as P

QUERY_HEADS = 16
KEY_VALUE_HEADS = 8
HEAD = 128
STEP = 5
LONGEST = 800
BLOCK = 128
LOCAL = 1024
BACK = 896
QUERIES = 256
WINDOW = BACK + QUERIES

epsilon = 1e-06
theta = 1000000.0
beta_first = 0.9
beta_second = 0.95
adam_epsilon = 1e-08
weight_decay = 0.1

low = jnp.bfloat16
wide = jnp.float32
MIB = 1024 * 1024
H_PROJECT = 1
H_ATTEND = 150
H_GRADS = 1
H_ATTEND_BACK = 47
H_HEADS_BACK = 1
H_BACK = 1
H_FIRST = 1
H_ADAM = 1

epsilon = 1e-06
theta = 1000000.0
beta_first = 0.9
beta_second = 0.95
adam_epsilon = 1e-08
weight_decay = 0.1

low = jnp.bfloat16
wide = jnp.float32
MIB = 1024 * 1024
ATTEND_HINT = 300
ATTEND_BACK_HINT = 260


def rms_norm(values, gain):
    return values * lax.rsqrt(jnp.mean(values * values, axis=-1, keepdims=True) + epsilon) * gain


def swiglu(gate, upward):
    return jax.nn.silu(gate) * upward


def adam(weight, first, second, grad, rate, decay_rate):
    mean = beta_first * first + (1.0 - beta_first) * grad
    square = beta_second * second + (1.0 - beta_second) * grad * grad
    mean_hat = mean / (1.0 - beta_first**STEP)
    square_hat = square / (1.0 - beta_second**STEP)
    updated = weight - rate * (
        mean_hat / (jnp.sqrt(square_hat) + adam_epsilon) + decay_rate * weight
    )
    return (mean, square, updated)


def dot(left, right, dims):
    return lax.dot_general(left, right, ((dims[:1], dims[1:]), ((), ())), preferred_element_type=wide)


def move(values, axis, pairs):
    return lax.ppermute(values, axis, pairs)


def shift(values, steps):
    return move(values, "x", [(i, (i + steps) % 4) for i in range(4)])


def other_core(values):
    return move(values, "core", [(0, 1), (1, 0)])


def trade(values):
    return move(values, ("core", "yl"), [(a * 2 + b, b * 2 + a) for a in range(2) for b in range(2)])


def to_group(values):
    pairs = [
        ((a * 2 + b) * 2 + d, (d * 2 + a) * 2 + b)
        for a in range(2)
        for b in range(2)
        for d in range(2)
    ]
    return move(values, ("core", "yh", "yl"), pairs)


def to_owner(values):
    pairs = [
        ((d * 2 + a) * 2 + b, (a * 2 + b) * 2 + d)
        for a in range(2)
        for b in range(2)
        for d in range(2)
    ]
    return move(values, ("core", "yh", "yl"), pairs)


def gather_rows(values, *others):
    pieces = (values, shift(values, 1), shift(values, 2), shift(values, 3))
    mine = jnp.concatenate(after(pieces, *others) if others else pieces, axis=0)
    return mine, other_core(mine)


def core_sum(mine, away):
    return (mine.astype(wide) + other_core(away).astype(wide)).astype(low)


def chip_sum(both):
    pieces = both.reshape(4, BLOCK, -1)
    total = pieces[0].astype(wide)
    for k in (2, 1, 3):
        total = total + shift(pieces[k], 4 - k).astype(wide)
    return total


def chip_blocks(mine, away, x):
    mine, away = mine.reshape(4, BLOCK, -1), away.reshape(4, BLOCK, -1)
    pick = lambda v, i: lax.dynamic_index_in_dim(v, lax.rem(x - i + 4, 4), 0).astype(wide)
    return jnp.concatenate([(pick(mine, i) + pick(away, i)).astype(low) for i in range(4)], axis=0)


def chip_sum_at_once(blocks):
    return jnp.sum(lax.all_to_all(blocks, "x", 0, 0, tiled=True).astype(wide), axis=0)


def after(values, *others):
    return lax.optimization_barrier((values, *others))[0]


def sum_z(pieces):
    total = pieces[0].astype(wide)
    for k in (2, 1, 3):
        there = move(pieces[k], "z", [(i, (i + k) % 4) for i in range(4)])
        total = total + there.astype(wide)
    return total


def flip(values, a, b):
    pairs = [
        ((c * 2 + h) * 2 + d, ((d ^ b) * 2 + (h ^ a)) * 2 + c)
        for c in range(2)
        for h in range(2)
        for d in range(2)
    ]
    return move(values, ("core", "yh", "yl"), pairs)


def sum_flips(pieces):
    total = 0.0
    for a in (1, 0):
        for b in (1, 0):
            total = total + flip(pieces[a, b], a, b).astype(wide)
    return total


GROUP = ("z", "yh", "yl")


def spec(shape, index):
    return pl.BlockSpec(shape, index)


def once(shape, index):
    return pl.BlockSpec(shape, index, pipeline_mode=pl.Buffered(1))


def params(mib):
    return pltpu.CompilerParams(vmem_limit_bytes=mib * MIB)


def cost(flops, moved, special=0, hint=1):
    return pl.CostEstimate(
        flops=flops * hint, bytes_accessed=moved * hint, transcendentals=special * hint
    )


def choose_kernel(place, flag, own, away, out, arrived):
    def copies(source):
        return [
            pltpu.make_async_copy(
                source.at[pl.ds(pl.multiple_of(place[i] * BLOCK, BLOCK), BLOCK)],
                out.at[pl.ds(i * BLOCK, BLOCK)],
                arrived.at[i],
            )
            for i in range(8)
        ]

    @pl.when(flag[0] == 1)
    def _():
        for copy in copies(own):
            copy.start()

    @pl.when(flag[0] == 0)
    def _():
        for copy in copies(away):
            copy.start()

    for copy in copies(own):
        copy.wait()


def choose(place, flag, own, away):
    scalar = pl.BlockSpec(memory_space=pltpu.SMEM)
    there = pl.BlockSpec(memory_space=pl.ANY)
    return pl.pallas_call(
        choose_kernel,
        out_shape=jax.ShapeDtypeStruct(own.shape, own.dtype),
        in_specs=[scalar, scalar, there, there],
        out_specs=there,
        scratch_shapes=[pltpu.SemaphoreType.DMA((8,))],
        compiler_params=params(4),
        cost_estimate=cost(0, 2 * own.size * 2),
    )(place, flag, own, away)


def project_kernel(
    place, mine, away, weight, gain, gq, gk, cosine, sine, normed, raw, scale, query, pair
):
    i = pl.program_id(0)

    def work(rows):
        v = rows[...].astype(wide)
        r = lax.rsqrt(jnp.mean(v * v, axis=-1, keepdims=True) + epsilon)
        n = (v * r * gain[...]).astype(low)
        normed[...] = n
        scale[...] = jnp.broadcast_to(r, scale.shape)
        raw[...] = dot(n, weight[...], (1, 0))

    pl.when(i < 2)(lambda: work(mine))
    pl.when(i >= 2)(lambda: work(away))
    for k in range(2):
        here = slice(k * BLOCK, (k + 1) * BLOCK)
        there = pl.ds(pl.multiple_of(place[2 * i + k] * BLOCK, BLOCK), BLOCK)
        c, s = cosine[there], sine[there]
        for h in range(4):
            part = slice(h * HEAD, (h + 1) * HEAD)
            v = raw[here, part]
            if h < 3:
                v = rms_norm(v, gq[...] if h < 2 else gk[...])
                v = v * c + pltpu.roll(v, HEAD // 2, 1) * s
            if h < 2:
                query[there, part] = v.astype(low)
            else:
                pair[there, (h - 2) * HEAD : (h - 1) * HEAD] = v.astype(low)


SCALARS = pl.BlockSpec(memory_space=pltpu.SMEM)
WHOLE = pl.BlockSpec(memory_space=pltpu.VMEM)


def project(place, rows, weight, gain, gq, gk, cosine, sine):
    width = rows[0].shape[1]
    fixed = lambda i, p: (0, 0)
    moving = lambda i, p: (i, 0)
    tall = 2 * BLOCK
    return pl.pallas_call(
        project_kernel,
        out_shape=[
            jax.ShapeDtypeStruct((LOCAL, width), low),
            jax.ShapeDtypeStruct((LOCAL, 4 * HEAD), wide),
            jax.ShapeDtypeStruct((LOCAL, HEAD), wide),
            jax.ShapeDtypeStruct((LOCAL, 2 * HEAD), low),
            jax.ShapeDtypeStruct((LOCAL, 2 * HEAD), low),
        ],
        grid_spec=pltpu.PrefetchScalarGridSpec(
            num_scalar_prefetch=1,
            grid=(LOCAL // tall,),
            in_specs=[
                spec((tall, width), lambda i, p: (jnp.minimum(i, 1), 0)),
                spec((tall, width), lambda i, p: (jnp.maximum(i - 2, 0), 0)),
                once((width, 4 * HEAD), fixed),
                once((1, width), fixed),
                once((1, HEAD), fixed),
                once((1, HEAD), fixed),
                once((LOCAL, HEAD), fixed),
                once((LOCAL, HEAD), fixed),
            ],
            out_specs=[
                spec((tall, width), moving),
                spec((tall, 4 * HEAD), moving),
                spec((tall, HEAD), moving),
                once((LOCAL, 2 * HEAD), fixed),
                once((LOCAL, 2 * HEAD), fixed),
            ],
        ),
        compiler_params=params(52),
        cost_estimate=cost(2 * LOCAL * width * 512, 16 * MIB, hint=H_PROJECT),
    )(place, *rows, weight, gain, gq, gk, cosine, sine)


def turn_back(d, v, c, s, g):
    d = d * c + pltpu.roll(d * s, HEAD // 2, 1)
    r = lax.rsqrt(jnp.mean(v * v, axis=-1, keepdims=True) + epsilon)
    u = v * r
    e = d * g
    before = r * (e - u * jnp.mean(u * e, axis=-1, keepdims=True))
    return before.astype(low), jnp.sum(d * u, axis=0, keepdims=True)


def query_back_kernel(place, raw, cosine, sine, gq, dquery, draw, dgain):
    total = 0.0
    for i in range(8):
        here = pl.ds(i * BLOCK, BLOCK)
        there = pl.ds(pl.multiple_of(place[i] * BLOCK, BLOCK), BLOCK)
        for h in range(2):
            part = slice(h * HEAD, (h + 1) * HEAD)
            draw[here, part], add = turn_back(
                dquery[there, part], raw[here, part], cosine[there], sine[there], gq[...]
            )
            total += add
    dgain[...] = jnp.broadcast_to(total, dgain.shape)


def pair_back_kernel(place, raw, cosine, sine, gk, dpair, later, draw, dgain):
    total = 0.0
    for i in range(8):
        here = pl.ds(i * BLOCK, BLOCK)
        there = pl.ds(pl.multiple_of(place[i] * BLOCK, BLOCK), BLOCK)
        dp = dpair[pl.ds(pl.multiple_of(place[i] * BLOCK + BACK, BLOCK), BLOCK)]
        from_later = later[pl.ds(pl.multiple_of(jnp.maximum(place[i] - 1, 0) * BLOCK, BLOCK), BLOCK)]
        dp = dp + jnp.where(place[i] > 0, from_later.astype(wide), 0.0)
        draw[here, :HEAD], add = turn_back(
            dp[:, :HEAD], raw[here, 2 * HEAD : 3 * HEAD], cosine[there], sine[there], gk[...]
        )
        draw[here, HEAD:] = dp[:, HEAD:].astype(low)
        total += add
    dgain[...] = jnp.broadcast_to(total, dgain.shape)


def heads_back(kernel, place, *inputs):
    return pl.pallas_call(
        kernel,
        out_shape=[
            jax.ShapeDtypeStruct((LOCAL, 2 * HEAD), low),
            jax.ShapeDtypeStruct((8, HEAD), wide),
        ],
        in_specs=[SCALARS] + [WHOLE] * len(inputs),
        out_specs=[WHOLE] * 2,
        compiler_params=params(16),
        cost_estimate=cost(LOCAL * 512 * 10, LOCAL * 512 * 6, hint=H_HEADS_BACK),
    )(place, *inputs)


ROWS = 256


def both_dots(lefts, rights, dims):
    return dot(lefts[0][...], rights[0][...], dims) + dot(lefts[1][...], rights[1][...], dims)


def grads_kernel(*refs):
    lefts, rights, out = refs[:4], refs[4:8], refs[8]
    n = rights[0].shape[1]
    out[:, :n] = both_dots(lefts[:2], rights[:2], (0, 0)).astype(low)
    out[:, n:] = both_dots(lefts[2:], rights[2:], (0, 0)).astype(low)


def grads(lefts, rights):
    depth, rows = lefts[0].shape
    total = rights[0].shape[1] + rights[2].shape[1]
    return pl.pallas_call(
        grads_kernel,
        out_shape=jax.ShapeDtypeStruct((rows, total), low),
        grid=(rows // ROWS,),
        in_specs=[spec((depth, ROWS), lambda i: (0, i))] * 4
        + [once(v.shape, lambda i: (0, 0)) for v in rights],
        out_specs=spec((ROWS, total), lambda i: (i, 0)),
        compiler_params=params(28),
        cost_estimate=cost(
            4 * depth * rows * total, 8 * depth * rows + 2 * total * (rows + depth), hint=H_GRADS
        ),
    )(*lefts, *rights)


def back_kernel(parts, *refs):
    *lefts, right, out_mine, out_away = refs
    turned = right[...].T
    half = LOCAL // 2
    if parts:
        depth = lefts[0].shape[1]
        pick = lambda rows: sum(
            dot(left[rows], turned[k * depth : (k + 1) * depth], (1, 0))
            for k, left in enumerate(lefts)
        )
        mine, away = pick(pl.ds(0, half)), pick(pl.ds(half, half))
    else:
        mine, away = [dot(left[...], turned, (1, 0)) for left in lefts]
    out_away[...] = away.astype(low)
    out_mine[...] = mine.astype(low)


def back_products(lefts, right, at=0, parts=False, hint=1):
    rows = LOCAL // 2
    depth = sum(v.shape[1] for v in lefts) if parts else lefts[0].shape[1]
    width = right.shape[0]
    return pl.pallas_call(
        functools.partial(back_kernel, parts),
        out_shape=[jax.ShapeDtypeStruct((rows, width), low)] * 2,
        grid=(width // ROWS,),
        in_specs=[once(v.shape, lambda i: (0, 0)) for v in lefts]
        + [spec((ROWS, depth), lambda i: (i, at))],
        out_specs=[spec((rows, ROWS), lambda i: (0, i))] * 2,
        compiler_params=params(20),
        cost_estimate=cost(
            4 * rows * depth * width, 2 * width * (depth + 2 * rows), hint=hint
        ),
    )(*lefts, right)


def adam_kernel(columns, flipped, rates, extras, *refs):
    grad = refs[0]
    for k, (turn, rate) in enumerate(zip(flipped, rates)):
        weight, first, second = refs[1 + 3 * k : 4 + 3 * k]
        outs = refs[1 + extras + 3 * (len(rates) + k) : 4 + extras + 3 * (len(rates) + k)]
        g = [grad[:BLOCK, at : at + n] for at, n in columns[k]]
        g = (jnp.concatenate(g, axis=1) if len(g) > 1 else g[0]).astype(wide)
        if turn:
            g = g.T
        for out, value in zip(outs, adam(weight[...], first[...], second[...], g, rate, weight_decay)):
            out[...] = value
    for k in range(extras):
        refs[k - extras][...] = refs[1 + 3 * len(rates) + k][...]


def adam_weights(grad, columns, weights, flipped, rates, extras=()):
    states = [v for group in weights for v in group] + list(extras)
    out = pl.pallas_call(
        functools.partial(adam_kernel, columns, flipped, rates, len(extras)),
        out_shape=[jax.ShapeDtypeStruct(v.shape, v.dtype) for v in states],
        in_specs=[WHOLE] * (1 + len(states)),
        out_specs=[WHOLE] * len(states),
        compiler_params=params(24),
        cost_estimate=cost(20 * grad.size, 26 * grad.size, hint=H_ADAM),
    )(grad, *states)
    return [tuple(out[3 * k : 3 * k + 3]) for k in range(len(weights))] + list(out[3 * len(weights) :])


PART = 2 * HEAD
TALL = BLOCK + 16


def project_grad(normed, draw, weight, gain, dgain):
    project = dot(normed[...], draw[...], (0, 0))
    product = (project * weight[...].astype(wide)).astype(low)
    dgain[...] = dot(jnp.ones((8, PART), low), product, (1, 1)) / gain[...]
    return project.astype(low)


def query_grads_kernel(spot, normed, draw, weight, gain, mine, away, attended, *outs):
    *outs, dgain = outs
    project = project_grad(normed, draw, weight, gain, dgain)
    half = LOCAL // 2
    output = dot(mine[...], attended[:half], (0, 0)) + dot(away[...], attended[half:], (0, 0))
    output = output.astype(low)
    i = pl.program_id(0)
    steps = lax.rem(i // 2 - spot[2] + 4, 4)
    for k, out in enumerate(outs):

        @pl.when(steps == k)
        def _():
            for j in range(2):
                rows = slice(j * BLOCK, (j + 1) * BLOCK)
                out[j ^ spot[0], i % 2 ^ spot[1], :, :PART] = project[rows]
                out[j ^ spot[0], i % 2 ^ spot[1], :, PART:] = output[rows]


def pair_grads_kernel(spot, normed, draw, weight, gain, out, dgain):
    project = project_grad(normed, draw, weight, gain, dgain)
    for j in range(2):
        out[0, j ^ spot[0], 0, :BLOCK] = project[j * BLOCK : (j + 1) * BLOCK]


def first_grads(spot, normed, draw, weight, gain, part, out, block, others=()):
    whole = lambda i, s: (0, 0)
    columns = lambda i, s: (0, i)
    rows = 2 * BLOCK
    return pl.pallas_call(
        query_grads_kernel if others else pair_grads_kernel,
        out_shape=[jax.ShapeDtypeStruct(v, low) for v in out]
        + [jax.ShapeDtypeStruct((8, 16 * BLOCK), wide)],
        grid_spec=pltpu.PrefetchScalarGridSpec(
            num_scalar_prefetch=1,
            grid=(8,),
            in_specs=[
                spec((LOCAL, rows), columns),
                once((LOCAL, PART), whole),
                spec((rows, PART), lambda i, s: (i, part)),
                spec((1, rows), columns),
            ]
            + [spec((LOCAL // 2, rows), columns)] * len(others[:2])
            + [once((LOCAL, PART), whole)] * len(others[2:]),
            out_specs=[spec(*v) for v in block] + [spec((8, rows), columns)],
        ),
        compiler_params=params(24),
        cost_estimate=cost(2 * LOCAL * 2048 * 256, 8 * MIB, hint=H_FIRST),
    )(spot, normed, draw, weight, gain, *others)


def query_grads(spot, normed, draw, weight, gain, dmiddle, attended):
    shape = (2, 2, BLOCK, 2 * PART)
    outs = [shape] * 4, [(shape, lambda i, s: (0, 0, 0, 0))] * 4
    *left, dgain = first_grads(
        spot, normed, draw, weight, gain, 0, *outs, (*dmiddle, attended)
    )
    return left, dgain


def pair_grads(spot, normed, draw, weight, gain):
    place = lambda i, s: (lax.rem(i // 2 - s[2] + 4, 4), 0, i % 2 ^ s[1], 0, 0)
    outs = [(4, 2, 2, TALL, PART)], [((1, 2, 1, TALL, PART), place)]
    return first_grads(spot, normed, draw, weight, gain, 1, *outs)


SCALE = HEAD ** (-0.5)


def allowed(query_ids, key_ids, start):
    keys = key_ids[:, pl.ds(start, WINDOW)]
    row = lax.broadcasted_iota(jnp.int32, (QUERIES, WINDOW), 0)
    column = lax.broadcasted_iota(jnp.int32, (QUERIES, WINDOW), 1)
    return (query_ids[...] == keys) & (column <= row + BACK)


def attend_kernel(turn, core, query, pair, query_ids, key_ids, out, logsum):
    i = pl.program_id(0)
    start = pl.multiple_of(i * QUERIES, QUERIES)
    mask = allowed(query_ids, key_ids, start)
    logs = []
    for h in range(2):
        part = slice(h * HEAD, (h + 1) * HEAD)
        scores = dot(query[:, part], pair[pl.ds(start, WINDOW), :HEAD], (1, 1)) * SCALE
        scores = jnp.where(mask, scores, -1e30)
        top = jnp.max(scores, axis=-1, keepdims=True)
        unnormed = jnp.exp(scores - top)
        total = jnp.sum(unnormed, axis=-1, keepdims=True)
        probs = (unnormed * (1.0 / total)).astype(low)
        result = dot(probs, pair[pl.ds(start, WINDOW), HEAD:], (1, 0)).astype(low)
        for j in range(2):
            out[j ^ core[0], 0, :, part] = result[j * BLOCK : (j + 1) * BLOCK]
        logs.append(top + jnp.log(total))
    lane = lax.broadcasted_iota(jnp.int32, (QUERIES, HEAD), 1)
    logsum[...] = jnp.where(lane < HEAD // 2, logs[0], logs[1])


def attend(turn, core, query, pair, query_ids, key_ids):
    rows = lambda i, t, c: (i, 0)
    whole = lambda i, t, c: (0, 0)
    keys = BACK + LOCAL
    return pl.pallas_call(
        attend_kernel,
        out_shape=[
            jax.ShapeDtypeStruct((2, 4, BLOCK, 2 * HEAD), low),
            jax.ShapeDtypeStruct((LOCAL, HEAD), wide),
        ],
        grid_spec=pltpu.PrefetchScalarGridSpec(
            num_scalar_prefetch=2,
            grid=(LOCAL // QUERIES,),
            in_specs=[
                spec((QUERIES, 2 * HEAD), rows),
                once((keys, 2 * HEAD), whole),
                spec((QUERIES, 1), rows),
                spec((1, keys), whole),
            ],
            out_specs=[
                spec((2, 1, BLOCK, 2 * HEAD), lambda i, t, c: (0, t[i], 0, 0)),
                spec((QUERIES, HEAD), rows),
            ],
        ),
        compiler_params=params(24),
        cost_estimate=cost(
            8 * LOCAL * WINDOW * HEAD, 4 * LOCAL * 512, 2 * LOCAL * WINDOW, hint=H_ATTEND
        ),
    )(turn, core, query, pair, query_ids, key_ids)


def attend_back_kernel(
    turn, core, query, pair, query_ids, key_ids, grad, logsum, dquery, dpair
):
    i = pl.program_id(0)

    @pl.when(i == 0)
    def _():
        dpair[...] = jnp.zeros_like(dpair)

    start = pl.multiple_of(i * QUERIES, QUERIES)
    window = pl.ds(start, WINDOW)
    mask = allowed(query_ids, key_ids, start)
    dkey, dvalue = None, None
    for h in range(2):
        part = slice(h * HEAD, (h + 1) * HEAD)
        q = query[:, part]
        g = jnp.concatenate([grad[j ^ core[0], 0, :, part] for j in range(2)], axis=0)
        scores = dot(q, pair[window, :HEAD], (1, 1)) * SCALE
        probs = jnp.where(mask, jnp.exp(scores - logsum[:, h * 64 : h * 64 + 1]), 0.0)
        dprobs = dot(g, pair[window, HEAD:], (1, 1))
        inner = jnp.sum(probs * dprobs, axis=-1, keepdims=True)
        dscores = (probs * (dprobs - inner)).astype(low)
        dquery[:, part] = dot(dscores, pair[window, :HEAD], (1, 0)) * SCALE
        dv = dot(probs.astype(low), g, (0, 0))
        dk = dot(dscores, q, (0, 0))
        dkey = dk if dkey is None else dkey + dk
        dvalue = dv if dvalue is None else dvalue + dv
    dpair[window, :HEAD] += dkey * SCALE
    dpair[window, HEAD:] += dvalue


def attend_back(turn, core, query, pair, query_ids, key_ids, grad, logsum):
    rows = lambda i, t, c: (i, 0)
    whole = lambda i, t, c: (0, 0)
    keys = BACK + LOCAL
    return pl.pallas_call(
        attend_back_kernel,
        out_shape=[
            jax.ShapeDtypeStruct((LOCAL, 2 * HEAD), wide),
            jax.ShapeDtypeStruct((keys, 2 * HEAD), wide),
        ],
        grid_spec=pltpu.PrefetchScalarGridSpec(
            num_scalar_prefetch=2,
            grid=(LOCAL // QUERIES,),
            in_specs=[
                spec((QUERIES, 2 * HEAD), rows),
                once((keys, 2 * HEAD), whole),
                spec((QUERIES, 1), rows),
                spec((1, keys), whole),
                spec((2, 1, BLOCK, 2 * HEAD), lambda i, t, c: (0, t[i], 0, 0)),
                spec((QUERIES, HEAD), rows),
            ],
            out_specs=[spec((QUERIES, 2 * HEAD), rows), once((keys, 2 * HEAD), whole)],
        ),
        compiler_params=params(28),
        cost_estimate=cost(
            20 * LOCAL * WINDOW * HEAD, 8 * LOCAL * 512, 2 * LOCAL * WINDOW, hint=H_ATTEND_BACK
        ),
    )(turn, core, query, pair, query_ids, key_ids, grad, logsum)


def per_device(
    inputs,
    cotangent,
    document_index,
    positions,
    gains,
    gains_first,
    gains_second,
    project_weight,
    project_first,
    project_second,
    output_weight,
    output_first,
    output_second,
    expand_weight,
    expand_first,
    expand_second,
    shrink_weight,
    shrink_first,
    shrink_second,
):
    core, x = lax.axis_index("core"), lax.axis_index("x")
    half, yl = lax.axis_index("yh"), lax.axis_index("yl")
    width = inputs.shape[-1]
    qkv = project_weight.shape[1]
    ff = shrink_weight.shape[0]
    at_home = core == yl
    steps = jnp.arange(8, dtype=jnp.int32)
    place = lax.rem(x - steps % 4 + 4, 4) * 2 + (core ^ (steps // 4))
    turn = lax.rem(x - jnp.arange(4, dtype=jnp.int32) + 4, 4)
    core_of = core.reshape(1).astype(jnp.int32)
    flag = at_home.astype(jnp.int32).reshape(1)

    marks = jnp.stack([document_index[0], positions[0] // 32, positions[0] % 32])
    marks = jnp.pad(marks.astype(low), ((0, 13), (0, 0)))
    message = trade(jnp.concatenate([inputs[0], marks], axis=0))
    rows = message[:BLOCK]
    marks = message[BLOCK:].astype(jnp.int32)
    ids, places = marks[0], marks[1] * 32 + marks[2]

    gain_block = jnp.pad(gains.astype(low), (0, BLOCK * BLOCK - gains.shape[0])).reshape(BLOCK, BLOCK)
    first_shard = jnp.concatenate(
        [project_weight.astype(low), output_weight.astype(low).T, gain_block], axis=1
    )
    second_shard = jnp.concatenate([expand_weight.astype(low), shrink_weight.astype(low).T], axis=1)
    first_all = lax.all_gather(to_group(first_shard), GROUP, axis=0, tiled=True)
    second_shard = to_group(after(second_shard, message))
    rows_all = gather_rows(rows, second_shard)
    second_all = lax.all_gather(after(second_shard, first_all), GROUP, axis=0, tiled=True)
    project_all = first_all[:, :qkv]
    output_all = first_all[:, qkv : qkv + 2 * HEAD]
    expand_all = second_all[:, : 2 * ff]
    shrink_all = second_all[:, 2 * ff :]
    gain_all = first_all.reshape(16, BLOCK, -1)[:, :3, qkv + 2 * HEAD :].reshape(16, 3 * BLOCK)
    gain_all = gain_all[:, : gains.shape[0]].reshape(-1).astype(wide)
    gain_one = gain_all[:width]
    gain_two = gain_all[width : 2 * width]
    gain_query = gain_all[2 * width : 2 * width + HEAD].reshape(1, HEAD)
    gain_key = gain_all[2 * width + HEAD :].reshape(1, HEAD)

    ids_here = lax.dynamic_slice_in_dim(ids, half * LOCAL, LOCAL)
    places_here = lax.dynamic_slice_in_dim(places, half * LOCAL, LOCAL)
    ids_keys = jnp.where(
        half == 0,
        jnp.concatenate([jnp.full((BACK,), -1, jnp.int32), ids[:LOCAL]]),
        ids[LOCAL - BACK :],
    )
    query_ids, key_ids = ids_here.reshape(-1, 1), ids_keys.reshape(1, -1)
    frequency = jnp.exp(jnp.arange(HEAD // 2, dtype=wide) * (-2.0 * math.log(theta) / HEAD))
    angle = places_here.astype(wide)[:, None] * frequency
    cosine, sine = jnp.cos(angle), jnp.sin(angle)
    cosine = jnp.concatenate([cosine, cosine], axis=1)
    sine = jnp.concatenate([-sine, sine], axis=1)

    values = rows.astype(wide)
    normed, raw, scale, query, pair = project(
        place, rows_all, first_all, gain_one.reshape(1, -1), gain_query, gain_key, cosine, sine
    )
    earlier = move(pair[LOCAL - BACK :], "yh", [(0, 1)])
    back_all = choose(place, flag, cotangent[0], other_core(cotangent[0]))
    back = [back_all[: LOCAL // 2], back_all[LOCAL // 2 :]]
    pair_all = jnp.concatenate([after(earlier, back_all), pair], axis=0)
    attended, logsum = attend(turn, core_of, query, pair_all, query_ids, key_ids)
    attended = attended.reshape(LOCAL, 2 * HEAD)
    mine = dot(attended[: LOCAL // 2], output_all, (1, 1)).astype(low)
    away = dot(attended[LOCAL // 2 :], output_all, (1, 1)).astype(low)
    middle = values + chip_sum(core_sum(mine, away))

    normed_two = gather_rows(rms_norm(middle, gain_two).astype(low))
    hidden, dexpanded = [], []
    for v, dy in zip(normed_two, back):
        expanded = dot(v, expand_all, (1, 0))
        activated, pull_act = jax.vjp(swiglu, expanded[:, :ff], expanded[:, ff:])
        hidden.append(activated.astype(low))
        dgate, dup = pull_act(dot(dy, shrink_all, (1, 0)))
        dexpanded.append(jnp.concatenate([dgate, dup], axis=1).astype(low))
    both_two = core_sum(*back_products(dexpanded, second_all))
    drows_two = chip_sum(both_two)
    second_grads = grads(
        [*after(tuple(normed_two), both_two), *back], [*dexpanded, *hidden]
    )
    second_red = lax.psum_scatter(second_grads, GROUP, scatter_dimension=0, tiled=True)
    drows_two = after(drows_two, second_grads)

    _, pull_two = jax.vjp(rms_norm, middle, gain_two)
    dmiddle, dgain_two = pull_two(drows_two)
    dmiddle = back[0][:BLOCK].astype(wide) + dmiddle
    shrunk = back_products(after(tuple(hidden), second_grads), second_all, at=2, hint=0)
    shrunk = shrunk[0], other_core(shrunk[1])
    dmiddle_all = gather_rows(dmiddle.astype(low))
    dmiddle_all = after(tuple(dmiddle_all), *shrunk)
    shrunk = chip_blocks(*after(shrunk, dmiddle_all), x)
    mlp = lax.all_to_all(shrunk, "x", 0, 0, tiled=True)
    dattended = jnp.stack([dot(v, output_all, (1, 0)).astype(low) for v in dmiddle_all])
    dquery, dpair = attend_back(
        turn,
        core_of,
        query,
        pair_all,
        query_ids,
        key_ids,
        dattended.reshape(2, 4, BLOCK, 2 * HEAD),
        logsum,
    )
    later = move(dpair[:BACK].astype(low), "yh", [(1, 0)])
    draw_query, dgain_query = heads_back(
        query_back_kernel, place, raw, cosine, sine, gain_query, dquery
    )
    spot = jnp.stack([half, yl, lax.axis_index("z")]).astype(jnp.int32)
    gain_row = gain_one.reshape(1, -1)
    left, dgain_one = query_grads(
        spot, normed, draw_query, first_all, gain_row, dmiddle_all, attended
    )
    left_grads = left
    left = sum_z(left)
    mlp = jnp.sum(after(mlp, *left_grads).astype(wide), axis=0)
    later = after(later, mlp)
    draw_pair, dgain_key = heads_back(
        pair_back_kernel, place, raw, cosine, sine, gain_key, dpair, later
    )
    outputs = trade((middle + after(mlp, draw_pair)).astype(low))

    pair_right, dgain_rest = pair_grads(spot, normed, draw_pair, first_all, gain_row)
    dgains = jnp.concatenate([(dgain_one + dgain_rest)[0], dgain_two, dgain_query[0], dgain_key[0]])
    dgains = jnp.pad(dgains.reshape(-1, BLOCK), ((0, 6), (0, 0)))
    dgains = dgains + other_core(dgains)
    dgains = dgains + shift(dgains, 1) + shift(dgains, 2) + shift(dgains, 3)
    dgains = dgains[:-6].astype(low).reshape(4, 2, 2, 1, -1)
    dgains = jnp.where(half == 0, dgains, dgains[:, :, ::-1])
    dgains = jnp.where(yl == 0, dgains, dgains[:, ::-1]).transpose(0, 2, 1, 3, 4)
    dgains = jnp.roll(dgains, -lax.axis_index("z"), axis=0)
    over = dgains[..., PART:]
    dgains = jnp.concatenate([dgains[..., :PART], jnp.pad(over, ((0, 0),) * 4 + ((0, PART - over.shape[-1]),))], axis=3)
    dgains = jnp.pad(dgains, ((0, 0), (0, 0), (0, 0), (0, 14), (0, 0)))
    right = lax.dynamic_update_slice(pair_right, dgains, (0, 0, 0, BLOCK, 0))
    second_red = to_owner(after(second_red, draw_pair))
    mine, away = back_products(
        after((draw_query, draw_pair), dgain_rest, second_red), first_all, parts=True, hint=H_BACK
    )
    right = sum_z(right)
    drows_one = chip_sum_at_once(chip_blocks(mine, other_core(away), x))
    expand_new, shrink_new = adam_weights(
        second_red,
        (((0, 2 * ff),), ((2 * ff, ff),)),
        [(expand_weight, expand_first, expand_second), (shrink_weight, shrink_first, shrink_second)],
        (False, True),
        (0.05, 0.03),
    )
    left = after(left, outputs)
    both = jnp.concatenate([jnp.pad(left, ((0, 0), (0, 0), (0, 16), (0, 0))), right], axis=3)
    first_red = sum_flips(both.astype(low))

    _, pull_one = jax.vjp(rms_norm, values, gain_one)
    dvalues, _ = pull_one(drows_one)
    input_grad = trade((dmiddle + dvalues).astype(low))

    dgains = first_red[BLOCK : BLOCK + 8, 2 * PART :]
    project_new, output_new, outputs, input_grad = adam_weights(
        first_red,
        (((0, PART), (2 * PART, PART)), ((PART, PART),)),
        [(project_weight, project_first, project_second), (output_weight, output_first, output_second)],
        (False, True),
        (0.05, 0.4),
        (outputs, input_grad),
    )
    dgains = dgains[:2].reshape(-1)[: gains.shape[0]]
    return (
        outputs[None],
        input_grad[None],
        *adam(gains, gains_first, gains_second, dgains, 0.5, 0.0),
        *project_new,
        *output_new,
        *expand_new,
        *shrink_new,
    )


def solution(mesh):
    fine = Mesh(mesh.devices.reshape(4, 2, 2, 4, 2), ("z", "core", "yh", "x", "yl"))
    tokens = P(("z", "core"), ("yh", "x", "yl"), None)
    marks = P(("z", "core"), None)
    gain = P(("z", "core", "yh"))
    tall = P(("z", "core", "yh"), ("x", "yl"))
    flat = P(("x", "yl"), ("z", "core", "yh"))
    in_specs = (
        tokens,
        P(("z", "core"), "yh", None),
        marks,
        marks,
        *[gain] * 3,
        *[tall] * 3,
        *[flat] * 3,
        *[tall] * 3,
        *[flat] * 3,
    )
    out_specs = (
        tokens,
        tokens,
        *[gain] * 3,
        *[tall] * 3,
        *[flat] * 3,
        *[tall] * 3,
        *[flat] * 3,
    )
    return jax.shard_map(
        per_device, mesh=fine, in_specs=in_specs, out_specs=out_specs, check_vma=False
    )
```
